32 devices in a mesh: replica: 8 (over z, core), group: 4 (over y, x).
Axes of the slice: x: 2, y: 2, z: 4, core: 2. Of those that a mesh axis runs over, the one named last changes fastest.
Arguments:
- tokens: bfloat16 [4, 8192, 768], P('group', 'replica'), may hold values from -6 to 6
- cotangent: bfloat16 [4, 8192, 768], P('group', 'replica'), may hold values from -6 to 6
- lengths: int32 [4, 16], P('group'), may hold values from 256 to 768, as said below
- dealing: int32 [4, 16], P('group'), may hold values from 0 to 15, as said below
- offsets: int32 [4, 8, 2], P('group'), may hold values from 0 to 768, as said below
- attn_gain: float32 [768], P('group'), may hold values from 0.1 to 1.9
- qkv_weight: float32 [768, 2304], P('group'), may hold values from -0.21875 to 0.21875
- out_weight: float32 [768, 768], P('group'), may hold values from -0.875 to 0.875
- mlp_gain: float32 [768], P('group'), may hold values from 0.1 to 1.9
- in_weight: float32 [768, 2304], P('group'), may hold values from -0.21875 to 0.21875
- down_weight: float32 [1152, 768], P('group'), may hold values from -0.1875 to 0.1875
Outputs:
- output: bfloat16 [4, 8192, 768], P('group', 'replica')
- input_grad: bfloat16 [4, 8192, 768], P('group', 'replica')
- attn_gain_grad: float32 [768], P('group')
- qkv_grad: float32 [768, 2304], P('group')
- out_grad: float32 [768, 768], P('group')
- mlp_gain_grad: float32 [768], P('group')
- in_grad: float32 [768, 2304], P('group')
- down_grad: float32 [1152, 768], P('group')
The draws below stay inside these ranges and needn't reach their ends.
Inputs may be any that keep to these rules, and one draw needn't show every extreme that they name: `lengths`: the 16 sequences of a column lie end to end over its 8192 tokens; the two sequences dealt to one replica index hold 1024 tokens together. `dealing`: for each column a permutation of its sequences: entry k is the given-order number of the sequence that is k-th in dealt order; replica index r takes dealt sequences 2 * r to 2 * r + 1. `offsets`: exclusive running sums of the lengths of each replica index's dealt sequences, in dealt order.
All inputs are finite; a program needn't handle non-finite values.
Results may differ from the reference program's by a relative error of at most 0.02.
Values may be sent and summed in bfloat16 or wider, within the bound.
No kernel may reach another device: no remote copies, remote signals or barrier semaphores. Data moves between devices by JAX's collectives and lax.ppermute only.
A program may use at most 256 MiB of HBM per device.

```python
import math
import jax
import jax.numpy as jnp
from jax import lax

D = 768
HEADS = 12
HEAD_DIM = 64
FF = 1152
TOK_DEV = 1024
MINLEN = 256
TOK_COL = 8192
SEQ_COL = 16
N_REPLICA = 8
N_GROUP = 4


def dealt_plan(key):
    base = jax.random.fold_in(key, 11)
    first_key, forced_key, order_key = jax.random.split(base, 3)
    first_len = jax.random.randint(first_key, (N_GROUP, N_REPLICA), MINLEN, TOK_DEV - MINLEN + 1)
    forced = jax.random.randint(forced_key, (N_GROUP, 1), 0, N_REPLICA)
    columns = jnp.arange(N_REPLICA)[None, :]
    first_len = jnp.where(columns == forced, MINLEN, first_len)
    first_len = jnp.where(columns == (forced + 1) % N_REPLICA, TOK_DEV - MINLEN, first_len)
    dealt_len = jnp.stack([first_len, TOK_DEV - first_len], axis=-1).reshape(N_GROUP, SEQ_COL)
    orders = jax.vmap(lambda sub_key: jax.random.permutation(sub_key, SEQ_COL))(jax.random.split(order_key, N_GROUP))
    inverse = jnp.argsort(orders, axis=-1)
    given_len = jnp.take_along_axis(dealt_len, inverse, axis=-1)
    starts = jnp.stack([jnp.zeros_like(first_len), first_len], axis=-1)
    return (given_len.astype(jnp.int32), orders.astype(jnp.int32), starts.astype(jnp.int32))


def draw_lengths(key, part):
    return dealt_plan(key)[0]


def draw_dealing(key, part):
    return dealt_plan(key)[1]


def draw_offsets(key, part):
    return dealt_plan(key)[2]


def shard_levels(rng, shape, cuts, least, top_value):
    gain, own = 1.0, jax.random.fold_in(rng, 6)
    for dim, shards_of in cuts:
        heights = jnp.exp(jax.random.uniform(jax.random.fold_in(own, dim), (shards_of,), jnp.float32, least / len(cuts), top_value / len(cuts)))
        gain = gain * jnp.repeat(heights, shape[dim] // shards_of).reshape([-1 if axis == dim else 1 for axis in range(len(shape))])
    return gain


def normal_values(rng, dims, scale, most, cuts=(), kind=jnp.bfloat16):
    values = scale * jax.random.normal(rng, dims, jnp.float32)
    if cuts:
        values = values * shard_levels(rng, dims, cuts, -0.22, 0.18)
    return jnp.clip(values, -most, most).astype(kind)


def setup_inputs(seed: int = 0) -> dict:
    arg_keys = jax.random.split(jax.random.key(seed), 12)
    return {
        "tokens": normal_values(arg_keys[0], (N_GROUP, TOK_COL, D), 1.0, 6.0, ((0, 4), (1, 8))),
        "cotangent": normal_values(arg_keys[1], (N_GROUP, TOK_COL, D), 1.0, 6.0, ((0, 4), (1, 8))),
        "lengths": draw_lengths(jax.random.fold_in(arg_keys[11], 71), 0),
        "dealing": draw_dealing(jax.random.fold_in(arg_keys[11], 71), 0),
        "offsets": draw_offsets(jax.random.fold_in(arg_keys[11], 71), 0),
        "attn_gain": jnp.clip(1.0 + 0.18 * jax.random.normal(arg_keys[5], (D,), jnp.float32), 0.1, 1.9),
        "qkv_weight": normal_values(arg_keys[6], (D, 3 * D), D ** -0.5, 0.21875, ((0, 4),), jnp.float32),
        "out_weight": normal_values(arg_keys[7], (D, D), (D // 16) ** -0.5, 0.875, ((0, 4),), jnp.float32),
        "mlp_gain": jnp.clip(1.0 + 0.18 * jax.random.normal(arg_keys[8], (D,), jnp.float32), 0.1, 1.9),
        "in_weight": normal_values(arg_keys[9], (D, 2 * FF), D ** -0.5, 0.21875, ((0, 4),), jnp.float32),
        "down_weight": normal_values(arg_keys[10], (FF, D), FF ** -0.5, 0.1875, ((0, 4),), jnp.float32),
    }


@jax.custom_vjp
def low(v):
    return lax.optimization_barrier(v.astype(jnp.bfloat16)).astype(jnp.float32)

@jax.custom_vjp
def low_back(v):
    return v

def low_keep(v):
    return (low(v), None)

def low_pass(kept, grad):
    return (grad,)

def back_keep(v):
    return (v, None)

def back_low(kept, grad):
    return (low(grad),)
low.defvjp(low_keep, low_pass)
low_back.defvjp(back_keep, back_low)
epsilon = 1e-05
big_negative = -1e+30
rope_base = 160000.0

def column_starts(lengths):
    return (jnp.cumsum(lengths) - lengths).astype(jnp.int32)

def dealt_map(lengths, dealing, offsets, replica_index, tok_rows):
    seq_count = lengths.shape[0]
    per_device = offsets.shape[1]
    starts = column_starts(lengths)
    slot_ids = jnp.arange(tok_rows, dtype=jnp.int32)
    own_starts = lax.dynamic_index_in_dim(offsets, replica_index, 0, keepdims=False)
    segment = lax.optimization_barrier(jnp.sum((slot_ids[:, None] >= own_starts[None, 1:]).astype(jnp.int32), axis=1)).astype(jnp.int32)
    choose = segment[:, None] == jnp.arange(per_device, dtype=jnp.int32)[None, :]
    begin_at = lax.optimization_barrier(jnp.sum(jnp.where(choose, own_starts[None, :], 0), axis=1)).astype(jnp.int32)
    positions = (slot_ids - begin_at).astype(jnp.int32)
    dealt = (replica_index * per_device + segment).astype(jnp.int32)
    seq_range = jnp.arange(seq_count, dtype=jnp.int32)
    dealt_hits = dealt[:, None] == seq_range[None, :]
    given = lax.optimization_barrier(jnp.sum(jnp.where(dealt_hits, dealing[None, :], 0), axis=1)).astype(jnp.int32)
    found_seq = given[:, None] == seq_range[None, :]
    first_at = lax.optimization_barrier(jnp.sum(jnp.where(found_seq, starts[None, :], 0), axis=1)).astype(jnp.int32)
    source = jnp.clip(first_at + positions, 0, tok_rows * offsets.shape[0] - 1).astype(jnp.int32)
    return (source, segment, positions)

def given_map(lengths, dealing, offsets, column_pos, tok_rows):
    seq_count = lengths.shape[0]
    per_device = offsets.shape[1]
    starts = column_starts(lengths)
    seq_range = jnp.arange(seq_count, dtype=jnp.int32)
    seq_id = lax.optimization_barrier(jnp.sum((column_pos[:, None] >= starts[None, 1:]).astype(jnp.int32), axis=1)).astype(jnp.int32)
    found_seq = seq_id[:, None] == seq_range[None, :]
    first_at = lax.optimization_barrier(jnp.sum(jnp.where(found_seq, starts[None, :], 0), axis=1)).astype(jnp.int32)
    positions = column_pos - first_at
    matches = dealing[None, :] == seq_id[:, None]
    dealt = lax.optimization_barrier(jnp.sum(jnp.where(matches, seq_range[None, :], 0), axis=1)).astype(jnp.int32)
    flat_starts = offsets.reshape(-1)
    dealt_hits = dealt[:, None] == seq_range[None, :]
    begin_at = lax.optimization_barrier(jnp.sum(jnp.where(dealt_hits, flat_starts[None, :], 0), axis=1)).astype(jnp.int32)
    target = dealt // per_device * tok_rows + begin_at + positions
    return jnp.clip(target, 0, tok_rows * offsets.shape[0] - 1).astype(jnp.int32)

def rotary(values, positions, head_count, head_dim):
    tok_rows = values.shape[0]
    half_dim = head_dim // 2
    frequency = jnp.exp(-(jnp.arange(half_dim, dtype=jnp.float32) * (2.0 / head_dim)) * math.log(rope_base))
    angles = positions.astype(jnp.float32)[:, None] * frequency[None, :]
    cosine = jnp.cos(angles)[:, None, :]
    sine_part = jnp.sin(angles)[:, None, :]
    shaped = values.reshape(tok_rows, head_count, head_dim)
    lower_half = shaped[..., :half_dim]
    upper_half = shaped[..., half_dim:]
    turned = jnp.concatenate([lower_half * cosine - upper_half * sine_part, upper_half * cosine + lower_half * sine_part], axis=-1)
    return turned.reshape(tok_rows, head_count * head_dim)

def layer_norm(values, gain_vec):
    row_mean = lax.optimization_barrier(jnp.mean(values, axis=-1, keepdims=True))
    centred = values - row_mean
    spread = lax.optimization_barrier(jnp.mean(centred * centred, axis=-1, keepdims=True))
    return centred * lax.rsqrt(spread + epsilon) * gain_vec

def matmul(left, right):
    return jnp.dot(left, right, precision=lax.Precision.HIGHEST)

def attend_block(queries, seg_query, key_heads, value_heads, seg_keys):
    score_scale = HEAD_DIM ** (-0.5)
    scores = jnp.einsum('qhd,khd->hqk', queries, key_heads, precision=lax.Precision.HIGHEST) * score_scale
    scores = low_back(scores)
    same_seq = seg_query[:, None] == seg_keys[None, :]
    masked = jnp.where(same_seq[None], scores, big_negative)
    row_top = lax.optimization_barrier(jnp.max(masked, axis=-1, keepdims=True))
    exponent = jnp.exp(masked - row_top)
    row_total = lax.optimization_barrier(jnp.sum(exponent, axis=-1, keepdims=True))
    weights_soft = low(exponent / row_total)
    attended = jnp.einsum('hqk,khd->qhd', weights_soft, value_heads, precision=lax.Precision.HIGHEST)
    return low(low_back(attended))

def layer(rows_in, segment, positions, weights):
    gain_one, w_qkv, w_out, gain_two, w_in, w_down = weights
    tok_rows, model_width = rows_in.shape
    normed = low(layer_norm(rows_in, gain_one))
    mixed_proj = low_back(matmul(normed, w_qkv))
    queries = low(rotary(mixed_proj[:, :model_width], positions, HEADS, HEAD_DIM)).reshape(tok_rows, HEADS, HEAD_DIM)
    key_heads = low(rotary(mixed_proj[:, model_width:2 * model_width], positions, HEADS, HEAD_DIM)).reshape(tok_rows, HEADS, HEAD_DIM)
    value_heads = low(mixed_proj[:, 2 * model_width:]).reshape(tok_rows, HEADS, HEAD_DIM)
    block_rows = min(512, tok_rows)
    block_count = tok_rows // block_rows
    query_blocks = queries.reshape(block_count, block_rows, HEADS, HEAD_DIM)
    seg_blocks = segment.reshape(block_count, block_rows)

    def one_block(pair_item):
        return attend_block(pair_item[0], pair_item[1], key_heads, value_heads, segment)
    attended = lax.map(jax.checkpoint(one_block), (query_blocks, seg_blocks)).reshape(tok_rows, model_width)
    branch = low_back(matmul(attended, w_out))
    middle = rows_in + branch
    normed_two = low(layer_norm(middle, gain_two))
    lifted = low_back(matmul(normed_two, w_in))
    hidden = low(jax.nn.gelu(lifted[:, :FF], approximate=False) * lifted[:, FF:])
    return middle + low_back(matmul(hidden, w_down))

def reference(tokens, cotangent, lengths, dealing, offsets, attn_gain, qkv_weight, out_weight, mlp_gain, in_weight, down_weight):
    replicas = jnp.arange(N_REPLICA, dtype=jnp.int32)

    def column_plan(col_lengths, col_dealing, col_offsets):
        source, segment, positions = jax.vmap(lambda replica_index: dealt_map(col_lengths, col_dealing, col_offsets, replica_index, TOK_DEV))(replicas)
        target = given_map(col_lengths, col_dealing, col_offsets, jnp.arange(TOK_COL, dtype=jnp.int32), TOK_DEV)
        return (source, segment, positions, target)
    source, segment, positions, target = jax.vmap(column_plan)(lengths, dealing, offsets)
    seg_flat = segment.reshape(N_GROUP * N_REPLICA, TOK_DEV)
    pos_flat = positions.reshape(N_GROUP * N_REPLICA, TOK_DEV)

    def forward(inputs, gain_one, w_qkv, w_out, gain_two, w_in, w_down):
        weights = (low(gain_one), low(w_qkv), low(w_out), low(gain_two), low(w_in), low(w_down))
        dealt = jax.vmap(lambda col_rows, col_source: col_rows[col_source])(inputs, source.reshape(N_GROUP, TOK_COL))
        dealt = dealt.reshape(N_GROUP * N_REPLICA, TOK_DEV, inputs.shape[2])

        def run_block(rows_in, seg_block, pos_block):
            return layer(rows_in, seg_block, pos_block, weights)
        checked = jax.checkpoint(run_block)

        def scan_step(carry, scan_item):
            return (carry, checked(scan_item[0], scan_item[1], scan_item[2]))
        _, results = lax.scan(scan_step, jnp.zeros((), jnp.float32), (dealt, seg_flat, pos_flat))
        results = results.reshape(N_GROUP, TOK_COL, inputs.shape[2])
        return jax.vmap(lambda col_rows, col_target: col_rows[col_target])(results, target)
    floats = (tokens.astype(jnp.float32), attn_gain, qkv_weight, out_weight, mlp_gain, in_weight, down_weight)
    result, pullback = jax.vjp(forward, *floats)
    grads = pullback(cotangent.astype(jnp.float32))
    return (result.astype(jnp.bfloat16), grads[0].astype(jnp.bfloat16), grads[1], grads[2], grads[3], grads[4], grads[5], grads[6])
```

```python
import functools
import math

import jax
import jax.numpy as jnp
from jax import lax
from jax.experimental import pallas as pl
from jax.experimental.pallas import tpu as pltpu
from jax.sharding import PartitionSpec as P

HEADS = 12
HEAD_DIM = 64
LANES = 128
HALO = 768
RB = 256
QB = 128
KB = 256
EPS = 1e-05
BIG = -1e30
ROPE_BASE = 160000.0
LOG2E = 1.4426950408889634
LN2 = 0.6931471805599453
BF = jnp.bfloat16
F32 = jnp.float32
VMEM = 60 * 1024 * 1024


def nt(a, b):
    return lax.dot_general(a, b, (((1,), (1,)), ((), ())), preferred_element_type=F32)


def nn(a, b):
    return lax.dot_general(a, b, (((1,), (0,)), ((), ())), preferred_element_type=F32)


def partner(x):
    lane = lax.broadcasted_iota(jnp.int32, x.shape, 1) % HEAD_DIM
    return jnp.where(lane < HEAD_DIM // 2, pltpu.roll(x, 96, 1), pltpu.roll(x, 32, 1))


def params(**kw):
    return pltpu.CompilerParams(vmem_limit_bytes=VMEM, **kw)


def plan(lengths, replica, n_replica, tok):
    ext = tok + 2 * HALO + RB
    n_seq = lengths.shape[0]
    order = jnp.arange(n_seq, dtype=jnp.int32)
    starts = jnp.sum(jnp.where(order[None, :] < order[:, None], lengths[None, :], 0), axis=1)
    ends = starts + lengths
    total = n_replica * tok
    base = replica * tok - HALO

    def look(g):
        seg = jnp.sum((g[:, None] >= starts[None, :]).astype(jnp.int32), axis=1) - 1
        seg = seg + (g >= total).astype(jnp.int32)
        first = jnp.max(jnp.where(g[:, None] >= starts[None, :], starts[None, :], 0), axis=1)
        last = jnp.min(jnp.where(g[:, None] < ends[None, :], ends[None, :], total), axis=1)
        return seg, first, last

    rows = base + jnp.arange(ext, dtype=jnp.int32)
    seg, first, _ = look(rows)
    pos = jnp.maximum(rows - first, 0)
    n_qb = (tok + 2 * HALO) // QB
    heads_of = base + jnp.arange(n_qb, dtype=jnp.int32) * QB
    _, f0, l0 = look(heads_of)
    _, f1, l1 = look(heads_of + (QB - 1))
    own_lo, own_hi = HALO, HALO + tok
    _, fe, le = look(base + jnp.array([own_lo, own_hi - 1], dtype=jnp.int32))
    lo_e, hi_e = fe[0] - base, le[1] - base
    idx = jnp.arange(n_qb, dtype=jnp.int32)
    left, right = idx < own_lo // QB, idx >= own_hi // QB
    k_lo = jnp.where(left, own_lo, jnp.where(right, fe[1] - base, f0 - base))
    k_hi = jnp.where(left, le[0] - base, jnp.where(right, own_hi, l1 - base))
    k_lo = k_lo // QB
    k_n = (k_hi - k_lo * QB + (KB - 1)) // KB
    q_lo, q_hi = lo_e // QB, (hi_e + QB - 1) // QB
    blk = jnp.arange(ext // RB, dtype=jnp.int32) * RB
    need = ((blk + RB > lo_e) & (blk < hi_e)).astype(jnp.int32)
    scal = jnp.concatenate([k_lo, k_n, jnp.stack([q_lo, q_hi]), need])
    return seg, pos, scal


def features(seg):
    lane = jnp.arange(LANES, dtype=jnp.int32)
    hot = (seg[:, None] & 15) == lane[None, :]
    qf = jnp.where(hot, BIG, 0.0).astype(BF)
    kf = jnp.where(hot | (lane >= 16)[None, :], 0.0, 1.0).astype(BF)
    return qf, kf


def rope_tables(pos):
    half = HEAD_DIM // 2
    lane = jnp.arange(LANES, dtype=jnp.int32)
    freq = jnp.exp(-((lane % half).astype(F32) * (2.0 / HEAD_DIM)) * math.log(ROPE_BASE))
    ang = pos.astype(F32)[:, None] * freq[None, :]
    sign = jnp.where(lane % HEAD_DIM < half, -1.0, 1.0).astype(F32)
    return jnp.cos(ang), jnp.sin(ang) * sign[None, :]


def qkv_kernel(n_qb, own_b, need_off, scal, xl, xc, xr, w, g1, cos, sin, qkv, kt, vt, n1o):
    i = pl.program_id(0)
    left_b = HALO // RB

    @pl.when(scal[need_off + i] == 0)
    def _():
        qkv[...] = jnp.zeros_like(qkv)
        kt[...] = jnp.zeros_like(kt)
        vt[...] = jnp.zeros_like(vt)

    @pl.when(scal[need_off + i] != 0)
    def _():
        x = jnp.where(i < left_b, xl[...], jnp.where(i < left_b + own_b, xc[...], xr[...])).astype(F32)
        mean = jnp.mean(x, axis=-1, keepdims=True)
        cen = x - mean
        var = jnp.mean(cen * cen, axis=-1, keepdims=True)
        n1 = (cen * lax.rsqrt(var + EPS) * g1[...]).astype(BF)

        @pl.when((i >= left_b) & (i < left_b + own_b))
        def _():
            n1o[...] = n1

        width = n1.shape[1]
        co, si = cos[...], sin[...]
        sc = HEAD_DIM ** -0.5 * LOG2E
        cq, sq = co * sc, si * sc
        for c in range(3 * width // 256):
            a = nn(n1, w[:, 256 * c : 256 * c + 256])
            part = 256 * c // width
            if part < 2:
                cc, ss = (cq, sq) if part == 0 else (co, si)
                halves = []
                for h in range(2):
                    b = a[:, 128 * h : 128 * h + 128]
                    halves.append((b * cc + partner(b) * ss).astype(BF))
                r = jnp.concatenate(halves, axis=1)
            else:
                r = a.astype(BF)
            qkv[:, 256 * c : 256 * c + 256] = r
            off = 256 * c - width * part
            if part == 1:
                kt[off : off + 256, :] = r.T
            if part == 2:
                vt[off : off + 256, :] = r.T


def qkv_call(scal, xl, xc, xr, w, g1, cos, sin, n_qb):
    tok, width = xc.shape
    ext = cos.shape[0]
    own_b, lb = tok // RB, HALO // RB
    blocks = ext // RB
    need_off = 2 * n_qb + 2
    clampi = lambda lo, n: (lambda i, s: (jnp.clip(i - lo, 0, n - 1), 0))
    row = lambda i, s: (i, 0)
    fix = lambda i, s: (0, 0)
    col = lambda i, s: (0, i)
    return pl.pallas_call(
        functools.partial(qkv_kernel, n_qb, own_b, need_off),
        grid_spec=pltpu.PrefetchScalarGridSpec(
            num_scalar_prefetch=1,
            grid=(blocks,),
            in_specs=[
                pl.BlockSpec((RB, width), clampi(0, lb)),
                pl.BlockSpec((RB, width), clampi(lb, own_b)),
                pl.BlockSpec((RB, width), clampi(lb + own_b, lb)),
                pl.BlockSpec((width, 3 * width), fix),
                pl.BlockSpec((1, width), fix),
                pl.BlockSpec((RB, LANES), row),
                pl.BlockSpec((RB, LANES), row),
            ],
            out_specs=[
                pl.BlockSpec((RB, 3 * width), row),
                pl.BlockSpec((width, RB), col),
                pl.BlockSpec((width, RB), col),
                pl.BlockSpec((RB, width), clampi(lb, own_b)),
            ],
        ),
        out_shape=[
            jax.ShapeDtypeStruct((ext, 3 * width), BF),
            jax.ShapeDtypeStruct((width, ext), BF),
            jax.ShapeDtypeStruct((width, ext), BF),
            jax.ShapeDtypeStruct((tok, width), BF),
        ],
        compiler_params=params(dimension_semantics=("arbitrary",)),
        cost_estimate=pl.CostEstimate(flops=2 * 2000 * width * 3 * width, bytes_accessed=30_000_000, transcendentals=0),
        name="qkv",
    )(scal, xl, xc, xr, w, g1, cos, sin)


def split_heads(x):
    low = lax.broadcasted_iota(jnp.int32, x.shape, 1) < HEAD_DIM
    zero = jnp.zeros_like(x)
    return jnp.concatenate([jnp.where(low, x, zero), jnp.where(low, zero, x)], axis=0)


def fwd_kernel(pg, n_qb, tok, scal, q, k, vt, qf, kf, out, lse, q2, s_buf):
    first_qb = HALO // QB
    ones = jnp.ones((16, KB), BF)

    def per_q(qi, _):
        qb = first_qb + qi
        r0 = pl.multiple_of(qb * QB, QB)
        o0 = pl.multiple_of(qi * QB, QB)
        k_lo, k_n = scal[qb], scal[n_qb + qb]
        fq = qf[pl.ds(r0, QB), :]
        f2 = jnp.concatenate([fq, fq], axis=0)
        for p in range(pg):
            both = split_heads(q[pl.ds(r0, QB), LANES * p : LANES * p + LANES])
            q2[p] = jnp.concatenate([both, f2], axis=1)

        def scores(t, tops):
            k0 = pl.multiple_of(k_lo * QB + t * KB, QB)
            fk = kf[pl.ds(k0, KB), :]
            new = []
            for p in range(pg):
                kk = jnp.concatenate([k[pl.ds(k0, KB), LANES * p : LANES * p + LANES], fk], axis=1)
                s = nt(kk, q2[p])
                s_buf[p, pl.ds(pl.multiple_of(t * KB, KB), KB), :] = s
                new.append(jnp.maximum(tops[p], jnp.max(s.reshape(KB // 8, 8, 2 * QB), axis=0)))
            return tuple(new)

        tops = lax.fori_loop(0, k_n, scores, tuple(jnp.full((8, 2 * QB), BIG, F32) for _ in range(pg)))
        tops = [jnp.max(t, axis=0, keepdims=True) for t in tops]

        def mix(t, accs):
            k0 = pl.multiple_of(k_lo * QB + t * KB, QB)
            new = []
            for p in range(pg):
                s = s_buf[p, pl.ds(pl.multiple_of(t * KB, KB), KB), :]
                pb = jnp.exp2(s - tops[p]).astype(BF)
                va = jnp.concatenate([vt[LANES * p : LANES * p + LANES, pl.ds(k0, KB)], ones], axis=0)
                new.append(accs[p] + nn(va, pb))
            return tuple(new)

        accs = lax.fori_loop(0, k_n, mix, tuple(jnp.zeros((LANES + 16, 2 * QB), F32) for _ in range(pg)))
        for p in range(pg):
            acc = accs[p]
            total = acc[LANES : LANES + 1, :]
            inv = 1.0 / total
            o_t = jnp.concatenate([acc[:HEAD_DIM, :QB] * inv[:, :QB], acc[HEAD_DIM:LANES, QB:] * inv[:, QB:]], axis=0)
            out[pl.ds(o0, QB), LANES * p : LANES * p + LANES] = o_t.T.astype(BF)
            st = tops[p] + jnp.log2(total)
            lse[p, 0:1, pl.ds(o0, QB)] = st[:, :QB]
            lse[p, 1:2, pl.ds(o0, QB)] = st[:, QB:]
        return 0

    lax.fori_loop(0, tok // QB, per_q, 0)


def fwd_call(scal, qkv, vt, qf, kf, tok, width, n_qb, pg):
    ext = qkv.shape[0]
    pairs = width // LANES
    steps = pairs // pg
    col = lambda off: (lambda i, s: (0, off + i))
    fix = lambda i, s: (0, 0)
    s_rows = -(-(QB + 2 * HALO) // KB) * KB + KB
    return pl.pallas_call(
        functools.partial(fwd_kernel, pg, n_qb, tok),
        grid_spec=pltpu.PrefetchScalarGridSpec(
            num_scalar_prefetch=1,
            grid=(steps,),
            in_specs=[
                pl.BlockSpec((ext, LANES * pg), col(0)),
                pl.BlockSpec((ext, LANES * pg), col(steps)),
                pl.BlockSpec((LANES * pg, ext), lambda i, s: (i, 0)),
                pl.BlockSpec((ext, LANES), fix),
                pl.BlockSpec((ext, LANES), fix),
            ],
            out_specs=[
                pl.BlockSpec((tok, LANES * pg), col(0)),
                pl.BlockSpec((pg, 2, tok), lambda i, s: (i, 0, 0)),
            ],
            scratch_shapes=[
                pltpu.VMEM((pg, 2 * QB, 2 * LANES), BF),
                pltpu.VMEM((pg, s_rows, 2 * QB), F32),
            ],
        ),
        out_shape=[
            jax.ShapeDtypeStruct((tok, width), BF),
            jax.ShapeDtypeStruct((pairs, 2, tok), F32),
        ],
        compiler_params=params(dimension_semantics=("arbitrary",)),
        cost_estimate=pl.CostEstimate(flops=30_000_000_000, bytes_accessed=15_000_000, transcendentals=0),
        name="attn_forward",
    )(scal, qkv, qkv, vt, qf, kf)


def mid_kernel(x, o, gy, wo, wi, wd, g2, ind, out, m_o, gu_o, n2_o, gh2_o, gh2b_o, go_o, dlt, dg2):
    ff = wd.shape[0]
    h2 = x[...].astype(F32) + nn(o[...], wo[...])
    mean = jnp.mean(h2, axis=-1, keepdims=True)
    cen = h2 - mean
    r2 = lax.rsqrt(jnp.mean(cen * cen, axis=-1, keepdims=True) + EPS)
    nh = cen * r2
    g = g2[...]
    n2 = (nh * g).astype(BF)
    n2_o[...] = n2
    gyb = gy[...]
    y = h2
    gn2 = jnp.zeros_like(h2)
    step = 384
    for c in range(ff // step):
        lo = c * step
        a = nn(n2, wi[:, lo : lo + step])
        b = nn(n2, wi[:, ff + lo : ff + lo + step])
        gm = nt(gyb, wd[lo : lo + step, :])
        half = 0.5 * (1.0 + lax.erf(a * (2.0 ** -0.5)))
        gel = a * half
        mm = (gel * b).astype(BF)
        m_o[:, lo : lo + step] = mm
        y = y + nn(mm, wd[lo : lo + step, :])
        dgel = half + a * (jnp.exp(-0.5 * a * a) * (1.0 / math.sqrt(2.0 * math.pi)))
        ga = (gm * b * dgel).astype(BF)
        gb = (gm * gel).astype(BF)
        gu_o[:, lo : lo + step] = ga
        gu_o[:, ff + lo : ff + lo + step] = gb
        gn2 = gn2 + nt(ga, wi[:, lo : lo + step]) + nt(gb, wi[:, ff + lo : ff + lo + step])
    out[...] = y.astype(BF)

    @pl.when(pl.program_id(0) == 0)
    def _():
        dg2[...] = jnp.zeros_like(dg2)

    dg2[...] += jnp.sum(gn2 * nh, axis=0, keepdims=True)
    t = gn2 * g
    gh2 = gyb.astype(F32) + r2 * (t - jnp.mean(t, axis=-1, keepdims=True) - nh * jnp.mean(t * nh, axis=-1, keepdims=True))
    gh2_o[...] = gh2
    gb16 = gh2.astype(BF)
    gh2b_o[...] = gb16
    go = nt(gb16, wo[...]).astype(BF)
    go_o[...] = go
    prod = go.astype(F32) * o[...].astype(F32)
    hi = prod.astype(BF)
    lo_part = (prod - hi.astype(F32)).astype(BF)
    dlt[...] = nt(ind[...], hi) + nt(ind[...], lo_part)


def mid_call(x, o, gy, wo, wi, wd, g2):
    tok, width = x.shape
    ff = wd.shape[0]
    heads = jnp.arange(16, dtype=jnp.int32)
    ind = (heads[:, None] == (jnp.arange(width, dtype=jnp.int32) // HEAD_DIM)[None, :]).astype(BF)
    row = lambda i: (i, 0)
    fix = lambda i: (0, 0)
    rs = lambda n: pl.BlockSpec((RB, n), row)
    fs = lambda a: pl.BlockSpec(a.shape, fix)
    sh = jax.ShapeDtypeStruct
    return pl.pallas_call(
        mid_kernel,
        grid=(tok // RB,),
        in_specs=[rs(width), rs(width), rs(width), fs(wo), fs(wi), fs(wd), fs(g2), fs(ind)],
        out_specs=[rs(width), rs(ff), rs(2 * ff), rs(width), rs(width), rs(width), rs(width),
                   pl.BlockSpec((16, RB), lambda i: (0, i)), pl.BlockSpec((1, width), fix)],
        out_shape=[sh((tok, width), BF), sh((tok, ff), BF), sh((tok, 2 * ff), BF), sh((tok, width), BF),
                   sh((tok, width), F32), sh((tok, width), BF), sh((tok, width), BF),
                   sh((16, tok), F32), sh((1, width), F32)],
        compiler_params=params(dimension_semantics=("arbitrary",)),
        cost_estimate=pl.CostEstimate(flops=13_000_000_000 * 2, bytes_accessed=30_000_000, transcendentals=0),
        name="middle",
    )(x, o, gy, wo, wi, wd, g2, ind)


def bwd_kernel(pg, n_qb, tok, scal, q, k, v, kt, qf, kf, gl, gc, gr, lse, dlt, cos, sin,
               gq_o, gk_o, gv_o, q2, g2, go, gka, gva):
    first_qb, last_qb = HALO // QB, (HALO + tok) // QB
    ext = q.shape[0]
    go[0:HALO, :] = gl[...]
    go[HALO : HALO + tok, :] = gc[...]
    go[HALO + tok : HALO + tok + HALO, :] = gr[...]
    gka[...] = jnp.zeros_like(gka)
    gva[...] = jnp.zeros_like(gva)
    sc = HEAD_DIM ** -0.5

    def per_q(qb, _):
        r0 = pl.multiple_of(qb * QB, QB)
        k_lo, k_n = scal[qb], scal[n_qb + qb]
        fq = qf[pl.ds(r0, QB), :]
        f2 = jnp.concatenate([fq, fq], axis=0)
        tops, dels = [], []
        for p in range(pg):
            both = split_heads(q[pl.ds(r0, QB), LANES * p : LANES * p + LANES])
            q2[p] = jnp.concatenate([both, f2], axis=1)
            g2[p] = split_heads(go[pl.ds(r0, QB), LANES * p : LANES * p + LANES])
            tops.append(jnp.concatenate([lse[p, 0:1, pl.ds(r0, QB)], lse[p, 1:2, pl.ds(r0, QB)]], axis=1))
            dels.append(jnp.concatenate([dlt[p, 0:1, pl.ds(r0, QB)], dlt[p, 1:2, pl.ds(r0, QB)]], axis=1))

        def body(t, accs):
            k0 = pl.multiple_of(k_lo * QB + t * KB, QB)
            fk = kf[pl.ds(k0, KB), :]
            new = []
            for p in range(pg):
                cols = slice(LANES * p, LANES * p + LANES)
                kk = jnp.concatenate([k[pl.ds(k0, KB), cols], fk], axis=1)
                pr = jnp.exp2(nt(kk, q2[p]) - tops[p])
                gp = nt(v[pl.ds(k0, KB), cols], g2[p])
                ds = (pr * (gp - dels[p])).astype(BF)
                gva[p, pl.ds(k0, KB), :] += nn(pr.astype(BF), g2[p])
                gka[p, pl.ds(k0, KB), :] += nn(ds, q2[p, :, :LANES])
                new.append(accs[p] + nn(kt[LANES * p : LANES * p + LANES, pl.ds(k0, KB)], ds))
            return tuple(new)

        accs = lax.fori_loop(0, k_n, body, tuple(jnp.zeros((LANES, 2 * QB), F32) for _ in range(pg)))

        @pl.when((qb >= first_qb) & (qb < last_qb))
        def _():
            o0 = pl.multiple_of((qb - first_qb) * QB, QB)
            co, si = cos[pl.ds(o0, QB), :] * sc, sin[pl.ds(o0, QB), :] * sc
            for p in range(pg):
                gt = jnp.concatenate([accs[p][:HEAD_DIM, :QB], accs[p][HEAD_DIM:, QB:]], axis=0).T
                gq_o[pl.ds(o0, QB), LANES * p : LANES * p + LANES] = (gt * co - partner(gt) * si).astype(BF)
        return 0

    lax.fori_loop(scal[2 * n_qb], scal[2 * n_qb + 1], per_q, 0)

    def finish(i, _):
        o0 = pl.multiple_of(i * QB, QB)
        r0 = pl.multiple_of(HALO + i * QB, QB)
        co, si = cos[pl.ds(o0, QB), :] * LN2, sin[pl.ds(o0, QB), :] * LN2
        for p in range(pg):
            cols = slice(LANES * p, LANES * p + LANES)
            a = gka[p, pl.ds(r0, QB), :]
            gk_o[pl.ds(o0, QB), cols] = (a * co - partner(a) * si).astype(BF)
            gv_o[pl.ds(o0, QB), cols] = gva[p, pl.ds(r0, QB), :].astype(BF)
        return 0

    lax.fori_loop(0, tok // QB, finish, 0)


def bwd_call(scal, qkv, kt, qf, kf, gl, gc, gr, lse, dlt, cos, sin, tok, width, n_qb, pg):
    ext = qkv.shape[0]
    pairs = width // LANES
    steps = pairs // pg
    col = lambda off: (lambda i, s: (0, off + i))
    fix = lambda i, s: (0, 0)
    wide = LANES * pg
    sh = jax.ShapeDtypeStruct
    return pl.pallas_call(
        functools.partial(bwd_kernel, pg, n_qb, tok),
        grid_spec=pltpu.PrefetchScalarGridSpec(
            num_scalar_prefetch=1,
            grid=(steps,),
            in_specs=[
                pl.BlockSpec((ext, wide), col(0)),
                pl.BlockSpec((ext, wide), col(steps)),
                pl.BlockSpec((ext, wide), col(2 * steps)),
                pl.BlockSpec((wide, ext), lambda i, s: (i, 0)),
                pl.BlockSpec((ext, LANES), fix),
                pl.BlockSpec((ext, LANES), fix),
                pl.BlockSpec((HALO, wide), col(0)),
                pl.BlockSpec((tok, wide), col(0)),
                pl.BlockSpec((HALO, wide), col(0)),
                pl.BlockSpec((pg, 2, lse.shape[2]), lambda i, s: (i, 0, 0)),
                pl.BlockSpec((pg, 2, lse.shape[2]), lambda i, s: (i, 0, 0)),
                pl.BlockSpec((tok, LANES), fix),
                pl.BlockSpec((tok, LANES), fix),
            ],
            out_specs=[pl.BlockSpec((tok, wide), col(0))] * 3,
            scratch_shapes=[
                pltpu.VMEM((pg, 2 * QB, 2 * LANES), BF),
                pltpu.VMEM((pg, 2 * QB, LANES), BF),
                pltpu.VMEM((ext, wide), BF),
                pltpu.VMEM((pg, ext, LANES), F32),
                pltpu.VMEM((pg, ext, LANES), F32),
            ],
        ),
        out_shape=[sh((tok, width), BF)] * 3,
        compiler_params=params(dimension_semantics=("arbitrary",)),
        cost_estimate=pl.CostEstimate(flops=80_000_000_000, bytes_accessed=20_000_000, transcendentals=0),
        name="attn_backward",
    )(scal, qkv, qkv, qkv, kt, qf, kf, gl, gc, gr, lse, dlt, cos, sin)


def gx_kernel(gq, gk, gv, w, x, gh2, g1, out, dg1):
    width = x.shape[1]
    gn = nt(gq[...], w[:, :width]) + nt(gk[...], w[:, width : 2 * width]) + nt(gv[...], w[:, 2 * width :])
    xf = x[...].astype(F32)
    mean = jnp.mean(xf, axis=-1, keepdims=True)
    cen = xf - mean
    r1 = lax.rsqrt(jnp.mean(cen * cen, axis=-1, keepdims=True) + EPS)
    nh = cen * r1

    @pl.when(pl.program_id(0) == 0)
    def _():
        dg1[...] = jnp.zeros_like(dg1)

    dg1[...] += jnp.sum(gn * nh, axis=0, keepdims=True)
    t = gn * g1[...]
    gx = gh2[...] + r1 * (t - jnp.mean(t, axis=-1, keepdims=True) - nh * jnp.mean(t * nh, axis=-1, keepdims=True))
    out[...] = gx.astype(BF)


def gx_call(gq, gk, gv, w, x, gh2, g1):
    tok, width = x.shape
    row = lambda i: (i, 0)
    fix = lambda i: (0, 0)
    rs = pl.BlockSpec((RB, width), row)
    return pl.pallas_call(
        gx_kernel,
        grid=(tok // RB,),
        in_specs=[rs, rs, rs, pl.BlockSpec(w.shape, fix), rs, rs, pl.BlockSpec(g1.shape, fix)],
        out_specs=[rs, pl.BlockSpec((1, width), fix)],
        out_shape=[jax.ShapeDtypeStruct((tok, width), BF), jax.ShapeDtypeStruct((1, width), F32)],
        compiler_params=params(dimension_semantics=("arbitrary",)),
        cost_estimate=pl.CostEstimate(flops=4_000_000_000, bytes_accessed=15_000_000, transcendentals=0),
        name="input_gradient",
    )(gq, gk, gv, w, x, gh2, g1)


def tn(a, b):
    return lax.dot_general(a, b, (((0,), (0,)), ((), ())), preferred_element_type=F32)


def on_device(tokens, cotangent, lengths, dealing, offsets, attn_gain, qkv_weight, out_weight,
              mlp_gain, in_weight, down_weight, *, n_replica, n_group):
    x, gy = tokens[0], cotangent[0]
    tok, width = x.shape
    n_qb = (tok + 2 * HALO) // QB
    replica = lax.axis_index("replica")
    right = [(i, i + 1) for i in range(n_replica - 1)]
    left = [(i + 1, i) for i in range(n_replica - 1)]

    gather = lambda a: lax.all_gather(a.astype(BF), "group", axis=0, tiled=True)
    x_l = lax.ppermute(x[tok - HALO :], "replica", right)
    x_r = lax.ppermute(x[:HALO], "replica", left)
    w_qkv = gather(qkv_weight)
    gains = lax.all_gather(jnp.stack([attn_gain, mlp_gain]).astype(BF), "group", axis=1, tiled=True).astype(F32)
    w_o, w_i, w_d = gather(out_weight), gather(in_weight), gather(down_weight)
    g1, g2 = gains[0:1], gains[1:2]

    seg, pos, scal = plan(lengths[0], replica, n_replica, tok)
    qf, kf = features(seg)
    cos, sin = rope_tables(pos)

    qkv, kt, vt, n1 = qkv_call(scal, x_l, x, x_r, w_qkv, g1, cos, sin, n_qb)
    o, lse = fwd_call(scal, qkv, vt, qf, kf, tok, width, n_qb, 2)
    out, m, gu, n2, gh2, gh2b, go, dlt, dg2 = mid_call(x, o, gy, w_o, w_i, w_d, g2)

    go_l = lax.ppermute(go[tok - HALO :], "replica", right)
    go_r = lax.ppermute(go[:HALO], "replica", left)
    pairs = width // LANES
    stats = jnp.concatenate([lse, dlt[: 2 * pairs].reshape(pairs, 2, tok)], axis=0)
    st_l = lax.ppermute(stats[:, :, tok - HALO :], "replica", right)
    st_r = lax.ppermute(stats[:, :, :HALO], "replica", left)
    st = jnp.concatenate([st_l, stats, st_r], axis=2)

    d_down = tn(m, gy)
    d_in = tn(n2, gu)
    d_out = tn(o, gh2b)

    co, si = cos[HALO : HALO + tok], sin[HALO : HALO + tok]
    gq, gk, gv = bwd_call(scal, qkv, kt, qf, kf, go_l, go, go_r, st[:pairs], st[pairs:], co, si, tok, width, n_qb, 2)
    d_qkv = jnp.concatenate([tn(n1, gq), tn(n1, gk), tn(n1, gv)], axis=1)
    gx, dg1 = gx_call(gq, gk, gv, w_qkv, x, gh2, g1)

    def reduce(a):
        s = lax.psum_scatter(a.astype(BF), "group", scatter_dimension=0, tiled=True)
        return lax.psum(s, "replica").astype(F32)

    dg = jnp.concatenate([dg1, dg2], axis=0).T
    dgs = reduce(dg)
    return (out[None], gx[None], dgs[:, 0], reduce(d_qkv), reduce(d_out), dgs[:, 1], reduce(d_in), reduce(d_down))


def solution(mesh):
    body = functools.partial(on_device, n_replica=mesh.shape["replica"], n_group=mesh.shape["group"])
    return jax.shard_map(
        body,
        mesh=mesh,
        in_specs=(
            P("group", "replica", None),
            P("group", "replica", None),
            P("group", None),
            P("group", None),
            P("group", None, None),
            P("group"),
            P("group", None),
            P("group", None),
            P("group"),
            P("group", None),
            P("group", None),
        ),
        out_specs=(
            P("group", "replica", None),
            P("group", "replica", None),
            P("group"),
            P("group", None),
            P("group", None),
            P("group"),
            P("group", None),
            P("group", None),
        ),
        check_vma=False,
    )
```

```python
import functools
import math

import jax
import jax.numpy as jnp
from jax import lax
from jax.experimental import pallas as pl
from jax.experimental.pallas import tpu as pltpu
from jax.sharding import PartitionSpec as P

HEADS = 12
HEAD_DIM = 64
LANES = 128
HALO = 768
RB = 256
QB = 128
KB = 256
EPS = 1e-05
BIG = -1e30
ROPE_BASE = 160000.0
LOG2E = 1.4426950408889634
LN2 = 0.6931471805599453
BF = jnp.bfloat16
F32 = jnp.float32


def nt(a, b):
    return lax.dot_general(a, b, (((1,), (1,)), ((), ())), preferred_element_type=F32)


def nn(a, b):
    return lax.dot_general(a, b, (((1,), (0,)), ((), ())), preferred_element_type=F32)


def partner(x):
    lane = lax.broadcasted_iota(jnp.int32, x.shape, 1) % HEAD_DIM
    return jnp.where(lane < HEAD_DIM // 2, pltpu.roll(x, 96, 1), pltpu.roll(x, 32, 1))


def half_of(rows):
    return -(-rows // 32) * 16


def row_of(place, rows):
    return pl.multiple_of((place // 2) * rows + (place % 2) * (rows - half_of(rows)), 16)


def params(mib, **kw):
    return pltpu.CompilerParams(vmem_limit_bytes=mib * 1024 * 1024, **kw)


class Sizes:
    def __init__(self, tok, width):
        self.tok, self.width = tok, width
        self.ext = tok + 2 * HALO + RB
        self.n_qb = (tok + 2 * HALO) // QB
        self.own_qb, self.own_lo = tok // QB, HALO // QB
        self.own_hi = self.own_lo + self.own_qb
        tiles = -(-(QB + 2 * HALO + QB) // KB)
        self.cap_f = self.own_qb * tiles + 2
        self.cap_b = self.own_qb * tiles + 2 * self.own_lo * -(-(HALO + QB) // KB) + 2
        self.k_lo, self.k_n = 0, self.n_qb
        self.q_lo, self.q_hi = 2 * self.n_qb, 2 * self.n_qb + 1
        self.need_lo, self.need_hi = 2 * self.n_qb + 2, 2 * self.n_qb + 3
        self.blocks = self.ext // RB
        self.fwd_q = self.need_hi + 1
        self.fwd_k, self.fwd_n = self.fwd_q + self.cap_f, self.fwd_q + 2 * self.cap_f
        self.bwd_q = self.fwd_n + 1
        self.bwd_k, self.bwd_n = self.bwd_q + self.cap_b, self.bwd_q + 2 * self.cap_b
        self.places = self.bwd_n + 1


def plan_kernel(sz, n_replica, n_group, where, lengths, scal, qf, kf, cos, sin, starts, seg_buf, pos_buf):
    n_seq = lengths.shape[1]
    total = n_replica * sz.tok
    replica, group = where[0], where[1]
    base = replica * sz.tok - HALO
    at = jnp.int32(0)
    for j in range(n_seq):
        starts[j] = at
        at = at + lengths[0, j]
    starts[n_seq] = at

    def first_of(g):
        return lax.fori_loop(0, n_seq, lambda j, f: jnp.where(g >= starts[j], starts[j], f), jnp.int32(0))

    def last_of(g):
        return lax.fori_loop(0, n_seq, lambda j, l: jnp.where(g >= starts[j], starts[j + 1], l), jnp.int32(total))

    own_a, own_b = base + HALO, base + HALO + sz.tok - 1
    first_a, last_a = first_of(own_a) - base, last_of(own_a) - base
    first_b, last_b = first_of(own_b) - base, last_of(own_b) - base
    q_lo, q_hi = first_a // QB, (last_b + QB - 1) // QB
    scal[sz.q_lo], scal[sz.q_hi] = q_lo, q_hi

    def block(i, _):
        e = i * QB
        left, right = i < sz.own_lo, i >= sz.own_hi
        lo = jnp.where(left, HALO, jnp.where(right, first_b, first_of(base + e) - base)) // QB
        hi = jnp.where(left, last_a, jnp.where(right, HALO + sz.tok, last_of(base + e + QB - 1) - base))
        n = (hi - lo * QB + (KB - 1)) // KB
        scal[sz.k_lo + i] = lo
        scal[sz.k_n + i] = jnp.where((i >= q_lo) & (i < q_hi), n, 0)
        return 0

    lax.fori_loop(0, sz.n_qb, block, 0)
    scal[sz.need_lo], scal[sz.need_hi] = first_a // RB, (last_b + KB - 1 + RB - 1) // RB

    def tiles(first, count, at_q, at_k, at_n):
        def of_block(i, c):
            lo, n = scal[sz.k_lo + i], scal[sz.k_n + i]

            def one(t, c):
                scal[at_q + c] = i - first
                scal[at_k + c] = lo + t * (KB // QB)
                return c + 1

            return lax.fori_loop(0, n, one, c)

        c = lax.fori_loop(first, first + count, of_block, jnp.int32(0))
        scal[at_n] = c
        for extra in range(2):
            scal[at_q + c + extra] = jnp.int32(count)
            scal[at_k + c + extra] = jnp.int32(sz.own_lo)

    tiles(sz.own_lo, sz.own_qb, sz.fwd_q, sz.fwd_k, sz.fwd_n)
    tiles(0, sz.n_qb, sz.bwd_q, sz.bwd_k, sz.bwd_n)
    core = replica % 2
    for k in range(n_group):
        for h in range(2):
            scal[sz.places + 2 * k + h] = 2 * (group ^ k) + (core ^ h)

    half = HEAD_DIM // 2
    blocks = sz.ext // QB
    g = base + QB * lax.broadcasted_iota(jnp.int32, (blocks, QB), 0) + lax.broadcasted_iota(jnp.int32, (blocks, QB), 1)
    seg = jnp.full((blocks, QB), -1, jnp.int32)
    first = jnp.zeros((blocks, QB), jnp.int32)
    for j in range(n_seq):
        hit = g >= starts[j]
        seg = jnp.where(hit, j, seg)
        first = jnp.where(hit, starts[j], first)
    seg_buf[...] = jnp.where(g >= total, n_seq, seg) & 15
    pos_buf[...] = jnp.maximum(g - first, 0).astype(F32)
    freq = jnp.exp(lax.broadcasted_iota(jnp.int32, (half, QB), 0).astype(F32) * (-2.0 / HEAD_DIM * math.log(ROPE_BASE)))

    def rows(b, _):
        r0 = pl.multiple_of(b * QB, QB)
        hot = (seg_buf[pl.ds(b, 1), :] == lax.broadcasted_iota(jnp.int32, (LANES, QB), 0)).astype(F32).T
        qf[pl.ds(r0, QB), :] = (hot * BIG).astype(BF)
        lane = lax.broadcasted_iota(jnp.int32, (QB, LANES), 1)
        kf[pl.ds(r0, QB), :] = jnp.where(lane < 16, 1.0 - hot, 0.0).astype(BF)
        ang = freq * pos_buf[pl.ds(b, 1), :]
        co, si = jnp.cos(ang), jnp.sin(ang)
        cos[pl.ds(r0, QB), :] = jnp.concatenate([co] * 4, axis=0).T
        sin[pl.ds(r0, QB), :] = jnp.concatenate([-si, si, -si, si], axis=0).T
        return 0

    lax.fori_loop(0, blocks, rows, 0)


def plan_call(sz, n_replica, n_group, where, lengths):
    sh = jax.ShapeDtypeStruct
    smem = pl.BlockSpec(memory_space=pltpu.SMEM)
    vmem = pl.BlockSpec(memory_space=pltpu.VMEM)
    n_seq = lengths.shape[1]
    return pl.pallas_call(
        functools.partial(plan_kernel, sz, n_replica, n_group),
        in_specs=[smem, smem],
        out_specs=[smem] + [vmem] * 4,
        out_shape=[sh((sz.places + 2 * n_group,), jnp.int32)] + [sh((sz.ext, LANES), BF)] * 2 + [sh((sz.ext, LANES), F32)] * 2,
        scratch_shapes=[pltpu.SMEM((n_seq + 1,), jnp.int32), pltpu.VMEM((sz.ext // QB, QB), jnp.int32), pltpu.VMEM((sz.ext // QB, QB), F32)],
        compiler_params=params(60),
        cost_estimate=pl.CostEstimate(flops=10_000_000_000, bytes_accessed=5_000_000, transcendentals=0),
        name="plan",
    )(where, lengths)


def fetch_qkv(place, pieces, w, sem):
    copies = []
    shard = w.shape[0] // (len(pieces) // 2)
    for t, piece in enumerate(pieces):
        copies.append(pltpu.make_async_copy(piece, w.at[pl.ds(row_of(place(t), shard), piece.shape[0]), :], sem.at[t]))
    return copies


def qkv_kernel(sz, n_pieces, scal, xl, xc, xr, *rest):
    pieces, (g1, cos, sin, qkv, kt, vt, n1t, w, sem) = rest[:n_pieces], rest[n_pieces:]
    i = pl.program_id(0)
    left_b, own_b = HALO // RB, sz.tok // RB
    own = (i >= left_b) & (i < left_b + own_b)

    @pl.when(i == 0)
    def _():
        copies = fetch_qkv(lambda t: scal[sz.places + t], pieces, w, sem)
        for c in copies:
            c.start()
        for c in copies:
            c.wait()

    @pl.when((i >= scal[sz.need_lo]) & (i < scal[sz.need_hi]))
    def _():
        x = jnp.where(i < left_b, xl[...], jnp.where(i < left_b + own_b, xc[...], xr[...])).astype(F32)
        mean = jnp.mean(x, axis=-1, keepdims=True)
        cen = x - mean
        var = jnp.mean(cen * cen, axis=-1, keepdims=True)
        n1 = (cen * lax.rsqrt(var + EPS) * g1[...]).astype(BF)

        @pl.when(own)
        def _():
            n1t[...] = n1.T

        width = n1.shape[1]
        co, si = cos[...], sin[...]
        sc = HEAD_DIM ** -0.5 * LOG2E
        cq, sq = co * sc, si * sc
        for c in range(3 * width // 256):
            a = nn(n1, w[:, 256 * c : 256 * c + 256])
            part = 256 * c // width
            off = 256 * c - width * part
            if part < 2:
                cc, ss = (cq, sq) if part == 0 else (co, si)
                halves = []
                for h in range(2):
                    b = a[:, 128 * h : 128 * h + 128]
                    halves.append((b * cc + partner(b) * ss).astype(BF))
                r = jnp.concatenate(halves, axis=1)
            else:
                r = a.astype(BF)
            qkv[:, 256 * c : 256 * c + 256] = r
            if part == 1:
                kt[off : off + 256, :] = r.T
            if part == 2:
                vt[off : off + 256, :] = r.T


def qkv_call(sz, scal, xl, xc, xr, pieces, g1, cos, sin):
    tok, width, ext = sz.tok, sz.width, sz.ext
    own_b, lb = tok // RB, HALO // RB
    clampi = lambda lo, n: (lambda i, s: (jnp.clip(i - lo, 0, n - 1), 0))
    used = lambda i, s: jnp.clip(i, s[sz.need_lo], s[sz.need_hi] - 1)
    row = lambda i, s: (used(i, s), 0)
    fix = lambda i, s: (0, 0)
    col = lambda i, s: (0, used(i, s))
    sh = jax.ShapeDtypeStruct
    return pl.pallas_call(
        functools.partial(qkv_kernel, sz, len(pieces)),
        grid_spec=pltpu.PrefetchScalarGridSpec(
            num_scalar_prefetch=1,
            grid=(sz.blocks,),
            in_specs=[
                pl.BlockSpec((RB, width), clampi(0, lb)),
                pl.BlockSpec((RB, width), clampi(lb, own_b)),
                pl.BlockSpec((RB, width), clampi(lb + own_b, lb)),
                *[pl.BlockSpec(memory_space=pl.ANY)] * len(pieces),
                pl.BlockSpec((1, width), fix),
                pl.BlockSpec((RB, LANES), row),
                pl.BlockSpec((RB, LANES), row),
            ],
            out_specs=[
                pl.BlockSpec((RB, 3 * width), row),
                pl.BlockSpec((width, RB), col),
                pl.BlockSpec((width, RB), col),
                pl.BlockSpec((width, RB), lambda i, s: (0, jnp.clip(i - lb, 0, own_b - 1))),
            ],
            scratch_shapes=[pltpu.VMEM((width, 3 * width), BF), pltpu.SemaphoreType.DMA((len(pieces),))],
        ),
        out_shape=[sh((ext, 3 * width), BF), sh((width, ext), BF), sh((width, ext), BF), sh((width, tok), BF)],
        compiler_params=params(60, dimension_semantics=("arbitrary",)),
        cost_estimate=pl.CostEstimate(flops=14_000_000_000, bytes_accessed=30_000_000, transcendentals=0),
        name="qkv",
    )(scal, xl, xc, xr, *pieces, g1, cos, sin)


def split_heads(x):
    low = lax.broadcasted_iota(jnp.int32, x.shape, 1) < HEAD_DIM
    zero = jnp.zeros_like(x)
    return jnp.concatenate([jnp.where(low, x, zero), jnp.where(low, zero, x)], axis=0)


def lanes_of(p):
    return slice(LANES * p, LANES * p + LANES)


def fwd_kernel(sz, pg, scal, q, k, vt, qf, kf, out, out_t, lse, q2, buf_a, buf_b, acc, tops):
    nq = sz.own_qb
    ones = jnp.ones((16, KB), BF)
    for qi in range(nq):
        r0 = HALO + qi * QB
        fq = qf[r0 : r0 + QB, :]
        f2 = jnp.concatenate([fq, fq], axis=0)
        for p in range(pg):
            q2[qi, p] = jnp.concatenate([split_heads(q[r0 : r0 + QB, lanes_of(p)]), f2], axis=1)

    def zero(i, _):
        for p in range(pg):
            acc[i, p] = jnp.zeros((LANES + 16, 2 * QB), F32)
            tops[i, p] = jnp.zeros((8, 2 * QB), F32)
        return 0

    lax.fori_loop(0, nq + 1, zero, 0)

    def scores(qi, k0, p, fk):
        return nt(jnp.concatenate([k[pl.ds(k0, KB), lanes_of(p)], fk], axis=1), q2[qi, p])

    def mixed(k0, p, probs):
        va = jnp.concatenate([vt[lanes_of(p), pl.ds(k0, KB)], ones], axis=0)
        return nn(va, probs.astype(BF))

    def tile(i):
        return scal[sz.fwd_q + i], pl.multiple_of(scal[sz.fwd_k + i] * QB, QB)

    def score_tile(i, buf):
        qi, k0 = tile(i)
        qi = jnp.minimum(qi, nq - 1)
        fk = kf[pl.ds(k0, KB), :]
        for p in range(pg):
            buf[p] = scores(qi, k0, p, fk)

    def mix_tile(i, buf):
        qi, k0 = tile(i)
        for p in range(pg):
            acc[qi, p] += mixed(k0, p, jnp.exp2(buf[p]))

    score_tile(0, buf_a)

    def body(j, _):
        score_tile(2 * j + 1, buf_b)
        mix_tile(2 * j, buf_a)
        score_tile(2 * j + 2, buf_a)
        mix_tile(2 * j + 1, buf_b)
        return 0

    lax.fori_loop(0, (scal[sz.fwd_n] + 1) // 2, body, 0)

    low = high = acc[0, 0, LANES : LANES + 1, :]
    for qi in range(nq):
        for p in range(pg):
            total = acc[qi, p, LANES : LANES + 1, :]
            low, high = jnp.minimum(low, total), jnp.maximum(high, total)
    safe = (jnp.min(low) > 2.0 ** -60) & (jnp.max(high) < 2.0 ** 100)

    @pl.when(jnp.logical_not(safe))
    def _():
        lax.fori_loop(0, nq, zero, 0)

        def per_q(qi, _):
            lo, n = scal[sz.k_lo + sz.own_lo + qi], scal[sz.k_n + sz.own_lo + qi]
            for p in range(pg):
                def top(t, m):
                    k0 = pl.multiple_of(lo * QB + t * KB, QB)
                    return jnp.maximum(m, jnp.max(scores(qi, k0, p, kf[pl.ds(k0, KB), :]), axis=0, keepdims=True))

                m = lax.fori_loop(0, n, top, jnp.full((1, 2 * QB), BIG, F32))
                tops[qi, p] = jnp.broadcast_to(m, (8, 2 * QB))

                def add(t, _):
                    k0 = pl.multiple_of(lo * QB + t * KB, QB)
                    acc[qi, p] += mixed(k0, p, jnp.exp2(scores(qi, k0, p, kf[pl.ds(k0, KB), :]) - m))
                    return 0

                lax.fori_loop(0, n, add, 0)
            return 0

        lax.fori_loop(0, nq, per_q, 0)

    def finish(qi, _):
        o0 = pl.multiple_of(qi * QB, QB)
        for p in range(pg):
            a = acc[qi, p]
            total = a[LANES : LANES + 1, :]
            inv = 1.0 / total
            o_t = jnp.concatenate([a[:HEAD_DIM, :QB] * inv[:, :QB], a[HEAD_DIM:LANES, QB:] * inv[:, QB:]], axis=0).astype(BF)
            out_t[lanes_of(p), pl.ds(o0, QB)] = o_t
            out[pl.ds(o0, QB), lanes_of(p)] = o_t.T
            st = tops[qi, p, 0:1, :] + jnp.log2(total)
            lse[p, 0:1, pl.ds(o0, QB)] = st[:, :QB]
            lse[p, 1:2, pl.ds(o0, QB)] = st[:, QB:]
        return 0

    lax.fori_loop(0, nq, finish, 0)


def fwd_call(sz, scal, qkv, vt, qf, kf, pg):
    ext, tok, width = sz.ext, sz.tok, sz.width
    pairs = width // LANES
    steps = pairs // pg
    wide = LANES * pg
    col = lambda off: (lambda i, s: (0, off + i))
    fix = lambda i, s: (0, 0)
    sh = jax.ShapeDtypeStruct
    return pl.pallas_call(
        functools.partial(fwd_kernel, sz, pg),
        grid_spec=pltpu.PrefetchScalarGridSpec(
            num_scalar_prefetch=1,
            grid=(steps,),
            in_specs=[
                pl.BlockSpec((ext, wide), col(0)),
                pl.BlockSpec((ext, wide), col(steps)),
                pl.BlockSpec((wide, ext), lambda i, s: (i, 0)),
                pl.BlockSpec((ext, LANES), fix),
                pl.BlockSpec((ext, LANES), fix),
            ],
            out_specs=[
                pl.BlockSpec((tok, wide), col(0)),
                pl.BlockSpec((wide, tok), lambda i, s: (i, 0)),
                pl.BlockSpec((pg, 2, tok), lambda i, s: (i, 0, 0)),
            ],
            scratch_shapes=[
                pltpu.VMEM((sz.own_qb, pg, 2 * QB, 2 * LANES), BF),
                pltpu.VMEM((pg, KB, 2 * QB), F32),
                pltpu.VMEM((pg, KB, 2 * QB), F32),
                pltpu.VMEM((sz.own_qb + 1, pg, LANES + 16, 2 * QB), F32),
                pltpu.VMEM((sz.own_qb + 1, pg, 8, 2 * QB), F32),
            ],
        ),
        out_shape=[sh((tok, width), BF), sh((width, tok), BF), sh((pairs, 2, tok), F32)],
        compiler_params=params(60, dimension_semantics=("arbitrary",)),
        cost_estimate=pl.CostEstimate(flops=30_000_000_000, bytes_accessed=15_000_000, transcendentals=0),
        name="attn_forward",
    )(scal, qkv, qkv, vt, qf, kf)


def fetch_mlp(place, pieces, wo, wi, wd, sem, width):
    copies = []
    shards = len(pieces) // 2
    half, half_d = half_of(wo.shape[0] // shards), half_of(wd.shape[0] // shards)
    t_cols = wi.shape[1] // width
    for t, piece in enumerate(pieces):
        row0 = row_of(place(t), wo.shape[0] // shards)
        row_d = row_of(place(t), wd.shape[0] // shards)
        copies.append(pltpu.make_async_copy(piece.at[0:half, :], wo.at[pl.ds(row0, half), :], sem.at[t, 0]))
        for j in range(t_cols):
            copies.append(pltpu.make_async_copy(
                piece.at[half * (j + 1) : half * (j + 2), :],
                wi.at[pl.ds(row0, half), width * j : width * j + width], sem.at[t, j + 1]))
        lo = half * (t_cols + 1)
        copies.append(pltpu.make_async_copy(piece.at[lo : lo + half_d, :], wd.at[pl.ds(row_d, half_d), :], sem.at[t, t_cols + 1]))
    return copies


def mid_kernel(n_pieces, at, scal, *refs):
    pieces, refs = refs[:n_pieces], refs[n_pieces:]
    wo, wi, wd, sem = refs[-4:]

    @pl.when(pl.program_id(0) == 0)
    def _():
        copies = fetch_mlp(lambda t: scal[at + t], pieces, wo, wi, wd, sem, wo.shape[1])
        for c in copies:
            c.start()
        for c in copies:
            c.wait()

    x, o, gy, g2, ind = refs[:5]
    mid_body(x, o, gy, wo, wi, wd, g2, ind, *refs[5:-4])


def mid_body(x, o, gy, wo, wi, wd, g2, ind, out, mt_o, gu_o, n2t_o, gh2b_o, go_o, dlt):
    ff = wd.shape[0]
    h2 = x[...].astype(F32) + nn(o[...], wo[...])
    mean = jnp.mean(h2, axis=-1, keepdims=True)
    cen = h2 - mean
    r2 = lax.rsqrt(jnp.mean(cen * cen, axis=-1, keepdims=True) + EPS)
    nh = cen * r2
    g = g2[...]
    n2 = (nh * g).astype(BF)
    n2t_o[...] = n2.T
    gyb = gy[...]
    y = h2
    gn2 = jnp.zeros_like(h2)
    step = 384
    for c in range(ff // step):
        lo = c * step
        a = nn(n2, wi[:, lo : lo + step])
        b = nn(n2, wi[:, ff + lo : ff + lo + step])
        gm = nt(gyb, wd[lo : lo + step, :])
        half = 0.5 * (1.0 + lax.erf(a * (2.0 ** -0.5)))
        gel = a * half
        mm = (gel * b).astype(BF)
        mt_o[lo : lo + step, :] = mm.T
        y = y + nn(mm, wd[lo : lo + step, :])
        dgel = half + a * (jnp.exp(-0.5 * a * a) * (1.0 / math.sqrt(2.0 * math.pi)))
        ga = (gm * b * dgel).astype(BF)
        gb = (gm * gel).astype(BF)
        gu_o[:, lo : lo + step] = ga
        gu_o[:, ff + lo : ff + lo + step] = gb
        gn2 = gn2 + nt(ga, wi[:, lo : lo + step]) + nt(gb, wi[:, ff + lo : ff + lo + step])
    out[...] = y.astype(BF)

    t = gn2 * g
    gh2 = gyb.astype(F32) + r2 * (t - jnp.mean(t, axis=-1, keepdims=True) - nh * jnp.mean(t * nh, axis=-1, keepdims=True))
    gb16 = gh2.astype(BF)
    gh2b_o[...] = gb16
    go = nt(gb16, wo[...]).astype(BF)
    go_o[...] = go
    prod = go.astype(F32) * o[...].astype(F32)
    hi = prod.astype(BF)
    lo_part = (prod - hi.astype(F32)).astype(BF)
    sums = nt(ind[...], hi) + nt(ind[...], lo_part)
    for p in range(dlt.shape[0]):
        dlt[p] = sums[2 * p : 2 * p + 2, :]


def mid_call(sz, scal, pieces, x, o, gy, g2, ff):
    tok, width = x.shape
    heads = jnp.arange(16, dtype=jnp.int32)
    ind = (heads[:, None] == (jnp.arange(width, dtype=jnp.int32) // HEAD_DIM)[None, :]).astype(BF)
    row = lambda i, s: (i, 0)
    fix = lambda i, s: (0, 0)
    rs = lambda n: pl.BlockSpec((RB, n), row)
    cs = lambda n: pl.BlockSpec((n, RB), lambda i, s: (0, i))
    fs = lambda a: pl.BlockSpec(a.shape, fix)
    sh = jax.ShapeDtypeStruct
    n = len(pieces)
    return pl.pallas_call(
        functools.partial(mid_kernel, n, sz.places),
        grid_spec=pltpu.PrefetchScalarGridSpec(
            num_scalar_prefetch=1,
            grid=(tok // RB,),
            in_specs=[*[pl.BlockSpec(memory_space=pl.ANY)] * n, rs(width), rs(width), rs(width), fs(g2), fs(ind)],
            out_specs=[rs(width), cs(ff), rs(2 * ff), cs(width), rs(width), rs(width),
                       pl.BlockSpec((width // LANES, 2, RB), lambda i, s: (0, 0, i))],
            scratch_shapes=[pltpu.VMEM((width, width), BF), pltpu.VMEM((width, 2 * ff), BF), pltpu.VMEM((ff, width), BF),
                            pltpu.SemaphoreType.DMA((n, 2 * ff // width + 2))],
        ),
        out_shape=[sh((tok, width), BF), sh((ff, tok), BF), sh((tok, 2 * ff), BF), sh((width, tok), BF),
                   sh((tok, width), BF), sh((tok, width), BF),
                   sh((width // LANES, 2, tok), F32)],
        compiler_params=params(60, dimension_semantics=("arbitrary",)),
        cost_estimate=pl.CostEstimate(flops=13_000_000_000 * 2, bytes_accessed=30_000_000, transcendentals=0),
        name="middle",
    )(scal, *pieces, x, o, gy, g2, ind)


def put_halves(core, keep, send, rows0, values, n_group):
    rows = values.shape[0] // n_group
    half = half_of(rows)

    def store(first, second):
        for g in range(n_group):
            lo, hi = rows * g, rows * (g + 1)
            first[g, pl.ds(rows0, half), :] = values[lo : lo + half, :]
            second[g, pl.ds(rows0, half), :] = values[hi - half : hi, :]

    @pl.when(core == 0)
    def _():
        store(keep, send)

    @pl.when(core != 0)
    def _():
        store(send, keep)


def put_halves(core, keep, send, rows0, values, n_group):
    rows = values.shape[0] // n_group
    half = half_of(rows)

    def store(first, second):
        for g in range(n_group):
            lo, hi = rows * g, rows * (g + 1)
            first[g, pl.ds(rows0, half), :] = values[lo : lo + half, :]
            second[g, pl.ds(rows0, half), :] = values[hi - half : hi, :]

    @pl.when(core == 0)
    def _():
        store(keep, send)

    @pl.when(core != 0)
    def _():
        store(send, keep)


def in_grad_kernel(n_group, at, scal, n2t, gu, keep, send):
    half = half_of(n2t.shape[0] // n_group)
    row0 = pl.multiple_of(pl.program_id(0) * half, 16)
    put_halves(scal[at] % 2, keep, send, row0, nn(n2t[...], gu[...]).astype(BF), n_group)


def in_grad_call(sz, scal, n2t, gu, n_group):
    width, tok = n2t.shape
    n_cols = gu.shape[1] // width
    rows = n_cols * half_of(width // n_group)
    out = jax.ShapeDtypeStruct((n_group, rows, width), BF)
    return pl.pallas_call(
        functools.partial(in_grad_kernel, n_group, sz.places),
        grid_spec=pltpu.PrefetchScalarGridSpec(
            num_scalar_prefetch=1,
            grid=(n_cols,),
            in_specs=[pl.BlockSpec((width, tok), lambda j, s: (0, 0)), pl.BlockSpec((tok, width), lambda j, s: (0, j))],
            out_specs=[pl.BlockSpec((n_group, rows, width), lambda j, s: (0, 0, 0))] * 2,
        ),
        out_shape=[out, out],
        compiler_params=params(60, dimension_semantics=("arbitrary",)),
        cost_estimate=pl.CostEstimate(flops=8_000_000_000, bytes_accessed=10_000_000, transcendentals=0),
        name="in_weight_gradient",
    )(scal, n2t, gu)


def down_out_kernel(n_group, at, scal, mt, gy, ot_h, gh_h, keep, send, ot, gh, sem):
    copies = [pltpu.make_async_copy(ot_h, ot, sem.at[0]), pltpu.make_async_copy(gh_h, gh, sem.at[1])]
    for c in copies:
        c.start()
    put_halves(scal[at] % 2, keep, send, 0, nn(mt[...], gy[...]).astype(BF), n_group)
    for c in copies:
        c.wait()
    put_halves(scal[at] % 2, keep, send, half_of(mt.shape[0] // n_group), nn(ot[...], gh[...]).astype(BF), n_group)


def down_out_call(sz, scal, mt, gy, ot, gh, n_group):
    width, tok = ot.shape
    ff = mt.shape[0]
    rows = half_of(width // n_group) + half_of(ff // n_group)
    out = jax.ShapeDtypeStruct((n_group, rows, width), BF)
    anyspec = pl.BlockSpec(memory_space=pl.ANY)
    fix = lambda j, s: (0, 0)
    return pl.pallas_call(
        functools.partial(down_out_kernel, n_group, sz.places),
        grid_spec=pltpu.PrefetchScalarGridSpec(
            num_scalar_prefetch=1,
            grid=(1,),
            in_specs=[pl.BlockSpec((ff, tok), fix), pl.BlockSpec((tok, width), fix), anyspec, anyspec],
            out_specs=[pl.BlockSpec((n_group, rows, width), lambda j, s: (0, 0, 0))] * 2,
            scratch_shapes=[pltpu.VMEM((width, tok), BF), pltpu.VMEM((tok, width), BF), pltpu.SemaphoreType.DMA((2,))],
        ),
        out_shape=[out, out],
        compiler_params=params(60, dimension_semantics=("arbitrary",)),
        cost_estimate=pl.CostEstimate(flops=7_000_000_000, bytes_accessed=10_000_000, transcendentals=0),
        name="down_out_weight_gradients",
    )(scal, mt, gy, ot, gh)


def bwd_kernel(sz, pg, n_group, scal, q, k, v, kt, qf, kf, gl, gc, gr, lse_c, dlt_c, lse_l, dlt_l, lse_r, dlt_r,
               cos, sin, n1t, grad, keep, send, q2, g2, gka, gva, gqa, st, s_a, p_a, s_b, p_b):
    n_qb, tok = sz.n_qb, sz.tok
    q_lo, q_hi = scal[sz.q_lo], scal[sz.q_hi]
    for row, parts in ((0, (lse_l, lse_c, lse_r)), (1, (dlt_l, dlt_c, dlt_r))):
        for p in range(pg):
            at = 0
            for part in parts:
                for b in range(part.shape[2] // QB):
                    for h in range(2):
                        st[at, p, row : row + 1, QB * h : QB * h + QB] = part[p, h : h + 1, QB * b : QB * b + QB]
                    at += 1

    def prep(src, first, count):
        def one(i, _):
            r0 = pl.multiple_of(i * QB, QB)
            fq = qf[pl.ds(r0, QB), :]
            f2 = jnp.concatenate([fq, fq], axis=0)
            for p in range(pg):
                q2[i, p] = jnp.concatenate([split_heads(q[pl.ds(r0, QB), lanes_of(p)]), f2], axis=1)
                g2[i, p] = split_heads(src[pl.ds(pl.multiple_of((i - first) * QB, QB), QB), lanes_of(p)])
                gqa[i, p] = jnp.zeros((LANES, 2 * QB), F32)
                gka[p, pl.ds(r0, QB), :] = jnp.zeros((QB, LANES), F32)
                gva[p, pl.ds(r0, QB), :] = jnp.zeros((QB, LANES), F32)
            return 0

        lax.fori_loop(jnp.maximum(first, q_lo), jnp.minimum(first + count, q_hi), one, 0)

    prep(gl, 0, sz.own_lo)
    prep(gc, sz.own_lo, sz.own_qb)
    prep(gr, sz.own_hi, sz.own_lo)

    def tile(i):
        return jnp.minimum(scal[sz.bwd_q + i], q_hi - 1), pl.multiple_of(scal[sz.bwd_k + i] * QB, QB)

    def score_tile(i, s_buf, p_buf):
        qi, k0 = tile(i)
        fk = kf[pl.ds(k0, KB), :]
        for p in range(pg):
            s_buf[p] = nt(jnp.concatenate([k[pl.ds(k0, KB), lanes_of(p)], fk], axis=1), q2[qi, p])
            p_buf[p] = nt(v[pl.ds(k0, KB), lanes_of(p)], g2[qi, p])

    def grad_tile(i, s_buf, p_buf):
        qi, k0 = tile(i)
        dead = jnp.where(i < scal[sz.bwd_n], 0.0, 1e38).astype(F32)
        for p in range(pg):
            pr = jnp.exp2(s_buf[p] - (st[qi, p, 0:1, :] + dead))
            ds = (pr * (p_buf[p] - st[qi, p, 1:2, :])).astype(BF)
            gva[p, pl.ds(k0, KB), :] += nn(pr.astype(BF), g2[qi, p])
            gka[p, pl.ds(k0, KB), :] += nn(ds, q2[qi, p, :, :LANES])
            gqa[qi, p] += nn(kt[lanes_of(p), pl.ds(k0, KB)], ds)

    score_tile(0, s_a, p_a)

    def body(j, _):
        score_tile(2 * j + 1, s_b, p_b)
        grad_tile(2 * j, s_a, p_a)
        score_tile(2 * j + 2, s_a, p_a)
        grad_tile(2 * j + 1, s_b, p_b)
        return 0

    lax.fori_loop(0, (scal[sz.bwd_n] + 1) // 2, body, 0)

    sc = HEAD_DIM ** -0.5
    wide = LANES * pg

    def finish(i, _):
        o0 = pl.multiple_of(i * QB, QB)
        r0 = pl.multiple_of(HALO + i * QB, QB)
        co, si = cos[pl.ds(r0, QB), :], sin[pl.ds(r0, QB), :]
        for p in range(pg):
            a = gqa[sz.own_lo + i, p]
            gt = jnp.concatenate([a[:HEAD_DIM, :QB], a[HEAD_DIM:, QB:]], axis=0).T * sc
            grad[pl.ds(o0, QB), LANES * p : LANES * p + LANES] = (gt * co - partner(gt) * si).astype(BF)
            b = gka[p, pl.ds(r0, QB), :] * LN2
            lo = wide + LANES * p
            grad[pl.ds(o0, QB), lo : lo + LANES] = (b * co - partner(b) * si).astype(BF)
            lo = 2 * wide + LANES * p
            grad[pl.ds(o0, QB), lo : lo + LANES] = gva[p, pl.ds(r0, QB), :].astype(BF)
        return 0

    lax.fori_loop(0, sz.own_qb, finish, 0)
    for part in range(3):
        cols = slice(wide * part, wide * part + wide)
        values = nn(n1t[...], grad[:, cols]).astype(BF)
        put_halves(scal[sz.places] % 2, keep.at[:, :, cols], send.at[:, :, cols], 0, values, n_group)


def bwd_call(sz, scal, qkv, kt, qf, kf, gl, gc, gr, lse, dlt, st_l, st_r, cos, sin, n1t, pg, at, n_group):
    ext, tok, width, n_qb = sz.ext, sz.tok, sz.width, sz.n_qb
    pairs = width // LANES
    steps = pairs // pg
    wide = LANES * pg
    half = half_of(width // n_group)
    spec = lambda shape, *idx: pl.BlockSpec(shape, lambda i, s: idx, pipeline_mode=pl.Buffered(1))
    sh = jax.ShapeDtypeStruct
    side = [spec((pg, 2, HALO), at, 0, 0), spec((pg, 2, HALO), steps + at, 0, 0)]
    return pl.pallas_call(
        functools.partial(bwd_kernel, sz, pg, n_group),
        grid_spec=pltpu.PrefetchScalarGridSpec(
            num_scalar_prefetch=1,
            grid=(1,),
            in_specs=[
                spec((ext, wide), 0, at),
                spec((ext, wide), 0, steps + at),
                spec((ext, wide), 0, 2 * steps + at),
                spec((wide, ext), at, 0),
                spec((ext, LANES), 0, 0),
                spec((ext, LANES), 0, 0),
                spec((HALO, wide), 0, at),
                spec((tok, wide), 0, at),
                spec((HALO, wide), 0, at),
                spec((pg, 2, tok), at, 0, 0),
                spec((pg, 2, tok), at, 0, 0),
                *side,
                *side,
                spec((ext, LANES), 0, 0),
                spec((ext, LANES), 0, 0),
                spec((width, tok), 0, 0),
            ],
            out_specs=[spec((tok, 3 * wide), 0, 0), spec((n_group, half, 3 * wide), 0, 0, 0), spec((n_group, half, 3 * wide), 0, 0, 0)],
            scratch_shapes=[
                pltpu.VMEM((n_qb, pg, 2 * QB, 2 * LANES), BF),
                pltpu.VMEM((n_qb, pg, 2 * QB, LANES), BF),
                pltpu.VMEM((pg, ext, LANES), F32),
                pltpu.VMEM((pg, ext, LANES), F32),
                pltpu.VMEM((n_qb, pg, LANES, 2 * QB), F32),
                pltpu.VMEM((n_qb, pg, 8, 2 * QB), F32),
                *[pltpu.VMEM((pg, KB, 2 * QB), F32)] * 4,
            ],
        ),
        out_shape=[sh((tok, 3 * wide), BF), sh((n_group, half, 3 * wide), BF), sh((n_group, half, 3 * wide), BF)],
        compiler_params=params(60, dimension_semantics=("arbitrary",)),
        cost_estimate=pl.CostEstimate(flops=35_000_000_000, bytes_accessed=20_000_000, transcendentals=0),
        name="attn_backward",
    )(scal, qkv, qkv, qkv, kt, qf, kf, gl, gc, gr, lse, dlt, st_l, st_l, st_r, st_r, cos, sin, n1t)


def gx_kernel(n_pieces, n_grads, at, scal, *refs):
    pieces, grads = refs[:n_pieces], refs[n_pieces : n_pieces + n_grads]
    x, gh2, g1, out, w, sem = refs[n_pieces + n_grads :]

    @pl.when(pl.program_id(0) == 0)
    def _():
        copies = fetch_qkv(lambda t: scal[at + t], pieces, w, sem)
        for c in copies:
            c.start()
        for c in copies:
            c.wait()

    width = x.shape[1]
    gn = None
    wide = grads[0].shape[1] // 3
    for part in range(3):
        lhs = jnp.concatenate([grad[:, wide * part : wide * part + wide] for grad in grads], axis=1)
        term = nt(lhs, w[:, width * part : width * part + width])
        gn = term if gn is None else gn + term
    xf = x[...].astype(F32)
    mean = jnp.mean(xf, axis=-1, keepdims=True)
    cen = xf - mean
    r1 = lax.rsqrt(jnp.mean(cen * cen, axis=-1, keepdims=True) + EPS)
    nh = cen * r1

    t = gn * g1[...]
    gx = gh2[...].astype(F32) + r1 * (t - jnp.mean(t, axis=-1, keepdims=True) - nh * jnp.mean(t * nh, axis=-1, keepdims=True))
    out[...] = gx.astype(BF)


def gx_call(sz, scal, pieces, grads, x, gh2, g1):
    tok, width = x.shape
    row = lambda i, s: (i, 0)
    fix = lambda i, s: (0, 0)
    rs = pl.BlockSpec((RB, width), row)
    n = len(pieces)
    return pl.pallas_call(
        functools.partial(gx_kernel, n, len(grads), sz.places),
        grid_spec=pltpu.PrefetchScalarGridSpec(
            num_scalar_prefetch=1,
            grid=(tok // RB,),
            in_specs=[*[pl.BlockSpec(memory_space=pl.ANY)] * n,
                      *[pl.BlockSpec((RB, g.shape[1]), row) for g in grads],
                      rs, rs, pl.BlockSpec(g1.shape, fix)],
            out_specs=rs,
            scratch_shapes=[pltpu.VMEM((width, 3 * width), BF), pltpu.SemaphoreType.DMA((n,))],
        ),
        out_shape=jax.ShapeDtypeStruct((tok, width), BF),
        compiler_params=params(60, dimension_semantics=("arbitrary",)),
        cost_estimate=pl.CostEstimate(flops=4_000_000_000, bytes_accessed=15_000_000, transcendentals=0),
        name="input_gradient",
    )(scal, *pieces, *grads, x, gh2, g1)


class Net:
    def __init__(self, n_replica, n_group):
        self.n_replica, self.n_group, self.n_z = n_replica, n_group, n_replica // 2
        self.replica, self.group = lax.axis_index("replica"), lax.axis_index("group")
        self.core = self.replica & 1

    def shift(self, a, step):
        pairs = [(i, i + step) for i in range(self.n_replica) if 0 <= i + step < self.n_replica]
        return lax.ppermute(a, "replica", pairs)

    def core_swap(self, a):
        return lax.ppermute(a, "replica", [(i, i ^ 1) for i in range(self.n_replica)])

    def across(self, a, k):
        return lax.ppermute(a, "group", [(i, i ^ k) for i in range(self.n_group)])

    def across_swap(self, a, k):
        n = self.n_group
        pairs = [(r * n + g, (r ^ 1) * n + (g ^ k)) for r in range(self.n_replica) for g in range(n)]
        return lax.ppermute(a, ("replica", "group"), pairs)

    def gather_near(self, mine, other):
        got = {(0, 0): mine, (0, 1): other}
        for k in (1, 2) if self.n_group == 4 else range(1, self.n_group):
            got[k, 0] = self.across(mine, k)
        return got

    def gather_far(self, got):
        got = dict(got)
        if self.n_group == 4:
            got[3, 0] = self.across(got[2, 0], 1)
            got[3, 1] = self.across_swap(got[1, 0], 2)
        for k in range(1, self.n_group):
            if (k, 1) not in got:
                got[k, 1] = self.core_swap(got[k, 0])
        return [got[key] for key in sorted(got)]

    def parts(self, pairs):
        def part(k):
            at = lambda a: lax.dynamic_index_in_dim(a, self.group ^ k, 0, keepdims=False).astype(F32)
            return jnp.concatenate([at(keep) + at(got) for got, keep in pairs], axis=0)

        return [part(0)] + [part(k).astype(BF) for k in range(1, self.n_group)]

    def group_sum(self, parts):
        s = parts[0]
        for k in range(1, self.n_group):
            s = s + self.across(parts[k], k).astype(F32)
        return s

    def z_steps(self):
        z = self.replica // 2
        if self.n_z == 4:
            def first(s):
                a = lax.ppermute(s.astype(BF), "replica", [(0, 2), (1, 3), (6, 4), (7, 5)])
                return (s + a.astype(F32)).astype(BF)

            def second(s):
                b = lax.ppermute(s, "replica", [(2, 4), (3, 5), (4, 2), (5, 3)])
                return (s.astype(F32) + b.astype(F32)).astype(BF)

            def third(t):
                c = lax.ppermute(t, "replica", [(2, 0), (3, 1), (4, 6), (5, 7)])
                return jnp.where((z == 0) | (z == 3), c, t)

            return [first, second, third]

        def fold(k):
            def step(t):
                t = t.astype(BF)
                b = lax.ppermute(t, "replica", [(i, i ^ k) for i in range(self.n_replica)])
                return (t.astype(F32) + b.astype(F32)).astype(BF)
            return step

        return [fold(2 << i) for i in range(self.n_z.bit_length() - 1)]


def on_device(tokens, cotangent, lengths, dealing, offsets, attn_gain, qkv_weight, out_weight,
              mlp_gain, in_weight, down_weight, *, n_replica, n_group):
    net = Net(n_replica, n_group)
    x, gy = tokens[0], cotangent[0]
    tok, width = x.shape
    ff = in_weight.shape[1] // 2
    sz = Sizes(tok, width)
    pairs = width // LANES
    pg = 3
    tie = lax.optimization_barrier

    def half_rows(a, h):
        n = half_of(a.shape[0])
        return lax.dynamic_slice_in_dim(a, (net.core ^ h) * (a.shape[0] - n), n, 0).astype(BF)

    def pack(h):
        wi = half_rows(in_weight, h)
        cols = [wi[:, width * j : width * j + width] for j in range(2 * ff // width)]
        return jnp.concatenate([half_rows(out_weight, h), *cols, half_rows(down_weight, h)], axis=0)

    near = net.gather_near(half_rows(qkv_weight, 0), half_rows(qkv_weight, 1))
    own_gain = jnp.stack([attn_gain, mlp_gain]).astype(BF)
    by_offset = [own_gain] + [net.across(own_gain, k) for k in range(1, n_group)]
    packs = pack(0), pack(1)
    where = jnp.stack([net.replica, net.group]).astype(jnp.int32)
    near, by_offset, packs, where = tie((near, by_offset, packs, where))
    scal, qf, kf, cos, sin = plan_call(sz, n_replica, n_group, where, lengths)

    x_l = net.shift(x[tok - HALO :], 1)
    x_r = net.shift(x[:HALO], -1)
    qkv_pieces = net.gather_far(near)
    by_offset = jnp.stack(by_offset)
    hit = (jnp.arange(n_group)[:, None] ^ net.group) == jnp.arange(n_group)[None, :]
    gains = jnp.sum(jnp.where(hit[:, :, None, None], by_offset[None].astype(F32), 0.0), axis=1)
    gains = gains.transpose(1, 0, 2).reshape(2, width)
    g1, g2 = gains[0:1], gains[1:2]
    packs, qkv_pieces, x_l, x_r, gains = tie((packs, qkv_pieces, x_l, x_r, gains))

    near = net.gather_near(*packs)
    qkv, kt, vt, n1t = qkv_call(sz, scal, x_l, x, x_r, qkv_pieces, g1, cos, sin)
    near, vt = tie((near, vt))
    mlp_pieces = net.gather_far(near)
    o, ot, lse = fwd_call(sz, scal, qkv, vt, qf, kf, pg)
    out, mt, gu, n2t, gh2b, go, dlt = mid_call(sz, scal, mlp_pieces, x, o, gy, g2, ff)

    go_l = net.shift(go[tok - HALO :], 1)
    go_r = net.shift(go[:HALO], -1)
    stats = jnp.concatenate([lse, dlt], axis=0)
    st_l = net.shift(stats[:, :, tok - HALO :], 1)
    st_r = net.shift(stats[:, :, :HALO], -1)

    keep_i, send_i = in_grad_call(sz, scal, n2t, gu, n_group)
    keep_d, send_d = down_out_call(sz, scal, mt, gy, ot, gh2b, n_group)
    mlp_parts = net.parts([(net.core_swap(send_i), keep_i), (net.core_swap(send_d), keep_d)])

    def attn_grad(at, dep):
        return bwd_call(sz, dep, qkv, kt, qf, kf, go_l, go, go_r, lse, dlt, st_l, st_r, cos, sin, n1t, pg, at, n_group)

    scal, mlp_parts = tie((scal, mlp_parts))
    grad0, keep0, send0 = attn_grad(0, scal)
    mlp_sum = net.group_sum(mlp_parts).astype(BF)
    parts0 = net.parts([(net.core_swap(send0), keep0)])
    scal, mlp_sum, parts0 = tie((scal, mlp_sum, parts0))
    z = net.z_steps()
    last = len(z) - 1
    mlp_sum = z[0](mlp_sum)
    grad1, keep1, send1 = attn_grad(1, scal)
    sum0 = net.group_sum(parts0)
    sum0, mlp_sum, scal, send1 = tie((sum0, mlp_sum, scal, send1))

    got1 = net.core_swap(send1)
    mlp_sum = z[1](mlp_sum)
    sum0 = z[0](sum0)
    got1, sum0 = tie((got1, sum0))
    gx = gx_call(sz, scal, qkv_pieces, [grad0, grad1], x, gh2b, g1)
    sum1 = net.group_sum(net.parts([(got1, keep1)]))
    sum0 = z[1](sum0)
    for i in range(2, last + 1):
        sum0, sum1, mlp_sum = tie((sum0, sum1, mlp_sum))
        sum1 = z[i - 2](sum1)
        sum0 = z[i](sum0)
        mlp_sum = z[i](mlp_sum)
    sum0, sum1 = tie((sum0, sum1))
    sum1 = z[last - 1](sum1)
    sib0 = net.core_swap(sum0)
    sib0, sum1, mlp_sum = tie((sib0, sum1, mlp_sum))
    sum1 = z[last](sum1)
    sib_mlp = net.core_swap(mlp_sum)
    sib_mlp, sum1 = tie((sib_mlp, sum1))
    sib1 = net.core_swap(sum1)

    def both(t, sib):
        first = net.core == 0
        return jnp.where(first, t, sib).astype(F32), jnp.where(first, sib, t).astype(F32)

    def rows_of(p, q, shard):
        return jnp.concatenate([p[: shard - p.shape[0]], q], axis=0)

    shard, shard_d = width // n_group, ff // n_group
    half, half_d = half_of(shard), half_of(shard_d)
    a, b = both(sum1, sib1)
    wide = LANES * pg
    qkv_half = lambda parts: jnp.concatenate([p[:half, wide * c : wide * c + wide] for c in range(3) for p in parts], axis=1)
    c, d = both(sum0, sib0)
    d_qkv = rows_of(qkv_half([c, a]), qkv_half([d, b]), shard)
    a, b = both(mlp_sum, sib_mlp)
    n_cols = 2 * ff // width
    wide_in = lambda p: jnp.concatenate([p[half * j : half * j + half] for j in range(n_cols)], axis=1)
    d_in = rows_of(wide_in(a), wide_in(b), shard)
    lo, hi = half * n_cols, half * n_cols + half_d
    d_down = rows_of(a[lo:hi], b[lo:hi], shard_d)
    d_out = rows_of(a[hi:], b[hi:], shard)
    low = lambda v: v.astype(BF).astype(F32)
    d_g1 = jnp.sum(low(qkv_weight) * d_qkv, axis=1) / low(attn_gain)
    d_g2 = jnp.sum(low(in_weight) * d_in, axis=1) / low(mlp_gain)
    return (out[None], gx[None], d_g1, d_qkv, d_out, d_g2, d_in, d_down)


def solution(mesh):
    body = functools.partial(on_device, n_replica=mesh.shape["replica"], n_group=mesh.shape["group"])
    return jax.shard_map(
        body,
        mesh=mesh,
        in_specs=(
            P("group", "replica", None),
            P("group", "replica", None),
            P("group", None),
            P("group", None),
            P("group", None, None),
            P("group"),
            P("group", None),
            P("group", None),
            P("group"),
            P("group", None),
            P("group", None),
        ),
        out_specs=(
            P("group", "replica", None),
            P("group", "replica", None),
            P("group"),
            P("group", None),
            P("group", None),
            P("group"),
            P("group", None),
            P("group", None),
        ),
        check_vma=False,
    )
```

```python
import functools
import math

import jax
import jax.numpy as jnp
from jax import lax
from jax.experimental import pallas as pl
from jax.experimental.pallas import tpu as pltpu
from jax.sharding import PartitionSpec as P

HEADS = 12
HEAD_DIM = 64
LANES = 128
HALO = 768
RB = 256
QB = 128
KB = 256
EPS = 1e-05
BIG = -1e30
ROPE_BASE = 160000.0
LOG2E = 1.4426950408889634
LN2 = 0.6931471805599453
BF = jnp.bfloat16
F32 = jnp.float32


def nt(a, b):
    return lax.dot_general(a, b, (((1,), (1,)), ((), ())), preferred_element_type=F32)


def nn(a, b):
    return lax.dot_general(a, b, (((1,), (0,)), ((), ())), preferred_element_type=F32)


def partner(x):
    lane = lax.broadcasted_iota(jnp.int32, x.shape, 1) % HEAD_DIM
    return jnp.where(lane < HEAD_DIM // 2, pltpu.roll(x, 96, 1), pltpu.roll(x, 32, 1))


def half_of(rows):
    return -(-rows // 32) * 16


def row_of(place, rows):
    return pl.multiple_of((place // 2) * rows + (place % 2) * (rows - half_of(rows)), 16)


def params(mib, **kw):
    return pltpu.CompilerParams(vmem_limit_bytes=mib * 1024 * 1024, **kw)


class Sizes:
    def __init__(self, tok, width):
        self.tok, self.width = tok, width
        self.ext = tok + 2 * HALO + RB
        self.n_qb = (tok + 2 * HALO) // QB
        self.own_qb, self.own_lo = tok // QB, HALO // QB
        self.own_hi = self.own_lo + self.own_qb
        tiles = -(-(QB + 2 * HALO + QB) // KB)
        self.cap_f = self.own_qb * tiles + 2
        halo_tiles = -(-(HALO + QB) // KB)
        caps = [self.own_qb * -(-tok // KB) + 2, 2 * self.own_qb * -(-HALO // KB) + 2, 2 * self.own_lo * halo_tiles + 2]
        self.k_lo, self.k_n = 0, self.n_qb
        self.q_lo, self.q_hi = 2 * self.n_qb, 2 * self.n_qb + 1
        self.need_lo, self.need_hi, self.full_hi = (2 * self.n_qb + i for i in (2, 3, 4))
        self.blocks = self.ext // RB
        self.fwd_q = self.full_hi + 1
        self.fwd_k, self.fwd_n = self.fwd_q + self.cap_f, self.fwd_q + 2 * self.cap_f
        self.lists, at = [], self.fwd_n + 1
        for cap in caps:
            self.lists.append((at, at + cap, at + 2 * cap))
            at += 2 * cap + 1
        self.places = at


def plan_kernel(sz, n_replica, n_group, where, lengths, scal, qf, kf, cos, sin, starts, k_end, seg_buf, pos_buf):
    n_seq = lengths.shape[1]
    total = n_replica * sz.tok
    replica, group = where[0], where[1]
    base = replica * sz.tok - HALO
    at = jnp.int32(0)
    for j in range(n_seq):
        starts[j] = at
        at = at + lengths[0, j]
    starts[n_seq] = at

    def first_of(g):
        return lax.fori_loop(0, n_seq, lambda j, f: jnp.where(g >= starts[j], starts[j], f), jnp.int32(0))

    def last_of(g):
        return lax.fori_loop(0, n_seq, lambda j, l: jnp.where(g >= starts[j], starts[j + 1], l), jnp.int32(total))

    own_a, own_b = base + HALO, base + HALO + sz.tok - 1
    first_a, last_a = first_of(own_a) - base, last_of(own_a) - base
    first_b, last_b = first_of(own_b) - base, last_of(own_b) - base
    q_lo, q_hi = first_a // QB, (last_b + QB - 1) // QB
    scal[sz.q_lo], scal[sz.q_hi] = q_lo, q_hi

    def block(i, _):
        e = i * QB
        left, right = i < sz.own_lo, i >= sz.own_hi
        lo = jnp.where(left, HALO, jnp.where(right, first_b, first_of(base + e) - base)) // QB
        hi = jnp.where(left, last_a, jnp.where(right, HALO + sz.tok, last_of(base + e + QB - 1) - base))
        n = (hi - lo * QB + (KB - 1)) // KB
        scal[sz.k_lo + i] = lo
        scal[sz.k_n + i] = jnp.where((i >= q_lo) & (i < q_hi), n, 0)
        k_end[i] = (hi + QB - 1) // QB
        return 0

    lax.fori_loop(0, sz.n_qb, block, 0)
    scal[sz.need_lo], scal[sz.need_hi] = first_a // RB, (last_b + KB - 1 + RB - 1) // RB
    scal[sz.full_hi] = (last_b + RB - 1) // RB

    step = KB // QB

    def emit(where, c, q, lo, n):
        def one(t, c):
            scal[where[0] + c] = q
            scal[where[1] + c] = lo + t * step
            return c + 1

        return lax.fori_loop(0, n, one, c)

    def close(where, c, q):
        scal[where[2]] = c
        for extra in range(2):
            scal[where[0] + c + extra] = q
            scal[where[1] + c + extra] = jnp.int32(sz.own_lo)

    fwd = (sz.fwd_q, sz.fwd_k, sz.fwd_n)
    both, far, back = sz.lists

    def own_block(i, counts):
        c_f, c_a, c_b = counts
        lo, end = scal[sz.k_lo + i], k_end[i]
        c_f = emit(fwd, c_f, i - sz.own_lo, lo, scal[sz.k_n + i])
        n = (jnp.maximum(sz.own_lo - lo, 0) + step - 1) // step
        c_b = emit(far, c_b, i, sz.own_lo - n * step, n)
        lo = jnp.maximum(lo, sz.own_lo)
        n = (jnp.minimum(end, sz.own_hi) - lo + step - 1) // step
        c_a = emit(both, c_a, i, lo, n)
        lo = lo + n * step
        c_b = emit(far, c_b, i, lo, (jnp.maximum(end - lo, 0) + step - 1) // step)
        return c_f, c_a, c_b

    zero = jnp.int32(0)
    c_f, c_a, c_b = lax.fori_loop(sz.own_lo, sz.own_hi, own_block, (zero, zero, zero))

    def halo_block(i, c):
        return emit(back, c, i, scal[sz.k_lo + i], scal[sz.k_n + i])

    c_c = lax.fori_loop(sz.own_hi, sz.n_qb, halo_block, lax.fori_loop(0, sz.own_lo, halo_block, zero))
    close(fwd, c_f, jnp.int32(sz.own_qb))
    for where_to, c in zip(sz.lists, (c_a, c_b, c_c)):
        close(where_to, c, jnp.int32(sz.own_lo))
    core = replica % 2
    for k in range(n_group):
        for h in range(2):
            scal[sz.places + 2 * k + h] = 2 * (group ^ k) + (core ^ h)

    half = HEAD_DIM // 2
    blocks = sz.ext // QB
    g = base + QB * lax.broadcasted_iota(jnp.int32, (blocks, QB), 0) + lax.broadcasted_iota(jnp.int32, (blocks, QB), 1)
    seg = jnp.full((blocks, QB), -1, jnp.int32)
    first = jnp.zeros((blocks, QB), jnp.int32)
    for j in range(n_seq):
        hit = g >= starts[j]
        seg = jnp.where(hit, j, seg)
        first = jnp.where(hit, starts[j], first)
    seg_buf[...] = jnp.where(g >= total, n_seq, seg) & 15
    pos_buf[...] = jnp.maximum(g - first, 0).astype(F32)
    freq = jnp.exp(lax.broadcasted_iota(jnp.int32, (half, QB), 0).astype(F32) * (-2.0 / HEAD_DIM * math.log(ROPE_BASE)))

    def rows(b, _):
        r0 = pl.multiple_of(b * QB, QB)
        hot = (seg_buf[pl.ds(b, 1), :] == lax.broadcasted_iota(jnp.int32, (LANES, QB), 0)).astype(F32).T
        qf[pl.ds(r0, QB), :] = (hot * BIG).astype(BF)
        lane = lax.broadcasted_iota(jnp.int32, (QB, LANES), 1)
        kf[pl.ds(r0, QB), :] = jnp.where(lane < 16, 1.0 - hot, 0.0).astype(BF)
        ang = freq * pos_buf[pl.ds(b, 1), :]
        co, si = jnp.cos(ang), jnp.sin(ang)
        cos[pl.ds(r0, QB), :] = jnp.concatenate([co] * 4, axis=0).T
        sin[pl.ds(r0, QB), :] = jnp.concatenate([-si, si, -si, si], axis=0).T
        return 0

    lax.fori_loop(0, blocks, rows, 0)


def plan_call(sz, n_replica, n_group, where, lengths):
    sh = jax.ShapeDtypeStruct
    smem = pl.BlockSpec(memory_space=pltpu.SMEM)
    vmem = pl.BlockSpec(memory_space=pltpu.VMEM)
    n_seq = lengths.shape[1]
    return pl.pallas_call(
        functools.partial(plan_kernel, sz, n_replica, n_group),
        in_specs=[smem, smem],
        out_specs=[smem] + [vmem] * 4,
        out_shape=[sh((sz.places + 2 * n_group,), jnp.int32)] + [sh((sz.ext, LANES), BF)] * 2 + [sh((sz.ext, LANES), F32)] * 2,
        scratch_shapes=[pltpu.SMEM((n_seq + 1,), jnp.int32), pltpu.SMEM((sz.n_qb,), jnp.int32), pltpu.VMEM((sz.ext // QB, QB), jnp.int32), pltpu.VMEM((sz.ext // QB, QB), F32)],
        compiler_params=params(60),
        cost_estimate=pl.CostEstimate(flops=10_000_000_000, bytes_accessed=5_000_000, transcendentals=0),
        name="plan",
    )(where, lengths)


def fetch_qkv(place, pieces, w, sem):
    copies = []
    shard = w.shape[0] // (len(pieces) // 2)
    for t, piece in enumerate(pieces):
        copies.append(pltpu.make_async_copy(piece, w.at[pl.ds(row_of(place(t), shard), piece.shape[0]), :], sem.at[t]))
    return copies


def qkv_kernel(sz, n_pieces, scal, xl, xc, xr, *rest):
    pieces, (g1, cos, sin, qkv, kt, vt, n1t, w, sem) = rest[:n_pieces], rest[n_pieces:]
    i = pl.program_id(0)
    left_b, own_b = HALO // RB, sz.tok // RB
    own = (i >= left_b) & (i < left_b + own_b)

    @pl.when(i == 0)
    def _():
        copies = fetch_qkv(lambda t: scal[sz.places + t], pieces, w, sem)
        for c in copies:
            c.start()
        for c in copies:
            c.wait()

    @pl.when((i >= scal[sz.full_hi]) & (i < scal[sz.need_hi]))
    def _():
        qkv[...] = jnp.zeros_like(qkv)
        kt[...] = jnp.zeros_like(kt)
        vt[...] = jnp.zeros_like(vt)

    @pl.when((i >= scal[sz.need_lo]) & (i < scal[sz.full_hi]))
    def _():
        x = jnp.where(i < left_b, xl[...], jnp.where(i < left_b + own_b, xc[...], xr[...])).astype(F32)
        mean = jnp.mean(x, axis=-1, keepdims=True)
        cen = x - mean
        var = jnp.mean(cen * cen, axis=-1, keepdims=True)
        n1 = (cen * lax.rsqrt(var + EPS) * g1[...]).astype(BF)

        @pl.when(own)
        def _():
            n1t[...] = n1.T

        width = n1.shape[1]
        co, si = cos[...], sin[...]
        sc = HEAD_DIM ** -0.5 * LOG2E
        cq, sq = co * sc, si * sc
        for c in range(3 * width // 256):
            a = nn(n1, w[:, 256 * c : 256 * c + 256])
            part = 256 * c // width
            off = 256 * c - width * part
            if part < 2:
                cc, ss = (cq, sq) if part == 0 else (co, si)
                halves = []
                for h in range(2):
                    b = a[:, 128 * h : 128 * h + 128]
                    halves.append((b * cc + partner(b) * ss).astype(BF))
                r = jnp.concatenate(halves, axis=1)
            else:
                r = a.astype(BF)
            qkv[:, 256 * c : 256 * c + 256] = r
            if part == 1:
                kt[off : off + 256, :] = r.T
            if part == 2:
                vt[off : off + 256, :] = r.T


def qkv_call(sz, scal, xl, xc, xr, pieces, g1, cos, sin):
    tok, width, ext = sz.tok, sz.width, sz.ext
    own_b, lb = tok // RB, HALO // RB
    clampi = lambda lo, n: (lambda i, s: (jnp.clip(i - lo, 0, n - 1), 0))
    used = lambda i, s: jnp.clip(i, s[sz.need_lo], s[sz.need_hi] - 1)
    row = lambda i, s: (used(i, s), 0)
    fix = lambda i, s: (0, 0)
    col = lambda i, s: (0, used(i, s))
    sh = jax.ShapeDtypeStruct
    return pl.pallas_call(
        functools.partial(qkv_kernel, sz, len(pieces)),
        grid_spec=pltpu.PrefetchScalarGridSpec(
            num_scalar_prefetch=1,
            grid=(sz.blocks,),
            in_specs=[
                pl.BlockSpec((RB, width), clampi(0, lb)),
                pl.BlockSpec((RB, width), clampi(lb, own_b)),
                pl.BlockSpec((RB, width), clampi(lb + own_b, lb)),
                *[pl.BlockSpec(memory_space=pl.ANY)] * len(pieces),
                pl.BlockSpec((1, width), fix),
                pl.BlockSpec((RB, LANES), row),
                pl.BlockSpec((RB, LANES), row),
            ],
            out_specs=[
                pl.BlockSpec((RB, 3 * width), row),
                pl.BlockSpec((width, RB), col),
                pl.BlockSpec((width, RB), col),
                pl.BlockSpec((width, RB), lambda i, s: (0, jnp.clip(i - lb, 0, own_b - 1))),
            ],
            scratch_shapes=[pltpu.VMEM((width, 3 * width), BF), pltpu.SemaphoreType.DMA((len(pieces),))],
        ),
        out_shape=[sh((ext, 3 * width), BF), sh((width, ext), BF), sh((width, ext), BF), sh((width, tok), BF)],
        compiler_params=params(60, dimension_semantics=("arbitrary",)),
        cost_estimate=pl.CostEstimate(flops=14_000_000_000, bytes_accessed=30_000_000, transcendentals=0),
        name="qkv",
    )(scal, xl, xc, xr, *pieces, g1, cos, sin)


def split_heads(x):
    low = lax.broadcasted_iota(jnp.int32, x.shape, 1) < HEAD_DIM
    zero = jnp.zeros_like(x)
    return jnp.concatenate([jnp.where(low, x, zero), jnp.where(low, zero, x)], axis=0)


def lanes_of(p):
    return slice(LANES * p, LANES * p + LANES)


def fwd_kernel(sz, pg, scal, q, k, vt, qf, kf, out, out_t, lse, q2, buf_a, buf_b, acc, tops):
    nq = sz.own_qb
    ones = jnp.ones((16, KB), BF)
    for qi in range(nq):
        r0 = HALO + qi * QB
        fq = qf[r0 : r0 + QB, :]
        f2 = jnp.concatenate([fq, fq], axis=0)
        for p in range(pg):
            q2[qi, p] = jnp.concatenate([split_heads(q[r0 : r0 + QB, lanes_of(p)]), f2], axis=1)

    def zero(i, _):
        for p in range(pg):
            acc[i, p] = jnp.zeros((LANES + 16, 2 * QB), F32)
            tops[i, p] = jnp.zeros((8, 2 * QB), F32)
        return 0

    lax.fori_loop(0, nq + 1, zero, 0)

    def scores(qi, k0, p, fk):
        return nt(jnp.concatenate([k[pl.ds(k0, KB), lanes_of(p)], fk], axis=1), q2[qi, p])

    def mixed(k0, p, probs):
        va = jnp.concatenate([vt[lanes_of(p), pl.ds(k0, KB)], ones], axis=0)
        return nn(va, probs.astype(BF))

    def tile(i):
        return scal[sz.fwd_q + i], pl.multiple_of(scal[sz.fwd_k + i] * QB, QB)

    def score_tile(i, buf):
        qi, k0 = tile(i)
        qi = jnp.minimum(qi, nq - 1)
        fk = kf[pl.ds(k0, KB), :]
        for p in range(pg):
            buf[p] = scores(qi, k0, p, fk)

    def mix_tile(i, buf):
        qi, k0 = tile(i)
        for p in range(pg):
            acc[qi, p] += mixed(k0, p, jnp.exp2(buf[p]))

    score_tile(0, buf_a)

    def body(j, _):
        score_tile(2 * j + 1, buf_b)
        mix_tile(2 * j, buf_a)
        score_tile(2 * j + 2, buf_a)
        mix_tile(2 * j + 1, buf_b)
        return 0

    lax.fori_loop(0, (scal[sz.fwd_n] + 1) // 2, body, 0)

    low = high = acc[0, 0, LANES : LANES + 1, :]
    for qi in range(nq):
        for p in range(pg):
            total = acc[qi, p, LANES : LANES + 1, :]
            low, high = jnp.minimum(low, total), jnp.maximum(high, total)
    safe = (jnp.min(low) > 2.0 ** -60) & (jnp.max(high) < 2.0 ** 100)

    @pl.when(jnp.logical_not(safe))
    def _():
        lax.fori_loop(0, nq, zero, 0)

        def per_q(qi, _):
            lo, n = scal[sz.k_lo + sz.own_lo + qi], scal[sz.k_n + sz.own_lo + qi]
            for p in range(pg):
                def top(t, m):
                    k0 = pl.multiple_of(lo * QB + t * KB, QB)
                    return jnp.maximum(m, jnp.max(scores(qi, k0, p, kf[pl.ds(k0, KB), :]), axis=0, keepdims=True))

                m = lax.fori_loop(0, n, top, jnp.full((1, 2 * QB), BIG, F32))
                tops[qi, p] = jnp.broadcast_to(m, (8, 2 * QB))

                def add(t, _):
                    k0 = pl.multiple_of(lo * QB + t * KB, QB)
                    acc[qi, p] += mixed(k0, p, jnp.exp2(scores(qi, k0, p, kf[pl.ds(k0, KB), :]) - m))
                    return 0

                lax.fori_loop(0, n, add, 0)
            return 0

        lax.fori_loop(0, nq, per_q, 0)

    def finish(qi, _):
        o0 = pl.multiple_of(qi * QB, QB)
        for p in range(pg):
            a = acc[qi, p]
            total = a[LANES : LANES + 1, :]
            inv = 1.0 / total
            o_t = jnp.concatenate([a[:HEAD_DIM, :QB] * inv[:, :QB], a[HEAD_DIM:LANES, QB:] * inv[:, QB:]], axis=0).astype(BF)
            out_t[lanes_of(p), pl.ds(o0, QB)] = o_t
            out[pl.ds(o0, QB), lanes_of(p)] = o_t.T
            st = tops[qi, p, 0:1, :] + jnp.log2(total)
            lse[p, 0:1, pl.ds(o0, QB)] = st[:, :QB]
            lse[p, 1:2, pl.ds(o0, QB)] = st[:, QB:]
        return 0

    lax.fori_loop(0, nq, finish, 0)


def fwd_call(sz, scal, qkv, vt, qf, kf, pg):
    ext, tok, width = sz.ext, sz.tok, sz.width
    pairs = width // LANES
    steps = pairs // pg
    wide = LANES * pg
    col = lambda off: (lambda i, s: (0, off + i))
    fix = lambda i, s: (0, 0)
    sh = jax.ShapeDtypeStruct
    return pl.pallas_call(
        functools.partial(fwd_kernel, sz, pg),
        grid_spec=pltpu.PrefetchScalarGridSpec(
            num_scalar_prefetch=1,
            grid=(steps,),
            in_specs=[
                pl.BlockSpec((ext, wide), col(0)),
                pl.BlockSpec((ext, wide), col(steps)),
                pl.BlockSpec((wide, ext), lambda i, s: (i, 0)),
                pl.BlockSpec((ext, LANES), fix),
                pl.BlockSpec((ext, LANES), fix),
            ],
            out_specs=[
                pl.BlockSpec((tok, wide), col(0)),
                pl.BlockSpec((wide, tok), lambda i, s: (i, 0)),
                pl.BlockSpec((pg, 2, tok), lambda i, s: (i, 0, 0)),
            ],
            scratch_shapes=[
                pltpu.VMEM((sz.own_qb, pg, 2 * QB, 2 * LANES), BF),
                pltpu.VMEM((pg, KB, 2 * QB), F32),
                pltpu.VMEM((pg, KB, 2 * QB), F32),
                pltpu.VMEM((sz.own_qb + 1, pg, LANES + 16, 2 * QB), F32),
                pltpu.VMEM((sz.own_qb + 1, pg, 8, 2 * QB), F32),
            ],
        ),
        out_shape=[sh((tok, width), BF), sh((width, tok), BF), sh((pairs, 2, tok), F32)],
        compiler_params=params(60, dimension_semantics=("arbitrary",)),
        cost_estimate=pl.CostEstimate(flops=30_000_000_000, bytes_accessed=15_000_000, transcendentals=0),
        name="attn_forward",
    )(scal, qkv, qkv, vt, qf, kf)


def fetch_mlp(place, pieces, wo, wi, wd, sem, width):
    copies = []
    shards = len(pieces) // 2
    half, half_d = half_of(wo.shape[0] // shards), half_of(wd.shape[0] // shards)
    t_cols = wi.shape[1] // width
    for t, piece in enumerate(pieces):
        row0 = row_of(place(t), wo.shape[0] // shards)
        row_d = row_of(place(t), wd.shape[0] // shards)
        copies.append(pltpu.make_async_copy(piece.at[0:half, :], wo.at[pl.ds(row0, half), :], sem.at[t, 0]))
        for j in range(t_cols):
            copies.append(pltpu.make_async_copy(
                piece.at[half * (j + 1) : half * (j + 2), :],
                wi.at[pl.ds(row0, half), width * j : width * j + width], sem.at[t, j + 1]))
        lo = half * (t_cols + 1)
        copies.append(pltpu.make_async_copy(piece.at[lo : lo + half_d, :], wd.at[pl.ds(row_d, half_d), :], sem.at[t, t_cols + 1]))
    return copies


def mid_kernel(n_pieces, at, scal, *refs):
    pieces, refs = refs[:n_pieces], refs[n_pieces:]
    wo, wi, wd, sem = refs[-4:]

    @pl.when(pl.program_id(0) == 0)
    def _():
        copies = fetch_mlp(lambda t: scal[at + t], pieces, wo, wi, wd, sem, wo.shape[1])
        for c in copies:
            c.start()
        for c in copies:
            c.wait()

    x, o, gy, g2, ind = refs[:5]
    mid_body(x, o, gy, wo, wi, wd, g2, ind, *refs[5:-4])


def mid_body(x, o, gy, wo, wi, wd, g2, ind, out, mt_o, gu_o, n2t_o, gh2b_o, go_o, dlt):
    ff = wd.shape[0]
    h2 = x[...].astype(F32) + nn(o[...], wo[...])
    mean = jnp.mean(h2, axis=-1, keepdims=True)
    cen = h2 - mean
    r2 = lax.rsqrt(jnp.mean(cen * cen, axis=-1, keepdims=True) + EPS)
    nh = cen * r2
    g = g2[...]
    n2 = (nh * g).astype(BF)
    n2t_o[...] = n2.T
    gyb = gy[...]
    y = h2
    gn2 = jnp.zeros_like(h2)
    step = 384
    for c in range(ff // step):
        lo = c * step
        a = nn(n2, wi[:, lo : lo + step])
        b = nn(n2, wi[:, ff + lo : ff + lo + step])
        gm = nt(gyb, wd[lo : lo + step, :])
        half = 0.5 * (1.0 + lax.erf(a * (2.0 ** -0.5)))
        gel = a * half
        mm = (gel * b).astype(BF)
        mt_o[lo : lo + step, :] = mm.T
        y = y + nn(mm, wd[lo : lo + step, :])
        dgel = half + a * (jnp.exp(-0.5 * a * a) * (1.0 / math.sqrt(2.0 * math.pi)))
        ga = (gm * b * dgel).astype(BF)
        gb = (gm * gel).astype(BF)
        gu_o[:, lo : lo + step] = ga
        gu_o[:, ff + lo : ff + lo + step] = gb
        gn2 = gn2 + nt(ga, wi[:, lo : lo + step]) + nt(gb, wi[:, ff + lo : ff + lo + step])
    out[...] = y.astype(BF)

    t = gn2 * g
    gh2 = gyb.astype(F32) + r2 * (t - jnp.mean(t, axis=-1, keepdims=True) - nh * jnp.mean(t * nh, axis=-1, keepdims=True))
    gb16 = gh2.astype(BF)
    gh2b_o[...] = gb16
    go = nt(gb16, wo[...]).astype(BF)
    go_o[...] = go
    prod = go.astype(F32) * o[...].astype(F32)
    hi = prod.astype(BF)
    lo_part = (prod - hi.astype(F32)).astype(BF)
    sums = nt(ind[...], hi) + nt(ind[...], lo_part)
    for p in range(dlt.shape[0]):
        dlt[p] = sums[2 * p : 2 * p + 2, :]


def mid_call(sz, scal, pieces, x, o, gy, g2, ff):
    tok, width = x.shape
    heads = jnp.arange(16, dtype=jnp.int32)
    ind = (heads[:, None] == (jnp.arange(width, dtype=jnp.int32) // HEAD_DIM)[None, :]).astype(BF)
    row = lambda i, s: (i, 0)
    fix = lambda i, s: (0, 0)
    rs = lambda n: pl.BlockSpec((RB, n), row)
    cs = lambda n: pl.BlockSpec((n, RB), lambda i, s: (0, i))
    fs = lambda a: pl.BlockSpec(a.shape, fix)
    sh = jax.ShapeDtypeStruct
    n = len(pieces)
    return pl.pallas_call(
        functools.partial(mid_kernel, n, sz.places),
        grid_spec=pltpu.PrefetchScalarGridSpec(
            num_scalar_prefetch=1,
            grid=(tok // RB,),
            in_specs=[*[pl.BlockSpec(memory_space=pl.ANY)] * n, rs(width), rs(width), rs(width), fs(g2), fs(ind)],
            out_specs=[rs(width), cs(ff), rs(2 * ff), cs(width), rs(width), rs(width),
                       pl.BlockSpec((width // LANES, 2, RB), lambda i, s: (0, 0, i))],
            scratch_shapes=[pltpu.VMEM((width, width), BF), pltpu.VMEM((width, 2 * ff), BF), pltpu.VMEM((ff, width), BF),
                            pltpu.SemaphoreType.DMA((n, 2 * ff // width + 2))],
        ),
        out_shape=[sh((tok, width), BF), sh((ff, tok), BF), sh((tok, 2 * ff), BF), sh((width, tok), BF),
                   sh((tok, width), BF), sh((tok, width), BF),
                   sh((width // LANES, 2, tok), F32)],
        compiler_params=params(60, dimension_semantics=("arbitrary",)),
        cost_estimate=pl.CostEstimate(flops=13_000_000_000 * 2, bytes_accessed=30_000_000, transcendentals=0),
        name="middle",
    )(scal, *pieces, x, o, gy, g2, ind)


def put_halves(core, keep, send, rows0, values, n_group):
    rows = values.shape[0] // n_group
    half = half_of(rows)

    def store(first, second):
        for g in range(n_group):
            lo, hi = rows * g, rows * (g + 1)
            first[g, pl.ds(rows0, half), :] = values[lo : lo + half, :]
            second[g, pl.ds(rows0, half), :] = values[hi - half : hi, :]

    @pl.when(core == 0)
    def _():
        store(keep, send)

    @pl.when(core != 0)
    def _():
        store(send, keep)


def put_halves(core, keep, send, rows0, values, n_group):
    rows = values.shape[0] // n_group
    half = half_of(rows)

    def store(first, second):
        for g in range(n_group):
            lo, hi = rows * g, rows * (g + 1)
            first[g, pl.ds(rows0, half), :] = values[lo : lo + half, :]
            second[g, pl.ds(rows0, half), :] = values[hi - half : hi, :]

    @pl.when(core == 0)
    def _():
        store(keep, send)

    @pl.when(core != 0)
    def _():
        store(send, keep)


def in_grad_kernel(n_group, at, scal, n2t, gu, keep, send):
    half = half_of(n2t.shape[0] // n_group)
    row0 = pl.multiple_of(pl.program_id(0) * half, 16)
    put_halves(scal[at] % 2, keep, send, row0, nn(n2t[...], gu[...]).astype(BF), n_group)


def in_grad_call(sz, scal, n2t, gu, n_group):
    width, tok = n2t.shape
    n_cols = gu.shape[1] // width
    rows = n_cols * half_of(width // n_group)
    out = jax.ShapeDtypeStruct((n_group, rows, width), BF)
    return pl.pallas_call(
        functools.partial(in_grad_kernel, n_group, sz.places),
        grid_spec=pltpu.PrefetchScalarGridSpec(
            num_scalar_prefetch=1,
            grid=(n_cols,),
            in_specs=[pl.BlockSpec((width, tok), lambda j, s: (0, 0)), pl.BlockSpec((tok, width), lambda j, s: (0, j))],
            out_specs=[pl.BlockSpec((n_group, rows, width), lambda j, s: (0, 0, 0))] * 2,
        ),
        out_shape=[out, out],
        compiler_params=params(60, dimension_semantics=("arbitrary",)),
        cost_estimate=pl.CostEstimate(flops=8_000_000_000, bytes_accessed=10_000_000, transcendentals=0),
        name="in_weight_gradient",
    )(scal, n2t, gu)


def down_out_kernel(n_group, at, scal, mt, gy, ot_h, gh_h, keep, send, ot, gh, sem):
    copies = [pltpu.make_async_copy(ot_h, ot, sem.at[0]), pltpu.make_async_copy(gh_h, gh, sem.at[1])]
    for c in copies:
        c.start()
    put_halves(scal[at] % 2, keep, send, 0, nn(mt[...], gy[...]).astype(BF), n_group)
    for c in copies:
        c.wait()
    used = half_of(mt.shape[0] // n_group) + half_of(ot.shape[0] // n_group)
    put_halves(scal[at] % 2, keep, send, half_of(mt.shape[0] // n_group), nn(ot[...], gh[...]).astype(BF), n_group)
    if used < keep.shape[1]:
        for ref in (keep, send):
            ref[:, used:, :] = jnp.zeros((n_group, keep.shape[1] - used, keep.shape[2]), BF)


def down_out_call(sz, scal, mt, gy, ot, gh, n_group, rows):
    width, tok = ot.shape
    ff = mt.shape[0]
    out = jax.ShapeDtypeStruct((n_group, rows, width), BF)
    anyspec = pl.BlockSpec(memory_space=pl.ANY)
    fix = lambda j, s: (0, 0)
    return pl.pallas_call(
        functools.partial(down_out_kernel, n_group, sz.places),
        grid_spec=pltpu.PrefetchScalarGridSpec(
            num_scalar_prefetch=1,
            grid=(1,),
            in_specs=[pl.BlockSpec((ff, tok), fix), pl.BlockSpec((tok, width), fix), anyspec, anyspec],
            out_specs=[pl.BlockSpec((n_group, rows, width), lambda j, s: (0, 0, 0))] * 2,
            scratch_shapes=[pltpu.VMEM((width, tok), BF), pltpu.VMEM((tok, width), BF), pltpu.SemaphoreType.DMA((2,))],
        ),
        out_shape=[out, out],
        compiler_params=params(60, dimension_semantics=("arbitrary",)),
        cost_estimate=pl.CostEstimate(flops=7_000_000_000, bytes_accessed=10_000_000, transcendentals=0),
        name="down_out_weight_gradients",
    )(scal, mt, gy, ot, gh)


def bwd_kernel(sz, pg, at, n_group, scal, qkv_h, kt_h, qf_h, kf_h, gl_h, gc_h, gr_h, cos_h, sin_h, n1t_h,
               lse_c, dlt_c, lse_l, dlt_l, lse_r, dlt_r, grad, keep, send,
               q, k, v, kt, qf, kf, go, cos, sin, n1t, q2, g2, gka, gva, gqa, st, s_a, p_a, s_b, p_b, sem):
    n_qb, tok, width = sz.n_qb, sz.tok, sz.width
    wide = LANES * pg
    q_lo, q_hi = scal[sz.q_lo], scal[sz.q_hi]
    ext = q.shape[0]
    cols = lambda part: pl.ds(part * width + at * wide, wide)
    near, left = pl.ds(HALO, tok + QB), pl.ds(0, HALO)
    right, own = pl.ds(HALO + tok + QB, ext - HALO - tok - QB), pl.ds(HALO, tok)

    def rows(seg):
        return [(qkv_h.at[seg, cols(part)], dst.at[seg, :]) for part, dst in ((0, q), (1, k), (2, v))] + [
            (kt_h.at[cols(0), seg], kt.at[:, seg])]

    first = [(gc_h.at[:, cols(0)], go.at[own, :]), (qf_h, qf), (kf_h, kf), *rows(near)]
    second = [*rows(left), *rows(right), (gl_h.at[:, cols(0)], go.at[left, :]),
              (gr_h.at[:, cols(0)], go.at[pl.ds(HALO + tok, HALO), :])]
    third = [(cos_h.at[own, :], cos), (sin_h.at[own, :], sin), (n1t_h, n1t)]
    copies = [pltpu.make_async_copy(a, b, sem.at[t]) for t, (a, b) in enumerate(first + second + third)]
    n_first, n_second = len(first), len(first) + len(second)
    for c in copies:
        c.start()

    for row, parts in ((0, (lse_l, lse_c, lse_r)), (1, (dlt_l, dlt_c, dlt_r))):
        for p in range(pg):
            b_at = 0
            for part in parts:
                for b in range(part.shape[2] // QB):
                    for h in range(2):
                        st[b_at, p, row : row + 1, QB * h : QB * h + QB] = part[p, h : h + 1, QB * b : QB * b + QB]
                    b_at += 1

    for c in copies[:n_first]:
        c.wait()

    def prep(i, _):
        r0 = pl.multiple_of(i * QB, QB)
        fq = qf[pl.ds(r0, QB), :]
        f2 = jnp.concatenate([fq, fq], axis=0)
        for p in range(pg):
            q2[i, p] = jnp.concatenate([split_heads(q[pl.ds(r0, QB), lanes_of(p)]), f2], axis=1)
            g2[i, p] = split_heads(go[pl.ds(r0, QB), lanes_of(p)])
            gqa[i, p] = jnp.zeros((LANES, 2 * QB), F32)
            gka[p, pl.ds(r0, QB), :] = jnp.zeros((QB, LANES), F32)
            gva[p, pl.ds(r0, QB), :] = jnp.zeros((QB, LANES), F32)
        return 0

    lax.fori_loop(sz.own_lo, sz.own_hi, prep, 0)

    def run(where, for_keys, for_queries):
        def tile(i):
            return scal[where[0] + i], pl.multiple_of(scal[where[1] + i] * QB, QB)

        def score_tile(i, s_buf, p_buf):
            qi, k0 = tile(i)
            fk = kf[pl.ds(k0, KB), :]
            for p in range(pg):
                s_buf[p] = nt(jnp.concatenate([k[pl.ds(k0, KB), lanes_of(p)], fk], axis=1), q2[qi, p])
                p_buf[p] = nt(v[pl.ds(k0, KB), lanes_of(p)], g2[qi, p])

        def grad_tile(i, s_buf, p_buf):
            qi, k0 = tile(i)
            dead = jnp.where(i < scal[where[2]], 0.0, 1e38).astype(F32)
            for p in range(pg):
                pr = jnp.exp2(s_buf[p] - (st[qi, p, 0:1, :] + dead))
                ds = (pr * (p_buf[p] - st[qi, p, 1:2, :])).astype(BF)
                if for_keys:
                    gva[p, pl.ds(k0, KB), :] += nn(pr.astype(BF), g2[qi, p])
                    gka[p, pl.ds(k0, KB), :] += nn(ds, q2[qi, p, :, :LANES])
                if for_queries:
                    gqa[qi, p] += nn(kt[lanes_of(p), pl.ds(k0, KB)], ds)

        @pl.when(scal[where[2]] > 0)
        def _():
            score_tile(0, s_a, p_a)

            def body(j, _):
                score_tile(2 * j + 1, s_b, p_b)
                grad_tile(2 * j, s_a, p_a)
                score_tile(2 * j + 2, s_a, p_a)
                grad_tile(2 * j + 1, s_b, p_b)
                return 0

            lax.fori_loop(0, (scal[where[2]] + 1) // 2, body, 0)

    run(sz.lists[0], True, True)
    for c in copies[n_first:n_second]:
        c.wait()
    lax.fori_loop(q_lo, sz.own_lo, prep, 0)
    lax.fori_loop(sz.own_hi, q_hi, prep, 0)
    run(sz.lists[1], False, True)
    run(sz.lists[2], True, False)
    copies[n_second].wait()
    copies[n_second + 1].wait()

    sc = HEAD_DIM ** -0.5

    def finish(i, _):
        o0 = pl.multiple_of(i * QB, QB)
        r0 = pl.multiple_of(HALO + i * QB, QB)
        co, si = cos[pl.ds(o0, QB), :], sin[pl.ds(o0, QB), :]
        for p in range(pg):
            a = gqa[sz.own_lo + i, p]
            gt = jnp.concatenate([a[:HEAD_DIM, :QB], a[HEAD_DIM:, QB:]], axis=0).T * sc
            grad[pl.ds(o0, QB), LANES * p : LANES * p + LANES] = (gt * co - partner(gt) * si).astype(BF)
            b = gka[p, pl.ds(r0, QB), :] * LN2
            lo = wide + LANES * p
            grad[pl.ds(o0, QB), lo : lo + LANES] = (b * co - partner(b) * si).astype(BF)
            lo = 2 * wide + LANES * p
            grad[pl.ds(o0, QB), lo : lo + LANES] = gva[p, pl.ds(r0, QB), :].astype(BF)
        return 0

    lax.fori_loop(0, sz.own_qb, finish, 0)
    copies[n_second + 2].wait()
    for part in range(3):
        lanes = slice(wide * part, wide * part + wide)
        values = nn(n1t[...], grad[:, lanes]).astype(BF)
        put_halves(scal[sz.places] % 2, keep.at[:, :, lanes], send.at[:, :, lanes], 0, values, n_group)


def bwd_call(sz, scal, qkv, kt, qf, kf, gl, gc, gr, lse, dlt, st_l, st_r, cos, sin, n1t, pg, at, n_group):
    ext, tok, width, n_qb = sz.ext, sz.tok, sz.width, sz.n_qb
    steps = width // LANES // pg
    wide = LANES * pg
    half = half_of(width // n_group)
    spec = lambda shape, *idx: pl.BlockSpec(shape, lambda i, s: idx)
    sh = jax.ShapeDtypeStruct
    side = [spec((pg, 2, HALO), at, 0, 0), spec((pg, 2, HALO), steps + at, 0, 0)]
    out_spec = lambda shape: pl.BlockSpec(shape, lambda i, s: (0,) * len(shape), pipeline_mode=pl.Buffered(1))
    outs = [(tok, 3 * wide), (n_group, half, 3 * wide), (n_group, half, 3 * wide)]
    return pl.pallas_call(
        functools.partial(bwd_kernel, sz, pg, at, n_group),
        grid_spec=pltpu.PrefetchScalarGridSpec(
            num_scalar_prefetch=1,
            grid=(1,),
            in_specs=[pl.BlockSpec(memory_space=pl.ANY)] * 10
            + [spec((pg, 2, tok), at, 0, 0), spec((pg, 2, tok), at, 0, 0), *side, *side],
            out_specs=[out_spec(o) for o in outs],
            scratch_shapes=[
                *[pltpu.VMEM((ext, wide), BF)] * 3,
                pltpu.VMEM((wide, ext), BF),
                pltpu.VMEM((ext, LANES), BF),
                pltpu.VMEM((ext, LANES), BF),
                pltpu.VMEM((tok + 2 * HALO, wide), BF),
                pltpu.VMEM((tok, LANES), F32),
                pltpu.VMEM((tok, LANES), F32),
                pltpu.VMEM((width, tok), BF),
                pltpu.VMEM((n_qb, pg, 2 * QB, 2 * LANES), BF),
                pltpu.VMEM((n_qb, pg, 2 * QB, LANES), BF),
                pltpu.VMEM((pg, ext, LANES), F32),
                pltpu.VMEM((pg, ext, LANES), F32),
                pltpu.VMEM((n_qb, pg, LANES, 2 * QB), F32),
                pltpu.VMEM((n_qb, pg, 8, 2 * QB), F32),
                *[pltpu.VMEM((pg, KB, 2 * QB), F32)] * 4,
                pltpu.SemaphoreType.DMA((20,)),
            ],
        ),
        out_shape=[sh(o, BF) for o in outs],
        compiler_params=params(60, dimension_semantics=("arbitrary",)),
        cost_estimate=pl.CostEstimate(flops=35_000_000_000, bytes_accessed=20_000_000, transcendentals=0),
        name="attn_backward",
    )(scal, qkv, kt, qf, kf, gl, gc, gr, cos, sin, n1t, lse, dlt, st_l, st_l, st_r, st_r)


def gx_kernel(n_pieces, n_grads, at, scal, *refs):
    pieces, grads = refs[:n_pieces], refs[n_pieces : n_pieces + n_grads]
    x, gh2, g1, out, w, sem = refs[n_pieces + n_grads :]

    @pl.when(pl.program_id(0) == 0)
    def _():
        copies = fetch_qkv(lambda t: scal[at + t], pieces, w, sem)
        for c in copies:
            c.start()
        for c in copies:
            c.wait()

    width = x.shape[1]
    gn = None
    wide = grads[0].shape[1] // 3
    for part in range(3):
        lhs = jnp.concatenate([grad[:, wide * part : wide * part + wide] for grad in grads], axis=1)
        term = nt(lhs, w[:, width * part : width * part + width])
        gn = term if gn is None else gn + term
    xf = x[...].astype(F32)
    mean = jnp.mean(xf, axis=-1, keepdims=True)
    cen = xf - mean
    r1 = lax.rsqrt(jnp.mean(cen * cen, axis=-1, keepdims=True) + EPS)
    nh = cen * r1

    t = gn * g1[...]
    gx = gh2[...].astype(F32) + r1 * (t - jnp.mean(t, axis=-1, keepdims=True) - nh * jnp.mean(t * nh, axis=-1, keepdims=True))
    out[...] = gx.astype(BF)


def gx_call(sz, scal, pieces, grads, x, gh2, g1):
    tok, width = x.shape
    row = lambda i, s: (i, 0)
    fix = lambda i, s: (0, 0)
    rs = pl.BlockSpec((RB, width), row)
    n = len(pieces)
    return pl.pallas_call(
        functools.partial(gx_kernel, n, len(grads), sz.places),
        grid_spec=pltpu.PrefetchScalarGridSpec(
            num_scalar_prefetch=1,
            grid=(tok // RB,),
            in_specs=[*[pl.BlockSpec(memory_space=pl.ANY)] * n,
                      *[pl.BlockSpec((RB, g.shape[1]), row) for g in grads],
                      rs, rs, pl.BlockSpec(g1.shape, fix)],
            out_specs=rs,
            scratch_shapes=[pltpu.VMEM((width, 3 * width), BF), pltpu.SemaphoreType.DMA((n,))],
        ),
        out_shape=jax.ShapeDtypeStruct((tok, width), BF),
        compiler_params=params(60, dimension_semantics=("arbitrary",)),
        cost_estimate=pl.CostEstimate(flops=4_000_000_000, bytes_accessed=15_000_000, transcendentals=0),
        name="input_gradient",
    )(scal, *pieces, *grads, x, gh2, g1)


def gain_row(w, grad, gain):
    low = lambda v: v.astype(BF).astype(F32)
    total = jnp.sum(low(w) * grad, axis=1, keepdims=True)
    return jnp.broadcast_to(total, (total.shape[0], LANES)).T[0:1, :] / low(gain)


def in_core_order(core, mine, other, use):
    @pl.when(core == 0)
    def _():
        use(mine, other)

    @pl.when(core != 0)
    def _():
        use(other, mine)


def qkv_end_kernel(at, scal, t0, s0, t1, s1, w, gain, out, g_out):
    shard = w.shape[0]
    half = t0.shape[0]
    wide = t0.shape[1] // 3

    def use(first, second):
        for refs, lo in ((first, 0), (second, shard - half)):
            for j, ref in enumerate(refs):
                for part in range(3):
                    c = wide * (len(refs) * part + j)
                    out[lo : lo + half, c : c + wide] = ref[:, wide * part : wide * part + wide].astype(F32)

    in_core_order(scal[at] % 2, (t0, t1), (s0, s1), use)
    g_out[...] = gain_row(w[...], out[...], gain[...])


def mlp_end_kernel(at, scal, t, s, w, gain, d_in, d_down, d_out, g_out):
    shard, shard_d, width = w.shape[0], d_down.shape[0], d_out.shape[1]
    half, half_d = half_of(shard), half_of(shard_d)
    n_cols = w.shape[1] // width

    def use(first, second):
        for ref, h in ((first, 0), (second, 1)):
            lo, lo_d = h * (shard - half), h * (shard_d - half_d)
            for j in range(n_cols):
                d_in[lo : lo + half, width * j : width * j + width] = ref[half * j : half * j + half, :].astype(F32)
            at_d = half * n_cols
            d_down[lo_d : lo_d + half_d, :] = ref[at_d : at_d + half_d, :].astype(F32)
            d_out[lo : lo + half, :] = ref[at_d + half_d : at_d + half_d + half, :].astype(F32)

    in_core_order(scal[at] % 2, t, s, use)
    g_out[...] = gain_row(w[...], d_in[...], gain[...])


def end_call(kernel, name, sz, scal, arrays, w, gain, shapes):
    smem = pl.BlockSpec(memory_space=pltpu.SMEM)
    vmem = pl.BlockSpec(memory_space=pltpu.VMEM)
    outs = [*shapes, (1, w.shape[0])]
    return pl.pallas_call(
        functools.partial(kernel, sz.places),
        in_specs=[smem] + [vmem] * (len(arrays) + 2),
        out_specs=[vmem] * len(outs),
        out_shape=[jax.ShapeDtypeStruct(o, F32) for o in outs],
        compiler_params=params(60),
        cost_estimate=pl.CostEstimate(flops=3_000_000_000, bytes_accessed=5_000_000, transcendentals=0),
        name=name,
    )(scal, *arrays, w, gain.reshape(1, -1))


class Net:
    def __init__(self, n_replica, n_group):
        self.n_replica, self.n_group, self.n_z = n_replica, n_group, n_replica // 2
        self.replica, self.group = lax.axis_index("replica"), lax.axis_index("group")
        self.core = self.replica & 1

    def shift(self, a, step):
        pairs = [(i, i + step) for i in range(self.n_replica) if 0 <= i + step < self.n_replica]
        return lax.ppermute(a, "replica", pairs)

    def core_swap(self, a):
        return lax.ppermute(a, "replica", [(i, i ^ 1) for i in range(self.n_replica)])

    def across(self, a, k):
        return lax.ppermute(a, "group", [(i, i ^ k) for i in range(self.n_group)])

    def across_swap(self, a, k):
        n = self.n_group
        pairs = [(r * n + g, (r ^ 1) * n + (g ^ k)) for r in range(self.n_replica) for g in range(n)]
        return lax.ppermute(a, ("replica", "group"), pairs)

    def gather_near(self, mine, other):
        got = {(0, 0): mine, (0, 1): other}
        for k in (1, 2) if self.n_group == 4 else range(1, self.n_group):
            got[k, 0] = self.across(mine, k)
        return got

    def gather_far(self, got):
        got = dict(got)
        if self.n_group == 4:
            got[3, 0] = self.across(got[2, 0], 1)
            got[3, 1] = self.across_swap(got[1, 0], 2)
        for k in range(1, self.n_group):
            if (k, 1) not in got:
                got[k, 1] = self.core_swap(got[k, 0])
        return [got[key] for key in sorted(got)]

    def parts(self, pairs):
        def part(k):
            at = lambda a: lax.dynamic_index_in_dim(a, self.group ^ k, 0, keepdims=False).astype(F32)
            return jnp.concatenate([at(keep) + at(got) for got, keep in pairs], axis=0)

        return [part(0)] + [part(k).astype(BF) for k in range(1, self.n_group)]

    def group_send(self, parts):
        return parts[0], [self.across(parts[k], k) for k in range(1, self.n_group)]

    def add(self, own, moved):
        for m in moved:
            own = own + m.astype(F32)
        return own

    def along(self, a, k):
        return lax.ppermute(a, "replica", [(i, i ^ (2 * k)) for i in range(self.n_replica)])

    def z_scatter(self, s):
        shares = s.reshape(self.n_z, s.shape[0] // self.n_z, s.shape[1])
        share = lambda k: lax.dynamic_index_in_dim(shares, (self.replica // 2) ^ k, 0, keepdims=False)
        return share(0), [self.along(share(k).astype(BF), k) for k in range(1, self.n_z)]

    def z_gather(self, own, moved):
        t = self.add(own, moved).astype(BF)
        return [t] + [self.along(t, k) for k in range(1, self.n_z)]

    def z_join(self, shares):
        z = self.replica // 2
        return jnp.concatenate([lax.select_n(z, *[shares[j ^ i] for i in range(self.n_z)]) for j in range(self.n_z)], axis=0)


def on_device(tokens, cotangent, lengths, dealing, offsets, attn_gain, qkv_weight, out_weight,
              mlp_gain, in_weight, down_weight, *, n_replica, n_group):
    net = Net(n_replica, n_group)
    x, gy = tokens[0], cotangent[0]
    tok, width = x.shape
    ff = in_weight.shape[1] // 2
    sz = Sizes(tok, width)
    pairs = width // LANES
    pg = 3
    tie = lax.optimization_barrier

    def half_rows(a, h):
        n = half_of(a.shape[0])
        return lax.dynamic_slice_in_dim(a, (net.core ^ h) * (a.shape[0] - n), n, 0).astype(BF)

    def pack(h):
        wi = half_rows(in_weight, h)
        cols = [wi[:, width * j : width * j + width] for j in range(2 * ff // width)]
        return jnp.concatenate([half_rows(out_weight, h), *cols, half_rows(down_weight, h)], axis=0)

    near = net.gather_near(half_rows(qkv_weight, 0), half_rows(qkv_weight, 1))
    own_gain = jnp.stack([attn_gain, mlp_gain]).astype(BF)
    by_offset = [own_gain] + [net.across(own_gain, k) for k in range(1, n_group)]
    packs = pack(0), pack(1)
    where = jnp.stack([net.replica, net.group]).astype(jnp.int32)
    near, by_offset, packs, where = tie((near, by_offset, packs, where))
    scal, qf, kf, cos, sin = plan_call(sz, n_replica, n_group, where, lengths)

    x_l = net.shift(x[tok - HALO :], 1)
    x_r = net.shift(x[:HALO], -1)
    qkv_pieces = net.gather_far(near)
    by_offset = jnp.stack(by_offset)
    hit = (jnp.arange(n_group)[:, None] ^ net.group) == jnp.arange(n_group)[None, :]
    gains = jnp.sum(jnp.where(hit[:, :, None, None], by_offset[None].astype(F32), 0.0), axis=1)
    gains = gains.transpose(1, 0, 2).reshape(2, width)
    g1, g2 = gains[0:1], gains[1:2]
    packs, qkv_pieces, x_l, x_r, gains = tie((packs, qkv_pieces, x_l, x_r, gains))

    near = net.gather_near(*packs)
    qkv, kt, vt, n1t = qkv_call(sz, scal, x_l, x, x_r, qkv_pieces, g1, cos, sin)
    near, vt = tie((near, vt))
    mlp_pieces = net.gather_far(near)
    o, ot, lse = fwd_call(sz, scal, qkv, vt, qf, kf, pg)
    out, mt, gu, n2t, gh2b, go, dlt = mid_call(sz, scal, mlp_pieces, x, o, gy, g2, ff)

    go_l = net.shift(go[tok - HALO :], 1)
    go_r = net.shift(go[:HALO], -1)
    stats = jnp.concatenate([lse, dlt], axis=0)
    st_l = net.shift(stats[:, :, tok - HALO :], 1)
    st_r = net.shift(stats[:, :, :HALO], -1)

    keep_i, send_i = in_grad_call(sz, scal, n2t, gu, n_group)
    used = half_of(width // n_group) + half_of(ff // n_group)
    rows = used + -(keep_i.shape[1] + used) % (16 * net.n_z)
    keep_d, send_d = down_out_call(sz, scal, mt, gy, ot, gh2b, n_group, rows)
    mlp_parts = net.parts([(net.core_swap(send_i), keep_i), (net.core_swap(send_d), keep_d)])

    def attn_grad(at, dep):
        return bwd_call(sz, dep, qkv, kt, qf, kf, go_l, go, go_r, lse, dlt, st_l, st_r, cos, sin, n1t, pg, at, n_group)

    scal, mlp_parts = tie((scal, mlp_parts))
    grad0, keep0, send0 = attn_grad(0, scal)
    mlp = net.group_send(mlp_parts)
    keep0, send0, mlp = tie((keep0, send0, mlp))
    parts0 = net.parts([(net.core_swap(send0), keep0)])
    mlp = net.z_scatter(net.add(*mlp))
    scal, parts0 = tie((scal, parts0))
    sum0 = net.group_send(parts0)
    grad1, keep1, send1 = attn_grad(1, scal)
    sum0, mlp, scal, send1 = tie((sum0, mlp, scal, send1))

    got1 = net.core_swap(send1)
    mlp = net.z_gather(*mlp)
    got1, sum0 = tie((got1, sum0))
    parts1 = net.parts([(got1, keep1)])
    parts1, sum0 = tie((parts1, sum0))
    sum1 = net.group_send(parts1)
    sum0 = net.z_scatter(net.add(*sum0))
    sum1, scal = tie((net.add(*sum1), scal))

    sum1 = net.z_scatter(sum1)
    sum0 = net.z_gather(*sum0)
    gx = gx_call(sz, scal, qkv_pieces, [grad0, grad1], x, gh2b, g1)
    sum1, mlp, gx = tie((sum1, mlp, gx))
    sum1 = net.z_gather(*sum1)
    mlp_sum = net.z_join(mlp)
    sib_mlp = net.core_swap(mlp_sum)
    sum0 = net.z_join(sum0)
    sib0 = net.core_swap(sum0)

    shard, shard_d = width // n_group, ff // n_group
    d_in, d_down, d_out, d_g2 = end_call(mlp_end_kernel, "mlp_gradients_end", sz, scal, [mlp_sum, sib_mlp], in_weight, mlp_gain,
                                         [in_weight.shape, (shard_d, width), (shard, width)])
    sum1, sib0, d_in = tie((sum1, sib0, d_in))
    sum1 = net.z_join(sum1)
    d_qkv, d_g1 = end_call(qkv_end_kernel, "qkv_gradient_end", sz, scal, [sum0, sib0, sum1, net.core_swap(sum1)], qkv_weight,
                           attn_gain, [qkv_weight.shape])
    return (out[None], gx[None], d_g1[0], d_qkv, d_out, d_g2[0], d_in, d_down)


def solution(mesh):
    body = functools.partial(on_device, n_replica=mesh.shape["replica"], n_group=mesh.shape["group"])
    return jax.shard_map(
        body,
        mesh=mesh,
        in_specs=(
            P("group", "replica", None),
            P("group", "replica", None),
            P("group", None),
            P("group", None),
            P("group", None, None),
            P("group"),
            P("group", None),
            P("group", None),
            P("group"),
            P("group", None),
            P("group", None),
        ),
        out_specs=(
            P("group", "replica", None),
            P("group", "replica", None),
            P("group"),
            P("group", None),
            P("group", None),
            P("group"),
            P("group", None),
            P("group", None),
        ),
        check_vma=False,
    )
```

```python
import functools
import math

import jax
import jax.numpy as jnp
from jax import lax
from jax.experimental import pallas as pl
from jax.experimental.pallas import tpu as pltpu
from jax.sharding import PartitionSpec as P

HEADS = 12
HEAD_DIM = 64
LANES = 128
HALO = 768
RB = 256
QB = 128
KB = 256
STAT = 16
EPS = 1e-05
BIG = -1e30
ROPE_BASE = 160000.0
LOG2E = 1.4426950408889634
LN2 = 0.6931471805599453
BF = jnp.bfloat16
F32 = jnp.float32


def nt(a, b):
    return lax.dot_general(a, b, (((1,), (1,)), ((), ())), preferred_element_type=F32)


def nn(a, b):
    return lax.dot_general(a, b, (((1,), (0,)), ((), ())), preferred_element_type=F32)


def partner(x):
    lane = lax.broadcasted_iota(jnp.int32, x.shape, 1) % HEAD_DIM
    return jnp.where(lane < HEAD_DIM // 2, pltpu.roll(x, 96, 1), pltpu.roll(x, 32, 1))


def half_of(rows):
    return -(-rows // 32) * 16


def row_of(place, rows):
    return pl.multiple_of((place // 2) * rows + (place % 2) * (rows - half_of(rows)), 16)


def params(mib, **kw):
    return pltpu.CompilerParams(vmem_limit_bytes=mib * 1024 * 1024, **kw)


class Sizes:
    def __init__(self, tok, width):
        self.tok, self.width = tok, width
        self.ext = tok + 2 * HALO + RB
        self.n_qb = (tok + 2 * HALO) // QB
        self.own_qb, self.own_lo = tok // QB, HALO // QB
        self.own_hi = self.own_lo + self.own_qb
        tiles = -(-(QB + 2 * HALO + QB) // KB)
        self.cap_f = self.own_qb * tiles + 2
        halo_tiles = -(-(HALO + QB) // KB)
        caps = [self.own_qb * -(-tok // KB) + 2, 2 * self.own_qb * -(-HALO // KB) + 2, 2 * self.own_lo * halo_tiles + 2]
        self.k_lo, self.k_n = 0, self.n_qb
        self.q_lo, self.q_hi = 2 * self.n_qb, 2 * self.n_qb + 1
        self.need_lo, self.need_hi, self.full_hi = (2 * self.n_qb + i for i in (2, 3, 4))
        self.blocks = self.ext // RB
        self.fwd_q = self.full_hi + 1
        self.fwd_k, self.fwd_n = self.fwd_q + self.cap_f, self.fwd_q + 2 * self.cap_f
        self.lists, at = [], self.fwd_n + 1
        for cap in caps:
            self.lists.append((at, at + cap, at + 2 * cap))
            at += 2 * cap + 1
        self.places = at


def plan_kernel(sz, n_replica, n_group, where, lengths, scal, qf, kf, cos, sin, starts, k_end, seg_buf, pos_buf):
    n_seq = lengths.shape[1]
    total = n_replica * sz.tok
    replica, group = where[0], where[1]
    base = replica * sz.tok - HALO
    at = jnp.int32(0)
    for j in range(n_seq):
        starts[j] = at
        at = at + lengths[0, j]
    starts[n_seq] = at

    def first_of(g):
        f = jnp.int32(0)
        for j in range(n_seq):
            f = jnp.where(g >= starts[j], starts[j], f)
        return f

    def last_of(g):
        f = jnp.int32(total)
        for j in range(n_seq):
            f = jnp.where(g >= starts[j], starts[j + 1], f)
        return f

    own_a, own_b = base + HALO, base + HALO + sz.tok - 1
    first_a, last_a = first_of(own_a) - base, last_of(own_a) - base
    first_b, last_b = first_of(own_b) - base, last_of(own_b) - base
    q_lo, q_hi = first_a // QB, (last_b + QB - 1) // QB
    scal[sz.q_lo], scal[sz.q_hi] = q_lo, q_hi

    def block(i, _):
        e = i * QB
        left, right = i < sz.own_lo, i >= sz.own_hi
        lo = jnp.where(left, HALO, jnp.where(right, first_b, first_of(base + e) - base)) // QB
        hi = jnp.where(left, last_a, jnp.where(right, HALO + sz.tok, last_of(base + e + QB - 1) - base))
        n = (hi - lo * QB + (KB - 1)) // KB
        scal[sz.k_lo + i] = lo
        scal[sz.k_n + i] = jnp.where((i >= q_lo) & (i < q_hi), n, 0)
        k_end[i] = (hi + QB - 1) // QB
        return 0

    lax.fori_loop(0, sz.n_qb, block, 0)
    scal[sz.need_lo], scal[sz.need_hi] = first_a // RB, (last_b + KB - 1 + RB - 1) // RB
    scal[sz.full_hi] = (last_b + RB - 1) // RB

    step = KB // QB

    def emit(where, c, q, lo, n):
        def one(t, c):
            scal[where[0] + c] = q
            scal[where[1] + c] = lo + t * step
            return c + 1

        return lax.fori_loop(0, n, one, c)

    def close(where, c, q):
        scal[where[2]] = c
        for extra in range(2):
            scal[where[0] + c + extra] = q
            scal[where[1] + c + extra] = jnp.int32(sz.own_lo)

    fwd = (sz.fwd_q, sz.fwd_k, sz.fwd_n)
    both, far, back = sz.lists

    def own_block(i, counts):
        c_f, c_a, c_b = counts
        lo, end = scal[sz.k_lo + i], k_end[i]
        c_f = emit(fwd, c_f, i - sz.own_lo, lo, scal[sz.k_n + i])
        n = (jnp.maximum(sz.own_lo - lo, 0) + step - 1) // step
        c_b = emit(far, c_b, i, sz.own_lo - n * step, n)
        lo = jnp.maximum(lo, sz.own_lo)
        n = (jnp.minimum(end, sz.own_hi) - lo + step - 1) // step
        c_a = emit(both, c_a, i, lo, n)
        lo = lo + n * step
        c_b = emit(far, c_b, i, lo, (jnp.maximum(end - lo, 0) + step - 1) // step)
        return c_f, c_a, c_b

    zero = jnp.int32(0)
    c_f, c_a, c_b = lax.fori_loop(sz.own_lo, sz.own_hi, own_block, (zero, zero, zero))

    def halo_block(i, c):
        return emit(back, c, i, scal[sz.k_lo + i], scal[sz.k_n + i])

    c_c = lax.fori_loop(sz.own_hi, sz.n_qb, halo_block, lax.fori_loop(0, sz.own_lo, halo_block, zero))
    close(fwd, c_f, jnp.int32(sz.own_qb))
    for where_to, c in zip(sz.lists, (c_a, c_b, c_c)):
        close(where_to, c, jnp.int32(sz.own_lo))
    core = replica % 2
    for k in range(n_group):
        for h in range(2):
            scal[sz.places + 2 * k + h] = 2 * (group ^ k) + (core ^ h)

    half = HEAD_DIM // 2
    blocks = sz.ext // QB
    g = base + QB * lax.broadcasted_iota(jnp.int32, (blocks, QB), 0) + lax.broadcasted_iota(jnp.int32, (blocks, QB), 1)
    seg = jnp.full((blocks, QB), -1, jnp.int32)
    first = jnp.zeros((blocks, QB), jnp.int32)
    for j in range(n_seq):
        hit = g >= starts[j]
        seg = jnp.where(hit, j, seg)
        first = jnp.where(hit, starts[j], first)
    seg_buf[...] = jnp.where(g >= total, n_seq, seg) & 15
    pos_buf[...] = jnp.maximum(g - first, 0).astype(F32)
    freq = jnp.exp(lax.broadcasted_iota(jnp.int32, (half, QB), 0).astype(F32) * (-2.0 / HEAD_DIM * math.log(ROPE_BASE)))

    def rows(b, _):
        r0 = pl.multiple_of(b * QB, QB)
        hot = (seg_buf[pl.ds(b, 1), :] == lax.broadcasted_iota(jnp.int32, (LANES, QB), 0)).astype(F32).T
        qf[pl.ds(r0, QB), :] = (hot * BIG).astype(BF)
        lane = lax.broadcasted_iota(jnp.int32, (QB, LANES), 1)
        kf[pl.ds(r0, QB), :] = jnp.where(lane < 16, 1.0 - hot, 0.0).astype(BF)
        ang = freq * pos_buf[pl.ds(b, 1), :]
        co, si = jnp.cos(ang), jnp.sin(ang)
        cos[pl.ds(r0, QB), :] = jnp.concatenate([co] * 4, axis=0).T
        sin[pl.ds(r0, QB), :] = jnp.concatenate([-si, si, -si, si], axis=0).T
        return 0

    lax.fori_loop(0, blocks, rows, 0)


def plan_call(sz, n_replica, n_group, where, lengths):
    sh = jax.ShapeDtypeStruct
    smem = pl.BlockSpec(memory_space=pltpu.SMEM)
    vmem = pl.BlockSpec(memory_space=pltpu.VMEM)
    n_seq = lengths.shape[1]
    return pl.pallas_call(
        functools.partial(plan_kernel, sz, n_replica, n_group),
        in_specs=[smem, smem],
        out_specs=[smem] + [vmem] * 4,
        out_shape=[sh((sz.places + 2 * n_group,), jnp.int32)] + [sh((sz.ext, LANES), BF)] * 2 + [sh((sz.ext, LANES), F32)] * 2,
        scratch_shapes=[pltpu.SMEM((n_seq + 1,), jnp.int32), pltpu.SMEM((sz.n_qb,), jnp.int32), pltpu.VMEM((sz.ext // QB, QB), jnp.int32), pltpu.VMEM((sz.ext // QB, QB), F32)],
        compiler_params=params(60),
        cost_estimate=pl.CostEstimate(flops=10_000_000_000, bytes_accessed=5_000_000, transcendentals=0),
        name="plan",
    )(where, lengths)


def pack_kernel(where, wo, wi, wd, mine, other):
    width = wo.shape[1]
    n_cols = wi.shape[1] // width

    def put(dst, h):
        at = 0
        for ref, col in [(wo, 0)] + [(wi, j) for j in range(n_cols)] + [(wd, 0)]:
            n = half_of(ref.shape[0])
            lo = h * (ref.shape[0] - n)
            dst[at : at + n, :] = ref[lo : lo + n, width * col : width * col + width].astype(BF)
            at += n

    @pl.when(where[0] % 2 == 0)
    def _():
        put(mine, 0)
        put(other, 1)

    @pl.when(where[0] % 2 != 0)
    def _():
        put(mine, 1)
        put(other, 0)


def pack_call(where, wo, wi, wd):
    vmem = pl.BlockSpec(memory_space=pltpu.VMEM)
    rows = half_of(wo.shape[0]) * (1 + wi.shape[1] // wo.shape[1]) + half_of(wd.shape[0])
    out = jax.ShapeDtypeStruct((rows, wo.shape[1]), BF)
    return pl.pallas_call(
        pack_kernel,
        in_specs=[pl.BlockSpec(memory_space=pltpu.SMEM), vmem, vmem, vmem],
        out_specs=[vmem, vmem],
        out_shape=[out, out],
        compiler_params=params(60),
        cost_estimate=pl.CostEstimate(flops=3_000_000_000, bytes_accessed=5_000_000, transcendentals=0),
        name="pack_weights",
    )(where, wo, wi, wd)


def fetch_qkv(place, pieces, w, sem):
    copies = []
    shard = w.shape[0] // (len(pieces) // 2)
    for t, piece in enumerate(pieces):
        copies.append(pltpu.make_async_copy(piece, w.at[pl.ds(row_of(place(t), shard), piece.shape[0]), :], sem.at[t]))
    return copies


def qkv_kernel(sz, n_pieces, scal, xl, xc, xr, *rest):
    pieces, (g1, cos, sin, qkv, kt, vt, n1t, w, sem) = rest[:n_pieces], rest[n_pieces:]
    i = pl.program_id(0)
    left_b, own_b = HALO // RB, sz.tok // RB
    own = (i >= left_b) & (i < left_b + own_b)

    @pl.when(i == 0)
    def _():
        copies = fetch_qkv(lambda t: scal[sz.places + t], pieces, w, sem)
        for c in copies:
            c.start()
        for c in copies:
            c.wait()

    @pl.when((i >= scal[sz.full_hi]) & (i < scal[sz.need_hi]))
    def _():
        qkv[...] = jnp.zeros_like(qkv)
        kt[...] = jnp.zeros_like(kt)
        vt[...] = jnp.zeros_like(vt)

    @pl.when((i >= scal[sz.need_lo]) & (i < scal[sz.full_hi]))
    def _():
        x = jnp.where(i < left_b, xl[...], jnp.where(i < left_b + own_b, xc[...], xr[...])).astype(F32)
        mean = jnp.mean(x, axis=-1, keepdims=True)
        cen = x - mean
        var = jnp.mean(cen * cen, axis=-1, keepdims=True)
        n1 = (cen * lax.rsqrt(var + EPS) * g1[...]).astype(BF)

        @pl.when(own)
        def _():
            n1t[...] = n1.T

        width = n1.shape[1]
        co, si = cos[...], sin[...]
        sc = HEAD_DIM ** -0.5 * LOG2E
        cq, sq = co * sc, si * sc
        for c in range(3 * width // 256):
            a = nn(n1, w[:, 256 * c : 256 * c + 256])
            part = 256 * c // width
            off = 256 * c - width * part
            if part < 2:
                cc, ss = (cq, sq) if part == 0 else (co, si)
                halves = []
                for h in range(2):
                    b = a[:, 128 * h : 128 * h + 128]
                    halves.append((b * cc + partner(b) * ss).astype(BF))
                r = jnp.concatenate(halves, axis=1)
            else:
                r = a.astype(BF)
            qkv[:, 256 * c : 256 * c + 256] = r
            if part == 1:
                kt[off : off + 256, :] = r.T
            if part == 2:
                vt[off : off + 256, :] = r.T


def qkv_call(sz, scal, xl, xc, xr, pieces, g1, cos, sin):
    tok, width, ext = sz.tok, sz.width, sz.ext
    own_b, lb = tok // RB, HALO // RB
    clampi = lambda lo, n: (lambda i, s: (jnp.clip(i - lo, 0, n - 1), 0))
    used = lambda i, s: jnp.clip(i, s[sz.need_lo], s[sz.need_hi] - 1)
    row = lambda i, s: (used(i, s), 0)
    fix = lambda i, s: (0, 0)
    col = lambda i, s: (0, used(i, s))
    sh = jax.ShapeDtypeStruct
    return pl.pallas_call(
        functools.partial(qkv_kernel, sz, len(pieces)),
        grid_spec=pltpu.PrefetchScalarGridSpec(
            num_scalar_prefetch=1,
            grid=(sz.blocks,),
            in_specs=[
                pl.BlockSpec((RB, width), clampi(0, lb)),
                pl.BlockSpec((RB, width), clampi(lb, own_b)),
                pl.BlockSpec((RB, width), clampi(lb + own_b, lb)),
                *[pl.BlockSpec(memory_space=pl.ANY)] * len(pieces),
                pl.BlockSpec((1, width), fix),
                pl.BlockSpec((RB, LANES), row),
                pl.BlockSpec((RB, LANES), row),
            ],
            out_specs=[
                pl.BlockSpec((RB, 3 * width), row),
                pl.BlockSpec((width, RB), col),
                pl.BlockSpec((width, RB), col),
                pl.BlockSpec((width, RB), lambda i, s: (0, jnp.clip(i - lb, 0, own_b - 1))),
            ],
            scratch_shapes=[pltpu.VMEM((width, 3 * width), BF), pltpu.SemaphoreType.DMA((len(pieces),))],
        ),
        out_shape=[sh((ext, 3 * width), BF), sh((width, ext), BF), sh((width, ext), BF), sh((width, tok), BF)],
        compiler_params=params(60, dimension_semantics=("arbitrary",)),
        cost_estimate=pl.CostEstimate(flops=14_000_000_000, bytes_accessed=30_000_000, transcendentals=0),
        name="qkv",
    )(scal, xl, xc, xr, *pieces, g1, cos, sin)


def split_heads(x):
    low = lax.broadcasted_iota(jnp.int32, x.shape, 1) < HEAD_DIM
    zero = jnp.zeros_like(x)
    return jnp.concatenate([jnp.where(low, x, zero), jnp.where(low, zero, x)], axis=0)


def lanes_of(p):
    return slice(LANES * p, LANES * p + LANES)


def fwd_kernel(sz, pg, scal, q, k, vt, qf, kf, out, out_t, lse, q2, buf_a, buf_b, acc, tops):
    nq = sz.own_qb
    ones = jnp.ones((16, KB), BF)
    for qi in range(nq):
        r0 = HALO + qi * QB
        fq = qf[r0 : r0 + QB, :]
        f2 = jnp.concatenate([fq, fq], axis=0)
        for p in range(pg):
            q2[qi, p] = jnp.concatenate([split_heads(q[r0 : r0 + QB, lanes_of(p)]), f2], axis=1)

    def zero(i, _):
        for p in range(pg):
            acc[i, p] = jnp.zeros((LANES + 16, 2 * QB), F32)
            tops[i, p] = jnp.zeros((8, 2 * QB), F32)
        return 0

    lax.fori_loop(0, nq + 1, zero, 0)

    def scores(qi, k0, p, fk):
        return nt(jnp.concatenate([k[pl.ds(k0, KB), lanes_of(p)], fk], axis=1), q2[qi, p])

    def mixed(k0, p, probs):
        va = jnp.concatenate([vt[lanes_of(p), pl.ds(k0, KB)], ones], axis=0)
        return nn(va, probs.astype(BF))

    def tile(i):
        return scal[sz.fwd_q + i], pl.multiple_of(scal[sz.fwd_k + i] * QB, QB)

    def score_tile(i, buf):
        qi, k0 = tile(i)
        qi = jnp.minimum(qi, nq - 1)
        fk = kf[pl.ds(k0, KB), :]
        for p in range(pg):
            buf[p] = scores(qi, k0, p, fk)

    def mix_tile(i, buf):
        qi, k0 = tile(i)
        for p in range(pg):
            acc[qi, p] += mixed(k0, p, jnp.exp2(buf[p]))

    score_tile(0, buf_a)

    def body(j, _):
        score_tile(2 * j + 1, buf_b)
        mix_tile(2 * j, buf_a)
        score_tile(2 * j + 2, buf_a)
        mix_tile(2 * j + 1, buf_b)
        return 0

    lax.fori_loop(0, (scal[sz.fwd_n] + 1) // 2, body, 0)

    low = high = acc[0, 0, LANES : LANES + 1, :]
    for qi in range(nq):
        for p in range(pg):
            total = acc[qi, p, LANES : LANES + 1, :]
            low, high = jnp.minimum(low, total), jnp.maximum(high, total)
    safe = (jnp.min(low) > 2.0 ** -60) & (jnp.max(high) < 2.0 ** 100)

    @pl.when(jnp.logical_not(safe))
    def _():
        lax.fori_loop(0, nq, zero, 0)

        def per_q(qi, _):
            lo, n = scal[sz.k_lo + sz.own_lo + qi], scal[sz.k_n + sz.own_lo + qi]
            for p in range(pg):
                def top(t, m):
                    k0 = pl.multiple_of(lo * QB + t * KB, QB)
                    return jnp.maximum(m, jnp.max(scores(qi, k0, p, kf[pl.ds(k0, KB), :]), axis=0, keepdims=True))

                m = lax.fori_loop(0, n, top, jnp.full((1, 2 * QB), BIG, F32))
                tops[qi, p] = jnp.broadcast_to(m, (8, 2 * QB))

                def add(t, _):
                    k0 = pl.multiple_of(lo * QB + t * KB, QB)
                    acc[qi, p] += mixed(k0, p, jnp.exp2(scores(qi, k0, p, kf[pl.ds(k0, KB), :]) - m))
                    return 0

                lax.fori_loop(0, n, add, 0)
            return 0

        lax.fori_loop(0, nq, per_q, 0)

    def finish(qi, _):
        o0 = pl.multiple_of(qi * QB, QB)
        for p in range(pg):
            a = acc[qi, p]
            total = a[LANES : LANES + 1, :]
            inv = 1.0 / total
            o_t = jnp.concatenate([a[:HEAD_DIM, :QB] * inv[:, :QB], a[HEAD_DIM:LANES, QB:] * inv[:, QB:]], axis=0).astype(BF)
            out_t[lanes_of(p), pl.ds(o0, QB)] = o_t
            out[pl.ds(o0, QB), lanes_of(p)] = o_t.T
            st = tops[qi, p, 0:1, :] + jnp.log2(total)
            lse[p, 0:1, pl.ds(o0, QB)] = st[:, :QB]
            lse[p, 1:2, pl.ds(o0, QB)] = st[:, QB:]
        return 0

    lax.fori_loop(0, nq, finish, 0)


def fwd_call(sz, scal, qkv, vt, qf, kf, pg):
    ext, tok, width = sz.ext, sz.tok, sz.width
    pairs = width // LANES
    steps = pairs // pg
    wide = LANES * pg
    col = lambda off: (lambda i, s: (0, off + i))
    fix = lambda i, s: (0, 0)
    sh = jax.ShapeDtypeStruct
    return pl.pallas_call(
        functools.partial(fwd_kernel, sz, pg),
        grid_spec=pltpu.PrefetchScalarGridSpec(
            num_scalar_prefetch=1,
            grid=(steps,),
            in_specs=[
                pl.BlockSpec((ext, wide), col(0)),
                pl.BlockSpec((ext, wide), col(steps)),
                pl.BlockSpec((wide, ext), lambda i, s: (i, 0)),
                pl.BlockSpec((ext, LANES), fix),
                pl.BlockSpec((ext, LANES), fix),
            ],
            out_specs=[
                pl.BlockSpec((tok, wide), col(0)),
                pl.BlockSpec((wide, tok), lambda i, s: (i, 0)),
                pl.BlockSpec((pg, 2, tok), lambda i, s: (i, 0, 0)),
            ],
            scratch_shapes=[
                pltpu.VMEM((sz.own_qb, pg, 2 * QB, 2 * LANES), BF),
                pltpu.VMEM((pg, KB, 2 * QB), F32),
                pltpu.VMEM((pg, KB, 2 * QB), F32),
                pltpu.VMEM((sz.own_qb + 1, pg, LANES + 16, 2 * QB), F32),
                pltpu.VMEM((sz.own_qb + 1, pg, 8, 2 * QB), F32),
            ],
        ),
        out_shape=[sh((tok, width), BF), sh((width, tok), BF), sh((pairs, 2, tok), F32)],
        compiler_params=params(60, dimension_semantics=("arbitrary",)),
        cost_estimate=pl.CostEstimate(flops=30_000_000_000, bytes_accessed=15_000_000, transcendentals=0),
        name="attn_forward",
    )(scal, qkv, qkv, vt, qf, kf)


def fetch_mlp(place, pieces, wo, wi, wd, sem, width):
    copies = [], [], []
    shards = len(pieces) // 2
    half, half_d = half_of(wo.shape[0] // shards), half_of(wd.shape[0] // shards)
    t_cols = wi.shape[1] // width
    for t, piece in enumerate(pieces):
        row0 = row_of(place(t), wo.shape[0] // shards)
        row_d = row_of(place(t), wd.shape[0] // shards)
        copies[0].append(pltpu.make_async_copy(piece.at[0:half, :], wo.at[pl.ds(row0, half), :], sem.at[t, 0]))
        for j in range(t_cols):
            copies[1].append(pltpu.make_async_copy(
                piece.at[half * (j + 1) : half * (j + 2), :],
                wi.at[pl.ds(row0, half), width * j : width * j + width], sem.at[t, j + 1]))
        lo = half * (t_cols + 1)
        copies[2].append(pltpu.make_async_copy(piece.at[lo : lo + half_d, :], wd.at[pl.ds(row_d, half_d), :], sem.at[t, t_cols + 1]))
    return copies


def three_parts(v):
    high = v.astype(BF).astype(F32)
    middle = (v - high).astype(BF).astype(F32)
    return high, middle, v - high - middle


def mid_kernel(sz, n_pieces, scal, *refs):
    pieces, refs = refs[:n_pieces], refs[n_pieces:]
    wo, wi, wd, sem = refs[-4:]
    step = pl.program_id(0)

    @pl.when(step == 0)
    def _():
        copies = fetch_mlp(lambda t: scal[sz.places + t], pieces, wo, wi, wd, sem, wo.shape[1])
        for group in copies:
            for c in group:
                c.start()

        def wait(which):
            for c in copies[which]:
                c.wait()

        mid_body(sz, wait, wo, wi, wd, *refs[:-4])

    @pl.when(step != 0)
    def _():
        mid_body(sz, lambda which: None, wo, wi, wd, *refs[:-4])


def mid_body(sz, wait, wo, wi, wd, x, o, gy, g2, ind, lse, out, mt_o, gu_o, n2t_o, gh2b_o, go_o, left_o, right_o, dlt):
    ff = wd.shape[0]
    wait(0)
    h2 = x[...].astype(F32) + nn(o[...], wo[...])
    mean = jnp.mean(h2, axis=-1, keepdims=True)
    cen = h2 - mean
    r2 = lax.rsqrt(jnp.mean(cen * cen, axis=-1, keepdims=True) + EPS)
    nh = cen * r2
    g = g2[...]
    n2 = (nh * g).astype(BF)
    n2t_o[...] = n2.T
    gyb = gy[...]
    y = h2
    gn2 = jnp.zeros_like(h2)
    wait(1)
    wait(2)
    step = 384
    for c in range(ff // step):
        lo = c * step
        a = nn(n2, wi[:, lo : lo + step])
        b = nn(n2, wi[:, ff + lo : ff + lo + step])
        gm = nt(gyb, wd[lo : lo + step, :])
        half = 0.5 * (1.0 + lax.erf(a * (2.0 ** -0.5)))
        gel = a * half
        mm = (gel * b).astype(BF)
        mt_o[lo : lo + step, :] = mm.T
        y = y + nn(mm, wd[lo : lo + step, :])
        dgel = half + a * (jnp.exp(-0.5 * a * a) * (1.0 / math.sqrt(2.0 * math.pi)))
        ga = (gm * b * dgel).astype(BF)
        gb = (gm * gel).astype(BF)
        gu_o[:, lo : lo + step] = ga
        gu_o[:, ff + lo : ff + lo + step] = gb
        gn2 = gn2 + nt(ga, wi[:, lo : lo + step]) + nt(gb, wi[:, ff + lo : ff + lo + step])
    out[...] = y.astype(BF)

    t = gn2 * g
    gh2 = gyb.astype(F32) + r2 * (t - jnp.mean(t, axis=-1, keepdims=True) - nh * jnp.mean(t * nh, axis=-1, keepdims=True))
    gb16 = gh2.astype(BF)
    gh2b_o[...] = gb16
    go = nt(gb16, wo[...]).astype(BF)
    go_o[...] = go
    prod = go.astype(F32) * o[...].astype(F32)
    hi = prod.astype(BF)
    lo_part = (prod - hi.astype(F32)).astype(BF)
    sums = nt(ind[...], hi) + nt(ind[...], lo_part)
    for p in range(dlt.shape[0]):
        dlt[p] = sums[2 * p : 2 * p + 2, :]
    heads = lse.shape[0] * 2
    top = jnp.concatenate([lse[p] for p in range(lse.shape[0])] + [jnp.zeros((STAT - heads, sums.shape[1]), F32)], axis=0)
    rows = [part for v in (top, sums) for part in three_parts(v)]
    rows.append(jnp.zeros((LANES - 6 * STAT, sums.shape[1]), F32))
    width = go.shape[1]
    stats = jnp.concatenate(rows, axis=0).T.astype(BF)
    step = pl.program_id(0)

    @pl.when(step < HALO // RB)
    def _():
        left_o[:, :width] = go
        left_o[:, width:] = stats

    @pl.when(step >= (sz.tok - HALO) // RB)
    def _():
        right_o[:, :width] = go
        right_o[:, width:] = stats


def mid_call(sz, scal, pieces, x, o, gy, g2, lse, ff):
    tok, width = x.shape
    heads = jnp.arange(16, dtype=jnp.int32)
    ind = (heads[:, None] == (jnp.arange(width, dtype=jnp.int32) // HEAD_DIM)[None, :]).astype(BF)
    row = lambda i, s: (i, 0)
    fix = lambda i, s: (0, 0)
    rs = lambda n: pl.BlockSpec((RB, n), row)
    cs = lambda n: pl.BlockSpec((n, RB), lambda i, s: (0, i))
    fs = lambda a: pl.BlockSpec(a.shape, fix)
    sh = jax.ShapeDtypeStruct
    n = len(pieces)
    stat = pl.BlockSpec((width // LANES, 2, RB), lambda i, s: (0, 0, i))
    halo = lambda lo: pl.BlockSpec((RB, width + LANES), lambda i, s: (jnp.clip(i - lo, 0, HALO // RB - 1), 0))
    halos = [halo(0), halo((tok - HALO) // RB)]
    return pl.pallas_call(
        functools.partial(mid_kernel, sz, n),
        grid_spec=pltpu.PrefetchScalarGridSpec(
            num_scalar_prefetch=1,
            grid=(tok // RB,),
            in_specs=[*[pl.BlockSpec(memory_space=pl.ANY)] * n, rs(width), rs(width), rs(width), fs(g2), fs(ind), stat],
            out_specs=[rs(width), cs(ff), rs(2 * ff), cs(width), rs(width), rs(width), *halos, stat],
            scratch_shapes=[pltpu.VMEM((width, width), BF), pltpu.VMEM((width, 2 * ff), BF), pltpu.VMEM((ff, width), BF),
                            pltpu.SemaphoreType.DMA((n, 2 * ff // width + 2))],
        ),
        out_shape=[sh((tok, width), BF), sh((ff, tok), BF), sh((tok, 2 * ff), BF), sh((width, tok), BF),
                   sh((tok, width), BF), sh((tok, width), BF),
                   sh((HALO, width + LANES), BF), sh((HALO, width + LANES), BF),
                   sh((width // LANES, 2, tok), F32)],
        compiler_params=params(60, dimension_semantics=("arbitrary",)),
        cost_estimate=pl.CostEstimate(flops=13_000_000_000 * 2, bytes_accessed=30_000_000, transcendentals=0),
        name="middle",
    )(scal, *pieces, x, o, gy, g2, ind, lse)


def put_halves(core, keep, send, rows0, values, n_group):
    rows = values.shape[0] // n_group
    half = half_of(rows)

    def store(first, second):
        for g in range(n_group):
            lo, hi = rows * g, rows * (g + 1)
            first[g, pl.ds(rows0, half), :] = values[lo : lo + half, :]
            second[g, pl.ds(rows0, half), :] = values[hi - half : hi, :]

    @pl.when(core == 0)
    def _():
        store(keep, send)

    @pl.when(core != 0)
    def _():
        store(send, keep)


def put_halves(core, keep, send, rows0, values, n_group):
    rows = values.shape[0] // n_group
    half = half_of(rows)

    def store(first, second):
        for g in range(n_group):
            lo, hi = rows * g, rows * (g + 1)
            first[g, pl.ds(rows0, half), :] = values[lo : lo + half, :]
            second[g, pl.ds(rows0, half), :] = values[hi - half : hi, :]

    @pl.when(core == 0)
    def _():
        store(keep, send)

    @pl.when(core != 0)
    def _():
        store(send, keep)


def in_grad_kernel(n_group, at, scal, n2t, gu, keep, send):
    half = half_of(n2t.shape[0] // n_group)
    row0 = pl.multiple_of(pl.program_id(0) * half, 16)
    put_halves(scal[at] % 2, keep, send, row0, nn(n2t[...], gu[...]).astype(BF), n_group)


def in_grad_call(sz, scal, n2t, gu, n_group):
    width, tok = n2t.shape
    n_cols = gu.shape[1] // width
    rows = n_cols * half_of(width // n_group)
    out = jax.ShapeDtypeStruct((n_group, rows, width), BF)
    return pl.pallas_call(
        functools.partial(in_grad_kernel, n_group, sz.places),
        grid_spec=pltpu.PrefetchScalarGridSpec(
            num_scalar_prefetch=1,
            grid=(n_cols,),
            in_specs=[pl.BlockSpec((width, tok), lambda j, s: (0, 0)), pl.BlockSpec((tok, width), lambda j, s: (0, j))],
            out_specs=[pl.BlockSpec((n_group, rows, width), lambda j, s: (0, 0, 0))] * 2,
        ),
        out_shape=[out, out],
        compiler_params=params(60, dimension_semantics=("arbitrary",)),
        cost_estimate=pl.CostEstimate(flops=8_000_000_000, bytes_accessed=10_000_000, transcendentals=0),
        name="in_weight_gradient",
    )(scal, n2t, gu)


def down_out_kernel(n_group, at, scal, mt, gy, ot_h, gh_h, keep, send, ot, gh, sem):
    copies = [pltpu.make_async_copy(ot_h, ot, sem.at[0]), pltpu.make_async_copy(gh_h, gh, sem.at[1])]
    for c in copies:
        c.start()
    put_halves(scal[at] % 2, keep, send, 0, nn(mt[...], gy[...]).astype(BF), n_group)
    for c in copies:
        c.wait()
    used = half_of(mt.shape[0] // n_group) + half_of(ot.shape[0] // n_group)
    put_halves(scal[at] % 2, keep, send, half_of(mt.shape[0] // n_group), nn(ot[...], gh[...]).astype(BF), n_group)
    if used < keep.shape[1]:
        for ref in (keep, send):
            ref[:, used:, :] = jnp.zeros((n_group, keep.shape[1] - used, keep.shape[2]), BF)


def down_out_call(sz, scal, mt, gy, ot, gh, n_group, rows):
    width, tok = ot.shape
    ff = mt.shape[0]
    out = jax.ShapeDtypeStruct((n_group, rows, width), BF)
    anyspec = pl.BlockSpec(memory_space=pl.ANY)
    fix = lambda j, s: (0, 0)
    return pl.pallas_call(
        functools.partial(down_out_kernel, n_group, sz.places),
        grid_spec=pltpu.PrefetchScalarGridSpec(
            num_scalar_prefetch=1,
            grid=(1,),
            in_specs=[pl.BlockSpec((ff, tok), fix), pl.BlockSpec((tok, width), fix), anyspec, anyspec],
            out_specs=[pl.BlockSpec((n_group, rows, width), lambda j, s: (0, 0, 0))] * 2,
            scratch_shapes=[pltpu.VMEM((width, tok), BF), pltpu.VMEM((tok, width), BF), pltpu.SemaphoreType.DMA((2,))],
        ),
        out_shape=[out, out],
        compiler_params=params(60, dimension_semantics=("arbitrary",)),
        cost_estimate=pl.CostEstimate(flops=100_000_000, bytes_accessed=100_000, transcendentals=0),
        name="down_out_weight_gradients",
    )(scal, mt, gy, ot, gh)


def bwd_kernel(sz, pg, at, n_group, scal, qkv_h, kt_h, qf_h, kf_h, gl_h, gc_h, gr_h, cos_h, sin_h, n1t_h,
               lse_c, dlt_c, grad, keep, send,
               q, k, v, kt, qf, kf, go, halo_st, cos, sin, n1t, q2, g2, gka, gva, gqa, st, s_a, p_a, s_b, p_b, sem):
    n_qb, tok, width = sz.n_qb, sz.tok, sz.width
    wide = LANES * pg
    q_lo, q_hi = scal[sz.q_lo], scal[sz.q_hi]
    ext = q.shape[0]
    cols = lambda part: pl.ds(part * width + at * wide, wide)
    near, left = pl.ds(HALO, tok + QB), pl.ds(0, HALO)
    right, own = pl.ds(HALO + tok + QB, ext - HALO - tok - QB), pl.ds(HALO, tok)

    def rows(seg):
        return [(qkv_h.at[seg, cols(part)], dst.at[seg, :]) for part, dst in ((0, q), (1, k), (2, v))] + [
            (kt_h.at[cols(0), seg], kt.at[:, seg])]

    first = [(gc_h.at[:, cols(0)], go.at[own, :]), (qf_h, qf), (kf_h, kf), *rows(near)]
    second = [*rows(left), *rows(right), (gl_h.at[:, cols(0)], go.at[left, :]),
              (gr_h.at[:, cols(0)], go.at[pl.ds(HALO + tok, HALO), :]),
              (gl_h.at[:, pl.ds(width, LANES)], halo_st.at[0]), (gr_h.at[:, pl.ds(width, LANES)], halo_st.at[1])]
    third = [(cos_h.at[own, :], cos), (sin_h.at[own, :], sin), (n1t_h, n1t)]
    copies = [pltpu.make_async_copy(a, b, sem.at[t]) for t, (a, b) in enumerate(first + second + third)]
    n_first, n_second = len(first), len(first) + len(second)
    for c in copies:
        c.start()

    for row, part in ((0, lse_c), (1, dlt_c)):
        for p in range(pg):
            for b in range(sz.own_qb):
                for h in range(2):
                    st[sz.own_lo + b, p, row : row + 1, QB * h : QB * h + QB] = part[p, h : h + 1, QB * b : QB * b + QB]

    def halo_stats(side, first):
        def one(i, _):
            rows_t = halo_st[side, pl.ds(pl.multiple_of((i - first) * QB, QB), QB), :].astype(F32).T
            for p in range(pg):
                for h in range(2):
                    for row in range(2):
                        lo = 3 * STAT * row + 2 * (pg * at + p) + h
                        parts = [rows_t[lo + STAT * t : lo + STAT * t + 1, :] for t in range(3)]
                        st[i, p, row : row + 1, QB * h : QB * h + QB] = parts[0] + parts[1] + parts[2]
            return 0

        return one

    for c in copies[:n_first]:
        c.wait()

    def prep(i, _):
        r0 = pl.multiple_of(i * QB, QB)
        fq = qf[pl.ds(r0, QB), :]
        f2 = jnp.concatenate([fq, fq], axis=0)
        for p in range(pg):
            q2[i, p] = jnp.concatenate([split_heads(q[pl.ds(r0, QB), lanes_of(p)]), f2], axis=1)
            g2[i, p] = split_heads(go[pl.ds(r0, QB), lanes_of(p)])
            gqa[i, p] = jnp.zeros((LANES, 2 * QB), F32)
            gka[p, pl.ds(r0, QB), :] = jnp.zeros((QB, LANES), F32)
            gva[p, pl.ds(r0, QB), :] = jnp.zeros((QB, LANES), F32)
        return 0

    lax.fori_loop(sz.own_lo, sz.own_hi, prep, 0)

    def run(where, for_keys, for_queries):
        def tile(i):
            return scal[where[0] + i], pl.multiple_of(scal[where[1] + i] * QB, QB)

        def score_tile(i, s_buf, p_buf):
            qi, k0 = tile(i)
            fk = kf[pl.ds(k0, KB), :]
            for p in range(pg):
                s_buf[p] = nt(jnp.concatenate([k[pl.ds(k0, KB), lanes_of(p)], fk], axis=1), q2[qi, p])
                p_buf[p] = nt(v[pl.ds(k0, KB), lanes_of(p)], g2[qi, p])

        def grad_tile(i, s_buf, p_buf):
            qi, k0 = tile(i)
            dead = jnp.where(i < scal[where[2]], 0.0, 1e38).astype(F32)
            for p in range(pg):
                pr = jnp.exp2(s_buf[p] - (st[qi, p, 0:1, :] + dead))
                ds = (pr * (p_buf[p] - st[qi, p, 1:2, :])).astype(BF)
                if for_keys:
                    gva[p, pl.ds(k0, KB), :] += nn(pr.astype(BF), g2[qi, p])
                    gka[p, pl.ds(k0, KB), :] += nn(ds, q2[qi, p, :, :LANES])
                if for_queries:
                    gqa[qi, p] += nn(kt[lanes_of(p), pl.ds(k0, KB)], ds)

        @pl.when(scal[where[2]] > 0)
        def _():
            score_tile(0, s_a, p_a)

            def body(j, _):
                score_tile(2 * j + 1, s_b, p_b)
                grad_tile(2 * j, s_a, p_a)
                score_tile(2 * j + 2, s_a, p_a)
                grad_tile(2 * j + 1, s_b, p_b)
                return 0

            lax.fori_loop(0, (scal[where[2]] + 1) // 2, body, 0)

    run(sz.lists[0], True, True)
    for c in copies[n_first:n_second]:
        c.wait()
    lax.fori_loop(q_lo, sz.own_lo, prep, 0)
    lax.fori_loop(sz.own_hi, q_hi, prep, 0)
    lax.fori_loop(q_lo, sz.own_lo, halo_stats(0, 0), 0)
    lax.fori_loop(sz.own_hi, q_hi, halo_stats(1, sz.own_hi), 0)
    run(sz.lists[1], False, True)
    run(sz.lists[2], True, False)
    copies[n_second].wait()
    copies[n_second + 1].wait()

    sc = HEAD_DIM ** -0.5

    def finish(i, _):
        o0 = pl.multiple_of(i * QB, QB)
        r0 = pl.multiple_of(HALO + i * QB, QB)
        co, si = cos[pl.ds(o0, QB), :], sin[pl.ds(o0, QB), :]
        for p in range(pg):
            a = gqa[sz.own_lo + i, p]
            gt = jnp.concatenate([a[:HEAD_DIM, :QB], a[HEAD_DIM:, QB:]], axis=0).T * sc
            grad[pl.ds(o0, QB), LANES * p : LANES * p + LANES] = (gt * co - partner(gt) * si).astype(BF)
            b = gka[p, pl.ds(r0, QB), :] * LN2
            lo = wide + LANES * p
            grad[pl.ds(o0, QB), lo : lo + LANES] = (b * co - partner(b) * si).astype(BF)
            lo = 2 * wide + LANES * p
            grad[pl.ds(o0, QB), lo : lo + LANES] = gva[p, pl.ds(r0, QB), :].astype(BF)
        return 0

    lax.fori_loop(0, sz.own_qb, finish, 0)
    copies[n_second + 2].wait()
    for part in range(3):
        lanes = slice(wide * part, wide * part + wide)
        values = nn(n1t[...], grad[:, lanes]).astype(BF)
        put_halves(scal[sz.places] % 2, keep.at[:, :, lanes], send.at[:, :, lanes], 0, values, n_group)


def bwd_call(sz, scal, qkv, kt, qf, kf, gl, gc, gr, lse, dlt, cos, sin, n1t, pg, at, n_group):
    ext, tok, width, n_qb = sz.ext, sz.tok, sz.width, sz.n_qb
    wide = LANES * pg
    half = half_of(width // n_group)
    spec = lambda shape, *idx: pl.BlockSpec(shape, lambda i, s: idx)
    sh = jax.ShapeDtypeStruct
    out_spec = lambda shape: pl.BlockSpec(shape, lambda i, s: (0,) * len(shape), pipeline_mode=pl.Buffered(1))
    outs = [(tok, 3 * wide), (n_group, half, 3 * wide), (n_group, half, 3 * wide)]
    return pl.pallas_call(
        functools.partial(bwd_kernel, sz, pg, at, n_group),
        grid_spec=pltpu.PrefetchScalarGridSpec(
            num_scalar_prefetch=1,
            grid=(1,),
            in_specs=[pl.BlockSpec(memory_space=pl.ANY)] * 10
            + [spec((pg, 2, tok), at, 0, 0), spec((pg, 2, tok), at, 0, 0)],
            out_specs=[out_spec(o) for o in outs],
            scratch_shapes=[
                *[pltpu.VMEM((ext, wide), BF)] * 3,
                pltpu.VMEM((wide, ext), BF),
                pltpu.VMEM((ext, LANES), BF),
                pltpu.VMEM((ext, LANES), BF),
                pltpu.VMEM((tok + 2 * HALO, wide), BF),
                pltpu.VMEM((2, HALO, LANES), BF),
                pltpu.VMEM((tok, LANES), F32),
                pltpu.VMEM((tok, LANES), F32),
                pltpu.VMEM((width, tok), BF),
                pltpu.VMEM((n_qb, pg, 2 * QB, 2 * LANES), BF),
                pltpu.VMEM((n_qb, pg, 2 * QB, LANES), BF),
                pltpu.VMEM((pg, ext, LANES), F32),
                pltpu.VMEM((pg, ext, LANES), F32),
                pltpu.VMEM((n_qb, pg, LANES, 2 * QB), F32),
                pltpu.VMEM((n_qb, pg, 8, 2 * QB), F32),
                *[pltpu.VMEM((pg, KB, 2 * QB), F32)] * 4,
                pltpu.SemaphoreType.DMA((22,)),
            ],
        ),
        out_shape=[sh(o, BF) for o in outs],
        compiler_params=params(60, dimension_semantics=("arbitrary",)),
        cost_estimate=pl.CostEstimate(flops=35_000_000_000, bytes_accessed=20_000_000, transcendentals=0),
        name="attn_backward",
    )(scal, qkv, kt, qf, kf, gl, gc, gr, cos, sin, n1t, lse, dlt)


def gx_kernel(n_pieces, n_grads, at, scal, *refs):
    pieces, grads = refs[:n_pieces], refs[n_pieces : n_pieces + n_grads]
    x, gh2, g1, out, w, sem = refs[n_pieces + n_grads :]

    @pl.when(pl.program_id(0) == 0)
    def _():
        copies = fetch_qkv(lambda t: scal[at + t], pieces, w, sem)
        for c in copies:
            c.start()
        for c in copies:
            c.wait()

    width = x.shape[1]
    gn = None
    wide = grads[0].shape[1] // 3
    for part in range(3):
        lhs = jnp.concatenate([grad[:, wide * part : wide * part + wide] for grad in grads], axis=1)
        term = nt(lhs, w[:, width * part : width * part + width])
        gn = term if gn is None else gn + term
    xf = x[...].astype(F32)
    mean = jnp.mean(xf, axis=-1, keepdims=True)
    cen = xf - mean
    r1 = lax.rsqrt(jnp.mean(cen * cen, axis=-1, keepdims=True) + EPS)
    nh = cen * r1

    t = gn * g1[...]
    gx = gh2[...].astype(F32) + r1 * (t - jnp.mean(t, axis=-1, keepdims=True) - nh * jnp.mean(t * nh, axis=-1, keepdims=True))
    out[...] = gx.astype(BF)


def gx_call(sz, scal, pieces, grads, x, gh2, g1):
    tok, width = x.shape
    row = lambda i, s: (i, 0)
    fix = lambda i, s: (0, 0)
    rs = pl.BlockSpec((RB, width), row)
    n = len(pieces)
    return pl.pallas_call(
        functools.partial(gx_kernel, n, len(grads), sz.places),
        grid_spec=pltpu.PrefetchScalarGridSpec(
            num_scalar_prefetch=1,
            grid=(tok // RB,),
            in_specs=[*[pl.BlockSpec(memory_space=pl.ANY)] * n,
                      *[pl.BlockSpec((RB, g.shape[1]), row) for g in grads],
                      rs, rs, pl.BlockSpec(g1.shape, fix)],
            out_specs=rs,
            scratch_shapes=[pltpu.VMEM((width, 3 * width), BF), pltpu.SemaphoreType.DMA((n,))],
        ),
        out_shape=jax.ShapeDtypeStruct((tok, width), BF),
        compiler_params=params(60, dimension_semantics=("arbitrary",)),
        cost_estimate=pl.CostEstimate(flops=4_000_000_000, bytes_accessed=15_000_000, transcendentals=0),
        name="input_gradient",
    )(scal, *pieces, *grads, x, gh2, g1)


def gain_row(w, grad, gain):
    low = lambda v: v.astype(BF).astype(F32)
    total = jnp.sum(low(w) * grad, axis=1, keepdims=True)
    return jnp.broadcast_to(total, (total.shape[0], LANES)).T[0:1, :] / low(gain)


def in_core_order(core, mine, other, use):
    @pl.when(core == 0)
    def _():
        use(mine, other)

    @pl.when(core != 0)
    def _():
        use(other, mine)


def qkv_end_kernel(at, scal, t, s, w, gain, out, g_out):
    shard = w.shape[0]
    half = half_of(shard)
    wide = t.shape[1] // 3
    calls = t.shape[0] // half

    def use(first, second):
        for ref, lo in ((first, 0), (second, shard - half)):
            for j in range(calls):
                for part in range(3):
                    c = wide * (calls * part + j)
                    out[lo : lo + half, c : c + wide] = ref[half * j : half * j + half, wide * part : wide * part + wide].astype(F32)

    in_core_order(scal[at] % 2, t, s, use)
    g_out[...] = gain_row(w[...], out[...], gain[...])


def mlp_end_kernel(at, scal, t, s, w, gain, d_in, d_down, d_out, g_out):
    shard, shard_d, width = w.shape[0], d_down.shape[0], d_out.shape[1]
    half, half_d = half_of(shard), half_of(shard_d)
    n_cols = w.shape[1] // width

    def use(first, second):
        for ref, h in ((first, 0), (second, 1)):
            lo, lo_d = h * (shard - half), h * (shard_d - half_d)
            for j in range(n_cols):
                d_in[lo : lo + half, width * j : width * j + width] = ref[half * j : half * j + half, :].astype(F32)
            at_d = half * n_cols
            d_down[lo_d : lo_d + half_d, :] = ref[at_d : at_d + half_d, :].astype(F32)
            d_out[lo : lo + half, :] = ref[at_d + half_d : at_d + half_d + half, :].astype(F32)

    in_core_order(scal[at] % 2, t, s, use)
    g_out[...] = gain_row(w[...], d_in[...], gain[...])


def end_call(kernel, name, sz, scal, arrays, w, gain, shapes):
    smem = pl.BlockSpec(memory_space=pltpu.SMEM)
    vmem = pl.BlockSpec(memory_space=pltpu.VMEM)
    outs = [*shapes, (1, w.shape[0])]
    return pl.pallas_call(
        functools.partial(kernel, sz.places),
        in_specs=[smem] + [vmem] * (len(arrays) + 2),
        out_specs=[vmem] * len(outs),
        out_shape=[jax.ShapeDtypeStruct(o, F32) for o in outs],
        compiler_params=params(60),
        cost_estimate=pl.CostEstimate(flops=3_000_000_000, bytes_accessed=5_000_000, transcendentals=0),
        name=name,
    )(scal, *arrays, w, gain.reshape(1, -1))


class Net:
    def __init__(self, n_replica, n_group):
        self.n_replica, self.n_group, self.n_z = n_replica, n_group, n_replica // 2
        self.replica, self.group = lax.axis_index("replica"), lax.axis_index("group")
        self.core = self.replica & 1

    def shift(self, a, step):
        pairs = [(i, i + step) for i in range(self.n_replica) if 0 <= i + step < self.n_replica]
        return lax.ppermute(a, "replica", pairs)

    def core_swap(self, a):
        return lax.ppermute(a, "replica", [(i, i ^ 1) for i in range(self.n_replica)])

    def across(self, a, k):
        return lax.ppermute(a, "group", [(i, i ^ k) for i in range(self.n_group)])

    def across_swap(self, a, k):
        n = self.n_group
        pairs = [(r * n + g, (r ^ 1) * n + (g ^ k)) for r in range(self.n_replica) for g in range(n)]
        return lax.ppermute(a, ("replica", "group"), pairs)

    def gather_near(self, mine, other):
        got = {(0, 0): mine, (0, 1): other}
        for k in (1, 2) if self.n_group == 4 else range(1, self.n_group):
            got[k, 0] = self.across(mine, k)
        return got

    def gather_far(self, got):
        got = dict(got)
        if self.n_group == 4:
            got[3, 0] = self.across(got[2, 0], 1)
            got[3, 1] = self.across_swap(got[1, 0], 2)
        for k in range(1, self.n_group):
            if (k, 1) not in got:
                got[k, 1] = self.core_swap(got[k, 0])
        return [got[key] for key in sorted(got)]

    def parts(self, pairs):
        def part(k):
            at = lambda a: lax.dynamic_index_in_dim(a, self.group ^ k, 0, keepdims=False).astype(F32)
            return jnp.concatenate([at(keep) + at(got) for got, keep in pairs], axis=0)

        return [part(0)] + [part(k).astype(BF) for k in range(1, self.n_group)]

    def group_send(self, parts):
        return parts[0], [self.across(parts[k], k) for k in range(1, self.n_group)]

    def add(self, own, moved):
        for m in moved:
            own = own + m.astype(F32)
        return own

    def along(self, a, k):
        return lax.ppermute(a, "replica", [(i, i ^ (2 * k)) for i in range(self.n_replica)])

    def z_scatter(self, s):
        shares = s.reshape(self.n_z, s.shape[0] // self.n_z, s.shape[1])
        share = lambda k: lax.dynamic_index_in_dim(shares, (self.replica // 2) ^ k, 0, keepdims=False)
        return share(0), [self.along(share(k).astype(BF), k) for k in range(1, self.n_z)]

    def z_gather(self, own, moved):
        t = self.add(own, moved).astype(BF)
        return [t] + [self.along(t, k) for k in range(1, self.n_z)]

    def z_join(self, shares):
        z = self.replica // 2
        return jnp.concatenate([lax.select_n(z, *[shares[j ^ i] for i in range(self.n_z)]) for j in range(self.n_z)], axis=0)


def on_device(tokens, cotangent, lengths, dealing, offsets, attn_gain, qkv_weight, out_weight,
              mlp_gain, in_weight, down_weight, *, n_replica, n_group):
    net = Net(n_replica, n_group)
    x, gy = tokens[0], cotangent[0]
    tok, width = x.shape
    ff = in_weight.shape[1] // 2
    sz = Sizes(tok, width)
    pairs = width // LANES
    pg = 3
    tie = lax.optimization_barrier

    def half_rows(a, h):
        n = half_of(a.shape[0])
        return lax.dynamic_slice_in_dim(a, (net.core ^ h) * (a.shape[0] - n), n, 0).astype(BF)

    near = net.gather_near(half_rows(qkv_weight, 0), half_rows(qkv_weight, 1))
    own_gain = jnp.stack([attn_gain, mlp_gain]).astype(BF)
    by_offset = [own_gain] + [net.across(own_gain, k) for k in range(1, n_group)]
    where = jnp.stack([net.replica, net.group]).astype(jnp.int32)
    packs = pack_call(where, out_weight, in_weight, down_weight)
    near, by_offset, packs, where = tie((near, by_offset, packs, where))
    scal, qf, kf, cos, sin = plan_call(sz, n_replica, n_group, where, lengths)

    x_l = net.shift(x[tok - HALO :], 1)
    x_r = net.shift(x[:HALO], -1)
    qkv_pieces = net.gather_far(near)
    by_offset = jnp.stack(by_offset)
    hit = (jnp.arange(n_group)[:, None] ^ net.group) == jnp.arange(n_group)[None, :]
    gains = jnp.sum(jnp.where(hit[:, :, None, None], by_offset[None].astype(F32), 0.0), axis=1)
    gains = gains.transpose(1, 0, 2).reshape(2, width)
    g1, g2 = gains[0:1], gains[1:2]
    packs, qkv_pieces, x_l, x_r, gains = tie((packs, qkv_pieces, x_l, x_r, gains))

    near = net.gather_near(*packs)
    qkv, kt, vt, n1t = qkv_call(sz, scal, x_l, x, x_r, qkv_pieces, g1, cos, sin)
    near, vt = tie((near, vt))
    mlp_pieces = net.gather_far(near)
    o, ot, lse = fwd_call(sz, scal, qkv, vt, qf, kf, pg)
    out, mt, gu, n2t, gh2b, go, to_left, to_right, dlt = mid_call(sz, scal, mlp_pieces, x, o, gy, g2, lse, ff)

    go_l = net.shift(to_right, 1)
    go_r = net.shift(to_left, -1)
    keep_i, send_i = in_grad_call(sz, scal, n2t, gu, n_group)
    used = half_of(width // n_group) + half_of(ff // n_group)
    rows = used + -(keep_i.shape[1] + used) % (8 * net.n_z)
    keep_d, send_d = down_out_call(sz, scal, mt, gy, ot, gh2b, n_group, rows)
    send_d, go_l, go_r = tie((send_d, go_l, go_r))
    mlp_parts = net.parts([(net.core_swap(send_i), keep_i), (net.core_swap(send_d), keep_d)])

    def attn_grad(at, dep):
        return bwd_call(sz, dep, qkv, kt, qf, kf, go_l, go, go_r, lse, dlt, cos, sin, n1t, pg, at, n_group)

    scal, mlp_parts = tie((scal, mlp_parts))
    grad0, keep0, send0 = attn_grad(0, scal)
    mlp = net.group_send(mlp_parts)
    keep0, send0, mlp = tie((keep0, send0, mlp))
    parts0 = net.parts([(net.core_swap(send0), keep0)])
    mlp = net.z_scatter(net.add(*mlp))
    scal, parts0 = tie((scal, parts0))
    sum0 = net.group_send(parts0)
    grad1, keep1, send1 = attn_grad(1, scal)
    sum0, mlp, scal, send1 = tie((sum0, mlp, scal, send1))

    got1 = net.core_swap(send1)
    mlp = net.z_gather(*mlp)
    got1, sum0 = tie((got1, sum0))
    parts1, scal = tie((net.parts([(got1, keep1)]), scal))
    sum1 = net.group_send(parts1)
    gx = gx_call(sz, scal, qkv_pieces, [grad0, grad1], x, gh2b, g1)
    sum1, sum0, gx = tie((sum1, sum0, gx))
    sum1, mlp = tie((sum1, mlp))

    qkv_sum = net.z_scatter(jnp.concatenate([net.add(*sum0), net.add(*sum1)], axis=0))
    mlp_sum = net.z_join(mlp)
    qkv_sum, mlp_sum = tie((qkv_sum, mlp_sum))
    sib_mlp = net.core_swap(mlp_sum)
    qkv_sum = net.z_gather(*qkv_sum)

    shard, shard_d = width // n_group, ff // n_group
    d_in, d_down, d_out, d_g2 = end_call(mlp_end_kernel, "mlp_gradients_end", sz, scal, [mlp_sum, sib_mlp], in_weight, mlp_gain,
                                         [in_weight.shape, (shard_d, width), (shard, width)])
    qkv_sum, d_in = tie((qkv_sum, d_in))
    qkv_sum = net.z_join(qkv_sum)
    d_qkv, d_g1 = end_call(qkv_end_kernel, "qkv_gradient_end", sz, scal, [qkv_sum, net.core_swap(qkv_sum)], qkv_weight,
                           attn_gain, [qkv_weight.shape])
    return (out[None], gx[None], d_g1[0], d_qkv, d_out, d_g2[0], d_in, d_down)


def solution(mesh):
    body = functools.partial(on_device, n_replica=mesh.shape["replica"], n_group=mesh.shape["group"])
    return jax.shard_map(
        body,
        mesh=mesh,
        in_specs=(
            P("group", "replica", None),
            P("group", "replica", None),
            P("group", None),
            P("group", None),
            P("group", None, None),
            P("group"),
            P("group", None),
            P("group", None),
            P("group"),
            P("group", None),
            P("group", None),
        ),
        out_specs=(
            P("group", "replica", None),
            P("group", "replica", None),
            P("group"),
            P("group", None),
            P("group", None),
            P("group"),
            P("group", None),
            P("group", None),
        ),
        check_vma=False,
    )
```

```python
import functools
import math

import jax
import jax.numpy as jnp
from jax import lax
from jax.experimental import pallas as pl
from jax.experimental.pallas import tpu as pltpu
from jax.sharding import PartitionSpec as P

HEADS = 12
HEAD_DIM = 64
LANES = 128
HALO = 768
RB = 256
QB = 128
KB = 256
STAT = 16
EPS = 1e-05
BIG = -1e30
ROPE_BASE = 160000.0
LOG2E = 1.4426950408889634
LN2 = 0.6931471805599453
BF = jnp.bfloat16
F32 = jnp.float32


def nt(a, b):
    return lax.dot_general(a, b, (((1,), (1,)), ((), ())), preferred_element_type=F32)


def nn(a, b):
    return lax.dot_general(a, b, (((1,), (0,)), ((), ())), preferred_element_type=F32)


def partner(x):
    lane = lax.broadcasted_iota(jnp.int32, x.shape, 1) % HEAD_DIM
    return jnp.where(lane < HEAD_DIM // 2, pltpu.roll(x, 96, 1), pltpu.roll(x, 32, 1))


def half_of(rows):
    return -(-rows // 32) * 16


def row_of(place, rows):
    return pl.multiple_of((place // 2) * rows + (place % 2) * (rows - half_of(rows)), 16)


def params(mib, **kw):
    return pltpu.CompilerParams(vmem_limit_bytes=mib * 1024 * 1024, **kw)


class Sizes:
    def __init__(self, tok, width):
        self.tok, self.width = tok, width
        self.ext = tok + 2 * HALO + RB
        self.n_qb = (tok + 2 * HALO) // QB
        self.own_qb, self.own_lo = tok // QB, HALO // QB
        self.own_hi = self.own_lo + self.own_qb
        tiles = -(-(QB + 2 * HALO + QB) // KB)
        self.cap_f = self.own_qb * tiles + 2
        halo_tiles = -(-(HALO + QB) // KB)
        caps = [self.own_qb * -(-tok // KB) + 2, 2 * self.own_qb * -(-HALO // KB) + 2, 2 * self.own_lo * halo_tiles + 2]
        self.k_lo, self.k_n = 0, self.n_qb
        self.q_lo, self.q_hi = 2 * self.n_qb, 2 * self.n_qb + 1
        self.need_lo, self.need_hi, self.full_hi = (2 * self.n_qb + i for i in (2, 3, 4))
        self.blocks = self.ext // RB
        self.fwd_q = self.full_hi + 1
        self.fwd_k, self.fwd_n = self.fwd_q + self.cap_f, self.fwd_q + 2 * self.cap_f
        self.lists, at = [], self.fwd_n + 1
        for cap in caps:
            self.lists.append((at, at + cap, at + 2 * cap))
            at += 2 * cap + 1
        self.places = at


def plan_kernel(sz, n_replica, n_group, where, lengths, scal, qf, kf, cos, sin, starts, k_end, seg_buf, pos_buf):
    n_seq = lengths.shape[1]
    total = n_replica * sz.tok
    replica, group = where[0], where[1]
    base = replica * sz.tok - HALO
    at = jnp.int32(0)
    for j in range(n_seq):
        starts[j] = at
        at = at + lengths[0, j]
    starts[n_seq] = at

    def first_of(g):
        f = jnp.int32(0)
        for j in range(n_seq):
            f = jnp.where(g >= starts[j], starts[j], f)
        return f

    def last_of(g):
        f = jnp.int32(total)
        for j in range(n_seq):
            f = jnp.where(g >= starts[j], starts[j + 1], f)
        return f

    own_a, own_b = base + HALO, base + HALO + sz.tok - 1
    first_a, last_a = first_of(own_a) - base, last_of(own_a) - base
    first_b, last_b = first_of(own_b) - base, last_of(own_b) - base
    q_lo, q_hi = first_a // QB, (last_b + QB - 1) // QB
    scal[sz.q_lo], scal[sz.q_hi] = q_lo, q_hi

    def block(i, _):
        e = i * QB
        left, right = i < sz.own_lo, i >= sz.own_hi
        lo = jnp.where(left, HALO, jnp.where(right, first_b, first_of(base + e) - base)) // QB
        hi = jnp.where(left, last_a, jnp.where(right, HALO + sz.tok, last_of(base + e + QB - 1) - base))
        n = (hi - lo * QB + (KB - 1)) // KB
        scal[sz.k_lo + i] = lo
        scal[sz.k_n + i] = jnp.where((i >= q_lo) & (i < q_hi), n, 0)
        k_end[i] = (hi + QB - 1) // QB
        return 0

    lax.fori_loop(0, sz.n_qb, block, 0)
    scal[sz.need_lo], scal[sz.need_hi] = first_a // RB, (last_b + KB - 1 + RB - 1) // RB
    scal[sz.full_hi] = (last_b + RB - 1) // RB

    step = KB // QB

    def emit(where, c, q, lo, n):
        def one(t, c):
            scal[where[0] + c] = q
            scal[where[1] + c] = lo + t * step
            return c + 1

        return lax.fori_loop(0, n, one, c)

    def close(where, c, q):
        scal[where[2]] = c
        for extra in range(2):
            scal[where[0] + c + extra] = q
            scal[where[1] + c + extra] = jnp.int32(sz.own_lo)

    fwd = (sz.fwd_q, sz.fwd_k, sz.fwd_n)
    both, far, back = sz.lists

    def own_block(i, counts):
        c_f, c_a, c_b = counts
        lo, end = scal[sz.k_lo + i], k_end[i]
        c_f = emit(fwd, c_f, i - sz.own_lo, lo, scal[sz.k_n + i])
        n = (jnp.maximum(sz.own_lo - lo, 0) + step - 1) // step
        c_b = emit(far, c_b, i, sz.own_lo - n * step, n)
        lo = jnp.maximum(lo, sz.own_lo)
        n = (jnp.minimum(end, sz.own_hi) - lo + step - 1) // step
        c_a = emit(both, c_a, i, lo, n)
        lo = lo + n * step
        c_b = emit(far, c_b, i, lo, (jnp.maximum(end - lo, 0) + step - 1) // step)
        return c_f, c_a, c_b

    zero = jnp.int32(0)
    c_f, c_a, c_b = lax.fori_loop(sz.own_lo, sz.own_hi, own_block, (zero, zero, zero))

    def halo_block(i, c):
        return emit(back, c, i, scal[sz.k_lo + i], scal[sz.k_n + i])

    c_c = lax.fori_loop(sz.own_hi, sz.n_qb, halo_block, lax.fori_loop(0, sz.own_lo, halo_block, zero))
    close(fwd, c_f, jnp.int32(sz.own_qb))
    for where_to, c in zip(sz.lists, (c_a, c_b, c_c)):
        close(where_to, c, jnp.int32(sz.own_lo))
    core = replica % 2
    for k in range(n_group):
        for h in range(2):
            scal[sz.places + 2 * k + h] = 2 * (group ^ k) + (core ^ h)

    half = HEAD_DIM // 2
    blocks = sz.ext // QB
    g = base + QB * lax.broadcasted_iota(jnp.int32, (blocks, QB), 0) + lax.broadcasted_iota(jnp.int32, (blocks, QB), 1)
    seg = jnp.full((blocks, QB), -1, jnp.int32)
    first = jnp.zeros((blocks, QB), jnp.int32)
    for j in range(n_seq):
        hit = g >= starts[j]
        seg = jnp.where(hit, j, seg)
        first = jnp.where(hit, starts[j], first)
    seg_buf[...] = jnp.where(g >= total, n_seq, seg) & 15
    pos_buf[...] = jnp.maximum(g - first, 0).astype(F32)
    freq = jnp.exp(lax.broadcasted_iota(jnp.int32, (half, QB), 0).astype(F32) * (-2.0 / HEAD_DIM * math.log(ROPE_BASE)))

    def rows(b, _):
        r0 = pl.multiple_of(b * QB, QB)
        hot = (seg_buf[pl.ds(b, 1), :] == lax.broadcasted_iota(jnp.int32, (LANES, QB), 0)).astype(F32).T
        qf[pl.ds(r0, QB), :] = (hot * BIG).astype(BF)
        lane = lax.broadcasted_iota(jnp.int32, (QB, LANES), 1)
        kf[pl.ds(r0, QB), :] = jnp.where(lane < 16, 1.0 - hot, 0.0).astype(BF)
        ang = freq * pos_buf[pl.ds(b, 1), :]
        co, si = jnp.cos(ang), jnp.sin(ang)
        cos[pl.ds(r0, QB), :] = jnp.concatenate([co] * 4, axis=0).T
        sin[pl.ds(r0, QB), :] = jnp.concatenate([-si, si, -si, si], axis=0).T
        return 0

    lax.fori_loop(0, blocks, rows, 0)


def plan_call(sz, n_replica, n_group, where, lengths):
    sh = jax.ShapeDtypeStruct
    smem = pl.BlockSpec(memory_space=pltpu.SMEM)
    vmem = pl.BlockSpec(memory_space=pltpu.VMEM)
    n_seq = lengths.shape[1]
    return pl.pallas_call(
        functools.partial(plan_kernel, sz, n_replica, n_group),
        in_specs=[smem, smem],
        out_specs=[smem] + [vmem] * 4,
        out_shape=[sh((sz.places + 2 * n_group,), jnp.int32)] + [sh((sz.ext, LANES), BF)] * 2 + [sh((sz.ext, LANES), F32)] * 2,
        scratch_shapes=[pltpu.SMEM((n_seq + 1,), jnp.int32), pltpu.SMEM((sz.n_qb,), jnp.int32), pltpu.VMEM((sz.ext // QB, QB), jnp.int32), pltpu.VMEM((sz.ext // QB, QB), F32)],
        compiler_params=params(60),
        cost_estimate=pl.CostEstimate(flops=10_000_000_000, bytes_accessed=5_000_000, transcendentals=0),
        name="plan",
    )(where, lengths)


def pack_kernel(where, wo, wi, wd, mine, other):
    width = wo.shape[1]
    n_cols = wi.shape[1] // width

    def put(dst, h):
        at = 0
        for ref, col in [(wo, 0)] + [(wi, j) for j in range(n_cols)] + [(wd, 0)]:
            n = half_of(ref.shape[0])
            lo = h * (ref.shape[0] - n)
            dst[at : at + n, :] = ref[lo : lo + n, width * col : width * col + width].astype(BF)
            at += n

    @pl.when(where[0] % 2 == 0)
    def _():
        put(mine, 0)
        put(other, 1)

    @pl.when(where[0] % 2 != 0)
    def _():
        put(mine, 1)
        put(other, 0)


def pack_qkv_kernel(where, w, gains, mine, other):
    width = w.shape[1]
    shard = w.shape[0]
    half = half_of(shard)
    side = jnp.concatenate([gains[...], jnp.zeros((LANES - gains.shape[0], shard), F32)], axis=0).T.astype(BF)

    def put(dst, h):
        lo = h * (shard - half)
        dst[:, :width] = w[lo : lo + half, :].astype(BF)
        dst[:, width:] = side[lo : lo + half, :]

    @pl.when(where[0] % 2 == 0)
    def _():
        put(mine, 0)
        put(other, 1)

    @pl.when(where[0] % 2 != 0)
    def _():
        put(mine, 1)
        put(other, 0)


def pack_qkv_call(where, w, gains):
    vmem = pl.BlockSpec(memory_space=pltpu.VMEM)
    out = jax.ShapeDtypeStruct((half_of(w.shape[0]), w.shape[1] + LANES), BF)
    return pl.pallas_call(
        pack_qkv_kernel,
        in_specs=[pl.BlockSpec(memory_space=pltpu.SMEM), vmem, vmem],
        out_specs=[vmem, vmem],
        out_shape=[out, out],
        compiler_params=params(60),
        cost_estimate=pl.CostEstimate(flops=2_000_000_000, bytes_accessed=3_000_000, transcendentals=0),
        name="pack_projection",
    )(where, w, gains)


def pack_call(where, wo, wi, wd):
    vmem = pl.BlockSpec(memory_space=pltpu.VMEM)
    rows = half_of(wo.shape[0]) * (1 + wi.shape[1] // wo.shape[1]) + half_of(wd.shape[0])
    out = jax.ShapeDtypeStruct((rows, wo.shape[1]), BF)
    return pl.pallas_call(
        pack_kernel,
        in_specs=[pl.BlockSpec(memory_space=pltpu.SMEM), vmem, vmem, vmem],
        out_specs=[vmem, vmem],
        out_shape=[out, out],
        compiler_params=params(60),
        cost_estimate=pl.CostEstimate(flops=3_000_000_000, bytes_accessed=5_000_000, transcendentals=0),
        name="pack_weights",
    )(where, wo, wi, wd)


def fetch_qkv(place, pieces, w, sem):
    copies = []
    shard = w.shape[0] // (len(pieces) // 2)
    for t, piece in enumerate(pieces):
        copies.append(pltpu.make_async_copy(piece.at[:, 0 : w.shape[1]], w.at[pl.ds(row_of(place(t), shard), piece.shape[0]), :], sem.at[t]))
    return copies


def qkv_kernel(sz, n_pieces, scal, xl, xc, xr, *rest):
    pieces, (cos, sin, qkv, kt, vt, n1t, gains, w, sem) = rest[:n_pieces], rest[n_pieces:]
    i = pl.program_id(0)
    left_b, own_b = HALO // RB, sz.tok // RB
    own = (i >= left_b) & (i < left_b + own_b)

    @pl.when(i == 0)
    def _():
        copies = fetch_qkv(lambda t: scal[sz.places + t], pieces, w, sem)
        for c in copies:
            c.start()
        for c in copies:
            c.wait()
        side = w[:, 3 * sz.width :].astype(F32)
        for b in range(sz.width // LANES):
            gains[:, lanes_of(b)] = side[LANES * b : LANES * b + LANES, :].T[:8, :]

    @pl.when((i >= scal[sz.full_hi]) & (i < scal[sz.need_hi]))
    def _():
        qkv[...] = jnp.zeros_like(qkv)
        kt[...] = jnp.zeros_like(kt)
        vt[...] = jnp.zeros_like(vt)

    @pl.when((i >= scal[sz.need_lo]) & (i < scal[sz.full_hi]))
    def _():
        x = jnp.where(i < left_b, xl[...], jnp.where(i < left_b + own_b, xc[...], xr[...])).astype(F32)
        mean = jnp.mean(x, axis=-1, keepdims=True)
        cen = x - mean
        var = jnp.mean(cen * cen, axis=-1, keepdims=True)
        n1 = (cen * lax.rsqrt(var + EPS) * gains[0:1, :]).astype(BF)

        @pl.when(own)
        def _():
            n1t[...] = n1.T

        width = n1.shape[1]
        co, si = cos[...], sin[...]
        sc = HEAD_DIM ** -0.5 * LOG2E
        cq, sq = co * sc, si * sc
        for c in range(3 * width // 256):
            a = nn(n1, w[:, 256 * c : 256 * c + 256])
            part = 256 * c // width
            off = 256 * c - width * part
            if part < 2:
                cc, ss = (cq, sq) if part == 0 else (co, si)
                halves = []
                for h in range(2):
                    b = a[:, 128 * h : 128 * h + 128]
                    halves.append((b * cc + partner(b) * ss).astype(BF))
                r = jnp.concatenate(halves, axis=1)
            else:
                r = a.astype(BF)
            qkv[:, 256 * c : 256 * c + 256] = r
            if part == 1:
                kt[off : off + 256, :] = r.T
            if part == 2:
                vt[off : off + 256, :] = r.T


def qkv_call(sz, scal, xl, xc, xr, pieces, cos, sin):
    tok, width, ext = sz.tok, sz.width, sz.ext
    own_b, lb = tok // RB, HALO // RB
    clampi = lambda lo, n: (lambda i, s: (jnp.clip(i - lo, 0, n - 1), 0))
    used = lambda i, s: jnp.clip(i, s[sz.need_lo], s[sz.need_hi] - 1)
    row = lambda i, s: (used(i, s), 0)
    fix = lambda i, s: (0, 0)
    col = lambda i, s: (0, used(i, s))
    sh = jax.ShapeDtypeStruct
    return pl.pallas_call(
        functools.partial(qkv_kernel, sz, len(pieces)),
        grid_spec=pltpu.PrefetchScalarGridSpec(
            num_scalar_prefetch=1,
            grid=(sz.blocks,),
            in_specs=[
                pl.BlockSpec((RB, width), clampi(0, lb)),
                pl.BlockSpec((RB, width), clampi(lb, own_b)),
                pl.BlockSpec((RB, width), clampi(lb + own_b, lb)),
                *[pl.BlockSpec(memory_space=pl.ANY)] * len(pieces),
                pl.BlockSpec((RB, LANES), row),
                pl.BlockSpec((RB, LANES), row),
            ],
            out_specs=[
                pl.BlockSpec((RB, 3 * width), row),
                pl.BlockSpec((width, RB), col),
                pl.BlockSpec((width, RB), col),
                pl.BlockSpec((width, RB), lambda i, s: (0, jnp.clip(i - lb, 0, own_b - 1))),
                pl.BlockSpec((8, width), fix),
            ],
            scratch_shapes=[pltpu.VMEM((width, 3 * width + LANES), BF), pltpu.SemaphoreType.DMA((len(pieces),))],
        ),
        out_shape=[sh((ext, 3 * width), BF), sh((width, ext), BF), sh((width, ext), BF), sh((width, tok), BF),
                   sh((8, width), F32)],
        compiler_params=params(60, dimension_semantics=("arbitrary",)),
        cost_estimate=pl.CostEstimate(flops=14_000_000_000, bytes_accessed=30_000_000, transcendentals=0),
        name="qkv",
    )(scal, xl, xc, xr, *pieces, cos, sin)


def split_heads(x):
    low = lax.broadcasted_iota(jnp.int32, x.shape, 1) < HEAD_DIM
    zero = jnp.zeros_like(x)
    return jnp.concatenate([jnp.where(low, x, zero), jnp.where(low, zero, x)], axis=0)


def lanes_of(p):
    return slice(LANES * p, LANES * p + LANES)


def fwd_kernel(sz, pg, scal, q, k, vt, qf, kf, out, out_t, lse, q2, buf_a, buf_b, acc, tops):
    nq = sz.own_qb
    ones = jnp.ones((16, KB), BF)
    for qi in range(nq):
        r0 = HALO + qi * QB
        fq = qf[r0 : r0 + QB, :]
        f2 = jnp.concatenate([fq, fq], axis=0)
        for p in range(pg):
            q2[qi, p] = jnp.concatenate([split_heads(q[r0 : r0 + QB, lanes_of(p)]), f2], axis=1)

    def zero(i, _):
        for p in range(pg):
            acc[i, p] = jnp.zeros((LANES + 16, 2 * QB), F32)
            tops[i, p] = jnp.zeros((8, 2 * QB), F32)
        return 0

    lax.fori_loop(0, nq + 1, zero, 0)

    def scores(qi, k0, p, fk):
        return nt(jnp.concatenate([k[pl.ds(k0, KB), lanes_of(p)], fk], axis=1), q2[qi, p])

    def mixed(k0, p, probs):
        va = jnp.concatenate([vt[lanes_of(p), pl.ds(k0, KB)], ones], axis=0)
        return nn(va, probs.astype(BF))

    def tile(i):
        return scal[sz.fwd_q + i], pl.multiple_of(scal[sz.fwd_k + i] * QB, QB)

    def score_tile(i, buf):
        qi, k0 = tile(i)
        qi = jnp.minimum(qi, nq - 1)
        fk = kf[pl.ds(k0, KB), :]
        for p in range(pg):
            buf[p] = scores(qi, k0, p, fk)

    def mix_tile(i, buf):
        qi, k0 = tile(i)
        for p in range(pg):
            acc[qi, p] += mixed(k0, p, jnp.exp2(buf[p]))

    score_tile(0, buf_a)

    def body(j, _):
        score_tile(2 * j + 1, buf_b)
        mix_tile(2 * j, buf_a)
        score_tile(2 * j + 2, buf_a)
        mix_tile(2 * j + 1, buf_b)
        return 0

    lax.fori_loop(0, (scal[sz.fwd_n] + 1) // 2, body, 0)

    low = high = acc[0, 0, LANES : LANES + 1, :]
    for qi in range(nq):
        for p in range(pg):
            total = acc[qi, p, LANES : LANES + 1, :]
            low, high = jnp.minimum(low, total), jnp.maximum(high, total)
    safe = (jnp.min(low) > 2.0 ** -60) & (jnp.max(high) < 2.0 ** 100)

    @pl.when(jnp.logical_not(safe))
    def _():
        lax.fori_loop(0, nq, zero, 0)

        def per_q(qi, _):
            lo, n = scal[sz.k_lo + sz.own_lo + qi], scal[sz.k_n + sz.own_lo + qi]
            for p in range(pg):
                def top(t, m):
                    k0 = pl.multiple_of(lo * QB + t * KB, QB)
                    return jnp.maximum(m, jnp.max(scores(qi, k0, p, kf[pl.ds(k0, KB), :]), axis=0, keepdims=True))

                m = lax.fori_loop(0, n, top, jnp.full((1, 2 * QB), BIG, F32))
                tops[qi, p] = jnp.broadcast_to(m, (8, 2 * QB))

                def add(t, _):
                    k0 = pl.multiple_of(lo * QB + t * KB, QB)
                    acc[qi, p] += mixed(k0, p, jnp.exp2(scores(qi, k0, p, kf[pl.ds(k0, KB), :]) - m))
                    return 0

                lax.fori_loop(0, n, add, 0)
            return 0

        lax.fori_loop(0, nq, per_q, 0)

    def finish(qi, _):
        o0 = pl.multiple_of(qi * QB, QB)
        for p in range(pg):
            a = acc[qi, p]
            total = a[LANES : LANES + 1, :]
            inv = 1.0 / total
            o_t = jnp.concatenate([a[:HEAD_DIM, :QB] * inv[:, :QB], a[HEAD_DIM:LANES, QB:] * inv[:, QB:]], axis=0).astype(BF)
            out_t[lanes_of(p), pl.ds(o0, QB)] = o_t
            out[pl.ds(o0, QB), lanes_of(p)] = o_t.T
            st = tops[qi, p, 0:1, :] + jnp.log2(total)
            lse[p, 0:1, pl.ds(o0, QB)] = st[:, :QB]
            lse[p, 1:2, pl.ds(o0, QB)] = st[:, QB:]
        return 0

    lax.fori_loop(0, nq, finish, 0)


def fwd_call(sz, scal, qkv, vt, qf, kf, pg):
    ext, tok, width = sz.ext, sz.tok, sz.width
    pairs = width // LANES
    steps = pairs // pg
    wide = LANES * pg
    col = lambda off: (lambda i, s: (0, off + i))
    fix = lambda i, s: (0, 0)
    sh = jax.ShapeDtypeStruct
    return pl.pallas_call(
        functools.partial(fwd_kernel, sz, pg),
        grid_spec=pltpu.PrefetchScalarGridSpec(
            num_scalar_prefetch=1,
            grid=(steps,),
            in_specs=[
                pl.BlockSpec((ext, wide), col(0)),
                pl.BlockSpec((ext, wide), col(steps)),
                pl.BlockSpec((wide, ext), lambda i, s: (i, 0)),
                pl.BlockSpec((ext, LANES), fix),
                pl.BlockSpec((ext, LANES), fix),
            ],
            out_specs=[
                pl.BlockSpec((tok, wide), col(0)),
                pl.BlockSpec((wide, tok), lambda i, s: (i, 0)),
                pl.BlockSpec((pg, 2, tok), lambda i, s: (i, 0, 0)),
            ],
            scratch_shapes=[
                pltpu.VMEM((sz.own_qb, pg, 2 * QB, 2 * LANES), BF),
                pltpu.VMEM((pg, KB, 2 * QB), F32),
                pltpu.VMEM((pg, KB, 2 * QB), F32),
                pltpu.VMEM((sz.own_qb + 1, pg, LANES + 16, 2 * QB), F32),
                pltpu.VMEM((sz.own_qb + 1, pg, 8, 2 * QB), F32),
            ],
        ),
        out_shape=[sh((tok, width), BF), sh((width, tok), BF), sh((pairs, 2, tok), F32)],
        compiler_params=params(60, dimension_semantics=("arbitrary",)),
        cost_estimate=pl.CostEstimate(flops=30_000_000_000, bytes_accessed=15_000_000, transcendentals=0),
        name="attn_forward",
    )(scal, qkv, qkv, vt, qf, kf)


def fetch_mlp(place, pieces, wo, wi, wd, sem, width):
    copies = [], [], []
    shards = len(pieces) // 2
    half, half_d = half_of(wo.shape[0] // shards), half_of(wd.shape[0] // shards)
    t_cols = wi.shape[1] // width
    for t, piece in enumerate(pieces):
        row0 = row_of(place(t), wo.shape[0] // shards)
        row_d = row_of(place(t), wd.shape[0] // shards)
        copies[0].append(pltpu.make_async_copy(piece.at[0:half, :], wo.at[pl.ds(row0, half), :], sem.at[t, 0]))
        for j in range(t_cols):
            copies[1].append(pltpu.make_async_copy(
                piece.at[half * (j + 1) : half * (j + 2), :],
                wi.at[pl.ds(row0, half), width * j : width * j + width], sem.at[t, j + 1]))
        lo = half * (t_cols + 1)
        copies[2].append(pltpu.make_async_copy(piece.at[lo : lo + half_d, :], wd.at[pl.ds(row_d, half_d), :], sem.at[t, t_cols + 1]))
    return copies


def three_parts(v):
    high = v.astype(BF).astype(F32)
    middle = (v - high).astype(BF).astype(F32)
    return high, middle, v - high - middle


def mid_kernel(sz, n_pieces, scal, *refs):
    pieces, refs = refs[:n_pieces], refs[n_pieces:]
    wo, wi, wd, sem = refs[-4:]
    step = pl.program_id(0)

    @pl.when(step == 0)
    def _():
        copies = fetch_mlp(lambda t: scal[sz.places + t], pieces, wo, wi, wd, sem, wo.shape[1])
        for group in copies:
            for c in group:
                c.start()

        def wait(which):
            for c in copies[which]:
                c.wait()

        mid_body(sz, wait, wo, wi, wd, *refs[:-4])

    @pl.when(step != 0)
    def _():
        mid_body(sz, lambda which: None, wo, wi, wd, *refs[:-4])


def mid_body(sz, wait, wo, wi, wd, x, o, gy, g2, ind, lse, out, mt_o, gu_o, n2t_o, gh2b_o, go_o, left_o, right_o, dlt):
    ff = wd.shape[0]
    wait(0)
    h2 = x[...].astype(F32) + nn(o[...], wo[...])
    mean = jnp.mean(h2, axis=-1, keepdims=True)
    cen = h2 - mean
    r2 = lax.rsqrt(jnp.mean(cen * cen, axis=-1, keepdims=True) + EPS)
    nh = cen * r2
    g = g2[1:2, :]
    n2 = (nh * g).astype(BF)
    n2t_o[...] = n2.T
    gyb = gy[...]
    hidden = []
    wait(1)
    wait(2)
    step = 384
    for c in range(ff // step):
        lo = c * step
        a = nn(n2, wi[:, lo : lo + step])
        b = nn(n2, wi[:, ff + lo : ff + lo + step])
        gm = nt(gyb, wd[lo : lo + step, :])
        half = 0.5 * (1.0 + lax.erf(a * (2.0 ** -0.5)))
        gel = a * half
        mm = (gel * b).astype(BF)
        mt_o[lo : lo + step, :] = mm.T
        hidden.append(mm)
        dgel = half + a * (jnp.exp(-0.5 * a * a) * (1.0 / math.sqrt(2.0 * math.pi)))
        ga = (gm * b * dgel).astype(BF)
        gb = (gm * gel).astype(BF)
        gu_o[:, lo : lo + step] = ga
        gu_o[:, ff + lo : ff + lo + step] = gb
    out[...] = (h2 + nn(jnp.concatenate(hidden, axis=1), wd[...])).astype(BF)
    gn2 = nt(gu_o[...], wi[...])

    t = gn2 * g
    gh2 = gyb.astype(F32) + r2 * (t - jnp.mean(t, axis=-1, keepdims=True) - nh * jnp.mean(t * nh, axis=-1, keepdims=True))
    gb16 = gh2.astype(BF)
    gh2b_o[...] = gb16
    go = nt(gb16, wo[...]).astype(BF)
    go_o[...] = go
    prod = go.astype(F32) * o[...].astype(F32)
    hi = prod.astype(BF)
    lo_part = (prod - hi.astype(F32)).astype(BF)
    sums = nt(ind[...], hi) + nt(ind[...], lo_part)
    for p in range(dlt.shape[0]):
        dlt[p] = sums[2 * p : 2 * p + 2, :]
    heads = lse.shape[0] * 2
    top = jnp.concatenate([lse[p] for p in range(lse.shape[0])] + [jnp.zeros((STAT - heads, sums.shape[1]), F32)], axis=0)
    rows = [part for v in (top, sums) for part in three_parts(v)]
    rows.append(jnp.zeros((LANES - 6 * STAT, sums.shape[1]), F32))
    width = go.shape[1]
    stats = jnp.concatenate(rows, axis=0).T.astype(BF)
    step = pl.program_id(0)

    @pl.when(step < HALO // RB)
    def _():
        left_o[:, :width] = go
        left_o[:, width:] = stats

    @pl.when(step >= (sz.tok - HALO) // RB)
    def _():
        right_o[:, :width] = go
        right_o[:, width:] = stats


def mid_call(sz, scal, pieces, x, o, gy, g2, lse, ff):
    tok, width = x.shape
    heads = jnp.arange(16, dtype=jnp.int32)
    ind = (heads[:, None] == (jnp.arange(width, dtype=jnp.int32) // HEAD_DIM)[None, :]).astype(BF)
    row = lambda i, s: (i, 0)
    fix = lambda i, s: (0, 0)
    rs = lambda n: pl.BlockSpec((RB, n), row)
    cs = lambda n: pl.BlockSpec((n, RB), lambda i, s: (0, i))
    fs = lambda a: pl.BlockSpec(a.shape, fix)
    sh = jax.ShapeDtypeStruct
    n = len(pieces)
    stat = pl.BlockSpec((width // LANES, 2, RB), lambda i, s: (0, 0, i))
    halo = lambda lo: pl.BlockSpec((RB, width + LANES), lambda i, s: (jnp.clip(i - lo, 0, HALO // RB - 1), 0))
    halos = [halo(0), halo((tok - HALO) // RB)]
    return pl.pallas_call(
        functools.partial(mid_kernel, sz, n),
        grid_spec=pltpu.PrefetchScalarGridSpec(
            num_scalar_prefetch=1,
            grid=(tok // RB,),
            in_specs=[*[pl.BlockSpec(memory_space=pl.ANY)] * n, rs(width), rs(width), rs(width), fs(g2), fs(ind), stat],
            out_specs=[rs(width), cs(ff), rs(2 * ff), cs(width), rs(width), rs(width), *halos, stat],
            scratch_shapes=[pltpu.VMEM((width, width), BF), pltpu.VMEM((width, 2 * ff), BF), pltpu.VMEM((ff, width), BF),
                            pltpu.SemaphoreType.DMA((n, 2 * ff // width + 2))],
        ),
        out_shape=[sh((tok, width), BF), sh((ff, tok), BF), sh((tok, 2 * ff), BF), sh((width, tok), BF),
                   sh((tok, width), BF), sh((tok, width), BF),
                   sh((HALO, width + LANES), BF), sh((HALO, width + LANES), BF),
                   sh((width // LANES, 2, tok), F32)],
        compiler_params=params(60, dimension_semantics=("arbitrary",)),
        cost_estimate=pl.CostEstimate(flops=13_000_000_000 * 2, bytes_accessed=30_000_000, transcendentals=0),
        name="middle",
    )(scal, *pieces, x, o, gy, g2, ind, lse)


def put_halves(core, keep, send, rows0, values, n_group):
    rows = values.shape[0] // n_group
    half = half_of(rows)

    def store(first, second):
        for g in range(n_group):
            lo, hi = rows * g, rows * (g + 1)
            first[g, pl.ds(rows0, half), :] = values[lo : lo + half, :]
            second[g, pl.ds(rows0, half), :] = values[hi - half : hi, :]

    @pl.when(core == 0)
    def _():
        store(keep, send)

    @pl.when(core != 0)
    def _():
        store(send, keep)


def put_halves(core, keep, send, rows0, values, n_group):
    rows = values.shape[0] // n_group
    half = half_of(rows)

    def store(first, second):
        for g in range(n_group):
            lo, hi = rows * g, rows * (g + 1)
            first[g, pl.ds(rows0, half), :] = values[lo : lo + half, :]
            second[g, pl.ds(rows0, half), :] = values[hi - half : hi, :]

    @pl.when(core == 0)
    def _():
        store(keep, send)

    @pl.when(core != 0)
    def _():
        store(send, keep)


def in_grad_kernel(n_group, at, scal, n2t, gu, keep, send):
    half = half_of(n2t.shape[0] // n_group)
    row0 = pl.multiple_of(pl.program_id(0) * half, 16)
    put_halves(scal[at] % 2, keep, send, row0, nn(n2t[...], gu[...]).astype(BF), n_group)


def in_grad_call(sz, scal, n2t, gu, n_group):
    width, tok = n2t.shape
    n_cols = gu.shape[1] // width
    rows = n_cols * half_of(width // n_group)
    out = jax.ShapeDtypeStruct((n_group, rows, width), BF)
    return pl.pallas_call(
        functools.partial(in_grad_kernel, n_group, sz.places),
        grid_spec=pltpu.PrefetchScalarGridSpec(
            num_scalar_prefetch=1,
            grid=(n_cols,),
            in_specs=[pl.BlockSpec((width, tok), lambda j, s: (0, 0)), pl.BlockSpec((tok, width), lambda j, s: (0, j))],
            out_specs=[pl.BlockSpec((n_group, rows, width), lambda j, s: (0, 0, 0))] * 2,
        ),
        out_shape=[out, out],
        compiler_params=params(60, dimension_semantics=("arbitrary",)),
        cost_estimate=pl.CostEstimate(flops=8_000_000_000, bytes_accessed=10_000_000, transcendentals=0),
        name="in_weight_gradient",
    )(scal, n2t, gu)


def down_out_kernel(n_group, at, scal, mt, gy, ot_h, gh_h, keep, send, ot, gh, sem):
    copies = [pltpu.make_async_copy(ot_h, ot, sem.at[0]), pltpu.make_async_copy(gh_h, gh, sem.at[1])]
    for c in copies:
        c.start()
    put_halves(scal[at] % 2, keep, send, 0, nn(mt[...], gy[...]).astype(BF), n_group)
    for c in copies:
        c.wait()
    used = half_of(mt.shape[0] // n_group) + half_of(ot.shape[0] // n_group)
    put_halves(scal[at] % 2, keep, send, half_of(mt.shape[0] // n_group), nn(ot[...], gh[...]).astype(BF), n_group)
    if used < keep.shape[1]:
        for ref in (keep, send):
            ref[:, used:, :] = jnp.zeros((n_group, keep.shape[1] - used, keep.shape[2]), BF)


def down_out_call(sz, scal, mt, gy, ot, gh, n_group, rows):
    width, tok = ot.shape
    ff = mt.shape[0]
    out = jax.ShapeDtypeStruct((n_group, rows, width), BF)
    anyspec = pl.BlockSpec(memory_space=pl.ANY)
    fix = lambda j, s: (0, 0)
    return pl.pallas_call(
        functools.partial(down_out_kernel, n_group, sz.places),
        grid_spec=pltpu.PrefetchScalarGridSpec(
            num_scalar_prefetch=1,
            grid=(1,),
            in_specs=[pl.BlockSpec((ff, tok), fix), pl.BlockSpec((tok, width), fix), anyspec, anyspec],
            out_specs=[pl.BlockSpec((n_group, rows, width), lambda j, s: (0, 0, 0))] * 2,
            scratch_shapes=[pltpu.VMEM((width, tok), BF), pltpu.VMEM((tok, width), BF), pltpu.SemaphoreType.DMA((2,))],
        ),
        out_shape=[out, out],
        compiler_params=params(60, dimension_semantics=("arbitrary",)),
        cost_estimate=pl.CostEstimate(flops=100_000_000, bytes_accessed=100_000, transcendentals=0),
        name="down_out_weight_gradients",
    )(scal, mt, gy, ot, gh)


def bwd_kernel(sz, pg, at, n_group, scal, qkv_h, kt_h, qf_h, kf_h, gl_h, gc_h, gr_h, cos_h, sin_h, n1t_h,
               lse_c, dlt_c, grad_h, keep_h, send_h, grad, keep, send,
               q, k, v, kt, qf, kf, go, halo_st, cos, sin, n1t, q2, g2, gka, gva, gqa, st, s_a, p_a, s_b, p_b, sem, out_sem):
    n_qb, tok, width = sz.n_qb, sz.tok, sz.width
    wide = LANES * pg
    q_lo, q_hi = scal[sz.q_lo], scal[sz.q_hi]
    ext = q.shape[0]
    cols = lambda part: pl.ds(part * width + at * wide, wide)
    near, left = pl.ds(HALO, tok + QB), pl.ds(0, HALO)
    right, own = pl.ds(HALO + tok + QB, ext - HALO - tok - QB), pl.ds(HALO, tok)

    def rows(seg):
        return [(qkv_h.at[seg, cols(part)], dst.at[seg, :]) for part, dst in ((0, q), (1, k), (2, v))] + [
            (kt_h.at[cols(0), seg], kt.at[:, seg])]

    near_q, *near_rest = rows(near)
    first = [(gc_h.at[:, cols(0)], go.at[own, :]), (qf_h, qf), near_q, (kf_h, kf), *near_rest]
    second = [*rows(left), *rows(right), (gl_h.at[:, cols(0)], go.at[left, :]),
              (gr_h.at[:, cols(0)], go.at[pl.ds(HALO + tok, HALO), :]),
              (gl_h.at[:, pl.ds(width, LANES)], halo_st.at[0]), (gr_h.at[:, pl.ds(width, LANES)], halo_st.at[1])]
    third = [(cos_h.at[own, :], cos), (sin_h.at[own, :], sin), (n1t_h, n1t)]
    copies = [pltpu.make_async_copy(a, b, sem.at[t]) for t, (a, b) in enumerate(first + second + third)]
    n_first, n_second = len(first), len(first) + len(second)
    for c in copies:
        c.start()

    for row, part in ((0, lse_c), (1, dlt_c)):
        for p in range(pg):
            for b in range(sz.own_qb):
                for h in range(2):
                    st[sz.own_lo + b, p, row : row + 1, QB * h : QB * h + QB] = part[p, h : h + 1, QB * b : QB * b + QB]

    def halo_stats(side, first):
        def one(i, _):
            rows_t = halo_st[side, pl.ds(pl.multiple_of((i - first) * QB, QB), QB), :].astype(F32).T
            for p in range(pg):
                for h in range(2):
                    for row in range(2):
                        lo = 3 * STAT * row + 2 * (pg * at + p) + h
                        parts = [rows_t[lo + STAT * t : lo + STAT * t + 1, :] for t in range(3)]
                        st[i, p, row : row + 1, QB * h : QB * h + QB] = parts[0] + parts[1] + parts[2]
            return 0

        return one

    for c in copies[:3]:
        c.wait()

    def prep(i, _):
        r0 = pl.multiple_of(i * QB, QB)
        fq = qf[pl.ds(r0, QB), :]
        f2 = jnp.concatenate([fq, fq], axis=0)
        for p in range(pg):
            q2[i, p] = jnp.concatenate([split_heads(q[pl.ds(r0, QB), lanes_of(p)]), f2], axis=1)
            g2[i, p] = split_heads(go[pl.ds(r0, QB), lanes_of(p)])
            gqa[i, p] = jnp.zeros((LANES, 2 * QB), F32)
            gka[p, pl.ds(r0, QB), :] = jnp.zeros((QB, LANES), F32)
            gva[p, pl.ds(r0, QB), :] = jnp.zeros((QB, LANES), F32)
        return 0

    lax.fori_loop(sz.own_lo, sz.own_hi, prep, 0)
    for c in copies[3:n_first]:
        c.wait()

    def run(where, for_keys, for_queries):
        def tile(i):
            return scal[where[0] + i], pl.multiple_of(scal[where[1] + i] * QB, QB)

        def score_tile(i, s_buf, p_buf):
            qi, k0 = tile(i)
            fk = kf[pl.ds(k0, KB), :]
            for p in range(pg):
                s_buf[p] = nt(jnp.concatenate([k[pl.ds(k0, KB), lanes_of(p)], fk], axis=1), q2[qi, p])
                p_buf[p] = nt(v[pl.ds(k0, KB), lanes_of(p)], g2[qi, p])

        def grad_tile(i, s_buf, p_buf):
            qi, k0 = tile(i)
            dead = jnp.where(i < scal[where[2]], 0.0, 1e38).astype(F32)
            for p in range(pg):
                pr = jnp.exp2(s_buf[p] - (st[qi, p, 0:1, :] + dead))
                ds = (pr * (p_buf[p] - st[qi, p, 1:2, :])).astype(BF)
                if for_keys:
                    gva[p, pl.ds(k0, KB), :] += nn(pr.astype(BF), g2[qi, p])
                    gka[p, pl.ds(k0, KB), :] += nn(ds, q2[qi, p, :, :LANES])
                if for_queries:
                    gqa[qi, p] += nn(kt[lanes_of(p), pl.ds(k0, KB)], ds)

        @pl.when(scal[where[2]] > 0)
        def _():
            score_tile(0, s_a, p_a)

            def body(j, _):
                score_tile(2 * j + 1, s_b, p_b)
                grad_tile(2 * j, s_a, p_a)
                score_tile(2 * j + 2, s_a, p_a)
                grad_tile(2 * j + 1, s_b, p_b)
                return 0

            lax.fori_loop(0, (scal[where[2]] + 1) // 2, body, 0)

    run(sz.lists[0], True, True)
    for c in copies[n_first:n_second]:
        c.wait()
    lax.fori_loop(q_lo, sz.own_lo, prep, 0)
    lax.fori_loop(sz.own_hi, q_hi, prep, 0)
    lax.fori_loop(q_lo, sz.own_lo, halo_stats(0, 0), 0)
    lax.fori_loop(sz.own_hi, q_hi, halo_stats(1, sz.own_hi), 0)
    run(sz.lists[1], False, True)
    run(sz.lists[2], True, False)
    copies[n_second].wait()
    copies[n_second + 1].wait()

    sc = HEAD_DIM ** -0.5

    def finish(i, _):
        o0 = pl.multiple_of(i * QB, QB)
        r0 = pl.multiple_of(HALO + i * QB, QB)
        co, si = cos[pl.ds(o0, QB), :], sin[pl.ds(o0, QB), :]
        for p in range(pg):
            a = gqa[sz.own_lo + i, p]
            gt = jnp.concatenate([a[:HEAD_DIM, :QB], a[HEAD_DIM:, QB:]], axis=0).T * sc
            grad[pl.ds(o0, QB), LANES * p : LANES * p + LANES] = (gt * co - partner(gt) * si).astype(BF)
            b = gka[p, pl.ds(r0, QB), :] * LN2
            lo = wide + LANES * p
            grad[pl.ds(o0, QB), lo : lo + LANES] = (b * co - partner(b) * si).astype(BF)
            lo = 2 * wide + LANES * p
            grad[pl.ds(o0, QB), lo : lo + LANES] = gva[p, pl.ds(r0, QB), :].astype(BF)
        return 0

    lax.fori_loop(0, sz.own_qb, finish, 0)
    leaving = [pltpu.make_async_copy(grad, grad_h, out_sem.at[0])]
    leaving[0].start()
    copies[n_second + 2].wait()
    for part in range(3):
        lanes = slice(wide * part, wide * part + wide)
        values = nn(n1t[...], grad[:, lanes]).astype(BF)
        put_halves(scal[sz.places] % 2, keep.at[:, :, lanes], send.at[:, :, lanes], 0, values, n_group)
        for t, (a, b) in enumerate(((keep, keep_h), (send, send_h))):
            leaving.append(pltpu.make_async_copy(a.at[:, :, lanes], b.at[:, :, lanes], out_sem.at[1 + 2 * part + t]))
            leaving[-1].start()
    for c in leaving:
        c.wait()


def bwd_call(sz, scal, qkv, kt, qf, kf, gl, gc, gr, lse, dlt, cos, sin, n1t, pg, at, n_group):
    ext, tok, width, n_qb = sz.ext, sz.tok, sz.width, sz.n_qb
    wide = LANES * pg
    half = half_of(width // n_group)
    spec = lambda shape, *idx: pl.BlockSpec(shape, lambda i, s: idx)
    sh = jax.ShapeDtypeStruct
    outs = [(tok, 3 * wide), (n_group, half, 3 * wide), (n_group, half, 3 * wide)]
    return pl.pallas_call(
        functools.partial(bwd_kernel, sz, pg, at, n_group),
        grid_spec=pltpu.PrefetchScalarGridSpec(
            num_scalar_prefetch=1,
            grid=(1,),
            in_specs=[pl.BlockSpec(memory_space=pl.ANY)] * 10
            + [spec((pg, 2, tok), at, 0, 0), spec((pg, 2, tok), at, 0, 0)],
            out_specs=[pl.BlockSpec(memory_space=pl.ANY)] * 3,
            scratch_shapes=[
                *[pltpu.VMEM(o, BF) for o in outs],
                *[pltpu.VMEM((ext, wide), BF)] * 3,
                pltpu.VMEM((wide, ext), BF),
                pltpu.VMEM((ext, LANES), BF),
                pltpu.VMEM((ext, LANES), BF),
                pltpu.VMEM((tok + 2 * HALO, wide), BF),
                pltpu.VMEM((2, HALO, LANES), BF),
                pltpu.VMEM((tok, LANES), F32),
                pltpu.VMEM((tok, LANES), F32),
                pltpu.VMEM((width, tok), BF),
                pltpu.VMEM((n_qb, pg, 2 * QB, 2 * LANES), BF),
                pltpu.VMEM((n_qb, pg, 2 * QB, LANES), BF),
                pltpu.VMEM((pg, ext, LANES), F32),
                pltpu.VMEM((pg, ext, LANES), F32),
                pltpu.VMEM((n_qb, pg, LANES, 2 * QB), F32),
                pltpu.VMEM((n_qb, pg, 8, 2 * QB), F32),
                *[pltpu.VMEM((pg, KB, 2 * QB), F32)] * 4,
                pltpu.SemaphoreType.DMA((22,)),
                pltpu.SemaphoreType.DMA((7,)),
            ],
        ),
        out_shape=[sh(o, BF) for o in outs],
        compiler_params=params(60, dimension_semantics=("arbitrary",)),
        cost_estimate=pl.CostEstimate(flops=35_000_000_000, bytes_accessed=20_000_000, transcendentals=0),
        name="attn_backward",
    )(scal, qkv, kt, qf, kf, gl, gc, gr, cos, sin, n1t, lse, dlt)


def gx_kernel(n_pieces, n_grads, at, scal, *refs):
    pieces, grads = refs[:n_pieces], refs[n_pieces : n_pieces + n_grads]
    x, gh2, g1, out, w, sem = refs[n_pieces + n_grads :]

    @pl.when(pl.program_id(0) == 0)
    def _():
        copies = fetch_qkv(lambda t: scal[at + t], pieces, w, sem)
        for c in copies:
            c.start()
        for c in copies:
            c.wait()

    width = x.shape[1]
    gn = None
    wide = grads[0].shape[1] // 3
    for part in range(3):
        lhs = jnp.concatenate([grad[:, wide * part : wide * part + wide] for grad in grads], axis=1)
        term = nt(lhs, w[:, width * part : width * part + width])
        gn = term if gn is None else gn + term
    xf = x[...].astype(F32)
    mean = jnp.mean(xf, axis=-1, keepdims=True)
    cen = xf - mean
    r1 = lax.rsqrt(jnp.mean(cen * cen, axis=-1, keepdims=True) + EPS)
    nh = cen * r1

    t = gn * g1[0:1, :]
    gx = gh2[...].astype(F32) + r1 * (t - jnp.mean(t, axis=-1, keepdims=True) - nh * jnp.mean(t * nh, axis=-1, keepdims=True))
    out[...] = gx.astype(BF)


def gx_call(sz, scal, pieces, grads, x, gh2, g1):
    tok, width = x.shape
    row = lambda i, s: (i, 0)
    fix = lambda i, s: (0, 0)
    rs = pl.BlockSpec((RB, width), row)
    n = len(pieces)
    return pl.pallas_call(
        functools.partial(gx_kernel, n, len(grads), sz.places),
        grid_spec=pltpu.PrefetchScalarGridSpec(
            num_scalar_prefetch=1,
            grid=(tok // RB,),
            in_specs=[*[pl.BlockSpec(memory_space=pl.ANY)] * n,
                      *[pl.BlockSpec((RB, g.shape[1]), row) for g in grads],
                      rs, rs, pl.BlockSpec(g1.shape, fix)],
            out_specs=rs,
            scratch_shapes=[pltpu.VMEM((width, 3 * width), BF), pltpu.SemaphoreType.DMA((n,))],
        ),
        out_shape=jax.ShapeDtypeStruct((tok, width), BF),
        compiler_params=params(60, dimension_semantics=("arbitrary",)),
        cost_estimate=pl.CostEstimate(flops=4_000_000_000, bytes_accessed=15_000_000, transcendentals=0),
        name="input_gradient",
    )(scal, *pieces, *grads, x, gh2, g1)


def gain_row(w, grad, gain):
    low = lambda v: v.astype(BF).astype(F32)
    total = jnp.sum(low(w) * grad, axis=1, keepdims=True)
    return jnp.broadcast_to(total, (total.shape[0], LANES)).T[0:1, :] / low(gain)


def in_core_order(core, mine, other, use):
    @pl.when(core == 0)
    def _():
        use(mine, other)

    @pl.when(core != 0)
    def _():
        use(other, mine)


def qkv_end_kernel(at, scal, t, s, w, gain, out, g_out):
    shard = w.shape[0]
    half = half_of(shard)
    wide = t.shape[1] // 3
    calls = t.shape[0] // half

    def use(first, second):
        for ref, lo in ((first, 0), (second, shard - half)):
            for j in range(calls):
                for part in range(3):
                    c = wide * (calls * part + j)
                    out[lo : lo + half, c : c + wide] = ref[half * j : half * j + half, wide * part : wide * part + wide].astype(F32)

    in_core_order(scal[at] % 2, t, s, use)
    g_out[...] = gain_row(w[...], out[...], gain[...])


def mlp_end_kernel(at, scal, t, s, w, gain, d_in, d_down, d_out, g_out):
    shard, shard_d, width = w.shape[0], d_down.shape[0], d_out.shape[1]
    half, half_d = half_of(shard), half_of(shard_d)
    n_cols = w.shape[1] // width

    def use(first, second):
        for ref, h in ((first, 0), (second, 1)):
            lo, lo_d = h * (shard - half), h * (shard_d - half_d)
            for j in range(n_cols):
                d_in[lo : lo + half, width * j : width * j + width] = ref[half * j : half * j + half, :].astype(F32)
            at_d = half * n_cols
            d_down[lo_d : lo_d + half_d, :] = ref[at_d : at_d + half_d, :].astype(F32)
            d_out[lo : lo + half, :] = ref[at_d + half_d : at_d + half_d + half, :].astype(F32)

    in_core_order(scal[at] % 2, t, s, use)
    g_out[...] = gain_row(w[...], d_in[...], gain[...])


def end_call(kernel, name, sz, scal, arrays, w, gain, shapes):
    smem = pl.BlockSpec(memory_space=pltpu.SMEM)
    vmem = pl.BlockSpec(memory_space=pltpu.VMEM)
    outs = [*shapes, (1, w.shape[0])]
    return pl.pallas_call(
        functools.partial(kernel, sz.places),
        in_specs=[smem] + [vmem] * (len(arrays) + 2),
        out_specs=[vmem] * len(outs),
        out_shape=[jax.ShapeDtypeStruct(o, F32) for o in outs],
        compiler_params=params(60),
        cost_estimate=pl.CostEstimate(flops=3_000_000_000, bytes_accessed=5_000_000, transcendentals=0),
        name=name,
    )(scal, *arrays, w, gain.reshape(1, -1))


class Net:
    def __init__(self, n_replica, n_group):
        self.n_replica, self.n_group, self.n_z = n_replica, n_group, n_replica // 2
        self.replica, self.group = lax.axis_index("replica"), lax.axis_index("group")
        self.core = self.replica & 1

    def shift(self, a, step):
        pairs = [(i, i + step) for i in range(self.n_replica) if 0 <= i + step < self.n_replica]
        return lax.ppermute(a, "replica", pairs)

    def core_swap(self, a):
        return lax.ppermute(a, "replica", [(i, i ^ 1) for i in range(self.n_replica)])

    def across(self, a, k):
        return lax.ppermute(a, "group", [(i, i ^ k) for i in range(self.n_group)])

    def across_swap(self, a, k):
        n = self.n_group
        pairs = [(r * n + g, (r ^ 1) * n + (g ^ k)) for r in range(self.n_replica) for g in range(n)]
        return lax.ppermute(a, ("replica", "group"), pairs)

    def gather_near(self, mine, other, relay=True):
        got = {(0, 0): mine, (0, 1): other}
        for k in (1, 2) if relay and self.n_group == 4 else range(1, self.n_group):
            got[k, 0] = self.across(mine, k)
        return got

    def gather_far(self, got):
        got = dict(got)
        if (self.n_group - 1, 0) not in got:
            got[3, 0] = self.across(got[2, 0], 1)
            got[3, 1] = self.across_swap(got[1, 0], 2)
        for k in range(1, self.n_group):
            if (k, 1) not in got:
                got[k, 1] = self.core_swap(got[k, 0])
        return [got[key] for key in sorted(got)]

    def parts(self, pairs):
        def part(k):
            at = lambda a: lax.dynamic_index_in_dim(a, self.group ^ k, 0, keepdims=False).astype(F32)
            return jnp.concatenate([at(keep) + at(got) for got, keep in pairs], axis=0)

        return [part(0)] + [part(k).astype(BF) for k in range(1, self.n_group)]

    def group_send(self, parts):
        return parts[0], [self.across(parts[k], k) for k in range(1, self.n_group)]

    def add(self, own, moved):
        for m in moved:
            own = own + m.astype(F32)
        return own

    def along(self, a, k):
        return lax.ppermute(a, "replica", [(i, i ^ (2 * k)) for i in range(self.n_replica)])

    def z_scatter(self, s):
        shares = s.reshape(self.n_z, s.shape[0] // self.n_z, s.shape[1])
        share = lambda k: lax.dynamic_index_in_dim(shares, (self.replica // 2) ^ k, 0, keepdims=False)
        return share(0), [self.along(share(k).astype(BF), k) for k in range(1, self.n_z)]

    def z_gather(self, own, moved):
        t = self.add(own, moved).astype(BF)
        return [t] + [self.along(t, k) for k in range(1, self.n_z)]

    def z_join(self, shares):
        z = self.replica // 2
        return jnp.concatenate([lax.select_n(z, *[shares[j ^ i] for i in range(self.n_z)]) for j in range(self.n_z)], axis=0)


def on_device(tokens, cotangent, lengths, dealing, offsets, attn_gain, qkv_weight, out_weight,
              mlp_gain, in_weight, down_weight, *, n_replica, n_group):
    net = Net(n_replica, n_group)
    x, gy = tokens[0], cotangent[0]
    tok, width = x.shape
    ff = in_weight.shape[1] // 2
    sz = Sizes(tok, width)
    pairs = width // LANES
    pg = 3
    tie = lax.optimization_barrier

    where = jnp.stack([net.replica, net.group]).astype(jnp.int32)
    near = net.gather_near(*pack_qkv_call(where, qkv_weight, jnp.stack([attn_gain, mlp_gain])), relay=False)
    packs = pack_call(where, out_weight, in_weight, down_weight)
    scal, qf, kf, cos, sin = plan_call(sz, n_replica, n_group, where, lengths)
    near, packs, scal = tie((near, packs, scal))

    x_l = net.shift(x[tok - HALO :], 1)
    x_r = net.shift(x[:HALO], -1)
    qkv_pieces = net.gather_far(near)
    packs, qkv_pieces, x_l, x_r = tie((packs, qkv_pieces, x_l, x_r))

    near = net.gather_near(*packs)
    qkv, kt, vt, n1t, gains = qkv_call(sz, scal, x_l, x, x_r, qkv_pieces, cos, sin)
    near, vt = tie((near, vt))
    mlp_pieces = net.gather_far(near)
    o, ot, lse = fwd_call(sz, scal, qkv, vt, qf, kf, pg)
    out, mt, gu, n2t, gh2b, go, to_left, to_right, dlt = mid_call(sz, scal, mlp_pieces, x, o, gy, gains, lse, ff)

    go_l = net.shift(to_right, 1)
    go_r = net.shift(to_left, -1)
    keep_i, send_i = in_grad_call(sz, scal, n2t, gu, n_group)
    used = half_of(width // n_group) + half_of(ff // n_group)
    rows = used + -(keep_i.shape[1] + used) % (8 * net.n_z)
    keep_d, send_d = down_out_call(sz, scal, mt, gy, ot, gh2b, n_group, rows)
    send_d, go_l, go_r = tie((send_d, go_l, go_r))
    mlp_parts = net.parts([(net.core_swap(send_i), keep_i), (net.core_swap(send_d), keep_d)])

    def attn_grad(at, dep):
        return bwd_call(sz, dep, qkv, kt, qf, kf, go_l, go, go_r, lse, dlt, cos, sin, n1t, pg, at, n_group)

    scal, mlp_parts = tie((scal, mlp_parts))
    grad0, keep0, send0 = attn_grad(0, scal)
    mlp = net.group_send(mlp_parts)
    keep0, send0, mlp = tie((keep0, send0, mlp))
    parts0 = net.parts([(net.core_swap(send0), keep0)])
    mlp = net.z_scatter(net.add(*mlp))
    scal, parts0 = tie((scal, parts0))
    sum0 = net.group_send(parts0)
    grad1, keep1, send1 = attn_grad(1, scal)
    sum0, mlp, scal, send1 = tie((sum0, mlp, scal, send1))

    got1 = net.core_swap(send1)
    mlp = net.z_gather(*mlp)
    got1, sum0 = tie((got1, sum0))
    parts1, scal = tie((net.parts([(got1, keep1)]), scal))
    sum1 = net.group_send(parts1)
    gx = gx_call(sz, scal, qkv_pieces, [grad0, grad1], x, gh2b, gains)
    sum1, sum0, gx = tie((sum1, sum0, gx))
    sum1, mlp = tie((sum1, mlp))

    qkv_sum = net.z_scatter(jnp.concatenate([net.add(*sum0), net.add(*sum1)], axis=0))
    mlp_sum = net.z_join(mlp)
    qkv_sum, mlp_sum = tie((qkv_sum, mlp_sum))
    sib_mlp = net.core_swap(mlp_sum)
    qkv_sum = net.z_gather(*qkv_sum)

    shard, shard_d = width // n_group, ff // n_group
    d_in, d_down, d_out, d_g2 = end_call(mlp_end_kernel, "mlp_gradients_end", sz, scal, [mlp_sum, sib_mlp], in_weight, mlp_gain,
                                         [in_weight.shape, (shard_d, width), (shard, width)])
    qkv_sum, d_in = tie((qkv_sum, d_in))
    qkv_sum = net.z_join(qkv_sum)
    d_qkv, d_g1 = end_call(qkv_end_kernel, "qkv_gradient_end", sz, scal, [qkv_sum, net.core_swap(qkv_sum)], qkv_weight,
                           attn_gain, [qkv_weight.shape])
    return (out[None], gx[None], d_g1[0], d_qkv, d_out, d_g2[0], d_in, d_down)


def solution(mesh):
    body = functools.partial(on_device, n_replica=mesh.shape["replica"], n_group=mesh.shape["group"])
    return jax.shard_map(
        body,
        mesh=mesh,
        in_specs=(
            P("group", "replica", None),
            P("group", "replica", None),
            P("group", None),
            P("group", None),
            P("group", None, None),
            P("group"),
            P("group", None),
            P("group", None),
            P("group"),
            P("group", None),
            P("group", None),
        ),
        out_specs=(
            P("group", "replica", None),
            P("group", "replica", None),
            P("group"),
            P("group", None),
            P("group", None),
            P("group"),
            P("group", None),
            P("group", None),
        ),
        check_vma=False,
    )
```

```python
import functools
import math

import jax
import jax.numpy as jnp
from jax import lax
from jax.experimental import pallas as pl
from jax.experimental.pallas import tpu as pltpu
from jax.sharding import PartitionSpec as P

HEADS = 12
HEAD_DIM = 64
LANES = 128
HALO = 768
RB = 256
QB = 128
KB = 256
STAT = 16
EPS = 1e-05
BIG = -1e30
ROPE_BASE = 160000.0
LOG2E = 1.4426950408889634
LN2 = 0.6931471805599453
BF = jnp.bfloat16
F32 = jnp.float32


def nt(a, b):
    return lax.dot_general(a, b, (((1,), (1,)), ((), ())), preferred_element_type=F32)


def nn(a, b):
    return lax.dot_general(a, b, (((1,), (0,)), ((), ())), preferred_element_type=F32)


def tn(a, b):
    return lax.dot_general(a, b, (((0,), (0,)), ((), ())), preferred_element_type=F32)


def partner(x):
    lane = lax.broadcasted_iota(jnp.int32, x.shape, 1) % HEAD_DIM
    return jnp.where(lane < HEAD_DIM // 2, pltpu.roll(x, 96, 1), pltpu.roll(x, 32, 1))


def half_of(rows):
    return -(-rows // 32) * 16


def row_of(place, rows):
    return pl.multiple_of((place // 2) * rows + (place % 2) * (rows - half_of(rows)), 16)


def params(mib, **kw):
    return pltpu.CompilerParams(vmem_limit_bytes=mib * 1024 * 1024, **kw)


class Sizes:
    def __init__(self, tok, width):
        self.tok, self.width = tok, width
        self.ext = tok + 2 * HALO + RB
        self.n_qb = (tok + 2 * HALO) // QB
        self.own_qb, self.own_lo = tok // QB, HALO // QB
        self.own_hi = self.own_lo + self.own_qb
        tiles = -(-(QB + 2 * HALO + QB) // KB)
        self.cap_f = self.own_qb * tiles + 2
        halo_tiles = -(-(HALO + QB) // KB)
        caps = [self.own_qb * -(-tok // KB) + 2, 2 * self.own_qb * -(-HALO // KB) + 2, 2 * self.own_lo * halo_tiles + 2]
        self.k_lo, self.k_n = 0, self.n_qb
        self.q_lo, self.q_hi = 2 * self.n_qb, 2 * self.n_qb + 1
        self.need_lo, self.need_hi, self.full_hi = (2 * self.n_qb + i for i in (2, 3, 4))
        self.blocks = self.ext // RB
        self.fwd_q = self.full_hi + 1
        self.fwd_k, self.fwd_n = self.fwd_q + self.cap_f, self.fwd_q + 2 * self.cap_f
        self.lists, at = [], self.fwd_n + 1
        for cap in caps:
            self.lists.append((at, at + cap, at + 2 * cap))
            at += 2 * cap + 1
        self.places = at


def plan_kernel(sz, n_replica, n_group, where, lengths, scal, qf, kf, cos, sin, starts, k_end, seg_buf, pos_buf):
    n_seq = lengths.shape[1]
    total = n_replica * sz.tok
    replica, group = where[0], where[1]
    base = replica * sz.tok - HALO
    at = jnp.int32(0)
    for j in range(n_seq):
        starts[j] = at
        at = at + lengths[0, j]
    starts[n_seq] = at

    def first_of(g):
        f = jnp.int32(0)
        for j in range(n_seq):
            f = jnp.where(g >= starts[j], starts[j], f)
        return f

    def last_of(g):
        f = jnp.int32(total)
        for j in range(n_seq):
            f = jnp.where(g >= starts[j], starts[j + 1], f)
        return f

    own_a, own_b = base + HALO, base + HALO + sz.tok - 1
    first_a, last_a = first_of(own_a) - base, last_of(own_a) - base
    first_b, last_b = first_of(own_b) - base, last_of(own_b) - base
    q_lo, q_hi = first_a // QB, (last_b + QB - 1) // QB
    scal[sz.q_lo], scal[sz.q_hi] = q_lo, q_hi

    def block(i, _):
        e = i * QB
        left, right = i < sz.own_lo, i >= sz.own_hi
        lo = jnp.where(left, HALO, jnp.where(right, first_b, first_of(base + e) - base)) // QB
        hi = jnp.where(left, last_a, jnp.where(right, HALO + sz.tok, last_of(base + e + QB - 1) - base))
        n = (hi - lo * QB + (KB - 1)) // KB
        scal[sz.k_lo + i] = lo
        scal[sz.k_n + i] = jnp.where((i >= q_lo) & (i < q_hi), n, 0)
        k_end[i] = (hi + QB - 1) // QB
        return 0

    lax.fori_loop(0, sz.n_qb, block, 0)
    scal[sz.need_lo], scal[sz.need_hi] = first_a // RB, (last_b + KB - 1 + RB - 1) // RB
    scal[sz.full_hi] = (last_b + RB - 1) // RB

    step = KB // QB

    def emit(where, c, q, lo, n):
        def one(t, c):
            scal[where[0] + c] = q
            scal[where[1] + c] = lo + t * step
            return c + 1

        return lax.fori_loop(0, n, one, c)

    def close(where, c, q):
        scal[where[2]] = c
        for extra in range(2):
            scal[where[0] + c + extra] = q
            scal[where[1] + c + extra] = jnp.int32(sz.own_lo)

    fwd = (sz.fwd_q, sz.fwd_k, sz.fwd_n)
    both, far, back = sz.lists

    def own_block(i, counts):
        c_f, c_a, c_b = counts
        lo, end = scal[sz.k_lo + i], k_end[i]
        c_f = emit(fwd, c_f, i - sz.own_lo, lo, scal[sz.k_n + i])
        n = (jnp.maximum(sz.own_lo - lo, 0) + step - 1) // step
        c_b = emit(far, c_b, i, sz.own_lo - n * step, n)
        lo = jnp.maximum(lo, sz.own_lo)
        n = (jnp.minimum(end, sz.own_hi) - lo + step - 1) // step
        c_a = emit(both, c_a, i, lo, n)
        lo = lo + n * step
        c_b = emit(far, c_b, i, lo, (jnp.maximum(end - lo, 0) + step - 1) // step)
        return c_f, c_a, c_b

    zero = jnp.int32(0)
    c_f, c_a, c_b = lax.fori_loop(sz.own_lo, sz.own_hi, own_block, (zero, zero, zero))

    def halo_block(i, c):
        return emit(back, c, i, scal[sz.k_lo + i], scal[sz.k_n + i])

    c_c = lax.fori_loop(sz.own_hi, sz.n_qb, halo_block, lax.fori_loop(0, sz.own_lo, halo_block, zero))
    close(fwd, c_f, jnp.int32(sz.own_qb))
    for where_to, c in zip(sz.lists, (c_a, c_b, c_c)):
        close(where_to, c, jnp.int32(sz.own_lo))
    core = replica % 2
    for k in range(n_group):
        for h in range(2):
            scal[sz.places + 2 * k + h] = 2 * (group ^ k) + (core ^ h)

    half = HEAD_DIM // 2
    blocks = sz.ext // QB
    g = base + QB * lax.broadcasted_iota(jnp.int32, (blocks, QB), 0) + lax.broadcasted_iota(jnp.int32, (blocks, QB), 1)
    seg = jnp.full((blocks, QB), -1, jnp.int32)
    first = jnp.zeros((blocks, QB), jnp.int32)
    for j in range(n_seq):
        hit = g >= starts[j]
        seg = jnp.where(hit, j, seg)
        first = jnp.where(hit, starts[j], first)
    seg_buf[...] = jnp.where(g >= total, n_seq, seg) & 15
    pos_buf[...] = jnp.maximum(g - first, 0).astype(F32)
    freq = jnp.exp(lax.broadcasted_iota(jnp.int32, (half, QB), 0).astype(F32) * (-2.0 / HEAD_DIM * math.log(ROPE_BASE)))

    def rows(b, _):
        r0 = pl.multiple_of(b * QB, QB)
        hot = (seg_buf[pl.ds(b, 1), :] == lax.broadcasted_iota(jnp.int32, (LANES, QB), 0)).astype(F32).T
        qf[pl.ds(r0, QB), :] = (hot * BIG).astype(BF)
        lane = lax.broadcasted_iota(jnp.int32, (QB, LANES), 1)
        kf[pl.ds(r0, QB), :] = jnp.where(lane < 16, 1.0 - hot, 0.0).astype(BF)
        ang = freq * pos_buf[pl.ds(b, 1), :]
        co, si = jnp.cos(ang), jnp.sin(ang)
        cos[pl.ds(r0, QB), :] = jnp.concatenate([co] * 4, axis=0).T
        sin[pl.ds(r0, QB), :] = jnp.concatenate([-si, si, -si, si], axis=0).T
        return 0

    lax.fori_loop(0, blocks, rows, 0)


def plan_call(sz, n_replica, n_group, where, lengths):
    sh = jax.ShapeDtypeStruct
    smem = pl.BlockSpec(memory_space=pltpu.SMEM)
    vmem = pl.BlockSpec(memory_space=pltpu.VMEM)
    n_seq = lengths.shape[1]
    return pl.pallas_call(
        functools.partial(plan_kernel, sz, n_replica, n_group),
        in_specs=[smem, smem],
        out_specs=[smem] + [vmem] * 4,
        out_shape=[sh((sz.places + 2 * n_group,), jnp.int32)] + [sh((sz.ext, LANES), BF)] * 2 + [sh((sz.ext, LANES), F32)] * 2,
        scratch_shapes=[pltpu.SMEM((n_seq + 1,), jnp.int32), pltpu.SMEM((sz.n_qb,), jnp.int32), pltpu.VMEM((sz.ext // QB, QB), jnp.int32), pltpu.VMEM((sz.ext // QB, QB), F32)],
        compiler_params=params(60),
        cost_estimate=pl.CostEstimate(flops=10_000_000_000, bytes_accessed=5_000_000, transcendentals=0),
        name="plan",
    )(where, lengths)


def pack_kernel(where, wo, wi, wd, mine, other):
    width = wo.shape[1]
    n_cols = wi.shape[1] // width

    def put(dst, h):
        at = 0
        for ref, col in [(wo, 0)] + [(wi, j) for j in range(n_cols)] + [(wd, 0)]:
            n = half_of(ref.shape[0])
            lo = h * (ref.shape[0] - n)
            dst[at : at + n, :] = ref[lo : lo + n, width * col : width * col + width].astype(BF)
            at += n

    @pl.when(where[0] % 2 == 0)
    def _():
        put(mine, 0)
        put(other, 1)

    @pl.when(where[0] % 2 != 0)
    def _():
        put(mine, 1)
        put(other, 0)


def pack_qkv_kernel(where, w, gains, mine, other):
    width = w.shape[1]
    shard = w.shape[0]
    half = half_of(shard)
    side = jnp.concatenate([gains[...], jnp.zeros((LANES - gains.shape[0], shard), F32)], axis=0).T.astype(BF)

    def put(dst, h):
        lo = h * (shard - half)
        dst[:, :width] = w[lo : lo + half, :].astype(BF)
        dst[:, width:] = side[lo : lo + half, :]

    @pl.when(where[0] % 2 == 0)
    def _():
        put(mine, 0)
        put(other, 1)

    @pl.when(where[0] % 2 != 0)
    def _():
        put(mine, 1)
        put(other, 0)


def pack_qkv_call(where, w, gains):
    vmem = pl.BlockSpec(memory_space=pltpu.VMEM)
    out = jax.ShapeDtypeStruct((half_of(w.shape[0]), w.shape[1] + LANES), BF)
    return pl.pallas_call(
        pack_qkv_kernel,
        in_specs=[pl.BlockSpec(memory_space=pltpu.SMEM), vmem, vmem],
        out_specs=[vmem, vmem],
        out_shape=[out, out],
        compiler_params=params(60),
        cost_estimate=pl.CostEstimate(flops=2_000_000_000, bytes_accessed=3_000_000, transcendentals=0),
        name="pack_projection",
    )(where, w, gains)


def pack_call(where, wo, wi, wd):
    vmem = pl.BlockSpec(memory_space=pltpu.VMEM)
    rows = half_of(wo.shape[0]) * (1 + wi.shape[1] // wo.shape[1]) + half_of(wd.shape[0])
    out = jax.ShapeDtypeStruct((rows, wo.shape[1]), BF)
    return pl.pallas_call(
        pack_kernel,
        in_specs=[pl.BlockSpec(memory_space=pltpu.SMEM), vmem, vmem, vmem],
        out_specs=[vmem, vmem],
        out_shape=[out, out],
        compiler_params=params(60),
        cost_estimate=pl.CostEstimate(flops=3_000_000_000, bytes_accessed=5_000_000, transcendentals=0),
        name="pack_weights",
    )(where, wo, wi, wd)


def fetch_qkv(place, pieces, w, sem):
    copies = []
    shard = w.shape[0] // (len(pieces) // 2)
    for t, piece in enumerate(pieces):
        copies.append(pltpu.make_async_copy(piece.at[:, 0 : w.shape[1]], w.at[pl.ds(row_of(place(t), shard), piece.shape[0]), :], sem.at[t]))
    return copies


def qkv_kernel(sz, n_pieces, scal, xl, xc, xr, *rest):
    pieces, (cos, sin, qkv, n1t, gains, w, sem) = rest[:n_pieces], rest[n_pieces:]
    i = pl.program_id(0)
    left_b, own_b = HALO // RB, sz.tok // RB
    own = (i >= left_b) & (i < left_b + own_b)

    @pl.when(i == 0)
    def _():
        copies = fetch_qkv(lambda t: scal[sz.places + t], pieces, w, sem)
        for c in copies:
            c.start()
        for c in copies:
            c.wait()
        side = w[:, 3 * sz.width :].astype(F32)
        for b in range(sz.width // LANES):
            gains[:, lanes_of(b)] = side[LANES * b : LANES * b + LANES, :].T[:8, :]

    @pl.when((i >= scal[sz.full_hi]) & (i < scal[sz.need_hi]))
    def _():
        qkv[...] = jnp.zeros_like(qkv)

    @pl.when((i >= scal[sz.need_lo]) & (i < scal[sz.full_hi]))
    def _():
        x = jnp.where(i < left_b, xl[...], jnp.where(i < left_b + own_b, xc[...], xr[...])).astype(F32)
        mean = jnp.mean(x, axis=-1, keepdims=True)
        cen = x - mean
        var = jnp.mean(cen * cen, axis=-1, keepdims=True)
        n1 = (cen * lax.rsqrt(var + EPS) * gains[0:1, :]).astype(BF)

        @pl.when(own)
        def _():
            n1t[...] = n1.T

        width = n1.shape[1]
        co, si = cos[...], sin[...]
        sc = HEAD_DIM ** -0.5 * LOG2E
        cq, sq = co * sc, si * sc
        for c in range(3 * width // 256):
            a = nn(n1, w[:, 256 * c : 256 * c + 256])
            part = 256 * c // width
            if part < 2:
                cc, ss = (cq, sq) if part == 0 else (co, si)
                halves = []
                for h in range(2):
                    b = a[:, 128 * h : 128 * h + 128]
                    halves.append((b * cc + partner(b) * ss).astype(BF))
                r = jnp.concatenate(halves, axis=1)
            else:
                r = a.astype(BF)
            qkv[:, 256 * c : 256 * c + 256] = r


def qkv_call(sz, scal, xl, xc, xr, pieces, cos, sin):
    tok, width, ext = sz.tok, sz.width, sz.ext
    own_b, lb = tok // RB, HALO // RB
    clampi = lambda lo, n: (lambda i, s: (jnp.clip(i - lo, 0, n - 1), 0))
    used = lambda i, s: jnp.clip(i, s[sz.need_lo], s[sz.need_hi] - 1)
    row = lambda i, s: (used(i, s), 0)
    fix = lambda i, s: (0, 0)
    sh = jax.ShapeDtypeStruct
    return pl.pallas_call(
        functools.partial(qkv_kernel, sz, len(pieces)),
        grid_spec=pltpu.PrefetchScalarGridSpec(
            num_scalar_prefetch=1,
            grid=(sz.blocks,),
            in_specs=[
                pl.BlockSpec((RB, width), clampi(0, lb)),
                pl.BlockSpec((RB, width), clampi(lb, own_b)),
                pl.BlockSpec((RB, width), clampi(lb + own_b, lb)),
                *[pl.BlockSpec(memory_space=pl.ANY)] * len(pieces),
                pl.BlockSpec((RB, LANES), row),
                pl.BlockSpec((RB, LANES), row),
            ],
            out_specs=[
                pl.BlockSpec((RB, 3 * width), row),
                pl.BlockSpec((width, RB), lambda i, s: (0, jnp.clip(i - lb, 0, own_b - 1))),
                pl.BlockSpec((8, width), fix),
            ],
            scratch_shapes=[pltpu.VMEM((width, 3 * width + LANES), BF), pltpu.SemaphoreType.DMA((len(pieces),))],
        ),
        out_shape=[sh((ext, 3 * width), BF), sh((width, tok), BF),
                   sh((8, width), F32)],
        compiler_params=params(60, dimension_semantics=("arbitrary",)),
        cost_estimate=pl.CostEstimate(flops=14_000_000_000, bytes_accessed=30_000_000, transcendentals=0),
        name="qkv",
    )(scal, xl, xc, xr, *pieces, cos, sin)


def split_heads(x):
    low = lax.broadcasted_iota(jnp.int32, x.shape, 1) < HEAD_DIM
    zero = jnp.zeros_like(x)
    return jnp.concatenate([jnp.where(low, x, zero), jnp.where(low, zero, x)], axis=0)


def lanes_of(p):
    return slice(LANES * p, LANES * p + LANES)


def fwd_kernel(sz, pg, scal, q, k, v, qf, kf, out, out_t, lse, q2, buf_a, buf_b, acc, tops):
    nq = sz.own_qb
    ones = jnp.ones((16, KB), BF)
    for qi in range(nq):
        r0 = HALO + qi * QB
        fq = qf[r0 : r0 + QB, :]
        f2 = jnp.concatenate([fq, fq], axis=0)
        for p in range(pg):
            q2[qi, p] = jnp.concatenate([split_heads(q[r0 : r0 + QB, lanes_of(p)]), f2], axis=1)

    def zero(i, _):
        for p in range(pg):
            acc[i, p] = jnp.zeros((LANES + 16, 2 * QB), F32)
            tops[i, p] = jnp.zeros((8, 2 * QB), F32)
        return 0

    lax.fori_loop(0, nq + 1, zero, 0)

    def scores(qi, k0, p, fk):
        return nt(jnp.concatenate([k[pl.ds(k0, KB), lanes_of(p)], fk], axis=1), q2[qi, p])

    def mixed(k0, p, probs):
        va = jnp.concatenate([v[pl.ds(k0, KB), lanes_of(p)].T, ones], axis=0)
        return nn(va, probs.astype(BF))

    def tile(i):
        return scal[sz.fwd_q + i], pl.multiple_of(scal[sz.fwd_k + i] * QB, QB)

    def score_tile(i, buf):
        qi, k0 = tile(i)
        qi = jnp.minimum(qi, nq - 1)
        fk = kf[pl.ds(k0, KB), :]
        for p in range(pg):
            buf[p] = scores(qi, k0, p, fk)

    def mix_tile(i, buf):
        qi, k0 = tile(i)
        for p in range(pg):
            acc[qi, p] += mixed(k0, p, jnp.exp2(buf[p]))

    score_tile(0, buf_a)

    def body(j, _):
        score_tile(2 * j + 1, buf_b)
        mix_tile(2 * j, buf_a)
        score_tile(2 * j + 2, buf_a)
        mix_tile(2 * j + 1, buf_b)
        return 0

    lax.fori_loop(0, (scal[sz.fwd_n] + 1) // 2, body, 0)

    low = high = acc[0, 0, LANES : LANES + 1, :]
    for qi in range(nq):
        for p in range(pg):
            total = acc[qi, p, LANES : LANES + 1, :]
            low, high = jnp.minimum(low, total), jnp.maximum(high, total)
    safe = (jnp.min(low) > 2.0 ** -60) & (jnp.max(high) < 2.0 ** 100)

    @pl.when(jnp.logical_not(safe))
    def _():
        lax.fori_loop(0, nq, zero, 0)

        def per_q(qi, _):
            lo, n = scal[sz.k_lo + sz.own_lo + qi], scal[sz.k_n + sz.own_lo + qi]
            for p in range(pg):
                def top(t, m):
                    k0 = pl.multiple_of(lo * QB + t * KB, QB)
                    return jnp.maximum(m, jnp.max(scores(qi, k0, p, kf[pl.ds(k0, KB), :]), axis=0, keepdims=True))

                m = lax.fori_loop(0, n, top, jnp.full((1, 2 * QB), BIG, F32))
                tops[qi, p] = jnp.broadcast_to(m, (8, 2 * QB))

                def add(t, _):
                    k0 = pl.multiple_of(lo * QB + t * KB, QB)
                    acc[qi, p] += mixed(k0, p, jnp.exp2(scores(qi, k0, p, kf[pl.ds(k0, KB), :]) - m))
                    return 0

                lax.fori_loop(0, n, add, 0)
            return 0

        lax.fori_loop(0, nq, per_q, 0)

    def finish(qi, _):
        o0 = pl.multiple_of(qi * QB, QB)
        for p in range(pg):
            a = acc[qi, p]
            total = a[LANES : LANES + 1, :]
            inv = 1.0 / total
            o_t = jnp.concatenate([a[:HEAD_DIM, :QB] * inv[:, :QB], a[HEAD_DIM:LANES, QB:] * inv[:, QB:]], axis=0).astype(BF)
            out_t[lanes_of(p), pl.ds(o0, QB)] = o_t
            out[pl.ds(o0, QB), lanes_of(p)] = o_t.T
            st = tops[qi, p, 0:1, :] + jnp.log2(total)
            lse[p, 0:1, pl.ds(o0, QB)] = st[:, :QB]
            lse[p, 1:2, pl.ds(o0, QB)] = st[:, QB:]
        return 0

    lax.fori_loop(0, nq, finish, 0)


def fwd_call(sz, scal, qkv, qf, kf, pg):
    ext, tok, width = sz.ext, sz.tok, sz.width
    pairs = width // LANES
    steps = pairs // pg
    wide = LANES * pg
    col = lambda off: (lambda i, s: (0, off + i))
    fix = lambda i, s: (0, 0)
    sh = jax.ShapeDtypeStruct
    return pl.pallas_call(
        functools.partial(fwd_kernel, sz, pg),
        grid_spec=pltpu.PrefetchScalarGridSpec(
            num_scalar_prefetch=1,
            grid=(steps,),
            in_specs=[
                pl.BlockSpec((ext, wide), col(0)),
                pl.BlockSpec((ext, wide), col(steps)),
                pl.BlockSpec((ext, wide), col(2 * steps)),
                pl.BlockSpec((ext, LANES), fix),
                pl.BlockSpec((ext, LANES), fix),
            ],
            out_specs=[
                pl.BlockSpec((tok, wide), col(0)),
                pl.BlockSpec((wide, tok), lambda i, s: (i, 0)),
                pl.BlockSpec((pg, 2, tok), lambda i, s: (i, 0, 0)),
            ],
            scratch_shapes=[
                pltpu.VMEM((sz.own_qb, pg, 2 * QB, 2 * LANES), BF),
                pltpu.VMEM((pg, KB, 2 * QB), F32),
                pltpu.VMEM((pg, KB, 2 * QB), F32),
                pltpu.VMEM((sz.own_qb + 1, pg, LANES + 16, 2 * QB), F32),
                pltpu.VMEM((sz.own_qb + 1, pg, 8, 2 * QB), F32),
            ],
        ),
        out_shape=[sh((tok, width), BF), sh((width, tok), BF), sh((pairs, 2, tok), F32)],
        compiler_params=params(60, dimension_semantics=("arbitrary",)),
        cost_estimate=pl.CostEstimate(flops=30_000_000_000, bytes_accessed=15_000_000, transcendentals=0),
        name="attn_forward",
    )(scal, qkv, qkv, qkv, qf, kf)


def fetch_mlp(place, pieces, wo, wi, wd, sem, width):
    copies = [], [], []
    shards = len(pieces) // 2
    half, half_d = half_of(wo.shape[0] // shards), half_of(wd.shape[0] // shards)
    t_cols = wi.shape[1] // width
    for t, piece in enumerate(pieces):
        row0 = row_of(place(t), wo.shape[0] // shards)
        row_d = row_of(place(t), wd.shape[0] // shards)
        copies[0].append(pltpu.make_async_copy(piece.at[0:half, :], wo.at[pl.ds(row0, half), :], sem.at[t, 0]))
        for j in range(t_cols):
            copies[1].append(pltpu.make_async_copy(
                piece.at[half * (j + 1) : half * (j + 2), :],
                wi.at[pl.ds(row0, half), width * j : width * j + width], sem.at[t, j + 1]))
        lo = half * (t_cols + 1)
        copies[2].append(pltpu.make_async_copy(piece.at[lo : lo + half_d, :], wd.at[pl.ds(row_d, half_d), :], sem.at[t, t_cols + 1]))
    return copies


def three_parts(v):
    high = v.astype(BF).astype(F32)
    middle = (v - high).astype(BF).astype(F32)
    return high, middle, v - high - middle


def mid_kernel(sz, n_pieces, scal, *refs):
    pieces, refs = refs[:n_pieces], refs[n_pieces:]
    wo, wi, wd, sem = refs[-4:]
    step = pl.program_id(0)

    @pl.when(step == 0)
    def _():
        copies = fetch_mlp(lambda t: scal[sz.places + t], pieces, wo, wi, wd, sem, wo.shape[1])
        for group in copies:
            for c in group:
                c.start()

        def wait(which):
            for c in copies[which]:
                c.wait()

        mid_body(sz, wait, wo, wi, wd, *refs[:-4])

    @pl.when(step != 0)
    def _():
        mid_body(sz, lambda which: None, wo, wi, wd, *refs[:-4])


def mid_body(sz, wait, wo, wi, wd, x, o, gy, g2, ind, lse, out, mt_o, gu_o, n2t_o, gh2b_o, go_o, left_o, right_o, dlt):
    ff = wd.shape[0]
    wait(0)
    h2 = x[...].astype(F32) + nn(o[...], wo[...])
    mean = jnp.mean(h2, axis=-1, keepdims=True)
    cen = h2 - mean
    r2 = lax.rsqrt(jnp.mean(cen * cen, axis=-1, keepdims=True) + EPS)
    nh = cen * r2
    g = g2[1:2, :]
    n2 = (nh * g).astype(BF)
    n2t_o[...] = n2.T
    gyb = gy[...]
    hidden = []
    wait(1)
    wait(2)
    step = 384
    for c in range(ff // step):
        lo = c * step
        a = nn(n2, wi[:, lo : lo + step])
        b = nn(n2, wi[:, ff + lo : ff + lo + step])
        gm = nt(gyb, wd[lo : lo + step, :])
        half = 0.5 * (1.0 + lax.erf(a * (2.0 ** -0.5)))
        gel = a * half
        mm = (gel * b).astype(BF)
        mt_o[lo : lo + step, :] = mm.T
        hidden.append(mm)
        dgel = half + a * (jnp.exp(-0.5 * a * a) * (1.0 / math.sqrt(2.0 * math.pi)))
        ga = (gm * b * dgel).astype(BF)
        gb = (gm * gel).astype(BF)
        gu_o[:, lo : lo + step] = ga
        gu_o[:, ff + lo : ff + lo + step] = gb
    out[...] = (h2 + nn(jnp.concatenate(hidden, axis=1), wd[...])).astype(BF)
    gn2 = nt(gu_o[...], wi[...])

    t = gn2 * g
    gh2 = gyb.astype(F32) + r2 * (t - jnp.mean(t, axis=-1, keepdims=True) - nh * jnp.mean(t * nh, axis=-1, keepdims=True))
    gb16 = gh2.astype(BF)
    gh2b_o[...] = gb16
    go = nt(gb16, wo[...]).astype(BF)
    go_o[...] = go
    prod = go.astype(F32) * o[...].astype(F32)
    hi = prod.astype(BF)
    lo_part = (prod - hi.astype(F32)).astype(BF)
    sums = nt(ind[...], hi) + nt(ind[...], lo_part)
    for p in range(dlt.shape[0]):
        dlt[p] = sums[2 * p : 2 * p + 2, :]
    heads = lse.shape[0] * 2
    top = jnp.concatenate([lse[p] for p in range(lse.shape[0])] + [jnp.zeros((STAT - heads, sums.shape[1]), F32)], axis=0)
    rows = [part for v in (top, sums) for part in three_parts(v)]
    rows.append(jnp.zeros((LANES - 6 * STAT, sums.shape[1]), F32))
    width = go.shape[1]
    stats = jnp.concatenate(rows, axis=0).T.astype(BF)
    step = pl.program_id(0)

    @pl.when(step < HALO // RB)
    def _():
        left_o[:, :width] = go
        left_o[:, width:] = stats

    @pl.when(step >= (sz.tok - HALO) // RB)
    def _():
        right_o[:, :width] = go
        right_o[:, width:] = stats


def mid_call(sz, scal, pieces, x, o, gy, g2, lse, ff):
    tok, width = x.shape
    heads = jnp.arange(16, dtype=jnp.int32)
    ind = (heads[:, None] == (jnp.arange(width, dtype=jnp.int32) // HEAD_DIM)[None, :]).astype(BF)
    row = lambda i, s: (i, 0)
    fix = lambda i, s: (0, 0)
    rs = lambda n: pl.BlockSpec((RB, n), row)
    cs = lambda n: pl.BlockSpec((n, RB), lambda i, s: (0, i))
    fs = lambda a: pl.BlockSpec(a.shape, fix)
    sh = jax.ShapeDtypeStruct
    n = len(pieces)
    stat = pl.BlockSpec((width // LANES, 2, RB), lambda i, s: (0, 0, i))
    halo = lambda lo: pl.BlockSpec((RB, width + LANES), lambda i, s: (jnp.clip(i - lo, 0, HALO // RB - 1), 0))
    halos = [halo(0), halo((tok - HALO) // RB)]
    return pl.pallas_call(
        functools.partial(mid_kernel, sz, n),
        grid_spec=pltpu.PrefetchScalarGridSpec(
            num_scalar_prefetch=1,
            grid=(tok // RB,),
            in_specs=[*[pl.BlockSpec(memory_space=pl.ANY)] * n, rs(width), rs(width), rs(width), fs(g2), fs(ind), stat],
            out_specs=[rs(width), cs(ff), rs(2 * ff), cs(width), rs(width), rs(width), *halos, stat],
            scratch_shapes=[pltpu.VMEM((width, width), BF), pltpu.VMEM((width, 2 * ff), BF), pltpu.VMEM((ff, width), BF),
                            pltpu.SemaphoreType.DMA((n, 2 * ff // width + 2))],
        ),
        out_shape=[sh((tok, width), BF), sh((ff, tok), BF), sh((tok, 2 * ff), BF), sh((width, tok), BF),
                   sh((tok, width), BF), sh((tok, width), BF),
                   sh((HALO, width + LANES), BF), sh((HALO, width + LANES), BF),
                   sh((width // LANES, 2, tok), F32)],
        compiler_params=params(60, dimension_semantics=("arbitrary",)),
        cost_estimate=pl.CostEstimate(flops=13_000_000_000 * 2, bytes_accessed=30_000_000, transcendentals=0),
        name="middle",
    )(scal, *pieces, x, o, gy, g2, ind, lse)


def put_halves(core, keep, send, rows0, values, n_group):
    rows = values.shape[0] // n_group
    half = half_of(rows)

    def store(first, second):
        for g in range(n_group):
            lo, hi = rows * g, rows * (g + 1)
            first[g, pl.ds(rows0, half), :] = values[lo : lo + half, :]
            second[g, pl.ds(rows0, half), :] = values[hi - half : hi, :]

    @pl.when(core == 0)
    def _():
        store(keep, send)

    @pl.when(core != 0)
    def _():
        store(send, keep)


def put_halves(core, keep, send, rows0, values, n_group):
    rows = values.shape[0] // n_group
    half = half_of(rows)

    def store(first, second):
        for g in range(n_group):
            lo, hi = rows * g, rows * (g + 1)
            first[g, pl.ds(rows0, half), :] = values[lo : lo + half, :]
            second[g, pl.ds(rows0, half), :] = values[hi - half : hi, :]

    @pl.when(core == 0)
    def _():
        store(keep, send)

    @pl.when(core != 0)
    def _():
        store(send, keep)


def in_grad_kernel(n_group, at, scal, n2t, gu, keep, send):
    half = half_of(n2t.shape[0] // n_group)
    row0 = pl.multiple_of(pl.program_id(0) * half, 16)
    put_halves(scal[at] % 2, keep, send, row0, nn(n2t[...], gu[...]).astype(BF), n_group)


def in_grad_call(sz, scal, n2t, gu, n_group):
    width, tok = n2t.shape
    n_cols = gu.shape[1] // width
    rows = n_cols * half_of(width // n_group)
    out = jax.ShapeDtypeStruct((n_group, rows, width), BF)
    return pl.pallas_call(
        functools.partial(in_grad_kernel, n_group, sz.places),
        grid_spec=pltpu.PrefetchScalarGridSpec(
            num_scalar_prefetch=1,
            grid=(n_cols,),
            in_specs=[pl.BlockSpec((width, tok), lambda j, s: (0, 0)), pl.BlockSpec((tok, width), lambda j, s: (0, j))],
            out_specs=[pl.BlockSpec((n_group, rows, width), lambda j, s: (0, 0, 0))] * 2,
        ),
        out_shape=[out, out],
        compiler_params=params(60, dimension_semantics=("arbitrary",)),
        cost_estimate=pl.CostEstimate(flops=8_000_000_000, bytes_accessed=10_000_000, transcendentals=0),
        name="in_weight_gradient",
    )(scal, n2t, gu)


def down_out_kernel(n_group, at, scal, mt, gy, ot_h, gh_h, keep, send, ot, gh, sem):
    copies = [pltpu.make_async_copy(ot_h, ot, sem.at[0]), pltpu.make_async_copy(gh_h, gh, sem.at[1])]
    for c in copies:
        c.start()
    put_halves(scal[at] % 2, keep, send, 0, nn(mt[...], gy[...]).astype(BF), n_group)
    for c in copies:
        c.wait()
    used = half_of(mt.shape[0] // n_group) + half_of(ot.shape[0] // n_group)
    put_halves(scal[at] % 2, keep, send, half_of(mt.shape[0] // n_group), nn(ot[...], gh[...]).astype(BF), n_group)
    if used < keep.shape[1]:
        for ref in (keep, send):
            ref[:, used:, :] = jnp.zeros((n_group, keep.shape[1] - used, keep.shape[2]), BF)


def down_out_call(sz, scal, mt, gy, ot, gh, n_group, rows):
    width, tok = ot.shape
    ff = mt.shape[0]
    out = jax.ShapeDtypeStruct((n_group, rows, width), BF)
    anyspec = pl.BlockSpec(memory_space=pl.ANY)
    fix = lambda j, s: (0, 0)
    return pl.pallas_call(
        functools.partial(down_out_kernel, n_group, sz.places),
        grid_spec=pltpu.PrefetchScalarGridSpec(
            num_scalar_prefetch=1,
            grid=(1,),
            in_specs=[pl.BlockSpec((ff, tok), fix), pl.BlockSpec((tok, width), fix), anyspec, anyspec],
            out_specs=[pl.BlockSpec((n_group, rows, width), lambda j, s: (0, 0, 0))] * 2,
            scratch_shapes=[pltpu.VMEM((width, tok), BF), pltpu.VMEM((tok, width), BF), pltpu.SemaphoreType.DMA((2,))],
        ),
        out_shape=[out, out],
        compiler_params=params(60, dimension_semantics=("arbitrary",)),
        cost_estimate=pl.CostEstimate(flops=100_000_000, bytes_accessed=100_000, transcendentals=0),
        name="down_out_weight_gradients",
    )(scal, mt, gy, ot, gh)


def bwd_kernel(sz, pg, at, n_group, scal, qkv_h, qf_h, kf_h, gl_h, gc_h, gr_h, cos_h, sin_h, n1t_h,
               lse_c, dlt_c, grad_h, keep_h, send_h, grad, keep, send,
               q, k, v, qf, kf, go, halo_st, cos, sin, n1t, q2, g2, gka, gva, gqa, st, s_a, p_a, s_b, p_b, sem, out_sem):
    n_qb, tok, width = sz.n_qb, sz.tok, sz.width
    wide = LANES * pg
    q_lo, q_hi = scal[sz.q_lo], scal[sz.q_hi]
    ext = q.shape[0]
    cols = lambda part: pl.ds(part * width + at * wide, wide)
    near, left = pl.ds(HALO, tok + QB), pl.ds(0, HALO)
    right, own = pl.ds(HALO + tok + QB, ext - HALO - tok - QB), pl.ds(HALO, tok)

    def rows(seg):
        return [(qkv_h.at[seg, cols(part)], dst.at[seg, :]) for part, dst in ((0, q), (1, k), (2, v))]

    near_q, *near_rest = rows(near)
    first = [(gc_h.at[:, cols(0)], go.at[own, :]), (qf_h, qf), near_q, (kf_h, kf), *near_rest]
    second = [*rows(left), *rows(right), (gl_h.at[:, cols(0)], go.at[left, :]),
              (gr_h.at[:, cols(0)], go.at[pl.ds(HALO + tok, HALO), :]),
              (gl_h.at[:, pl.ds(width, LANES)], halo_st.at[0]), (gr_h.at[:, pl.ds(width, LANES)], halo_st.at[1])]
    third = [(cos_h.at[own, :], cos), (sin_h.at[own, :], sin), (n1t_h, n1t)]
    copies = [pltpu.make_async_copy(a, b, sem.at[t]) for t, (a, b) in enumerate(first + second + third)]
    n_first, n_second = len(first), len(first) + len(second)
    for c in copies:
        c.start()

    for row, part in ((0, lse_c), (1, dlt_c)):
        for p in range(pg):
            for b in range(sz.own_qb):
                for h in range(2):
                    st[sz.own_lo + b, p, row : row + 1, QB * h : QB * h + QB] = part[p, h : h + 1, QB * b : QB * b + QB]

    def halo_stats(side, first):
        def one(i, _):
            rows_t = halo_st[side, pl.ds(pl.multiple_of((i - first) * QB, QB), QB), :].astype(F32).T
            for p in range(pg):
                for h in range(2):
                    for row in range(2):
                        lo = 3 * STAT * row + 2 * (pg * at + p) + h
                        parts = [rows_t[lo + STAT * t : lo + STAT * t + 1, :] for t in range(3)]
                        st[i, p, row : row + 1, QB * h : QB * h + QB] = parts[0] + parts[1] + parts[2]
            return 0

        return one

    for c in copies[:3]:
        c.wait()

    def prep(i, _):
        r0 = pl.multiple_of(i * QB, QB)
        fq = qf[pl.ds(r0, QB), :]
        f2 = jnp.concatenate([fq, fq], axis=0)
        for p in range(pg):
            q2[i, p] = jnp.concatenate([split_heads(q[pl.ds(r0, QB), lanes_of(p)]), f2], axis=1)
            g2[i, p] = split_heads(go[pl.ds(r0, QB), lanes_of(p)])
            gqa[i, p] = jnp.zeros((LANES, 2 * QB), F32)
            gka[p, pl.ds(r0, QB), :] = jnp.zeros((QB, LANES), F32)
            gva[p, pl.ds(r0, QB), :] = jnp.zeros((QB, LANES), F32)
        return 0

    lax.fori_loop(sz.own_lo, sz.own_hi, prep, 0)
    for c in copies[3:n_first]:
        c.wait()

    def run(where, for_keys, for_queries):
        def tile(i):
            return scal[where[0] + i], pl.multiple_of(scal[where[1] + i] * QB, QB)

        def score_tile(i, s_buf, p_buf):
            qi, k0 = tile(i)
            fk = kf[pl.ds(k0, KB), :]
            for p in range(pg):
                s_buf[p] = nt(jnp.concatenate([k[pl.ds(k0, KB), lanes_of(p)], fk], axis=1), q2[qi, p])
                p_buf[p] = nt(v[pl.ds(k0, KB), lanes_of(p)], g2[qi, p])

        def grad_tile(i, s_buf, p_buf):
            qi, k0 = tile(i)
            dead = jnp.where(i < scal[where[2]], 0.0, 1e38).astype(F32)
            for p in range(pg):
                pr = jnp.exp2(s_buf[p] - (st[qi, p, 0:1, :] + dead))
                ds = (pr * (p_buf[p] - st[qi, p, 1:2, :])).astype(BF)
                if for_keys:
                    gva[p, pl.ds(k0, KB), :] += nn(pr.astype(BF), g2[qi, p])
                    gka[p, pl.ds(k0, KB), :] += nn(ds, q2[qi, p, :, :LANES])
                if for_queries:
                    gqa[qi, p] += tn(k[pl.ds(k0, KB), lanes_of(p)], ds)

        @pl.when(scal[where[2]] > 0)
        def _():
            score_tile(0, s_a, p_a)

            def body(j, _):
                score_tile(2 * j + 1, s_b, p_b)
                grad_tile(2 * j, s_a, p_a)
                score_tile(2 * j + 2, s_a, p_a)
                grad_tile(2 * j + 1, s_b, p_b)
                return 0

            lax.fori_loop(0, (scal[where[2]] + 1) // 2, body, 0)

    run(sz.lists[0], True, True)
    for c in copies[n_first:n_second]:
        c.wait()
    lax.fori_loop(q_lo, sz.own_lo, prep, 0)
    lax.fori_loop(sz.own_hi, q_hi, prep, 0)
    lax.fori_loop(q_lo, sz.own_lo, halo_stats(0, 0), 0)
    lax.fori_loop(sz.own_hi, q_hi, halo_stats(1, sz.own_hi), 0)
    run(sz.lists[1], False, True)
    run(sz.lists[2], True, False)
    copies[n_second].wait()
    copies[n_second + 1].wait()

    sc = HEAD_DIM ** -0.5

    def finish(i, _):
        o0 = pl.multiple_of(i * QB, QB)
        r0 = pl.multiple_of(HALO + i * QB, QB)
        co, si = cos[pl.ds(o0, QB), :], sin[pl.ds(o0, QB), :]
        for p in range(pg):
            a = gqa[sz.own_lo + i, p]
            gt = jnp.concatenate([a[:HEAD_DIM, :QB], a[HEAD_DIM:, QB:]], axis=0).T * sc
            grad[pl.ds(o0, QB), LANES * p : LANES * p + LANES] = (gt * co - partner(gt) * si).astype(BF)
            b = gka[p, pl.ds(r0, QB), :] * LN2
            lo = wide + LANES * p
            grad[pl.ds(o0, QB), lo : lo + LANES] = (b * co - partner(b) * si).astype(BF)
            lo = 2 * wide + LANES * p
            grad[pl.ds(o0, QB), lo : lo + LANES] = gva[p, pl.ds(r0, QB), :].astype(BF)
        return 0

    lax.fori_loop(0, sz.own_qb, finish, 0)
    leaving = [pltpu.make_async_copy(grad, grad_h, out_sem.at[0])]
    leaving[0].start()
    copies[n_second + 2].wait()
    for part in range(3):
        lanes = slice(wide * part, wide * part + wide)
        values = nn(n1t[...], grad[:, lanes]).astype(BF)
        put_halves(scal[sz.places] % 2, keep.at[:, :, lanes], send.at[:, :, lanes], 0, values, n_group)
        for t, (a, b) in enumerate(((keep, keep_h), (send, send_h))):
            leaving.append(pltpu.make_async_copy(a.at[:, :, lanes], b.at[:, :, lanes], out_sem.at[1 + 2 * part + t]))
            leaving[-1].start()
    for c in leaving:
        c.wait()


def bwd_call(sz, scal, qkv, qf, kf, gl, gc, gr, lse, dlt, cos, sin, n1t, pg, at, n_group):
    ext, tok, width, n_qb = sz.ext, sz.tok, sz.width, sz.n_qb
    wide = LANES * pg
    half = half_of(width // n_group)
    spec = lambda shape, *idx: pl.BlockSpec(shape, lambda i, s: idx)
    sh = jax.ShapeDtypeStruct
    outs = [(tok, 3 * wide), (n_group, half, 3 * wide), (n_group, half, 3 * wide)]
    return pl.pallas_call(
        functools.partial(bwd_kernel, sz, pg, at, n_group),
        grid_spec=pltpu.PrefetchScalarGridSpec(
            num_scalar_prefetch=1,
            grid=(1,),
            in_specs=[pl.BlockSpec(memory_space=pl.ANY)] * 9
            + [spec((pg, 2, tok), at, 0, 0), spec((pg, 2, tok), at, 0, 0)],
            out_specs=[pl.BlockSpec(memory_space=pl.ANY)] * 3,
            scratch_shapes=[
                *[pltpu.VMEM(o, BF) for o in outs],
                *[pltpu.VMEM((ext, wide), BF)] * 3,
                pltpu.VMEM((ext, LANES), BF),
                pltpu.VMEM((ext, LANES), BF),
                pltpu.VMEM((tok + 2 * HALO, wide), BF),
                pltpu.VMEM((2, HALO, LANES), BF),
                pltpu.VMEM((tok, LANES), F32),
                pltpu.VMEM((tok, LANES), F32),
                pltpu.VMEM((width, tok), BF),
                pltpu.VMEM((n_qb, pg, 2 * QB, 2 * LANES), BF),
                pltpu.VMEM((n_qb, pg, 2 * QB, LANES), BF),
                pltpu.VMEM((pg, ext, LANES), F32),
                pltpu.VMEM((pg, ext, LANES), F32),
                pltpu.VMEM((n_qb, pg, LANES, 2 * QB), F32),
                pltpu.VMEM((n_qb, pg, 8, 2 * QB), F32),
                *[pltpu.VMEM((pg, KB, 2 * QB), F32)] * 4,
                pltpu.SemaphoreType.DMA((19,)),
                pltpu.SemaphoreType.DMA((7,)),
            ],
        ),
        out_shape=[sh(o, BF) for o in outs],
        compiler_params=params(60, dimension_semantics=("arbitrary",)),
        cost_estimate=pl.CostEstimate(flops=35_000_000_000, bytes_accessed=20_000_000, transcendentals=0),
        name="attn_backward",
    )(scal, qkv, qf, kf, gl, gc, gr, cos, sin, n1t, lse, dlt)


def gx_kernel(n_pieces, n_grads, at, scal, *refs):
    pieces, grads = refs[:n_pieces], refs[n_pieces : n_pieces + n_grads]
    x, gh2, g1, out, w, sem = refs[n_pieces + n_grads :]

    @pl.when(pl.program_id(0) == 0)
    def _():
        copies = fetch_qkv(lambda t: scal[at + t], pieces, w, sem)
        for c in copies:
            c.start()
        for c in copies:
            c.wait()

    width = x.shape[1]
    gn = None
    wide = grads[0].shape[1] // 3
    for part in range(3):
        lhs = jnp.concatenate([grad[:, wide * part : wide * part + wide] for grad in grads], axis=1)
        term = nt(lhs, w[:, width * part : width * part + width])
        gn = term if gn is None else gn + term
    xf = x[...].astype(F32)
    mean = jnp.mean(xf, axis=-1, keepdims=True)
    cen = xf - mean
    r1 = lax.rsqrt(jnp.mean(cen * cen, axis=-1, keepdims=True) + EPS)
    nh = cen * r1

    t = gn * g1[0:1, :]
    gx = gh2[...].astype(F32) + r1 * (t - jnp.mean(t, axis=-1, keepdims=True) - nh * jnp.mean(t * nh, axis=-1, keepdims=True))
    out[...] = gx.astype(BF)


def gx_call(sz, scal, pieces, grads, x, gh2, g1):
    tok, width = x.shape
    row = lambda i, s: (i, 0)
    fix = lambda i, s: (0, 0)
    rs = pl.BlockSpec((RB, width), row)
    n = len(pieces)
    return pl.pallas_call(
        functools.partial(gx_kernel, n, len(grads), sz.places),
        grid_spec=pltpu.PrefetchScalarGridSpec(
            num_scalar_prefetch=1,
            grid=(tok // RB,),
            in_specs=[*[pl.BlockSpec(memory_space=pl.ANY)] * n,
                      *[pl.BlockSpec((RB, g.shape[1]), row) for g in grads],
                      rs, rs, pl.BlockSpec(g1.shape, fix)],
            out_specs=rs,
            scratch_shapes=[pltpu.VMEM((width, 3 * width), BF), pltpu.SemaphoreType.DMA((n,))],
        ),
        out_shape=jax.ShapeDtypeStruct((tok, width), BF),
        compiler_params=params(60, dimension_semantics=("arbitrary",)),
        cost_estimate=pl.CostEstimate(flops=4_000_000_000, bytes_accessed=15_000_000, transcendentals=0),
        name="input_gradient",
    )(scal, *pieces, *grads, x, gh2, g1)


def gain_row(w, grad, gain):
    low = lambda v: v.astype(BF).astype(F32)
    total = jnp.sum(low(w) * grad, axis=1, keepdims=True)
    return jnp.broadcast_to(total, (total.shape[0], LANES)).T[0:1, :] / low(gain)


def in_core_order(core, mine, other, use):
    @pl.when(core == 0)
    def _():
        use(mine, other)

    @pl.when(core != 0)
    def _():
        use(other, mine)


def qkv_end_kernel(at, scal, t, s, w, gain, out, g_out):
    shard = w.shape[0]
    half = half_of(shard)
    wide = t.shape[1] // 3
    calls = t.shape[0] // half

    def use(first, second):
        for ref, lo in ((first, 0), (second, shard - half)):
            for j in range(calls):
                for part in range(3):
                    c = wide * (calls * part + j)
                    out[lo : lo + half, c : c + wide] = ref[half * j : half * j + half, wide * part : wide * part + wide].astype(F32)

    in_core_order(scal[at] % 2, t, s, use)
    g_out[...] = gain_row(w[...], out[...], gain[...])


def mlp_end_kernel(at, scal, t, s, w, gain, d_in, d_down, d_out, g_out):
    shard, shard_d, width = w.shape[0], d_down.shape[0], d_out.shape[1]
    half, half_d = half_of(shard), half_of(shard_d)
    n_cols = w.shape[1] // width

    def use(first, second):
        for ref, h in ((first, 0), (second, 1)):
            lo, lo_d = h * (shard - half), h * (shard_d - half_d)
            for j in range(n_cols):
                d_in[lo : lo + half, width * j : width * j + width] = ref[half * j : half * j + half, :].astype(F32)
            at_d = half * n_cols
            d_down[lo_d : lo_d + half_d, :] = ref[at_d : at_d + half_d, :].astype(F32)
            d_out[lo : lo + half, :] = ref[at_d + half_d : at_d + half_d + half, :].astype(F32)

    in_core_order(scal[at] % 2, t, s, use)
    g_out[...] = gain_row(w[...], d_in[...], gain[...])


def end_call(kernel, name, sz, scal, arrays, w, gain, shapes):
    smem = pl.BlockSpec(memory_space=pltpu.SMEM)
    vmem = pl.BlockSpec(memory_space=pltpu.VMEM)
    outs = [*shapes, (1, w.shape[0])]
    return pl.pallas_call(
        functools.partial(kernel, sz.places),
        in_specs=[smem] + [vmem] * (len(arrays) + 2),
        out_specs=[vmem] * len(outs),
        out_shape=[jax.ShapeDtypeStruct(o, F32) for o in outs],
        compiler_params=params(60),
        cost_estimate=pl.CostEstimate(flops=3_000_000_000, bytes_accessed=5_000_000, transcendentals=0),
        name=name,
    )(scal, *arrays, w, gain.reshape(1, -1))


class Net:
    def __init__(self, n_replica, n_group):
        self.n_replica, self.n_group, self.n_z = n_replica, n_group, n_replica // 2
        self.replica, self.group = lax.axis_index("replica"), lax.axis_index("group")
        self.core = self.replica & 1

    def shift(self, a, step):
        pairs = [(i, i + step) for i in range(self.n_replica) if 0 <= i + step < self.n_replica]
        return lax.ppermute(a, "replica", pairs)

    def core_swap(self, a):
        return lax.ppermute(a, "replica", [(i, i ^ 1) for i in range(self.n_replica)])

    def across(self, a, k):
        return lax.ppermute(a, "group", [(i, i ^ k) for i in range(self.n_group)])

    def across_swap(self, a, k):
        n = self.n_group
        pairs = [(r * n + g, (r ^ 1) * n + (g ^ k)) for r in range(self.n_replica) for g in range(n)]
        return lax.ppermute(a, ("replica", "group"), pairs)

    def gather_near(self, mine, other, relay=True):
        got = {(0, 0): mine, (0, 1): other}
        for k in (1, 2) if relay and self.n_group == 4 else range(1, self.n_group):
            got[k, 0] = self.across(mine, k)
        return got

    def gather_far(self, got):
        got = dict(got)
        if (self.n_group - 1, 0) not in got:
            got[3, 0] = self.across(got[2, 0], 1)
            got[3, 1] = self.across_swap(got[1, 0], 2)
        for k in range(1, self.n_group):
            if (k, 1) not in got:
                got[k, 1] = self.core_swap(got[k, 0])
        return [got[key] for key in sorted(got)]

    def parts(self, pairs):
        def part(k):
            at = lambda a: lax.dynamic_index_in_dim(a, self.group ^ k, 0, keepdims=False).astype(F32)
            return jnp.concatenate([at(keep) + at(got) for got, keep in pairs], axis=0)

        return [part(0)] + [part(k).astype(BF) for k in range(1, self.n_group)]

    def group_send(self, parts):
        return parts[0], [self.across(parts[k], k) for k in range(1, self.n_group)]

    def add(self, own, moved):
        for m in moved:
            own = own + m.astype(F32)
        return own

    def along(self, a, k):
        return lax.ppermute(a, "replica", [(i, i ^ (2 * k)) for i in range(self.n_replica)])

    def z_scatter(self, s):
        shares = s.reshape(self.n_z, s.shape[0] // self.n_z, s.shape[1])
        share = lambda k: lax.dynamic_index_in_dim(shares, (self.replica // 2) ^ k, 0, keepdims=False)
        return share(0), [self.along(share(k).astype(BF), k) for k in range(1, self.n_z)]

    def z_gather(self, own, moved):
        t = self.add(own, moved).astype(BF)
        return [t] + [self.along(t, k) for k in range(1, self.n_z)]

    def z_join(self, shares):
        z = self.replica // 2
        return jnp.concatenate([lax.select_n(z, *[shares[j ^ i] for i in range(self.n_z)]) for j in range(self.n_z)], axis=0)


def on_device(tokens, cotangent, lengths, dealing, offsets, attn_gain, qkv_weight, out_weight,
              mlp_gain, in_weight, down_weight, *, n_replica, n_group):
    net = Net(n_replica, n_group)
    x, gy = tokens[0], cotangent[0]
    tok, width = x.shape
    ff = in_weight.shape[1] // 2
    sz = Sizes(tok, width)
    pairs = width // LANES
    pg = 3
    tie = lax.optimization_barrier

    where = jnp.stack([net.replica, net.group]).astype(jnp.int32)
    near = net.gather_near(*pack_qkv_call(where, qkv_weight, jnp.stack([attn_gain, mlp_gain])), relay=False)
    packs = pack_call(where, out_weight, in_weight, down_weight)
    scal, qf, kf, cos, sin = plan_call(sz, n_replica, n_group, where, lengths)
    near, packs, scal = tie((near, packs, scal))

    x_l = net.shift(x[tok - HALO :], 1)
    x_r = net.shift(x[:HALO], -1)
    qkv_pieces = net.gather_far(near)
    packs, qkv_pieces, x_l, x_r = tie((packs, qkv_pieces, x_l, x_r))

    near = net.gather_near(*packs)
    qkv, n1t, gains = qkv_call(sz, scal, x_l, x, x_r, qkv_pieces, cos, sin)
    near, qkv = tie((near, qkv))
    mlp_pieces = net.gather_far(near)
    o, ot, lse = fwd_call(sz, scal, qkv, qf, kf, pg)
    out, mt, gu, n2t, gh2b, go, to_left, to_right, dlt = mid_call(sz, scal, mlp_pieces, x, o, gy, gains, lse, ff)

    go_l = net.shift(to_right, 1)
    go_r = net.shift(to_left, -1)
    keep_i, send_i = in_grad_call(sz, scal, n2t, gu, n_group)
    used = half_of(width // n_group) + half_of(ff // n_group)
    rows = used + -(keep_i.shape[1] + used) % (8 * net.n_z)
    keep_d, send_d = down_out_call(sz, scal, mt, gy, ot, gh2b, n_group, rows)
    send_d, go_l, go_r = tie((send_d, go_l, go_r))
    mlp_parts = net.parts([(net.core_swap(send_i), keep_i), (net.core_swap(send_d), keep_d)])

    def attn_grad(at, dep):
        return bwd_call(sz, dep, qkv, qf, kf, go_l, go, go_r, lse, dlt, cos, sin, n1t, pg, at, n_group)

    scal, mlp_parts = tie((scal, mlp_parts))
    grad0, keep0, send0 = attn_grad(0, scal)
    mlp = net.group_send(mlp_parts)
    keep0, send0, mlp = tie((keep0, send0, mlp))
    parts0 = net.parts([(net.core_swap(send0), keep0)])
    mlp = net.z_scatter(net.add(*mlp))
    scal, parts0 = tie((scal, parts0))
    sum0 = net.group_send(parts0)
    grad1, keep1, send1 = attn_grad(1, scal)
    sum0, mlp, scal, send1 = tie((sum0, mlp, scal, send1))

    got1 = net.core_swap(send1)
    mlp = net.z_gather(*mlp)
    got1, sum0 = tie((got1, sum0))
    parts1, scal = tie((net.parts([(got1, keep1)]), scal))
    sum1 = net.group_send(parts1)
    gx = gx_call(sz, scal, qkv_pieces, [grad0, grad1], x, gh2b, gains)
    sum1, sum0, gx = tie((sum1, sum0, gx))
    sum1, mlp = tie((sum1, mlp))

    qkv_sum = net.z_scatter(jnp.concatenate([net.add(*sum0), net.add(*sum1)], axis=0))
    mlp_sum = net.z_join(mlp)
    qkv_sum, mlp_sum = tie((qkv_sum, mlp_sum))
    sib_mlp = net.core_swap(mlp_sum)
    qkv_sum = net.z_gather(*qkv_sum)

    shard, shard_d = width // n_group, ff // n_group
    d_in, d_down, d_out, d_g2 = end_call(mlp_end_kernel, "mlp_gradients_end", sz, scal, [mlp_sum, sib_mlp], in_weight, mlp_gain,
                                         [in_weight.shape, (shard_d, width), (shard, width)])
    qkv_sum, d_in = tie((qkv_sum, d_in))
    qkv_sum = net.z_join(qkv_sum)
    d_qkv, d_g1 = end_call(qkv_end_kernel, "qkv_gradient_end", sz, scal, [qkv_sum, net.core_swap(qkv_sum)], qkv_weight,
                           attn_gain, [qkv_weight.shape])
    return (out[None], gx[None], d_g1[0], d_qkv, d_out, d_g2[0], d_in, d_down)


def solution(mesh):
    body = functools.partial(on_device, n_replica=mesh.shape["replica"], n_group=mesh.shape["group"])
    return jax.shard_map(
        body,
        mesh=mesh,
        in_specs=(
            P("group", "replica", None),
            P("group", "replica", None),
            P("group", None),
            P("group", None),
            P("group", None, None),
            P("group"),
            P("group", None),
            P("group", None),
            P("group"),
            P("group", None),
            P("group", None),
        ),
        out_specs=(
            P("group", "replica", None),
            P("group", "replica", None),
            P("group"),
            P("group", None),
            P("group", None),
            P("group"),
            P("group", None),
            P("group", None),
        ),
        check_vma=False,
    )
```

```python
import functools
import math

import jax
import jax.numpy as jnp
from jax import lax
from jax.experimental import pallas as pl
from jax.experimental.pallas import tpu as pltpu
from jax.sharding import PartitionSpec as P

HEADS = 12
HEAD_DIM = 64
LANES = 128
HALO = 768
RB = 256
QB = 128
KB = 256
STAT = 16
EPS = 1e-05
BIG = -1e30
ROPE_BASE = 160000.0
LOG2E = 1.4426950408889634
LN2 = 0.6931471805599453
BF = jnp.bfloat16
F32 = jnp.float32


def nt(a, b):
    return lax.dot_general(a, b, (((1,), (1,)), ((), ())), preferred_element_type=F32)


def nn(a, b):
    return lax.dot_general(a, b, (((1,), (0,)), ((), ())), preferred_element_type=F32)


def tn(a, b):
    return lax.dot_general(a, b, (((0,), (0,)), ((), ())), preferred_element_type=F32)


def partner(x):
    lane = lax.broadcasted_iota(jnp.int32, x.shape, 1) % HEAD_DIM
    return jnp.where(lane < HEAD_DIM // 2, pltpu.roll(x, 96, 1), pltpu.roll(x, 32, 1))


def half_of(rows):
    return -(-rows // 32) * 16


def row_of(place, rows):
    return pl.multiple_of((place // 2) * rows + (place % 2) * (rows - half_of(rows)), 16)


def params(mib, **kw):
    return pltpu.CompilerParams(vmem_limit_bytes=mib * 1024 * 1024, **kw)


class Sizes:
    def __init__(self, tok, width):
        self.tok, self.width = tok, width
        self.ext = tok + 2 * HALO + RB
        self.n_qb = (tok + 2 * HALO) // QB
        self.own_qb, self.own_lo = tok // QB, HALO // QB
        self.own_hi = self.own_lo + self.own_qb
        tiles = -(-(QB + 2 * HALO + QB) // KB)
        self.cap_f = self.own_qb * tiles + 2
        halo_tiles = -(-(HALO + QB) // KB)
        caps = [self.own_qb * -(-tok // KB) + 2, 2 * self.own_qb * -(-HALO // KB) + 2, 2 * self.own_lo * halo_tiles + 2]
        self.k_lo, self.k_n = 0, self.n_qb
        self.q_lo, self.q_hi = 2 * self.n_qb, 2 * self.n_qb + 1
        self.need_lo, self.need_hi, self.full_hi = (2 * self.n_qb + i for i in (2, 3, 4))
        self.blocks = self.ext // RB
        self.fwd_q = self.full_hi + 1
        self.fwd_k, self.fwd_n = self.fwd_q + self.cap_f, self.fwd_q + 2 * self.cap_f
        self.lists, at = [], self.fwd_n + 1
        for cap in caps:
            self.lists.append((at, at + cap, at + 2 * cap))
            at += 2 * cap + 1
        self.places = at


def plan_kernel(sz, n_replica, n_group, where, lengths, scal, qf, kf, cos, sin, starts, k_end, seg_buf, pos_buf):
    n_seq = lengths.shape[1]
    total = n_replica * sz.tok
    replica, group = where[0], where[1]
    base = replica * sz.tok - HALO
    at = jnp.int32(0)
    for j in range(n_seq):
        starts[j] = at
        at = at + lengths[0, j]
    starts[n_seq] = at

    def first_of(g):
        f = jnp.int32(0)
        for j in range(n_seq):
            f = jnp.where(g >= starts[j], starts[j], f)
        return f

    def last_of(g):
        f = jnp.int32(total)
        for j in range(n_seq):
            f = jnp.where(g >= starts[j], starts[j + 1], f)
        return f

    own_a, own_b = base + HALO, base + HALO + sz.tok - 1
    first_a, last_a = first_of(own_a) - base, last_of(own_a) - base
    first_b, last_b = first_of(own_b) - base, last_of(own_b) - base
    q_lo, q_hi = first_a // QB, (last_b + QB - 1) // QB
    scal[sz.q_lo], scal[sz.q_hi] = q_lo, q_hi

    def block(i, _):
        e = i * QB
        left, right = i < sz.own_lo, i >= sz.own_hi
        lo = jnp.where(left, HALO, jnp.where(right, first_b, first_of(base + e) - base)) // QB
        hi = jnp.where(left, last_a, jnp.where(right, HALO + sz.tok, last_of(base + e + QB - 1) - base))
        n = (hi - lo * QB + (KB - 1)) // KB
        scal[sz.k_lo + i] = lo
        scal[sz.k_n + i] = jnp.where((i >= q_lo) & (i < q_hi), n, 0)
        k_end[i] = (hi + QB - 1) // QB
        return 0

    lax.fori_loop(0, sz.n_qb, block, 0)
    scal[sz.need_lo], scal[sz.need_hi] = first_a // RB, (last_b + KB - 1 + RB - 1) // RB
    scal[sz.full_hi] = (last_b + RB - 1) // RB

    step = KB // QB

    def emit(where, c, q, lo, n):
        def one(t, c):
            scal[where[0] + c] = q
            scal[where[1] + c] = lo + t * step
            return c + 1

        return lax.fori_loop(0, n, one, c)

    def close(where, c, q):
        scal[where[2]] = c
        for extra in range(2):
            scal[where[0] + c + extra] = q
            scal[where[1] + c + extra] = jnp.int32(sz.own_lo)

    fwd = (sz.fwd_q, sz.fwd_k, sz.fwd_n)
    both, far, back = sz.lists

    def own_block(i, counts):
        c_f, c_a, c_b = counts
        lo, end = scal[sz.k_lo + i], k_end[i]
        c_f = emit(fwd, c_f, i - sz.own_lo, lo, scal[sz.k_n + i])
        n = (jnp.maximum(sz.own_lo - lo, 0) + step - 1) // step
        c_b = emit(far, c_b, i, sz.own_lo - n * step, n)
        lo = jnp.maximum(lo, sz.own_lo)
        n = (jnp.minimum(end, sz.own_hi) - lo + step - 1) // step
        c_a = emit(both, c_a, i, lo, n)
        lo = lo + n * step
        c_b = emit(far, c_b, i, lo, (jnp.maximum(end - lo, 0) + step - 1) // step)
        return c_f, c_a, c_b

    zero = jnp.int32(0)
    c_f, c_a, c_b = lax.fori_loop(sz.own_lo, sz.own_hi, own_block, (zero, zero, zero))

    def halo_block(i, c):
        return emit(back, c, i, scal[sz.k_lo + i], scal[sz.k_n + i])

    c_c = lax.fori_loop(sz.own_hi, sz.n_qb, halo_block, lax.fori_loop(0, sz.own_lo, halo_block, zero))
    close(fwd, c_f, jnp.int32(sz.own_qb))
    for where_to, c in zip(sz.lists, (c_a, c_b, c_c)):
        close(where_to, c, jnp.int32(sz.own_lo))
    core = replica % 2
    for k in range(n_group):
        for h in range(2):
            scal[sz.places + 2 * k + h] = 2 * (group ^ k) + (core ^ h)

    half = HEAD_DIM // 2
    blocks = sz.ext // QB
    g = base + QB * lax.broadcasted_iota(jnp.int32, (blocks, QB), 0) + lax.broadcasted_iota(jnp.int32, (blocks, QB), 1)
    seg = jnp.full((blocks, QB), -1, jnp.int32)
    first = jnp.zeros((blocks, QB), jnp.int32)
    for j in range(n_seq):
        hit = g >= starts[j]
        seg = jnp.where(hit, j, seg)
        first = jnp.where(hit, starts[j], first)
    seg_buf[...] = jnp.where(g >= total, n_seq, seg) & 15
    pos_buf[...] = jnp.maximum(g - first, 0).astype(F32)
    freq = jnp.exp(lax.broadcasted_iota(jnp.int32, (half, QB), 0).astype(F32) * (-2.0 / HEAD_DIM * math.log(ROPE_BASE)))

    def rows(b, _):
        r0 = pl.multiple_of(b * QB, QB)
        hot = (seg_buf[pl.ds(b, 1), :] == lax.broadcasted_iota(jnp.int32, (LANES, QB), 0)).astype(F32).T
        qf[pl.ds(r0, QB), :] = (hot * BIG).astype(BF)
        lane = lax.broadcasted_iota(jnp.int32, (QB, LANES), 1)
        kf[pl.ds(r0, QB), :] = jnp.where(lane < 16, 1.0 - hot, 0.0).astype(BF)
        ang = freq * pos_buf[pl.ds(b, 1), :]
        co, si = jnp.cos(ang), jnp.sin(ang)
        cos[pl.ds(r0, QB), :] = jnp.concatenate([co] * 4, axis=0).T
        sin[pl.ds(r0, QB), :] = jnp.concatenate([-si, si, -si, si], axis=0).T
        return 0

    per = RB // QB
    lax.fori_loop(scal[sz.need_lo] * per, jnp.minimum(scal[sz.need_hi] * per, blocks), rows, 0)


def plan_call(sz, n_replica, n_group, where, lengths):
    sh = jax.ShapeDtypeStruct
    smem = pl.BlockSpec(memory_space=pltpu.SMEM)
    vmem = pl.BlockSpec(memory_space=pltpu.VMEM)
    n_seq = lengths.shape[1]
    return pl.pallas_call(
        functools.partial(plan_kernel, sz, n_replica, n_group),
        in_specs=[smem, smem],
        out_specs=[smem] + [vmem] * 4,
        out_shape=[sh((sz.places + 2 * n_group,), jnp.int32)] + [sh((sz.ext, LANES), BF)] * 2 + [sh((sz.ext, LANES), F32)] * 2,
        scratch_shapes=[pltpu.SMEM((n_seq + 1,), jnp.int32), pltpu.SMEM((sz.n_qb,), jnp.int32), pltpu.VMEM((sz.ext // QB, QB), jnp.int32), pltpu.VMEM((sz.ext // QB, QB), F32)],
        compiler_params=params(60),
        cost_estimate=pl.CostEstimate(flops=10_000_000_000, bytes_accessed=5_000_000, transcendentals=0),
        name="plan",
    )(where, lengths)


def pack_kernel(where, wo, wi, wd, mine, other):
    width = wo.shape[1]
    n_cols = wi.shape[1] // width

    def put(dst, h):
        at = 0
        for ref, col in [(wo, 0)] + [(wi, j) for j in range(n_cols)] + [(wd, 0)]:
            n = half_of(ref.shape[0])
            lo = h * (ref.shape[0] - n)
            dst[at : at + n, :] = ref[lo : lo + n, width * col : width * col + width].astype(BF)
            at += n

    @pl.when(where[0] % 2 == 0)
    def _():
        put(mine, 0)
        put(other, 1)

    @pl.when(where[0] % 2 != 0)
    def _():
        put(mine, 1)
        put(other, 0)


def pack_qkv_kernel(where, w, gain_a, gain_b, mine, other):
    width = w.shape[1]
    shard = w.shape[0]
    half = half_of(shard)
    side = jnp.concatenate([gain_a[...], gain_b[...], jnp.zeros((LANES - 2, shard), F32)], axis=0).T.astype(BF)

    def put(dst, h):
        lo = h * (shard - half)
        dst[:, :width] = w[lo : lo + half, :].astype(BF)
        dst[:, width:] = side[lo : lo + half, :]

    @pl.when(where[0] % 2 == 0)
    def _():
        put(mine, 0)
        put(other, 1)

    @pl.when(where[0] % 2 != 0)
    def _():
        put(mine, 1)
        put(other, 0)


def pack_qkv_call(where, w, gain_a, gain_b):
    vmem = pl.BlockSpec(memory_space=pltpu.VMEM)
    out = jax.ShapeDtypeStruct((half_of(w.shape[0]), w.shape[1] + LANES), BF)
    return pl.pallas_call(
        pack_qkv_kernel,
        in_specs=[pl.BlockSpec(memory_space=pltpu.SMEM), vmem, vmem, vmem],
        out_specs=[vmem, vmem],
        out_shape=[out, out],
        compiler_params=params(60),
        cost_estimate=pl.CostEstimate(flops=2_000_000_000, bytes_accessed=3_000_000, transcendentals=0),
        name="pack_projection",
    )(where, w, gain_a.reshape(1, -1), gain_b.reshape(1, -1))


def pack_call(where, wo, wi, wd):
    vmem = pl.BlockSpec(memory_space=pltpu.VMEM)
    rows = half_of(wo.shape[0]) * (1 + wi.shape[1] // wo.shape[1]) + half_of(wd.shape[0])
    out = jax.ShapeDtypeStruct((rows, wo.shape[1]), BF)
    return pl.pallas_call(
        pack_kernel,
        in_specs=[pl.BlockSpec(memory_space=pltpu.SMEM), vmem, vmem, vmem],
        out_specs=[vmem, vmem],
        out_shape=[out, out],
        compiler_params=params(60),
        cost_estimate=pl.CostEstimate(flops=3_000_000_000, bytes_accessed=5_000_000, transcendentals=0),
        name="pack_weights",
    )(where, wo, wi, wd)


def fetch_qkv(place, pieces, w, sem):
    copies = []
    shard = w.shape[0] // (len(pieces) // 2)
    for t, piece in enumerate(pieces):
        copies.append(pltpu.make_async_copy(piece.at[:, 0 : w.shape[1]], w.at[pl.ds(row_of(place(t), shard), piece.shape[0]), :], sem.at[t]))
    return copies


def qkv_kernel(sz, n_pieces, scal, xl, xc, xr, *rest):
    pieces, (cos, sin, qkv, n1t, gains, w, sem) = rest[:n_pieces], rest[n_pieces:]
    i = pl.program_id(0)
    left_b, own_b = HALO // RB, sz.tok // RB
    own = (i >= left_b) & (i < left_b + own_b)

    @pl.when(i == 0)
    def _():
        copies = fetch_qkv(lambda t: scal[sz.places + t], pieces, w, sem)
        for c in copies:
            c.start()
        for c in copies:
            c.wait()
        side = w[:, 3 * sz.width :].astype(F32)
        for b in range(sz.width // LANES):
            gains[:, lanes_of(b)] = side[LANES * b : LANES * b + LANES, :].T[:8, :]

    @pl.when((i >= scal[sz.full_hi]) & (i < scal[sz.need_hi]))
    def _():
        qkv[...] = jnp.zeros_like(qkv)

    @pl.when((i >= scal[sz.need_lo]) & (i < scal[sz.full_hi]))
    def _():
        x = jnp.where(i < left_b, xl[...], jnp.where(i < left_b + own_b, xc[...], xr[...])).astype(F32)
        mean = jnp.mean(x, axis=-1, keepdims=True)
        cen = x - mean
        var = jnp.mean(cen * cen, axis=-1, keepdims=True)
        n1 = (cen * lax.rsqrt(var + EPS) * gains[0:1, :]).astype(BF)

        @pl.when(own)
        def _():
            n1t[...] = n1.T

        width = n1.shape[1]
        co, si = cos[...], sin[...]
        sc = HEAD_DIM ** -0.5 * LOG2E
        cq, sq = co * sc, si * sc
        for c in range(3 * width // 256):
            a = nn(n1, w[:, 256 * c : 256 * c + 256])
            part = 256 * c // width
            if part < 2:
                cc, ss = (cq, sq) if part == 0 else (co, si)
                halves = []
                for h in range(2):
                    b = a[:, 128 * h : 128 * h + 128]
                    halves.append((b * cc + partner(b) * ss).astype(BF))
                r = jnp.concatenate(halves, axis=1)
            else:
                r = a.astype(BF)
            qkv[:, 256 * c : 256 * c + 256] = r


def qkv_call(sz, scal, xl, xc, xr, pieces, cos, sin):
    tok, width, ext = sz.tok, sz.width, sz.ext
    own_b, lb = tok // RB, HALO // RB
    clampi = lambda lo, n: (lambda i, s: (jnp.clip(i - lo, 0, n - 1), 0))
    used = lambda i, s: jnp.clip(i, s[sz.need_lo], s[sz.need_hi] - 1)
    row = lambda i, s: (used(i, s), 0)
    fix = lambda i, s: (0, 0)
    sh = jax.ShapeDtypeStruct
    return pl.pallas_call(
        functools.partial(qkv_kernel, sz, len(pieces)),
        grid_spec=pltpu.PrefetchScalarGridSpec(
            num_scalar_prefetch=1,
            grid=(sz.blocks,),
            in_specs=[
                pl.BlockSpec((RB, width), clampi(0, lb)),
                pl.BlockSpec((RB, width), clampi(lb, own_b)),
                pl.BlockSpec((RB, width), clampi(lb + own_b, lb)),
                *[pl.BlockSpec(memory_space=pl.ANY)] * len(pieces),
                pl.BlockSpec((RB, LANES), row),
                pl.BlockSpec((RB, LANES), row),
            ],
            out_specs=[
                pl.BlockSpec((RB, 3 * width), row),
                pl.BlockSpec((width, RB), lambda i, s: (0, jnp.clip(i - lb, 0, own_b - 1))),
                pl.BlockSpec((8, width), fix),
            ],
            scratch_shapes=[pltpu.VMEM((width, 3 * width + LANES), BF), pltpu.SemaphoreType.DMA((len(pieces),))],
        ),
        out_shape=[sh((ext, 3 * width), BF), sh((width, tok), BF),
                   sh((8, width), F32)],
        compiler_params=params(60, dimension_semantics=("arbitrary",)),
        cost_estimate=pl.CostEstimate(flops=14_000_000_000, bytes_accessed=30_000_000, transcendentals=0),
        name="qkv",
    )(scal, xl, xc, xr, *pieces, cos, sin)


def split_heads(x):
    low = lax.broadcasted_iota(jnp.int32, x.shape, 1) < HEAD_DIM
    zero = jnp.zeros_like(x)
    return jnp.concatenate([jnp.where(low, x, zero), jnp.where(low, zero, x)], axis=0)


def lanes_of(p):
    return slice(LANES * p, LANES * p + LANES)


def fwd_kernel(sz, pg, scal, q, k, v, qf, kf, out, out_t, lse, q2, buf_a, buf_b, acc, tops):
    nq = sz.own_qb
    ones = jnp.ones((16, KB), BF)
    for qi in range(nq):
        r0 = HALO + qi * QB
        fq = qf[r0 : r0 + QB, :]
        f2 = jnp.concatenate([fq, fq], axis=0)
        for p in range(pg):
            q2[qi, p] = jnp.concatenate([split_heads(q[r0 : r0 + QB, lanes_of(p)]), f2], axis=1)

    def zero(i, _):
        for p in range(pg):
            acc[i, p] = jnp.zeros((LANES + 16, 2 * QB), F32)
            tops[i, p] = jnp.zeros((8, 2 * QB), F32)
        return 0

    lax.fori_loop(0, nq + 1, zero, 0)

    def scores(qi, k0, p, fk):
        return nt(jnp.concatenate([k[pl.ds(k0, KB), lanes_of(p)], fk], axis=1), q2[qi, p])

    def mixed(k0, p, probs):
        va = jnp.concatenate([v[pl.ds(k0, KB), lanes_of(p)].T, ones], axis=0)
        return nn(va, probs.astype(BF))

    def tile(i):
        return scal[sz.fwd_q + i], pl.multiple_of(scal[sz.fwd_k + i] * QB, QB)

    def score_tile(i, buf):
        qi, k0 = tile(i)
        qi = jnp.minimum(qi, nq - 1)
        fk = kf[pl.ds(k0, KB), :]
        for p in range(pg):
            buf[p] = scores(qi, k0, p, fk)

    def mix_tile(i, buf):
        qi, k0 = tile(i)
        for p in range(pg):
            acc[qi, p] += mixed(k0, p, jnp.exp2(buf[p]))

    score_tile(0, buf_a)

    def body(j, _):
        score_tile(2 * j + 1, buf_b)
        mix_tile(2 * j, buf_a)
        score_tile(2 * j + 2, buf_a)
        mix_tile(2 * j + 1, buf_b)
        return 0

    lax.fori_loop(0, (scal[sz.fwd_n] + 1) // 2, body, 0)

    low = high = acc[0, 0, LANES : LANES + 1, :]
    for qi in range(nq):
        for p in range(pg):
            total = acc[qi, p, LANES : LANES + 1, :]
            low, high = jnp.minimum(low, total), jnp.maximum(high, total)
    safe = (jnp.min(low) > 2.0 ** -60) & (jnp.max(high) < 2.0 ** 100)

    @pl.when(jnp.logical_not(safe))
    def _():
        lax.fori_loop(0, nq, zero, 0)

        def per_q(qi, _):
            lo, n = scal[sz.k_lo + sz.own_lo + qi], scal[sz.k_n + sz.own_lo + qi]
            for p in range(pg):
                def top(t, m):
                    k0 = pl.multiple_of(lo * QB + t * KB, QB)
                    return jnp.maximum(m, jnp.max(scores(qi, k0, p, kf[pl.ds(k0, KB), :]), axis=0, keepdims=True))

                m = lax.fori_loop(0, n, top, jnp.full((1, 2 * QB), BIG, F32))
                tops[qi, p] = jnp.broadcast_to(m, (8, 2 * QB))

                def add(t, _):
                    k0 = pl.multiple_of(lo * QB + t * KB, QB)
                    acc[qi, p] += mixed(k0, p, jnp.exp2(scores(qi, k0, p, kf[pl.ds(k0, KB), :]) - m))
                    return 0

                lax.fori_loop(0, n, add, 0)
            return 0

        lax.fori_loop(0, nq, per_q, 0)

    def finish(qi, _):
        o0 = pl.multiple_of(qi * QB, QB)
        for p in range(pg):
            a = acc[qi, p]
            total = a[LANES : LANES + 1, :]
            inv = 1.0 / total
            o_t = jnp.concatenate([a[:HEAD_DIM, :QB] * inv[:, :QB], a[HEAD_DIM:LANES, QB:] * inv[:, QB:]], axis=0).astype(BF)
            out_t[lanes_of(p), pl.ds(o0, QB)] = o_t
            out[pl.ds(o0, QB), lanes_of(p)] = o_t.T
            st = tops[qi, p, 0:1, :] + jnp.log2(total)
            lse[p, 0:1, pl.ds(o0, QB)] = st[:, :QB]
            lse[p, 1:2, pl.ds(o0, QB)] = st[:, QB:]
        return 0

    lax.fori_loop(0, nq, finish, 0)


def fwd_call(sz, scal, qkv, qf, kf, pg):
    ext, tok, width = sz.ext, sz.tok, sz.width
    pairs = width // LANES
    steps = pairs // pg
    wide = LANES * pg
    col = lambda off: (lambda i, s: (0, off + i))
    fix = lambda i, s: (0, 0)
    sh = jax.ShapeDtypeStruct
    return pl.pallas_call(
        functools.partial(fwd_kernel, sz, pg),
        grid_spec=pltpu.PrefetchScalarGridSpec(
            num_scalar_prefetch=1,
            grid=(steps,),
            in_specs=[
                pl.BlockSpec((ext, wide), col(0)),
                pl.BlockSpec((ext, wide), col(steps)),
                pl.BlockSpec((ext, wide), col(2 * steps)),
                pl.BlockSpec((ext, LANES), fix),
                pl.BlockSpec((ext, LANES), fix),
            ],
            out_specs=[
                pl.BlockSpec((tok, wide), col(0)),
                pl.BlockSpec((wide, tok), lambda i, s: (i, 0)),
                pl.BlockSpec((pg, 2, tok), lambda i, s: (i, 0, 0)),
            ],
            scratch_shapes=[
                pltpu.VMEM((sz.own_qb, pg, 2 * QB, 2 * LANES), BF),
                pltpu.VMEM((pg, KB, 2 * QB), F32),
                pltpu.VMEM((pg, KB, 2 * QB), F32),
                pltpu.VMEM((sz.own_qb + 1, pg, LANES + 16, 2 * QB), F32),
                pltpu.VMEM((sz.own_qb + 1, pg, 8, 2 * QB), F32),
            ],
        ),
        out_shape=[sh((tok, width), BF), sh((width, tok), BF), sh((pairs, 2, tok), F32)],
        compiler_params=params(60, dimension_semantics=("arbitrary",)),
        cost_estimate=pl.CostEstimate(flops=30_000_000_000, bytes_accessed=15_000_000, transcendentals=0),
        name="attn_forward",
    )(scal, qkv, qkv, qkv, qf, kf)


def fetch_mlp(place, pieces, wo, wi, wd, sem, width):
    copies = [], [], []
    shards = len(pieces) // 2
    half, half_d = half_of(wo.shape[0] // shards), half_of(wd.shape[0] // shards)
    t_cols = wi.shape[1] // width
    for t, piece in enumerate(pieces):
        row0 = row_of(place(t), wo.shape[0] // shards)
        row_d = row_of(place(t), wd.shape[0] // shards)
        copies[0].append(pltpu.make_async_copy(piece.at[0:half, :], wo.at[pl.ds(row0, half), :], sem.at[t, 0]))
        for j in range(t_cols):
            copies[1].append(pltpu.make_async_copy(
                piece.at[half * (j + 1) : half * (j + 2), :],
                wi.at[pl.ds(row0, half), width * j : width * j + width], sem.at[t, j + 1]))
        lo = half * (t_cols + 1)
        copies[2].append(pltpu.make_async_copy(piece.at[lo : lo + half_d, :], wd.at[pl.ds(row_d, half_d), :], sem.at[t, t_cols + 1]))
    return copies


def three_parts(v):
    high = v.astype(BF).astype(F32)
    middle = (v - high).astype(BF).astype(F32)
    return high, middle, v - high - middle


def mid_kernel(sz, n_pieces, scal, *refs):
    pieces, refs = refs[:n_pieces], refs[n_pieces:]
    wo, wi, wd, sem = refs[-4:]
    step = pl.program_id(0)

    @pl.when(step == 0)
    def _():
        copies = fetch_mlp(lambda t: scal[sz.places + t], pieces, wo, wi, wd, sem, wo.shape[1])
        for group in copies:
            for c in group:
                c.start()

        def wait(which):
            for c in copies[which]:
                c.wait()

        mid_body(sz, wait, wo, wi, wd, *refs[:-4])

    @pl.when(step != 0)
    def _():
        mid_body(sz, lambda which: None, wo, wi, wd, *refs[:-4])


def mid_body(sz, wait, wo, wi, wd, x, o, gy, g2, ind, lse, out, mt_o, gu_o, n2t_o, gh2b_o, go_o, left_o, right_o, dlt):
    ff = wd.shape[0]
    wait(0)
    h2 = x[...].astype(F32) + nn(o[...], wo[...])
    mean = jnp.mean(h2, axis=-1, keepdims=True)
    cen = h2 - mean
    r2 = lax.rsqrt(jnp.mean(cen * cen, axis=-1, keepdims=True) + EPS)
    nh = cen * r2
    g = g2[1:2, :]
    n2 = (nh * g).astype(BF)
    n2t_o[...] = n2.T
    gyb = gy[...]
    hidden = []
    wait(1)
    wait(2)
    step = 384
    for c in range(ff // step):
        lo = c * step
        a = nn(n2, wi[:, lo : lo + step])
        b = nn(n2, wi[:, ff + lo : ff + lo + step])
        gm = nt(gyb, wd[lo : lo + step, :])
        half = 0.5 * (1.0 + lax.erf(a * (2.0 ** -0.5)))
        gel = a * half
        mm = (gel * b).astype(BF)
        mt_o[lo : lo + step, :] = mm.T
        hidden.append(mm)
        dgel = half + a * (jnp.exp(-0.5 * a * a) * (1.0 / math.sqrt(2.0 * math.pi)))
        ga = (gm * b * dgel).astype(BF)
        gb = (gm * gel).astype(BF)
        gu_o[:, lo : lo + step] = ga
        gu_o[:, ff + lo : ff + lo + step] = gb
    out[...] = (h2 + nn(jnp.concatenate(hidden, axis=1), wd[...])).astype(BF)
    gn2 = nt(gu_o[...], wi[...])

    t = gn2 * g
    gh2 = gyb.astype(F32) + r2 * (t - jnp.mean(t, axis=-1, keepdims=True) - nh * jnp.mean(t * nh, axis=-1, keepdims=True))
    gb16 = gh2.astype(BF)
    gh2b_o[...] = gb16
    go = nt(gb16, wo[...]).astype(BF)
    go_o[...] = go
    prod = go.astype(F32) * o[...].astype(F32)
    hi = prod.astype(BF)
    lo_part = (prod - hi.astype(F32)).astype(BF)
    sums = nt(ind[...], hi) + nt(ind[...], lo_part)
    for p in range(dlt.shape[0]):
        dlt[p] = sums[2 * p : 2 * p + 2, :]
    heads = lse.shape[0] * 2
    top = jnp.concatenate([lse[p] for p in range(lse.shape[0])] + [jnp.zeros((STAT - heads, sums.shape[1]), F32)], axis=0)
    rows = [part for v in (top, sums) for part in three_parts(v)]
    rows.append(jnp.zeros((LANES - 6 * STAT, sums.shape[1]), F32))
    width = go.shape[1]
    stats = jnp.concatenate(rows, axis=0).T.astype(BF)
    step = pl.program_id(0)

    @pl.when(step < HALO // RB)
    def _():
        left_o[:, :width] = go
        left_o[:, width:] = stats

    @pl.when(step >= (sz.tok - HALO) // RB)
    def _():
        right_o[:, :width] = go
        right_o[:, width:] = stats


def mid_call(sz, scal, pieces, x, o, gy, g2, lse, ff):
    tok, width = x.shape
    heads = jnp.arange(16, dtype=jnp.int32)
    ind = (heads[:, None] == (jnp.arange(width, dtype=jnp.int32) // HEAD_DIM)[None, :]).astype(BF)
    row = lambda i, s: (i, 0)
    fix = lambda i, s: (0, 0)
    rs = lambda n: pl.BlockSpec((RB, n), row)
    cs = lambda n: pl.BlockSpec((n, RB), lambda i, s: (0, i))
    fs = lambda a: pl.BlockSpec(a.shape, fix)
    sh = jax.ShapeDtypeStruct
    n = len(pieces)
    stat = pl.BlockSpec((width // LANES, 2, RB), lambda i, s: (0, 0, i))
    halo = lambda lo: pl.BlockSpec((RB, width + LANES), lambda i, s: (jnp.clip(i - lo, 0, HALO // RB - 1), 0))
    halos = [halo(0), halo((tok - HALO) // RB)]
    return pl.pallas_call(
        functools.partial(mid_kernel, sz, n),
        grid_spec=pltpu.PrefetchScalarGridSpec(
            num_scalar_prefetch=1,
            grid=(tok // RB,),
            in_specs=[*[pl.BlockSpec(memory_space=pl.ANY)] * n, rs(width), rs(width), rs(width), fs(g2), fs(ind), stat],
            out_specs=[rs(width), cs(ff), rs(2 * ff), cs(width), rs(width), rs(width), *halos, stat],
            scratch_shapes=[pltpu.VMEM((width, width), BF), pltpu.VMEM((width, 2 * ff), BF), pltpu.VMEM((ff, width), BF),
                            pltpu.SemaphoreType.DMA((n, 2 * ff // width + 2))],
        ),
        out_shape=[sh((tok, width), BF), sh((ff, tok), BF), sh((tok, 2 * ff), BF), sh((width, tok), BF),
                   sh((tok, width), BF), sh((tok, width), BF),
                   sh((HALO, width + LANES), BF), sh((HALO, width + LANES), BF),
                   sh((width // LANES, 2, tok), F32)],
        compiler_params=params(60, dimension_semantics=("arbitrary",)),
        cost_estimate=pl.CostEstimate(flops=13_000_000_000 * 2, bytes_accessed=30_000_000, transcendentals=0),
        name="middle",
    )(scal, *pieces, x, o, gy, g2, ind, lse)


def put_halves(core, keep, send, rows0, values, n_group):
    rows = values.shape[0] // n_group
    half = half_of(rows)

    def store(first, second):
        for g in range(n_group):
            lo, hi = rows * g, rows * (g + 1)
            first[g, pl.ds(rows0, half), :] = values[lo : lo + half, :]
            second[g, pl.ds(rows0, half), :] = values[hi - half : hi, :]

    @pl.when(core == 0)
    def _():
        store(keep, send)

    @pl.when(core != 0)
    def _():
        store(send, keep)


def put_halves(core, keep, send, rows0, values, n_group):
    rows = values.shape[0] // n_group
    half = half_of(rows)

    def store(first, second):
        for g in range(n_group):
            lo, hi = rows * g, rows * (g + 1)
            first[g, pl.ds(rows0, half), :] = values[lo : lo + half, :]
            second[g, pl.ds(rows0, half), :] = values[hi - half : hi, :]

    @pl.when(core == 0)
    def _():
        store(keep, send)

    @pl.when(core != 0)
    def _():
        store(send, keep)


def in_grad_kernel(n_group, at, scal, n2t, gu, keep, send):
    half = half_of(n2t.shape[0] // n_group)
    row0 = pl.multiple_of(pl.program_id(0) * half, 16)
    put_halves(scal[at] % 2, keep, send, row0, nn(n2t[...], gu[...]).astype(BF), n_group)


def in_grad_call(sz, scal, n2t, gu, n_group):
    width, tok = n2t.shape
    n_cols = gu.shape[1] // width
    rows = n_cols * half_of(width // n_group)
    out = jax.ShapeDtypeStruct((n_group, rows, width), BF)
    return pl.pallas_call(
        functools.partial(in_grad_kernel, n_group, sz.places),
        grid_spec=pltpu.PrefetchScalarGridSpec(
            num_scalar_prefetch=1,
            grid=(n_cols,),
            in_specs=[pl.BlockSpec((width, tok), lambda j, s: (0, 0)), pl.BlockSpec((tok, width), lambda j, s: (0, j))],
            out_specs=[pl.BlockSpec((n_group, rows, width), lambda j, s: (0, 0, 0))] * 2,
        ),
        out_shape=[out, out],
        compiler_params=params(60, dimension_semantics=("arbitrary",)),
        cost_estimate=pl.CostEstimate(flops=8_000_000_000, bytes_accessed=10_000_000, transcendentals=0),
        name="in_weight_gradient",
    )(scal, n2t, gu)


def down_out_kernel(n_group, at, scal, mt, gy, ot_h, gh_h, keep, send, ot, gh, sem):
    copies = [pltpu.make_async_copy(ot_h, ot, sem.at[0]), pltpu.make_async_copy(gh_h, gh, sem.at[1])]
    for c in copies:
        c.start()
    put_halves(scal[at] % 2, keep, send, 0, nn(mt[...], gy[...]).astype(BF), n_group)
    for c in copies:
        c.wait()
    used = half_of(mt.shape[0] // n_group) + half_of(ot.shape[0] // n_group)
    put_halves(scal[at] % 2, keep, send, half_of(mt.shape[0] // n_group), nn(ot[...], gh[...]).astype(BF), n_group)
    if used < keep.shape[1]:
        for ref in (keep, send):
            ref[:, used:, :] = jnp.zeros((n_group, keep.shape[1] - used, keep.shape[2]), BF)


def down_out_call(sz, scal, mt, gy, ot, gh, n_group, rows):
    width, tok = ot.shape
    ff = mt.shape[0]
    out = jax.ShapeDtypeStruct((n_group, rows, width), BF)
    anyspec = pl.BlockSpec(memory_space=pl.ANY)
    fix = lambda j, s: (0, 0)
    return pl.pallas_call(
        functools.partial(down_out_kernel, n_group, sz.places),
        grid_spec=pltpu.PrefetchScalarGridSpec(
            num_scalar_prefetch=1,
            grid=(1,),
            in_specs=[pl.BlockSpec((ff, tok), fix), pl.BlockSpec((tok, width), fix), anyspec, anyspec],
            out_specs=[pl.BlockSpec((n_group, rows, width), lambda j, s: (0, 0, 0))] * 2,
            scratch_shapes=[pltpu.VMEM((width, tok), BF), pltpu.VMEM((tok, width), BF), pltpu.SemaphoreType.DMA((2,))],
        ),
        out_shape=[out, out],
        compiler_params=params(60, dimension_semantics=("arbitrary",)),
        cost_estimate=pl.CostEstimate(flops=100_000_000, bytes_accessed=100_000, transcendentals=0),
        name="down_out_weight_gradients",
    )(scal, mt, gy, ot, gh)


def bwd_kernel(sz, pg, at, n_group, scal, qkv_h, qf_h, kf_h, gl_h, gc_h, gr_h, cos_h, sin_h, n1t_h,
               lse_c, dlt_c, grad_h, keep_h, send_h, grad, keep, send,
               q, k, v, qf, kf, go, halo_st, cos, sin, n1t, q2, g2, gka, gva, gqa, st, s_a, p_a, s_b, p_b, sem, out_sem):
    n_qb, tok, width = sz.n_qb, sz.tok, sz.width
    wide = LANES * pg
    q_lo, q_hi = scal[sz.q_lo], scal[sz.q_hi]
    ext = q.shape[0]
    cols = lambda part: pl.ds(part * width + at * wide, wide)
    near, left = pl.ds(HALO, tok + QB), pl.ds(0, HALO)
    right, own = pl.ds(HALO + tok + QB, ext - HALO - tok - QB), pl.ds(HALO, tok)

    def rows(seg):
        return [(qkv_h.at[seg, cols(part)], dst.at[seg, :]) for part, dst in ((0, q), (1, k), (2, v))]

    near_q, *near_rest = rows(near)
    first = [(gc_h.at[:, cols(0)], go.at[own, :]), (qf_h, qf), near_q, (kf_h, kf), *near_rest]
    second = [*rows(left), *rows(right), (gl_h.at[:, cols(0)], go.at[left, :]),
              (gr_h.at[:, cols(0)], go.at[pl.ds(HALO + tok, HALO), :]),
              (gl_h.at[:, pl.ds(width, LANES)], halo_st.at[0]), (gr_h.at[:, pl.ds(width, LANES)], halo_st.at[1])]
    third = [(cos_h.at[own, :], cos), (sin_h.at[own, :], sin), (n1t_h, n1t)]
    copies = [pltpu.make_async_copy(a, b, sem.at[t]) for t, (a, b) in enumerate(first + second + third)]
    n_first, n_second = len(first), len(first) + len(second)
    for c in copies:
        c.start()

    for row, part in ((0, lse_c), (1, dlt_c)):
        for p in range(pg):
            for b in range(sz.own_qb):
                for h in range(2):
                    st[sz.own_lo + b, p, row : row + 1, QB * h : QB * h + QB] = part[p, h : h + 1, QB * b : QB * b + QB]

    def halo_stats(side, first):
        def one(i, _):
            rows_t = halo_st[side, pl.ds(pl.multiple_of((i - first) * QB, QB), QB), :].astype(F32).T
            for p in range(pg):
                for h in range(2):
                    for row in range(2):
                        lo = 3 * STAT * row + 2 * (pg * at + p) + h
                        parts = [rows_t[lo + STAT * t : lo + STAT * t + 1, :] for t in range(3)]
                        st[i, p, row : row + 1, QB * h : QB * h + QB] = parts[0] + parts[1] + parts[2]
            return 0

        return one

    for c in copies[:3]:
        c.wait()

    def prep(i, _):
        r0 = pl.multiple_of(i * QB, QB)
        fq = qf[pl.ds(r0, QB), :]
        f2 = jnp.concatenate([fq, fq], axis=0)
        for p in range(pg):
            q2[i, p] = jnp.concatenate([split_heads(q[pl.ds(r0, QB), lanes_of(p)]), f2], axis=1)
            g2[i, p] = split_heads(go[pl.ds(r0, QB), lanes_of(p)])
            gqa[i, p] = jnp.zeros((LANES, 2 * QB), F32)
            gka[p, pl.ds(r0, QB), :] = jnp.zeros((QB, LANES), F32)
            gva[p, pl.ds(r0, QB), :] = jnp.zeros((QB, LANES), F32)
        return 0

    lax.fori_loop(sz.own_lo, sz.own_hi, prep, 0)
    for c in copies[3:n_first]:
        c.wait()

    def run(where, for_keys, for_queries):
        def tile(i):
            return scal[where[0] + i], pl.multiple_of(scal[where[1] + i] * QB, QB)

        def score_tile(i, s_buf, p_buf):
            qi, k0 = tile(i)
            fk = kf[pl.ds(k0, KB), :]
            for p in range(pg):
                s_buf[p] = nt(jnp.concatenate([k[pl.ds(k0, KB), lanes_of(p)], fk], axis=1), q2[qi, p])
                p_buf[p] = nt(v[pl.ds(k0, KB), lanes_of(p)], g2[qi, p])

        def grad_tile(i, s_buf, p_buf):
            qi, k0 = tile(i)
            dead = jnp.where(i < scal[where[2]], 0.0, 1e38).astype(F32)
            for p in range(pg):
                pr = jnp.exp2(s_buf[p] - (st[qi, p, 0:1, :] + dead))
                ds = (pr * (p_buf[p] - st[qi, p, 1:2, :])).astype(BF)
                if for_keys:
                    gva[p, pl.ds(k0, KB), :] += nn(pr.astype(BF), g2[qi, p])
                    gka[p, pl.ds(k0, KB), :] += nn(ds, q2[qi, p, :, :LANES])
                if for_queries:
                    gqa[qi, p] += tn(k[pl.ds(k0, KB), lanes_of(p)], ds)

        @pl.when(scal[where[2]] > 0)
        def _():
            score_tile(0, s_a, p_a)

            def body(j, _):
                score_tile(2 * j + 1, s_b, p_b)
                grad_tile(2 * j, s_a, p_a)
                score_tile(2 * j + 2, s_a, p_a)
                grad_tile(2 * j + 1, s_b, p_b)
                return 0

            lax.fori_loop(0, (scal[where[2]] + 1) // 2, body, 0)

    run(sz.lists[0], True, True)
    for c in copies[n_first:n_second]:
        c.wait()
    lax.fori_loop(q_lo, sz.own_lo, prep, 0)
    lax.fori_loop(sz.own_hi, q_hi, prep, 0)
    lax.fori_loop(q_lo, sz.own_lo, halo_stats(0, 0), 0)
    lax.fori_loop(sz.own_hi, q_hi, halo_stats(1, sz.own_hi), 0)
    run(sz.lists[1], False, True)
    run(sz.lists[2], True, False)
    copies[n_second].wait()
    copies[n_second + 1].wait()

    sc = HEAD_DIM ** -0.5

    def finish(i, _):
        o0 = pl.multiple_of(i * QB, QB)
        r0 = pl.multiple_of(HALO + i * QB, QB)
        co, si = cos[pl.ds(o0, QB), :], sin[pl.ds(o0, QB), :]
        for p in range(pg):
            a = gqa[sz.own_lo + i, p]
            gt = jnp.concatenate([a[:HEAD_DIM, :QB], a[HEAD_DIM:, QB:]], axis=0).T * sc
            grad[pl.ds(o0, QB), LANES * p : LANES * p + LANES] = (gt * co - partner(gt) * si).astype(BF)
            b = gka[p, pl.ds(r0, QB), :] * LN2
            lo = wide + LANES * p
            grad[pl.ds(o0, QB), lo : lo + LANES] = (b * co - partner(b) * si).astype(BF)
            lo = 2 * wide + LANES * p
            grad[pl.ds(o0, QB), lo : lo + LANES] = gva[p, pl.ds(r0, QB), :].astype(BF)
        return 0

    lax.fori_loop(0, sz.own_qb, finish, 0)
    leaving = [pltpu.make_async_copy(grad, grad_h, out_sem.at[0])]
    leaving[0].start()
    copies[n_second + 2].wait()
    for part in range(3):
        lanes = slice(wide * part, wide * part + wide)
        values = nn(n1t[...], grad[:, lanes]).astype(BF)
        put_halves(scal[sz.places] % 2, keep.at[:, :, lanes], send.at[:, :, lanes], 0, values, n_group)
        for t, (a, b) in enumerate(((keep, keep_h), (send, send_h))):
            leaving.append(pltpu.make_async_copy(a.at[:, :, lanes], b.at[:, :, lanes], out_sem.at[1 + 2 * part + t]))
            leaving[-1].start()
    for c in leaving:
        c.wait()


def bwd_call(sz, scal, qkv, qf, kf, gl, gc, gr, lse, dlt, cos, sin, n1t, pg, at, n_group):
    ext, tok, width, n_qb = sz.ext, sz.tok, sz.width, sz.n_qb
    wide = LANES * pg
    half = half_of(width // n_group)
    spec = lambda shape, *idx: pl.BlockSpec(shape, lambda i, s: idx)
    sh = jax.ShapeDtypeStruct
    outs = [(tok, 3 * wide), (n_group, half, 3 * wide), (n_group, half, 3 * wide)]
    return pl.pallas_call(
        functools.partial(bwd_kernel, sz, pg, at, n_group),
        grid_spec=pltpu.PrefetchScalarGridSpec(
            num_scalar_prefetch=1,
            grid=(1,),
            in_specs=[pl.BlockSpec(memory_space=pl.ANY)] * 9
            + [spec((pg, 2, tok), at, 0, 0), spec((pg, 2, tok), at, 0, 0)],
            out_specs=[pl.BlockSpec(memory_space=pl.ANY)] * 3,
            scratch_shapes=[
                *[pltpu.VMEM(o, BF) for o in outs],
                *[pltpu.VMEM((ext, wide), BF)] * 3,
                pltpu.VMEM((ext, LANES), BF),
                pltpu.VMEM((ext, LANES), BF),
                pltpu.VMEM((tok + 2 * HALO, wide), BF),
                pltpu.VMEM((2, HALO, LANES), BF),
                pltpu.VMEM((tok, LANES), F32),
                pltpu.VMEM((tok, LANES), F32),
                pltpu.VMEM((width, tok), BF),
                pltpu.VMEM((n_qb, pg, 2 * QB, 2 * LANES), BF),
                pltpu.VMEM((n_qb, pg, 2 * QB, LANES), BF),
                pltpu.VMEM((pg, ext, LANES), F32),
                pltpu.VMEM((pg, ext, LANES), F32),
                pltpu.VMEM((n_qb, pg, LANES, 2 * QB), F32),
                pltpu.VMEM((n_qb, pg, 8, 2 * QB), F32),
                *[pltpu.VMEM((pg, KB, 2 * QB), F32)] * 4,
                pltpu.SemaphoreType.DMA((19,)),
                pltpu.SemaphoreType.DMA((7,)),
            ],
        ),
        out_shape=[sh(o, BF) for o in outs],
        compiler_params=params(60, dimension_semantics=("arbitrary",)),
        cost_estimate=pl.CostEstimate(flops=35_000_000_000, bytes_accessed=20_000_000, transcendentals=0),
        name="attn_backward",
    )(scal, qkv, qf, kf, gl, gc, gr, cos, sin, n1t, lse, dlt)


def gx_kernel(n_pieces, n_grads, at, scal, *refs):
    pieces, grads = refs[:n_pieces], refs[n_pieces : n_pieces + n_grads]
    x, gh2, g1, out, w, sem = refs[n_pieces + n_grads :]
    width = x.shape[1]
    step = pl.program_id(0)

    def body(wait):
        gn = None
        wide = grads[0].shape[1] // 3
        for part in range(3):
            wait(part)
            lhs = jnp.concatenate([grad[:, wide * part : wide * part + wide] for grad in grads], axis=1)
            term = nt(lhs, w[:, width * part : width * part + width])
            gn = term if gn is None else gn + term
        xf = x[...].astype(F32)
        mean = jnp.mean(xf, axis=-1, keepdims=True)
        cen = xf - mean
        r1 = lax.rsqrt(jnp.mean(cen * cen, axis=-1, keepdims=True) + EPS)
        nh = cen * r1
        t = gn * g1[0:1, :]
        gx = gh2[...].astype(F32) + r1 * (t - jnp.mean(t, axis=-1, keepdims=True) - nh * jnp.mean(t * nh, axis=-1, keepdims=True))
        out[...] = gx.astype(BF)

    @pl.when(step == 0)
    def _():
        shard = w.shape[0] // (n_pieces // 2)
        thirds = [[], [], []]
        for part in range(3):
            cols = pl.ds(width * part, width)
            for t, piece in enumerate(pieces):
                rows = pl.ds(row_of(scal[at + t], shard), piece.shape[0])
                thirds[part].append(pltpu.make_async_copy(piece.at[:, cols], w.at[rows, cols], sem.at[part, t]))
                thirds[part][-1].start()

        def wait(part):
            for c in thirds[part]:
                c.wait()

        body(wait)

    @pl.when(step != 0)
    def _():
        body(lambda part: None)


def gx_call(sz, scal, pieces, grads, x, gh2, g1):
    tok, width = x.shape
    row = lambda i, s: (i, 0)
    fix = lambda i, s: (0, 0)
    rs = pl.BlockSpec((RB, width), row)
    n = len(pieces)
    return pl.pallas_call(
        functools.partial(gx_kernel, n, len(grads), sz.places),
        grid_spec=pltpu.PrefetchScalarGridSpec(
            num_scalar_prefetch=1,
            grid=(tok // RB,),
            in_specs=[*[pl.BlockSpec(memory_space=pl.ANY)] * n,
                      *[pl.BlockSpec((RB, g.shape[1]), row) for g in grads],
                      rs, rs, pl.BlockSpec(g1.shape, fix)],
            out_specs=rs,
            scratch_shapes=[pltpu.VMEM((width, 3 * width), BF), pltpu.SemaphoreType.DMA((3, n))],
        ),
        out_shape=jax.ShapeDtypeStruct((tok, width), BF),
        compiler_params=params(60, dimension_semantics=("arbitrary",)),
        cost_estimate=pl.CostEstimate(flops=4_000_000_000, bytes_accessed=15_000_000, transcendentals=0),
        name="input_gradient",
    )(scal, *pieces, *grads, x, gh2, g1)


def gain_row(w, grad, gain):
    low = lambda v: v.astype(BF).astype(F32)
    total = jnp.sum(low(w) * grad, axis=1, keepdims=True)
    return jnp.broadcast_to(total, (total.shape[0], LANES)).T[0:1, :] / low(gain)


def in_core_order(core, mine, other, use):
    @pl.when(core == 0)
    def _():
        use(mine, other)

    @pl.when(core != 0)
    def _():
        use(other, mine)


def qkv_end_kernel(at, scal, t, s, w, gain, out, g_out):
    shard = w.shape[0]
    half = half_of(shard)
    wide = t.shape[1] // 3
    calls = t.shape[0] // half

    def use(first, second):
        for ref, lo in ((first, 0), (second, shard - half)):
            for j in range(calls):
                for part in range(3):
                    c = wide * (calls * part + j)
                    out[lo : lo + half, c : c + wide] = ref[half * j : half * j + half, wide * part : wide * part + wide].astype(F32)

    in_core_order(scal[at] % 2, t, s, use)
    g_out[...] = gain_row(w[...], out[...], gain[...])


def mlp_end_kernel(at, scal, t, s, w, gain, d_in, d_down, d_out, g_out):
    shard, shard_d, width = w.shape[0], d_down.shape[0], d_out.shape[1]
    half, half_d = half_of(shard), half_of(shard_d)
    n_cols = w.shape[1] // width

    def use(first, second):
        for ref, h in ((first, 0), (second, 1)):
            lo, lo_d = h * (shard - half), h * (shard_d - half_d)
            for j in range(n_cols):
                d_in[lo : lo + half, width * j : width * j + width] = ref[half * j : half * j + half, :].astype(F32)
            at_d = half * n_cols
            d_down[lo_d : lo_d + half_d, :] = ref[at_d : at_d + half_d, :].astype(F32)
            d_out[lo : lo + half, :] = ref[at_d + half_d : at_d + half_d + half, :].astype(F32)

    in_core_order(scal[at] % 2, t, s, use)
    g_out[...] = gain_row(w[...], d_in[...], gain[...])


def end_call(kernel, name, sz, scal, arrays, w, gain, shapes):
    smem = pl.BlockSpec(memory_space=pltpu.SMEM)
    vmem = pl.BlockSpec(memory_space=pltpu.VMEM)
    outs = [*shapes, (1, w.shape[0])]
    return pl.pallas_call(
        functools.partial(kernel, sz.places),
        in_specs=[smem] + [vmem] * (len(arrays) + 2),
        out_specs=[vmem] * len(outs),
        out_shape=[jax.ShapeDtypeStruct(o, F32) for o in outs],
        compiler_params=params(60),
        cost_estimate=pl.CostEstimate(flops=3_000_000_000, bytes_accessed=5_000_000, transcendentals=0),
        name=name,
    )(scal, *arrays, w, gain.reshape(1, -1))


class Net:
    def __init__(self, n_replica, n_group):
        self.n_replica, self.n_group, self.n_z = n_replica, n_group, n_replica // 2
        self.replica, self.group = lax.axis_index("replica"), lax.axis_index("group")
        self.core = self.replica & 1

    def shift(self, a, step):
        pairs = [(i, i + step) for i in range(self.n_replica) if 0 <= i + step < self.n_replica]
        return lax.ppermute(a, "replica", pairs)

    def core_swap(self, a):
        return lax.ppermute(a, "replica", [(i, i ^ 1) for i in range(self.n_replica)])

    def across(self, a, k):
        return lax.ppermute(a, "group", [(i, i ^ k) for i in range(self.n_group)])

    def across_swap(self, a, k):
        n = self.n_group
        pairs = [(r * n + g, (r ^ 1) * n + (g ^ k)) for r in range(self.n_replica) for g in range(n)]
        return lax.ppermute(a, ("replica", "group"), pairs)

    def gather_near(self, mine, other, relay=True):
        got = {(0, 0): mine, (0, 1): other}
        for k in (1, 2) if relay and self.n_group == 4 else range(1, self.n_group):
            got[k, 0] = self.across(mine, k)
        return got

    def gather_far(self, got):
        got = dict(got)
        if (self.n_group - 1, 0) not in got:
            got[3, 0] = self.across(got[2, 0], 1)
            got[3, 1] = self.across_swap(got[1, 0], 2)
        for k in range(1, self.n_group):
            if (k, 1) not in got:
                got[k, 1] = self.core_swap(got[k, 0])
        return [got[key] for key in sorted(got)]

    def parts(self, pairs):
        def part(k):
            at = lambda a: lax.dynamic_index_in_dim(a, self.group ^ k, 0, keepdims=False).astype(F32)
            return jnp.concatenate([at(keep) + at(got) for got, keep in pairs], axis=0)

        return [part(0)] + [part(k).astype(BF) for k in range(1, self.n_group)]

    def group_send(self, parts):
        return parts[0], [self.across(parts[k], k) for k in range(1, self.n_group)]

    def add(self, own, moved):
        for m in moved:
            own = own + m.astype(F32)
        return own

    def along(self, a, k):
        return lax.ppermute(a, "replica", [(i, i ^ (2 * k)) for i in range(self.n_replica)])

    def z_scatter(self, s):
        shares = s.reshape(self.n_z, s.shape[0] // self.n_z, s.shape[1])
        share = lambda k: lax.dynamic_index_in_dim(shares, (self.replica // 2) ^ k, 0, keepdims=False)
        return share(0), [self.along(share(k).astype(BF), k) for k in range(1, self.n_z)]

    def z_gather(self, own, moved, last=None):
        t = self.add(own, moved).astype(BF)
        return [t] + [self.along(t, k) for k in range(1, self.n_z if last is None else last + 1)]

    def z_join(self, shares):
        z = self.replica // 2
        return jnp.concatenate([lax.select_n(z, *[shares[j ^ i] for i in range(self.n_z)]) for j in range(self.n_z)], axis=0)


def on_device(tokens, cotangent, lengths, dealing, offsets, attn_gain, qkv_weight, out_weight,
              mlp_gain, in_weight, down_weight, *, n_replica, n_group):
    net = Net(n_replica, n_group)
    x, gy = tokens[0], cotangent[0]
    tok, width = x.shape
    ff = in_weight.shape[1] // 2
    sz = Sizes(tok, width)
    pairs = width // LANES
    pg = 3
    tie = lax.optimization_barrier

    where = jnp.stack([net.replica, net.group]).astype(jnp.int32)
    near = net.gather_near(*pack_qkv_call(where, qkv_weight, attn_gain, mlp_gain), relay=False)
    packs = pack_call(where, out_weight, in_weight, down_weight)
    scal, qf, kf, cos, sin = plan_call(sz, n_replica, n_group, where, lengths)
    near, packs, scal = tie((near, packs, scal))

    x_l = net.shift(x[tok - HALO :], 1)
    x_r = net.shift(x[:HALO], -1)
    qkv_pieces = net.gather_far(near)
    packs, qkv_pieces, x_l, x_r = tie((packs, qkv_pieces, x_l, x_r))

    near = net.gather_near(*packs)
    qkv, n1t, gains = qkv_call(sz, scal, x_l, x, x_r, qkv_pieces, cos, sin)
    near, qkv = tie((near, qkv))
    mlp_pieces = net.gather_far(near)
    o, ot, lse = fwd_call(sz, scal, qkv, qf, kf, pg)
    out, mt, gu, n2t, gh2b, go, to_left, to_right, dlt = mid_call(sz, scal, mlp_pieces, x, o, gy, gains, lse, ff)

    go_l = net.shift(to_right, 1)
    go_r = net.shift(to_left, -1)
    keep_i, send_i = in_grad_call(sz, scal, n2t, gu, n_group)
    used = half_of(width // n_group) + half_of(ff // n_group)
    rows = used + -(keep_i.shape[1] + used) % (8 * net.n_z)
    keep_d, send_d = down_out_call(sz, scal, mt, gy, ot, gh2b, n_group, rows)
    send_d, go_l, go_r = tie((send_d, go_l, go_r))
    mlp_parts = net.parts([(net.core_swap(send_i), keep_i), (net.core_swap(send_d), keep_d)])

    def attn_grad(at, dep):
        return bwd_call(sz, dep, qkv, qf, kf, go_l, go, go_r, lse, dlt, cos, sin, n1t, pg, at, n_group)

    scal, mlp_parts = tie((scal, mlp_parts))
    grad0, keep0, send0 = attn_grad(0, scal)
    mlp = net.group_send(mlp_parts)
    keep0, send0, mlp = tie((keep0, send0, mlp))
    parts0 = net.parts([(net.core_swap(send0), keep0)])
    mlp = net.z_scatter(net.add(*mlp))
    scal, parts0 = tie((scal, parts0))
    sum0 = net.group_send(parts0)
    grad1, keep1, send1 = attn_grad(1, scal)
    sum0, mlp, scal, send1 = tie((sum0, mlp, scal, send1))

    got1 = net.core_swap(send1)
    mlp = net.z_gather(*mlp, last=2)
    got1, sum0 = tie((got1, sum0))
    parts1, scal = tie((net.parts([(got1, keep1)]), scal))
    sum1 = net.group_send(parts1)
    gx = gx_call(sz, scal, qkv_pieces, [grad0, grad1], x, gh2b, gains)
    sum1, sum0, gx = tie((sum1, sum0, gx))
    rest, gx = tie((mlp[0], gx))
    sum1, mlp = tie((sum1, mlp))
    mlp = mlp + [net.along(rest, k) for k in range(3, net.n_z)]

    qkv_sum = net.z_scatter(jnp.concatenate([net.add(*sum0), net.add(*sum1)], axis=0))
    mlp_sum = net.z_join(mlp)
    qkv_sum, mlp_sum = tie((qkv_sum, mlp_sum))
    sib_mlp = net.core_swap(mlp_sum)
    qkv_sum = net.z_gather(*qkv_sum)

    shard, shard_d = width // n_group, ff // n_group
    d_in, d_down, d_out, d_g2 = end_call(mlp_end_kernel, "mlp_gradients_end", sz, scal, [mlp_sum, sib_mlp], in_weight, mlp_gain,
                                         [in_weight.shape, (shard_d, width), (shard, width)])
    qkv_sum, d_in = tie((qkv_sum, d_in))
    qkv_sum = net.z_join(qkv_sum)
    d_qkv, d_g1 = end_call(qkv_end_kernel, "qkv_gradient_end", sz, scal, [qkv_sum, net.core_swap(qkv_sum)], qkv_weight,
                           attn_gain, [qkv_weight.shape])
    return (out[None], gx[None], d_g1[0], d_qkv, d_out, d_g2[0], d_in, d_down)


def solution(mesh):
    body = functools.partial(on_device, n_replica=mesh.shape["replica"], n_group=mesh.shape["group"])
    return jax.shard_map(
        body,
        mesh=mesh,
        in_specs=(
            P("group", "replica", None),
            P("group", "replica", None),
            P("group", None),
            P("group", None),
            P("group", None, None),
            P("group"),
            P("group", None),
            P("group", None),
            P("group"),
            P("group", None),
            P("group", None),
        ),
        out_specs=(
            P("group", "replica", None),
            P("group", "replica", None),
            P("group"),
            P("group", None),
            P("group", None),
            P("group"),
            P("group", None),
            P("group", None),
        ),
        check_vma=False,
    )
```

```python
import functools
import math

import jax
import jax.numpy as jnp
from jax import lax
from jax.experimental import pallas as pl
from jax.experimental.pallas import tpu as pltpu
from jax.sharding import PartitionSpec as P

HEADS = 12
HEAD_DIM = 64
LANES = 128
HALO = 768
RB = 256
QB = 128
KB = 256
STAT = 16
EPS = 1e-05
BIG = -1e30
ROPE_BASE = 160000.0
LOG2E = 1.4426950408889634
LN2 = 0.6931471805599453
BF = jnp.bfloat16
F32 = jnp.float32


def nt(a, b):
    return lax.dot_general(a, b, (((1,), (1,)), ((), ())), preferred_element_type=F32)


def nn(a, b):
    return lax.dot_general(a, b, (((1,), (0,)), ((), ())), preferred_element_type=F32)


def tn(a, b):
    return lax.dot_general(a, b, (((0,), (0,)), ((), ())), preferred_element_type=F32)


def partner(x):
    lane = lax.broadcasted_iota(jnp.int32, x.shape, 1) % HEAD_DIM
    return jnp.where(lane < HEAD_DIM // 2, pltpu.roll(x, 96, 1), pltpu.roll(x, 32, 1))


def half_of(rows):
    return -(-rows // 32) * 16


def row_of(place, rows):
    return pl.multiple_of((place // 2) * rows + (place % 2) * (rows - half_of(rows)), 16)


def params(mib, **kw):
    return pltpu.CompilerParams(vmem_limit_bytes=mib * 1024 * 1024, **kw)


class Sizes:
    def __init__(self, tok, width):
        self.tok, self.width = tok, width
        self.ext = tok + 2 * HALO + RB
        self.n_qb = (tok + 2 * HALO) // QB
        self.own_qb, self.own_lo = tok // QB, HALO // QB
        self.own_hi = self.own_lo + self.own_qb
        tiles = -(-(QB + 2 * HALO + QB) // KB)
        self.cap_f = self.own_qb * tiles + 2
        halo_tiles = -(-(HALO + QB) // KB)
        caps = [self.own_qb * -(-tok // KB) + 2, 2 * self.own_qb * -(-HALO // KB) + 2, 2 * self.own_lo * halo_tiles + 2]
        self.k_lo, self.k_n = 0, self.n_qb
        self.q_lo, self.q_hi = 2 * self.n_qb, 2 * self.n_qb + 1
        self.need_lo, self.need_hi, self.full_hi = (2 * self.n_qb + i for i in (2, 3, 4))
        self.blocks = self.ext // RB
        self.fwd_q = self.full_hi + 1
        self.fwd_k, self.fwd_n = self.fwd_q + self.cap_f, self.fwd_q + 2 * self.cap_f
        self.lists, at = [], self.fwd_n + 1
        for cap in caps:
            self.lists.append((at, at + cap, at + 2 * cap))
            at += 2 * cap + 1
        self.places = at


def plan_kernel(sz, n_replica, n_group, where, lengths, scal, qf, kf, cos, sin, starts, k_end, seg_buf, pos_buf):
    n_seq = lengths.shape[1]
    total = n_replica * sz.tok
    replica, group = where[0], where[1]
    base = replica * sz.tok - HALO
    at = jnp.int32(0)
    for j in range(n_seq):
        starts[j] = at
        at = at + lengths[0, j]
    starts[n_seq] = at

    def first_of(g):
        f = jnp.int32(0)
        for j in range(n_seq):
            f = jnp.where(g >= starts[j], starts[j], f)
        return f

    def last_of(g):
        f = jnp.int32(total)
        for j in range(n_seq):
            f = jnp.where(g >= starts[j], starts[j + 1], f)
        return f

    own_a, own_b = base + HALO, base + HALO + sz.tok - 1
    first_a, last_a = first_of(own_a) - base, last_of(own_a) - base
    first_b, last_b = first_of(own_b) - base, last_of(own_b) - base
    q_lo, q_hi = first_a // QB, (last_b + QB - 1) // QB
    scal[sz.q_lo], scal[sz.q_hi] = q_lo, q_hi

    def block(i, _):
        e = i * QB
        left, right = i < sz.own_lo, i >= sz.own_hi
        lo = jnp.where(left, HALO, jnp.where(right, first_b, first_of(base + e) - base)) // QB
        hi = jnp.where(left, last_a, jnp.where(right, HALO + sz.tok, last_of(base + e + QB - 1) - base))
        n = (hi - lo * QB + (KB - 1)) // KB
        scal[sz.k_lo + i] = lo
        scal[sz.k_n + i] = jnp.where((i >= q_lo) & (i < q_hi), n, 0)
        k_end[i] = (hi + QB - 1) // QB
        return 0

    lax.fori_loop(0, sz.n_qb, block, 0)
    scal[sz.need_lo], scal[sz.need_hi] = first_a // RB, (last_b + KB - 1 + RB - 1) // RB
    scal[sz.full_hi] = (last_b + RB - 1) // RB

    step = KB // QB

    def emit(where, c, q, lo, n):
        def one(t, c):
            scal[where[0] + c] = q
            scal[where[1] + c] = lo + t * step
            return c + 1

        return lax.fori_loop(0, n, one, c)

    def close(where, c, q):
        scal[where[2]] = c
        for extra in range(2):
            scal[where[0] + c + extra] = q
            scal[where[1] + c + extra] = jnp.int32(sz.own_lo)

    fwd = (sz.fwd_q, sz.fwd_k, sz.fwd_n)
    both, far, back = sz.lists

    def own_block(i, counts):
        c_f, c_a, c_b = counts
        lo, end = scal[sz.k_lo + i], k_end[i]
        c_f = emit(fwd, c_f, i - sz.own_lo, lo, scal[sz.k_n + i])
        n = (jnp.maximum(sz.own_lo - lo, 0) + step - 1) // step
        c_b = emit(far, c_b, i, sz.own_lo - n * step, n)
        lo = jnp.maximum(lo, sz.own_lo)
        n = (jnp.minimum(end, sz.own_hi) - lo + step - 1) // step
        c_a = emit(both, c_a, i, lo, n)
        lo = lo + n * step
        c_b = emit(far, c_b, i, lo, (jnp.maximum(end - lo, 0) + step - 1) // step)
        return c_f, c_a, c_b

    zero = jnp.int32(0)
    c_f, c_a, c_b = lax.fori_loop(sz.own_lo, sz.own_hi, own_block, (zero, zero, zero))

    def halo_block(i, c):
        return emit(back, c, i, scal[sz.k_lo + i], scal[sz.k_n + i])

    c_c = lax.fori_loop(sz.own_hi, sz.n_qb, halo_block, lax.fori_loop(0, sz.own_lo, halo_block, zero))
    close(fwd, c_f, jnp.int32(sz.own_qb))
    for where_to, c in zip(sz.lists, (c_a, c_b, c_c)):
        close(where_to, c, jnp.int32(sz.own_lo))
    core = replica % 2
    for k in range(n_group):
        for h in range(2):
            scal[sz.places + 2 * k + h] = 2 * (group ^ k) + (core ^ h)

    half = HEAD_DIM // 2
    blocks = sz.ext // QB
    g = base + QB * lax.broadcasted_iota(jnp.int32, (blocks, QB), 0) + lax.broadcasted_iota(jnp.int32, (blocks, QB), 1)
    seg = jnp.full((blocks, QB), -1, jnp.int32)
    first = jnp.zeros((blocks, QB), jnp.int32)
    for j in range(n_seq):
        hit = g >= starts[j]
        seg = jnp.where(hit, j, seg)
        first = jnp.where(hit, starts[j], first)
    seg_buf[...] = jnp.where(g >= total, n_seq, seg) & 15
    pos_buf[...] = jnp.maximum(g - first, 0).astype(F32)
    freq = jnp.exp(lax.broadcasted_iota(jnp.int32, (half, QB), 0).astype(F32) * (-2.0 / HEAD_DIM * math.log(ROPE_BASE)))

    def rows(b, _):
        r0 = pl.multiple_of(b * QB, QB)
        hot = (seg_buf[pl.ds(b, 1), :] == lax.broadcasted_iota(jnp.int32, (LANES, QB), 0)).astype(F32).T
        qf[pl.ds(r0, QB), :] = (hot * BIG).astype(BF)
        lane = lax.broadcasted_iota(jnp.int32, (QB, LANES), 1)
        kf[pl.ds(r0, QB), :] = jnp.where(lane < 16, 1.0 - hot, 0.0).astype(BF)
        ang = freq * pos_buf[pl.ds(b, 1), :]
        co, si = jnp.cos(ang), jnp.sin(ang)
        cos[pl.ds(r0, QB), :] = jnp.concatenate([co] * 4, axis=0).T
        sin[pl.ds(r0, QB), :] = jnp.concatenate([-si, si, -si, si], axis=0).T
        return 0

    per = RB // QB
    lax.fori_loop(scal[sz.need_lo] * per, jnp.minimum(scal[sz.need_hi] * per, blocks), rows, 0)


def plan_call(sz, n_replica, n_group, where, lengths):
    sh = jax.ShapeDtypeStruct
    smem = pl.BlockSpec(memory_space=pltpu.SMEM)
    vmem = pl.BlockSpec(memory_space=pltpu.VMEM)
    n_seq = lengths.shape[1]
    return pl.pallas_call(
        functools.partial(plan_kernel, sz, n_replica, n_group),
        in_specs=[smem, smem],
        out_specs=[smem] + [vmem] * 4,
        out_shape=[sh((sz.places + 2 * n_group,), jnp.int32)] + [sh((sz.ext, LANES), BF)] * 2 + [sh((sz.ext, LANES), F32)] * 2,
        scratch_shapes=[pltpu.SMEM((n_seq + 1,), jnp.int32), pltpu.SMEM((sz.n_qb,), jnp.int32), pltpu.VMEM((sz.ext // QB, QB), jnp.int32), pltpu.VMEM((sz.ext // QB, QB), F32)],
        compiler_params=params(60),
        cost_estimate=pl.CostEstimate(flops=10_000_000_000, bytes_accessed=5_000_000, transcendentals=0),
        name="plan",
    )(where, lengths)


def pack_kernel(where, wo, wi, wd, mine, other):
    width = wo.shape[1]
    n_cols = wi.shape[1] // width

    def put(dst, h):
        at = 0
        for ref, col in [(wo, 0)] + [(wi, j) for j in range(n_cols)] + [(wd, 0)]:
            n = half_of(ref.shape[0])
            lo = h * (ref.shape[0] - n)
            dst[at : at + n, :] = ref[lo : lo + n, width * col : width * col + width].astype(BF)
            at += n

    @pl.when(where[0] % 2 == 0)
    def _():
        put(mine, 0)
        put(other, 1)

    @pl.when(where[0] % 2 != 0)
    def _():
        put(mine, 1)
        put(other, 0)


def pack_qkv_kernel(where, w, gain_a, gain_b, mine, other):
    width = w.shape[1]
    shard = w.shape[0]
    half = half_of(shard)
    side = jnp.concatenate([gain_a[...], gain_b[...], jnp.zeros((LANES - 2, shard), F32)], axis=0).T.astype(BF)

    def put(dst, h):
        lo = h * (shard - half)
        dst[:, :width] = w[lo : lo + half, :].astype(BF)
        dst[:, width:] = side[lo : lo + half, :]

    @pl.when(where[0] % 2 == 0)
    def _():
        put(mine, 0)
        put(other, 1)

    @pl.when(where[0] % 2 != 0)
    def _():
        put(mine, 1)
        put(other, 0)


def pack_qkv_call(where, w, gain_a, gain_b):
    vmem = pl.BlockSpec(memory_space=pltpu.VMEM)
    out = jax.ShapeDtypeStruct((half_of(w.shape[0]), w.shape[1] + LANES), BF)
    return pl.pallas_call(
        pack_qkv_kernel,
        in_specs=[pl.BlockSpec(memory_space=pltpu.SMEM), vmem, vmem, vmem],
        out_specs=[vmem, vmem],
        out_shape=[out, out],
        compiler_params=params(60),
        cost_estimate=pl.CostEstimate(flops=2_000_000_000, bytes_accessed=3_000_000, transcendentals=0),
        name="pack_projection",
    )(where, w, gain_a.reshape(1, -1), gain_b.reshape(1, -1))


def pack_call(where, wo, wi, wd):
    vmem = pl.BlockSpec(memory_space=pltpu.VMEM)
    rows = half_of(wo.shape[0]) * (1 + wi.shape[1] // wo.shape[1]) + half_of(wd.shape[0])
    out = jax.ShapeDtypeStruct((rows, wo.shape[1]), BF)
    return pl.pallas_call(
        pack_kernel,
        in_specs=[pl.BlockSpec(memory_space=pltpu.SMEM), vmem, vmem, vmem],
        out_specs=[vmem, vmem],
        out_shape=[out, out],
        compiler_params=params(60),
        cost_estimate=pl.CostEstimate(flops=3_000_000_000, bytes_accessed=5_000_000, transcendentals=0),
        name="pack_weights",
    )(where, wo, wi, wd)


def fetch_qkv(place, pieces, w, sem):
    copies = []
    shard = w.shape[0] // (len(pieces) // 2)
    for t, piece in enumerate(pieces):
        copies.append(pltpu.make_async_copy(piece.at[:, 0 : w.shape[1]], w.at[pl.ds(row_of(place(t), shard), piece.shape[0]), :], sem.at[t]))
    return copies


def qkv_kernel(sz, n_pieces, scal, xl, xc, xr, *rest):
    pieces, (cos, sin, qkv, n1t, gains, w, sem) = rest[:n_pieces], rest[n_pieces:]
    i = pl.program_id(0)
    left_b, own_b = HALO // RB, sz.tok // RB
    own = (i >= left_b) & (i < left_b + own_b)

    @pl.when(i == 0)
    def _():
        copies = fetch_qkv(lambda t: scal[sz.places + t], pieces, w, sem)
        for c in copies:
            c.start()
        for c in copies:
            c.wait()
        side = w[:, 3 * sz.width :].astype(F32)
        for b in range(sz.width // LANES):
            gains[:, lanes_of(b)] = side[LANES * b : LANES * b + LANES, :].T[:8, :]

    @pl.when((i >= scal[sz.full_hi]) & (i < scal[sz.need_hi]))
    def _():
        qkv[...] = jnp.zeros_like(qkv)

    @pl.when((i >= scal[sz.need_lo]) & (i < scal[sz.full_hi]))
    def _():
        x = jnp.where(i < left_b, xl[...], jnp.where(i < left_b + own_b, xc[...], xr[...])).astype(F32)
        mean = jnp.mean(x, axis=-1, keepdims=True)
        cen = x - mean
        var = jnp.mean(cen * cen, axis=-1, keepdims=True)
        n1 = (cen * lax.rsqrt(var + EPS) * gains[0:1, :]).astype(BF)

        @pl.when(own)
        def _():
            n1t[...] = n1.T

        width = n1.shape[1]
        co, si = cos[...], sin[...]
        sc = HEAD_DIM ** -0.5 * LOG2E
        cq, sq = co * sc, si * sc
        for c in range(3 * width // 256):
            a = nn(n1, w[:, 256 * c : 256 * c + 256])
            part = 256 * c // width
            if part < 2:
                cc, ss = (cq, sq) if part == 0 else (co, si)
                halves = []
                for h in range(2):
                    b = a[:, 128 * h : 128 * h + 128]
                    halves.append((b * cc + partner(b) * ss).astype(BF))
                r = jnp.concatenate(halves, axis=1)
            else:
                r = a.astype(BF)
            qkv[:, 256 * c : 256 * c + 256] = r


def qkv_call(sz, scal, xl, xc, xr, pieces, cos, sin):
    tok, width, ext = sz.tok, sz.width, sz.ext
    own_b, lb = tok // RB, HALO // RB
    clampi = lambda lo, n: (lambda i, s: (jnp.clip(i - lo, 0, n - 1), 0))
    used = lambda i, s: jnp.clip(i, s[sz.need_lo], s[sz.need_hi] - 1)
    row = lambda i, s: (used(i, s), 0)
    fix = lambda i, s: (0, 0)
    sh = jax.ShapeDtypeStruct
    return pl.pallas_call(
        functools.partial(qkv_kernel, sz, len(pieces)),
        grid_spec=pltpu.PrefetchScalarGridSpec(
            num_scalar_prefetch=1,
            grid=(sz.blocks,),
            in_specs=[
                pl.BlockSpec((RB, width), clampi(0, lb)),
                pl.BlockSpec((RB, width), clampi(lb, own_b)),
                pl.BlockSpec((RB, width), clampi(lb + own_b, lb)),
                *[pl.BlockSpec(memory_space=pl.ANY)] * len(pieces),
                pl.BlockSpec((RB, LANES), row),
                pl.BlockSpec((RB, LANES), row),
            ],
            out_specs=[
                pl.BlockSpec((RB, 3 * width), row),
                pl.BlockSpec((width, RB), lambda i, s: (0, jnp.clip(i - lb, 0, own_b - 1))),
                pl.BlockSpec((8, width), fix),
            ],
            scratch_shapes=[pltpu.VMEM((width, 3 * width + LANES), BF), pltpu.SemaphoreType.DMA((len(pieces),))],
        ),
        out_shape=[sh((ext, 3 * width), BF), sh((width, tok), BF),
                   sh((8, width), F32)],
        compiler_params=params(60, dimension_semantics=("arbitrary",)),
        cost_estimate=pl.CostEstimate(flops=14_000_000_000, bytes_accessed=30_000_000, transcendentals=0),
        name="qkv",
    )(scal, xl, xc, xr, *pieces, cos, sin)


def split_heads(x):
    low = lax.broadcasted_iota(jnp.int32, x.shape, 1) < HEAD_DIM
    zero = jnp.zeros_like(x)
    return jnp.concatenate([jnp.where(low, x, zero), jnp.where(low, zero, x)], axis=0)


def lanes_of(p):
    return slice(LANES * p, LANES * p + LANES)


def fwd_kernel(sz, pg, scal, q, k, v, qf, kf, out, out_t, lse, q2, buf_a, buf_b, acc, tops):
    nq = sz.own_qb
    ones = jnp.ones((16, KB), BF)
    for qi in range(nq):
        r0 = HALO + qi * QB
        fq = qf[r0 : r0 + QB, :]
        f2 = jnp.concatenate([fq, fq], axis=0)
        for p in range(pg):
            q2[qi, p] = jnp.concatenate([split_heads(q[r0 : r0 + QB, lanes_of(p)]), f2], axis=1)

    def zero(i, _):
        for p in range(pg):
            acc[i, p] = jnp.zeros((LANES + 16, 2 * QB), F32)
            tops[i, p] = jnp.zeros((8, 2 * QB), F32)
        return 0

    lax.fori_loop(0, nq + 1, zero, 0)

    def scores(qi, k0, p, fk):
        return nt(jnp.concatenate([k[pl.ds(k0, KB), lanes_of(p)], fk], axis=1), q2[qi, p])

    def mixed(k0, p, probs):
        va = jnp.concatenate([v[pl.ds(k0, KB), lanes_of(p)].T, ones], axis=0)
        return nn(va, probs.astype(BF))

    def tile(i):
        return scal[sz.fwd_q + i], pl.multiple_of(scal[sz.fwd_k + i] * QB, QB)

    def score_tile(i, buf):
        qi, k0 = tile(i)
        qi = jnp.minimum(qi, nq - 1)
        fk = kf[pl.ds(k0, KB), :]
        for p in range(pg):
            buf[p] = scores(qi, k0, p, fk)

    def mix_tile(i, buf):
        qi, k0 = tile(i)
        for p in range(pg):
            acc[qi, p] += mixed(k0, p, jnp.exp2(buf[p]))

    score_tile(0, buf_a)

    def body(j, _):
        score_tile(2 * j + 1, buf_b)
        mix_tile(2 * j, buf_a)
        score_tile(2 * j + 2, buf_a)
        mix_tile(2 * j + 1, buf_b)
        return 0

    lax.fori_loop(0, (scal[sz.fwd_n] + 1) // 2, body, 0)

    low = high = acc[0, 0, LANES : LANES + 1, :]
    for qi in range(nq):
        for p in range(pg):
            total = acc[qi, p, LANES : LANES + 1, :]
            low, high = jnp.minimum(low, total), jnp.maximum(high, total)
    safe = (jnp.min(low) > 2.0 ** -60) & (jnp.max(high) < 2.0 ** 100)

    @pl.when(jnp.logical_not(safe))
    def _():
        lax.fori_loop(0, nq, zero, 0)

        def per_q(qi, _):
            lo, n = scal[sz.k_lo + sz.own_lo + qi], scal[sz.k_n + sz.own_lo + qi]
            for p in range(pg):
                def top(t, m):
                    k0 = pl.multiple_of(lo * QB + t * KB, QB)
                    return jnp.maximum(m, jnp.max(scores(qi, k0, p, kf[pl.ds(k0, KB), :]), axis=0, keepdims=True))

                m = lax.fori_loop(0, n, top, jnp.full((1, 2 * QB), BIG, F32))
                tops[qi, p] = jnp.broadcast_to(m, (8, 2 * QB))

                def add(t, _):
                    k0 = pl.multiple_of(lo * QB + t * KB, QB)
                    acc[qi, p] += mixed(k0, p, jnp.exp2(scores(qi, k0, p, kf[pl.ds(k0, KB), :]) - m))
                    return 0

                lax.fori_loop(0, n, add, 0)
            return 0

        lax.fori_loop(0, nq, per_q, 0)

    def finish(qi, _):
        o0 = pl.multiple_of(qi * QB, QB)
        for p in range(pg):
            a = acc[qi, p]
            total = a[LANES : LANES + 1, :]
            inv = 1.0 / total
            o_t = jnp.concatenate([a[:HEAD_DIM, :QB] * inv[:, :QB], a[HEAD_DIM:LANES, QB:] * inv[:, QB:]], axis=0).astype(BF)
            out_t[lanes_of(p), pl.ds(o0, QB)] = o_t
            out[pl.ds(o0, QB), lanes_of(p)] = o_t.T
            st = tops[qi, p, 0:1, :] + jnp.log2(total)
            lse[p, 0:1, pl.ds(o0, QB)] = st[:, :QB]
            lse[p, 1:2, pl.ds(o0, QB)] = st[:, QB:]
        return 0

    lax.fori_loop(0, nq, finish, 0)


def fwd_call(sz, scal, qkv, qf, kf, pg):
    ext, tok, width = sz.ext, sz.tok, sz.width
    pairs = width // LANES
    steps = pairs // pg
    wide = LANES * pg
    col = lambda off: (lambda i, s: (0, off + i))
    fix = lambda i, s: (0, 0)
    sh = jax.ShapeDtypeStruct
    return pl.pallas_call(
        functools.partial(fwd_kernel, sz, pg),
        grid_spec=pltpu.PrefetchScalarGridSpec(
            num_scalar_prefetch=1,
            grid=(steps,),
            in_specs=[
                pl.BlockSpec((ext, wide), col(0)),
                pl.BlockSpec((ext, wide), col(steps)),
                pl.BlockSpec((ext, wide), col(2 * steps)),
                pl.BlockSpec((ext, LANES), fix),
                pl.BlockSpec((ext, LANES), fix),
            ],
            out_specs=[
                pl.BlockSpec((tok, wide), col(0)),
                pl.BlockSpec((wide, tok), lambda i, s: (i, 0)),
                pl.BlockSpec((pg, 2, tok), lambda i, s: (i, 0, 0)),
            ],
            scratch_shapes=[
                pltpu.VMEM((sz.own_qb, pg, 2 * QB, 2 * LANES), BF),
                pltpu.VMEM((pg, KB, 2 * QB), F32),
                pltpu.VMEM((pg, KB, 2 * QB), F32),
                pltpu.VMEM((sz.own_qb + 1, pg, LANES + 16, 2 * QB), F32),
                pltpu.VMEM((sz.own_qb + 1, pg, 8, 2 * QB), F32),
            ],
        ),
        out_shape=[sh((tok, width), BF), sh((width, tok), BF), sh((pairs, 2, tok), F32)],
        compiler_params=params(60, dimension_semantics=("arbitrary",)),
        cost_estimate=pl.CostEstimate(flops=30_000_000_000, bytes_accessed=15_000_000, transcendentals=0),
        name="attn_forward",
    )(scal, qkv, qkv, qkv, qf, kf)


def fetch_mlp(place, pieces, wo, wi, wd, sem, width):
    copies = [], [], []
    shards = len(pieces) // 2
    half, half_d = half_of(wo.shape[0] // shards), half_of(wd.shape[0] // shards)
    t_cols = wi.shape[1] // width
    for t, piece in enumerate(pieces):
        row0 = row_of(place(t), wo.shape[0] // shards)
        row_d = row_of(place(t), wd.shape[0] // shards)
        copies[0].append(pltpu.make_async_copy(piece.at[0:half, :], wo.at[pl.ds(row0, half), :], sem.at[t, 0]))
        for j in range(t_cols):
            copies[1].append(pltpu.make_async_copy(
                piece.at[half * (j + 1) : half * (j + 2), :],
                wi.at[pl.ds(row0, half), width * j : width * j + width], sem.at[t, j + 1]))
        lo = half * (t_cols + 1)
        copies[2].append(pltpu.make_async_copy(piece.at[lo : lo + half_d, :], wd.at[pl.ds(row_d, half_d), :], sem.at[t, t_cols + 1]))
    return copies


def three_parts(v):
    high = v.astype(BF).astype(F32)
    middle = (v - high).astype(BF).astype(F32)
    return high, middle, v - high - middle


def mid_kernel(sz, n_pieces, scal, *refs):
    pieces, refs = refs[:n_pieces], refs[n_pieces:]
    wo, wi, wd, sem = refs[-4:]
    step = pl.program_id(0)

    @pl.when(step == 0)
    def _():
        copies = fetch_mlp(lambda t: scal[sz.places + t], pieces, wo, wi, wd, sem, wo.shape[1])
        for group in copies:
            for c in group:
                c.start()

        def wait(which):
            for c in copies[which]:
                c.wait()

        mid_body(sz, wait, wo, wi, wd, *refs[:-4])

    @pl.when(step != 0)
    def _():
        mid_body(sz, lambda which: None, wo, wi, wd, *refs[:-4])


def mid_body(sz, wait, wo, wi, wd, x, o, gy, g2, ind, lse, out, mt_o, gu_o, n2t_o, gh2b_o, go_o, left_o, right_o, dlt):
    ff = wd.shape[0]
    wait(0)
    h2 = x[...].astype(F32) + nn(o[...], wo[...])
    mean = jnp.mean(h2, axis=-1, keepdims=True)
    cen = h2 - mean
    r2 = lax.rsqrt(jnp.mean(cen * cen, axis=-1, keepdims=True) + EPS)
    nh = cen * r2
    g = g2[1:2, :]
    n2 = (nh * g).astype(BF)
    n2t_o[...] = n2.T
    gyb = gy[...]
    hidden = []
    wait(1)
    wait(2)
    for lo, step in ((0, 768), (768, ff - 768)):
        a = nn(n2, wi[:, lo : lo + step])
        b = nn(n2, wi[:, ff + lo : ff + lo + step])
        gm = nt(gyb, wd[lo : lo + step, :])
        half = 0.5 * (1.0 + lax.erf(a * (2.0 ** -0.5)))
        gel = a * half
        mm = (gel * b).astype(BF)
        mt_o[lo : lo + step, :] = mm.T
        hidden.append(mm)
        dgel = half + a * (jnp.exp(-0.5 * a * a) * (1.0 / math.sqrt(2.0 * math.pi)))
        ga = (gm * b * dgel).astype(BF)
        gb = (gm * gel).astype(BF)
        gu_o[:, lo : lo + step] = ga
        gu_o[:, ff + lo : ff + lo + step] = gb
    out[...] = (h2 + nn(jnp.concatenate(hidden, axis=1), wd[...])).astype(BF)
    gn2 = nt(gu_o[...], wi[...])

    t = gn2 * g
    gh2 = gyb.astype(F32) + r2 * (t - jnp.mean(t, axis=-1, keepdims=True) - nh * jnp.mean(t * nh, axis=-1, keepdims=True))
    gb16 = gh2.astype(BF)
    gh2b_o[...] = gb16
    go = nt(gb16, wo[...]).astype(BF)
    go_o[...] = go
    prod = go.astype(F32) * o[...].astype(F32)
    hi = prod.astype(BF)
    lo_part = (prod - hi.astype(F32)).astype(BF)
    sums = nt(ind[...], hi) + nt(ind[...], lo_part)
    for p in range(dlt.shape[0]):
        dlt[p] = sums[2 * p : 2 * p + 2, :]
    heads = lse.shape[0] * 2
    top = jnp.concatenate([lse[p] for p in range(lse.shape[0])] + [jnp.zeros((STAT - heads, sums.shape[1]), F32)], axis=0)
    rows = [part for v in (top, sums) for part in three_parts(v)]
    rows.append(jnp.zeros((LANES - 6 * STAT, sums.shape[1]), F32))
    width = go.shape[1]
    stats = jnp.concatenate(rows, axis=0).T.astype(BF)
    step = pl.program_id(0)

    @pl.when(step < HALO // RB)
    def _():
        left_o[:, :width] = go
        left_o[:, width:] = stats

    @pl.when(step >= (sz.tok - HALO) // RB)
    def _():
        right_o[:, :width] = go
        right_o[:, width:] = stats


def mid_call(sz, scal, pieces, x, o, gy, g2, lse, ff):
    tok, width = x.shape
    heads = jnp.arange(16, dtype=jnp.int32)
    ind = (heads[:, None] == (jnp.arange(width, dtype=jnp.int32) // HEAD_DIM)[None, :]).astype(BF)
    row = lambda i, s: (i, 0)
    fix = lambda i, s: (0, 0)
    rs = lambda n: pl.BlockSpec((RB, n), row)
    cs = lambda n: pl.BlockSpec((n, RB), lambda i, s: (0, i))
    fs = lambda a: pl.BlockSpec(a.shape, fix)
    sh = jax.ShapeDtypeStruct
    n = len(pieces)
    stat = pl.BlockSpec((width // LANES, 2, RB), lambda i, s: (0, 0, i))
    halo = lambda lo: pl.BlockSpec((RB, width + LANES), lambda i, s: (jnp.clip(i - lo, 0, HALO // RB - 1), 0))
    halos = [halo(0), halo((tok - HALO) // RB)]
    return pl.pallas_call(
        functools.partial(mid_kernel, sz, n),
        grid_spec=pltpu.PrefetchScalarGridSpec(
            num_scalar_prefetch=1,
            grid=(tok // RB,),
            in_specs=[*[pl.BlockSpec(memory_space=pl.ANY)] * n, rs(width), rs(width), rs(width), fs(g2), fs(ind), stat],
            out_specs=[rs(width), cs(ff), rs(2 * ff), cs(width), rs(width), rs(width), *halos, stat],
            scratch_shapes=[pltpu.VMEM((width, width), BF), pltpu.VMEM((width, 2 * ff), BF), pltpu.VMEM((ff, width), BF),
                            pltpu.SemaphoreType.DMA((n, 2 * ff // width + 2))],
        ),
        out_shape=[sh((tok, width), BF), sh((ff, tok), BF), sh((tok, 2 * ff), BF), sh((width, tok), BF),
                   sh((tok, width), BF), sh((tok, width), BF),
                   sh((HALO, width + LANES), BF), sh((HALO, width + LANES), BF),
                   sh((width // LANES, 2, tok), F32)],
        compiler_params=params(60, dimension_semantics=("arbitrary",)),
        cost_estimate=pl.CostEstimate(flops=13_000_000_000 * 2, bytes_accessed=30_000_000, transcendentals=0),
        name="middle",
    )(scal, *pieces, x, o, gy, g2, ind, lse)


def put_halves(core, keep, send, rows0, values, n_group):
    rows = values.shape[0] // n_group
    half = half_of(rows)

    def store(first, second):
        for g in range(n_group):
            lo, hi = rows * g, rows * (g + 1)
            first[g, pl.ds(rows0, half), :] = values[lo : lo + half, :]
            second[g, pl.ds(rows0, half), :] = values[hi - half : hi, :]

    @pl.when(core == 0)
    def _():
        store(keep, send)

    @pl.when(core != 0)
    def _():
        store(send, keep)


def put_halves(core, keep, send, rows0, values, n_group):
    rows = values.shape[0] // n_group
    half = half_of(rows)

    def store(first, second):
        for g in range(n_group):
            lo, hi = rows * g, rows * (g + 1)
            first[g, pl.ds(rows0, half), :] = values[lo : lo + half, :]
            second[g, pl.ds(rows0, half), :] = values[hi - half : hi, :]

    @pl.when(core == 0)
    def _():
        store(keep, send)

    @pl.when(core != 0)
    def _():
        store(send, keep)


def in_grad_kernel(n_group, at, scal, n2t, gu, keep, send):
    half = half_of(n2t.shape[0] // n_group)
    row0 = pl.multiple_of(pl.program_id(0) * half, 16)
    put_halves(scal[at] % 2, keep, send, row0, nn(n2t[...], gu[...]).astype(BF), n_group)


def in_grad_call(sz, scal, n2t, gu, n_group):
    width, tok = n2t.shape
    n_cols = gu.shape[1] // width
    rows = n_cols * half_of(width // n_group)
    out = jax.ShapeDtypeStruct((n_group, rows, width), BF)
    return pl.pallas_call(
        functools.partial(in_grad_kernel, n_group, sz.places),
        grid_spec=pltpu.PrefetchScalarGridSpec(
            num_scalar_prefetch=1,
            grid=(n_cols,),
            in_specs=[pl.BlockSpec((width, tok), lambda j, s: (0, 0)), pl.BlockSpec((tok, width), lambda j, s: (0, j))],
            out_specs=[pl.BlockSpec((n_group, rows, width), lambda j, s: (0, 0, 0))] * 2,
        ),
        out_shape=[out, out],
        compiler_params=params(60, dimension_semantics=("arbitrary",)),
        cost_estimate=pl.CostEstimate(flops=8_000_000_000, bytes_accessed=10_000_000, transcendentals=0),
        name="in_weight_gradient",
    )(scal, n2t, gu)


def down_out_kernel(n_group, at, scal, mt, gy, ot_h, gh_h, keep, send, ot, gh, sem):
    copies = [pltpu.make_async_copy(ot_h, ot, sem.at[0]), pltpu.make_async_copy(gh_h, gh, sem.at[1])]
    for c in copies:
        c.start()
    put_halves(scal[at] % 2, keep, send, 0, nn(mt[...], gy[...]).astype(BF), n_group)
    for c in copies:
        c.wait()
    used = half_of(mt.shape[0] // n_group) + half_of(ot.shape[0] // n_group)
    put_halves(scal[at] % 2, keep, send, half_of(mt.shape[0] // n_group), nn(ot[...], gh[...]).astype(BF), n_group)
    if used < keep.shape[1]:
        for ref in (keep, send):
            ref[:, used:, :] = jnp.zeros((n_group, keep.shape[1] - used, keep.shape[2]), BF)


def down_out_call(sz, scal, mt, gy, ot, gh, n_group, rows):
    width, tok = ot.shape
    ff = mt.shape[0]
    out = jax.ShapeDtypeStruct((n_group, rows, width), BF)
    anyspec = pl.BlockSpec(memory_space=pl.ANY)
    fix = lambda j, s: (0, 0)
    return pl.pallas_call(
        functools.partial(down_out_kernel, n_group, sz.places),
        grid_spec=pltpu.PrefetchScalarGridSpec(
            num_scalar_prefetch=1,
            grid=(1,),
            in_specs=[pl.BlockSpec((ff, tok), fix), pl.BlockSpec((tok, width), fix), anyspec, anyspec],
            out_specs=[pl.BlockSpec((n_group, rows, width), lambda j, s: (0, 0, 0))] * 2,
            scratch_shapes=[pltpu.VMEM((width, tok), BF), pltpu.VMEM((tok, width), BF), pltpu.SemaphoreType.DMA((2,))],
        ),
        out_shape=[out, out],
        compiler_params=params(60, dimension_semantics=("arbitrary",)),
        cost_estimate=pl.CostEstimate(flops=100_000_000, bytes_accessed=100_000, transcendentals=0),
        name="down_out_weight_gradients",
    )(scal, mt, gy, ot, gh)


def bwd_kernel(sz, pg, at, n_group, scal, qkv_h, qf_h, kf_h, gl_h, gc_h, gr_h, cos_h, sin_h, n1t_h,
               lse_c, dlt_c, grad_h, keep_h, send_h, grad, keep, send,
               q, k, v, qf, kf, go, halo_st, cos, sin, n1t, q2, g2, gka, gva, gqa, st, s_a, p_a, s_b, p_b, sem, out_sem):
    n_qb, tok, width = sz.n_qb, sz.tok, sz.width
    wide = LANES * pg
    q_lo, q_hi = scal[sz.q_lo], scal[sz.q_hi]
    ext = q.shape[0]
    cols = lambda part: pl.ds(part * width + at * wide, wide)
    near, left = pl.ds(HALO, tok + QB), pl.ds(0, HALO)
    right, own = pl.ds(HALO + tok + QB, ext - HALO - tok - QB), pl.ds(HALO, tok)

    def rows(seg):
        return [(qkv_h.at[seg, cols(part)], dst.at[seg, :]) for part, dst in ((0, q), (1, k), (2, v))]

    near_q, *near_rest = rows(near)
    first = [(gc_h.at[:, cols(0)], go.at[own, :]), (qf_h, qf), near_q, (kf_h, kf), *near_rest]
    second = [*rows(left), *rows(right), (gl_h.at[:, cols(0)], go.at[left, :]),
              (gr_h.at[:, cols(0)], go.at[pl.ds(HALO + tok, HALO), :]),
              (gl_h.at[:, pl.ds(width, LANES)], halo_st.at[0]), (gr_h.at[:, pl.ds(width, LANES)], halo_st.at[1])]
    third = [(cos_h.at[own, :], cos), (sin_h.at[own, :], sin), (n1t_h, n1t)]
    copies = [pltpu.make_async_copy(a, b, sem.at[t]) for t, (a, b) in enumerate(first + second + third)]
    n_first, n_second = len(first), len(first) + len(second)
    for c in copies:
        c.start()

    for row, part in ((0, lse_c), (1, dlt_c)):
        for p in range(pg):
            for b in range(sz.own_qb):
                for h in range(2):
                    st[sz.own_lo + b, p, row : row + 1, QB * h : QB * h + QB] = part[p, h : h + 1, QB * b : QB * b + QB]

    def halo_stats(side, first):
        def one(i, _):
            rows_t = halo_st[side, pl.ds(pl.multiple_of((i - first) * QB, QB), QB), :].astype(F32).T
            for p in range(pg):
                for h in range(2):
                    for row in range(2):
                        lo = 3 * STAT * row + 2 * (pg * at + p) + h
                        parts = [rows_t[lo + STAT * t : lo + STAT * t + 1, :] for t in range(3)]
                        st[i, p, row : row + 1, QB * h : QB * h + QB] = parts[0] + parts[1] + parts[2]
            return 0

        return one

    for c in copies[:3]:
        c.wait()

    def prep(i, _):
        r0 = pl.multiple_of(i * QB, QB)
        fq = qf[pl.ds(r0, QB), :]
        f2 = jnp.concatenate([fq, fq], axis=0)
        for p in range(pg):
            q2[i, p] = jnp.concatenate([split_heads(q[pl.ds(r0, QB), lanes_of(p)]), f2], axis=1)
            g2[i, p] = split_heads(go[pl.ds(r0, QB), lanes_of(p)])
            gqa[i, p] = jnp.zeros((LANES, 2 * QB), F32)
            gka[p, pl.ds(r0, QB), :] = jnp.zeros((QB, LANES), F32)
            gva[p, pl.ds(r0, QB), :] = jnp.zeros((QB, LANES), F32)
        return 0

    lax.fori_loop(sz.own_lo, sz.own_hi, prep, 0)
    for c in copies[3:n_first]:
        c.wait()

    def run(where, for_keys, for_queries):
        def tile(i):
            return scal[where[0] + i], pl.multiple_of(scal[where[1] + i] * QB, QB)

        def score_tile(i, s_buf, p_buf):
            qi, k0 = tile(i)
            fk = kf[pl.ds(k0, KB), :]
            for p in range(pg):
                s_buf[p] = nt(jnp.concatenate([k[pl.ds(k0, KB), lanes_of(p)], fk], axis=1), q2[qi, p])
                p_buf[p] = nt(v[pl.ds(k0, KB), lanes_of(p)], g2[qi, p])

        def grad_tile(i, s_buf, p_buf):
            qi, k0 = tile(i)
            dead = jnp.where(i < scal[where[2]], 0.0, 1e38).astype(F32)
            for p in range(pg):
                pr = jnp.exp2(s_buf[p] - (st[qi, p, 0:1, :] + dead))
                ds = (pr * (p_buf[p] - st[qi, p, 1:2, :])).astype(BF)
                if for_keys:
                    gva[p, pl.ds(k0, KB), :] += nn(pr.astype(BF), g2[qi, p])
                    gka[p, pl.ds(k0, KB), :] += nn(ds, q2[qi, p, :, :LANES])
                if for_queries:
                    gqa[qi, p] += tn(k[pl.ds(k0, KB), lanes_of(p)], ds)

        @pl.when(scal[where[2]] > 0)
        def _():
            score_tile(0, s_a, p_a)

            def body(j, _):
                score_tile(2 * j + 1, s_b, p_b)
                grad_tile(2 * j, s_a, p_a)
                score_tile(2 * j + 2, s_a, p_a)
                grad_tile(2 * j + 1, s_b, p_b)
                return 0

            lax.fori_loop(0, (scal[where[2]] + 1) // 2, body, 0)

    run(sz.lists[0], True, True)
    for c in copies[n_first:n_second]:
        c.wait()
    lax.fori_loop(q_lo, sz.own_lo, prep, 0)
    lax.fori_loop(sz.own_hi, q_hi, prep, 0)
    lax.fori_loop(q_lo, sz.own_lo, halo_stats(0, 0), 0)
    lax.fori_loop(sz.own_hi, q_hi, halo_stats(1, sz.own_hi), 0)
    run(sz.lists[1], False, True)
    run(sz.lists[2], True, False)
    copies[n_second].wait()
    copies[n_second + 1].wait()

    sc = HEAD_DIM ** -0.5

    def finish(i, _):
        o0 = pl.multiple_of(i * QB, QB)
        r0 = pl.multiple_of(HALO + i * QB, QB)
        co, si = cos[pl.ds(o0, QB), :], sin[pl.ds(o0, QB), :]
        for p in range(pg):
            a = gqa[sz.own_lo + i, p]
            gt = jnp.concatenate([a[:HEAD_DIM, :QB], a[HEAD_DIM:, QB:]], axis=0).T * sc
            grad[pl.ds(o0, QB), LANES * p : LANES * p + LANES] = (gt * co - partner(gt) * si).astype(BF)
            b = gka[p, pl.ds(r0, QB), :] * LN2
            lo = wide + LANES * p
            grad[pl.ds(o0, QB), lo : lo + LANES] = (b * co - partner(b) * si).astype(BF)
            lo = 2 * wide + LANES * p
            grad[pl.ds(o0, QB), lo : lo + LANES] = gva[p, pl.ds(r0, QB), :].astype(BF)
        return 0

    lax.fori_loop(0, sz.own_qb, finish, 0)
    leaving = [pltpu.make_async_copy(grad, grad_h, out_sem.at[0])]
    leaving[0].start()
    copies[n_second + 2].wait()
    for part in range(3):
        lanes = slice(wide * part, wide * part + wide)
        values = nn(n1t[...], grad[:, lanes]).astype(BF)
        put_halves(scal[sz.places] % 2, keep.at[:, :, lanes], send.at[:, :, lanes], 0, values, n_group)
        for t, (a, b) in enumerate(((keep, keep_h), (send, send_h))):
            leaving.append(pltpu.make_async_copy(a.at[:, :, lanes], b.at[:, :, lanes], out_sem.at[1 + 2 * part + t]))
            leaving[-1].start()
    for c in leaving:
        c.wait()


def bwd_call(sz, scal, qkv, qf, kf, gl, gc, gr, lse, dlt, cos, sin, n1t, pg, at, n_group):
    ext, tok, width, n_qb = sz.ext, sz.tok, sz.width, sz.n_qb
    wide = LANES * pg
    half = half_of(width // n_group)
    spec = lambda shape, *idx: pl.BlockSpec(shape, lambda i, s: idx)
    sh = jax.ShapeDtypeStruct
    outs = [(tok, 3 * wide), (n_group, half, 3 * wide), (n_group, half, 3 * wide)]
    return pl.pallas_call(
        functools.partial(bwd_kernel, sz, pg, at, n_group),
        grid_spec=pltpu.PrefetchScalarGridSpec(
            num_scalar_prefetch=1,
            grid=(1,),
            in_specs=[pl.BlockSpec(memory_space=pl.ANY)] * 9
            + [spec((pg, 2, tok), at, 0, 0), spec((pg, 2, tok), at, 0, 0)],
            out_specs=[pl.BlockSpec(memory_space=pl.ANY)] * 3,
            scratch_shapes=[
                *[pltpu.VMEM(o, BF) for o in outs],
                *[pltpu.VMEM((ext, wide), BF)] * 3,
                pltpu.VMEM((ext, LANES), BF),
                pltpu.VMEM((ext, LANES), BF),
                pltpu.VMEM((tok + 2 * HALO, wide), BF),
                pltpu.VMEM((2, HALO, LANES), BF),
                pltpu.VMEM((tok, LANES), F32),
                pltpu.VMEM((tok, LANES), F32),
                pltpu.VMEM((width, tok), BF),
                pltpu.VMEM((n_qb, pg, 2 * QB, 2 * LANES), BF),
                pltpu.VMEM((n_qb, pg, 2 * QB, LANES), BF),
                pltpu.VMEM((pg, ext, LANES), F32),
                pltpu.VMEM((pg, ext, LANES), F32),
                pltpu.VMEM((n_qb, pg, LANES, 2 * QB), F32),
                pltpu.VMEM((n_qb, pg, 8, 2 * QB), F32),
                *[pltpu.VMEM((pg, KB, 2 * QB), F32)] * 4,
                pltpu.SemaphoreType.DMA((19,)),
                pltpu.SemaphoreType.DMA((7,)),
            ],
        ),
        out_shape=[sh(o, BF) for o in outs],
        compiler_params=params(60, dimension_semantics=("arbitrary",)),
        cost_estimate=pl.CostEstimate(flops=35_000_000_000, bytes_accessed=20_000_000, transcendentals=0),
        name="attn_backward",
    )(scal, qkv, qf, kf, gl, gc, gr, cos, sin, n1t, lse, dlt)


def gx_kernel(n_pieces, n_grads, at, scal, *refs):
    pieces, grads = refs[:n_pieces], refs[n_pieces : n_pieces + n_grads]
    x, gh2, g1, out, w, sem = refs[n_pieces + n_grads :]
    width = x.shape[1]
    step = pl.program_id(0)

    def body(wait):
        gn = None
        wide = grads[0].shape[1] // 3
        for part in range(3):
            wait(part)
            lhs = jnp.concatenate([grad[:, wide * part : wide * part + wide] for grad in grads], axis=1)
            term = nt(lhs, w[:, width * part : width * part + width])
            gn = term if gn is None else gn + term
        xf = x[...].astype(F32)
        mean = jnp.mean(xf, axis=-1, keepdims=True)
        cen = xf - mean
        r1 = lax.rsqrt(jnp.mean(cen * cen, axis=-1, keepdims=True) + EPS)
        nh = cen * r1
        t = gn * g1[0:1, :]
        gx = gh2[...].astype(F32) + r1 * (t - jnp.mean(t, axis=-1, keepdims=True) - nh * jnp.mean(t * nh, axis=-1, keepdims=True))
        out[...] = gx.astype(BF)

    @pl.when(step == 0)
    def _():
        shard = w.shape[0] // (n_pieces // 2)
        thirds = [[], [], []]
        for part in range(3):
            cols = pl.ds(width * part, width)
            for t, piece in enumerate(pieces):
                rows = pl.ds(row_of(scal[at + t], shard), piece.shape[0])
                thirds[part].append(pltpu.make_async_copy(piece.at[:, cols], w.at[rows, cols], sem.at[part, t]))
                thirds[part][-1].start()

        def wait(part):
            for c in thirds[part]:
                c.wait()

        body(wait)

    @pl.when(step != 0)
    def _():
        body(lambda part: None)


def gx_call(sz, scal, pieces, grads, x, gh2, g1):
    tok, width = x.shape
    row = lambda i, s: (i, 0)
    fix = lambda i, s: (0, 0)
    rs = pl.BlockSpec((RB, width), row)
    n = len(pieces)
    return pl.pallas_call(
        functools.partial(gx_kernel, n, len(grads), sz.places),
        grid_spec=pltpu.PrefetchScalarGridSpec(
            num_scalar_prefetch=1,
            grid=(tok // RB,),
            in_specs=[*[pl.BlockSpec(memory_space=pl.ANY)] * n,
                      *[pl.BlockSpec((RB, g.shape[1]), row) for g in grads],
                      rs, rs, pl.BlockSpec(g1.shape, fix)],
            out_specs=rs,
            scratch_shapes=[pltpu.VMEM((width, 3 * width), BF), pltpu.SemaphoreType.DMA((3, n))],
        ),
        out_shape=jax.ShapeDtypeStruct((tok, width), BF),
        compiler_params=params(60, dimension_semantics=("arbitrary",)),
        cost_estimate=pl.CostEstimate(flops=4_000_000_000, bytes_accessed=15_000_000, transcendentals=0),
        name="input_gradient",
    )(scal, *pieces, *grads, x, gh2, g1)


def gain_row(w, grad, gain):
    low = lambda v: v.astype(BF).astype(F32)
    total = jnp.sum(low(w) * grad, axis=1, keepdims=True)
    return jnp.broadcast_to(total, (total.shape[0], LANES)).T[0:1, :] / low(gain)


def in_core_order(core, mine, other, use):
    @pl.when(core == 0)
    def _():
        use(mine, other)

    @pl.when(core != 0)
    def _():
        use(other, mine)


def qkv_end_kernel(at, scal, t, s, w, gain, out, g_out):
    shard = w.shape[0]
    half = half_of(shard)
    wide = t.shape[1] // 3
    calls = t.shape[0] // half

    def use(first, second):
        for ref, lo in ((first, 0), (second, shard - half)):
            for j in range(calls):
                for part in range(3):
                    c = wide * (calls * part + j)
                    out[lo : lo + half, c : c + wide] = ref[half * j : half * j + half, wide * part : wide * part + wide].astype(F32)

    in_core_order(scal[at] % 2, t, s, use)
    g_out[...] = gain_row(w[...], out[...], gain[...])


def mlp_end_kernel(at, scal, t, s, w, gain, d_in, d_down, d_out, g_out):
    shard, shard_d, width = w.shape[0], d_down.shape[0], d_out.shape[1]
    half, half_d = half_of(shard), half_of(shard_d)
    n_cols = w.shape[1] // width

    def use(first, second):
        for ref, h in ((first, 0), (second, 1)):
            lo, lo_d = h * (shard - half), h * (shard_d - half_d)
            for j in range(n_cols):
                d_in[lo : lo + half, width * j : width * j + width] = ref[half * j : half * j + half, :].astype(F32)
            at_d = half * n_cols
            d_down[lo_d : lo_d + half_d, :] = ref[at_d : at_d + half_d, :].astype(F32)
            d_out[lo : lo + half, :] = ref[at_d + half_d : at_d + half_d + half, :].astype(F32)

    in_core_order(scal[at] % 2, t, s, use)
    g_out[...] = gain_row(w[...], d_in[...], gain[...])


def end_call(kernel, name, sz, scal, arrays, w, gain, shapes):
    smem = pl.BlockSpec(memory_space=pltpu.SMEM)
    vmem = pl.BlockSpec(memory_space=pltpu.VMEM)
    outs = [*shapes, (1, w.shape[0])]
    return pl.pallas_call(
        functools.partial(kernel, sz.places),
        in_specs=[smem] + [vmem] * (len(arrays) + 2),
        out_specs=[vmem] * len(outs),
        out_shape=[jax.ShapeDtypeStruct(o, F32) for o in outs],
        compiler_params=params(60),
        cost_estimate=pl.CostEstimate(flops=3_000_000_000, bytes_accessed=5_000_000, transcendentals=0),
        name=name,
    )(scal, *arrays, w, gain.reshape(1, -1))


class Net:
    def __init__(self, n_replica, n_group):
        self.n_replica, self.n_group, self.n_z = n_replica, n_group, n_replica // 2
        self.replica, self.group = lax.axis_index("replica"), lax.axis_index("group")
        self.core = self.replica & 1

    def shift(self, a, step):
        pairs = [(i, i + step) for i in range(self.n_replica) if 0 <= i + step < self.n_replica]
        return lax.ppermute(a, "replica", pairs)

    def core_swap(self, a):
        return lax.ppermute(a, "replica", [(i, i ^ 1) for i in range(self.n_replica)])

    def across(self, a, k):
        return lax.ppermute(a, "group", [(i, i ^ k) for i in range(self.n_group)])

    def across_swap(self, a, k):
        n = self.n_group
        pairs = [(r * n + g, (r ^ 1) * n + (g ^ k)) for r in range(self.n_replica) for g in range(n)]
        return lax.ppermute(a, ("replica", "group"), pairs)

    def gather_near(self, mine, other, relay=True):
        got = {(0, 0): mine, (0, 1): other}
        for k in (1, 2) if relay and self.n_group == 4 else range(1, self.n_group):
            got[k, 0] = self.across(mine, k)
        return got

    def gather_far(self, got):
        got = dict(got)
        if (self.n_group - 1, 0) not in got:
            got[3, 0] = self.across(got[2, 0], 1)
            got[3, 1] = self.across_swap(got[1, 0], 2)
        for k in range(1, self.n_group):
            if (k, 1) not in got:
                got[k, 1] = self.core_swap(got[k, 0])
        return [got[key] for key in sorted(got)]

    def parts(self, pairs):
        def part(k):
            at = lambda a: lax.dynamic_index_in_dim(a, self.group ^ k, 0, keepdims=False).astype(F32)
            return jnp.concatenate([at(keep) + at(got) for got, keep in pairs], axis=0)

        return [part(0)] + [part(k).astype(BF) for k in range(1, self.n_group)]

    def group_send(self, parts):
        return parts[0], [self.across(parts[k], k) for k in range(1, self.n_group)]

    def add(self, own, moved):
        for m in moved:
            own = own + m.astype(F32)
        return own

    def along(self, a, k):
        return lax.ppermute(a, "replica", [(i, i ^ (2 * k)) for i in range(self.n_replica)])

    def z_scatter(self, s):
        shares = s.reshape(self.n_z, s.shape[0] // self.n_z, s.shape[1])
        share = lambda k: lax.dynamic_index_in_dim(shares, (self.replica // 2) ^ k, 0, keepdims=False)
        return share(0), [self.along(share(k).astype(BF), k) for k in range(1, self.n_z)]

    def z_gather(self, own, moved, last=None):
        t = self.add(own, moved).astype(BF)
        return [t] + [self.along(t, k) for k in range(1, self.n_z if last is None else last + 1)]

    def z_join(self, shares):
        z = self.replica // 2
        return jnp.concatenate([lax.select_n(z, *[shares[j ^ i] for i in range(self.n_z)]) for j in range(self.n_z)], axis=0)


def on_device(tokens, cotangent, lengths, dealing, offsets, attn_gain, qkv_weight, out_weight,
              mlp_gain, in_weight, down_weight, *, n_replica, n_group):
    net = Net(n_replica, n_group)
    x, gy = tokens[0], cotangent[0]
    tok, width = x.shape
    ff = in_weight.shape[1] // 2
    sz = Sizes(tok, width)
    pairs = width // LANES
    pg = 3
    tie = lax.optimization_barrier

    where = jnp.stack([net.replica, net.group]).astype(jnp.int32)
    near = net.gather_near(*pack_qkv_call(where, qkv_weight, attn_gain, mlp_gain), relay=False)
    packs = pack_call(where, out_weight, in_weight, down_weight)
    scal, qf, kf, cos, sin = plan_call(sz, n_replica, n_group, where, lengths)
    near, packs, scal = tie((near, packs, scal))

    x_l = net.shift(x[tok - HALO :], 1)
    x_r = net.shift(x[:HALO], -1)
    qkv_pieces = net.gather_far(near)
    packs, qkv_pieces, x_l, x_r = tie((packs, qkv_pieces, x_l, x_r))

    near = net.gather_near(*packs)
    qkv, n1t, gains = qkv_call(sz, scal, x_l, x, x_r, qkv_pieces, cos, sin)
    near, qkv = tie((near, qkv))
    mlp_pieces = net.gather_far(near)
    o, ot, lse = fwd_call(sz, scal, qkv, qf, kf, pg)
    out, mt, gu, n2t, gh2b, go, to_left, to_right, dlt = mid_call(sz, scal, mlp_pieces, x, o, gy, gains, lse, ff)

    go_l = net.shift(to_right, 1)
    go_r = net.shift(to_left, -1)
    keep_i, send_i = in_grad_call(sz, scal, n2t, gu, n_group)
    used = half_of(width // n_group) + half_of(ff // n_group)
    rows = used + -(keep_i.shape[1] + used) % (8 * net.n_z)
    keep_d, send_d = down_out_call(sz, scal, mt, gy, ot, gh2b, n_group, rows)
    send_d, go_l, go_r = tie((send_d, go_l, go_r))
    mlp_parts = net.parts([(net.core_swap(send_i), keep_i), (net.core_swap(send_d), keep_d)])

    def attn_grad(at, dep):
        return bwd_call(sz, dep, qkv, qf, kf, go_l, go, go_r, lse, dlt, cos, sin, n1t, pg, at, n_group)

    scal, mlp_parts = tie((scal, mlp_parts))
    grad0, keep0, send0 = attn_grad(0, scal)
    mlp = net.group_send(mlp_parts)
    keep0, send0, mlp = tie((keep0, send0, mlp))
    parts0 = net.parts([(net.core_swap(send0), keep0)])
    mlp = net.z_scatter(net.add(*mlp))
    scal, parts0 = tie((scal, parts0))
    sum0 = net.group_send(parts0)
    grad1, keep1, send1 = attn_grad(1, scal)
    sum0, mlp, scal, send1 = tie((sum0, mlp, scal, send1))

    got1 = net.core_swap(send1)
    mlp = net.z_gather(*mlp, last=2)
    got1, sum0 = tie((got1, sum0))
    parts1, scal = tie((net.parts([(got1, keep1)]), scal))
    sum1 = net.group_send(parts1)
    gx = gx_call(sz, scal, qkv_pieces, [grad0, grad1], x, gh2b, gains)
    sum1, sum0, gx = tie((sum1, sum0, gx))
    rest, gx = tie((mlp[0], gx))
    sum1, mlp = tie((sum1, mlp))
    mlp = mlp + [net.along(rest, k) for k in range(3, net.n_z)]

    qkv_sum = net.z_scatter(jnp.concatenate([net.add(*sum0), net.add(*sum1)], axis=0))
    mlp_sum = net.z_join(mlp)
    qkv_sum, mlp_sum = tie((qkv_sum, mlp_sum))
    sib_mlp = net.core_swap(mlp_sum)
    qkv_sum = net.z_gather(*qkv_sum)

    shard, shard_d = width // n_group, ff // n_group
    d_in, d_down, d_out, d_g2 = end_call(mlp_end_kernel, "mlp_gradients_end", sz, scal, [mlp_sum, sib_mlp], in_weight, mlp_gain,
                                         [in_weight.shape, (shard_d, width), (shard, width)])
    qkv_sum, d_in = tie((qkv_sum, d_in))
    qkv_sum = net.z_join(qkv_sum)
    d_qkv, d_g1 = end_call(qkv_end_kernel, "qkv_gradient_end", sz, scal, [qkv_sum, net.core_swap(qkv_sum)], qkv_weight,
                           attn_gain, [qkv_weight.shape])
    return (out[None], gx[None], d_g1[0], d_qkv, d_out, d_g2[0], d_in, d_down)


def solution(mesh):
    body = functools.partial(on_device, n_replica=mesh.shape["replica"], n_group=mesh.shape["group"])
    return jax.shard_map(
        body,
        mesh=mesh,
        in_specs=(
            P("group", "replica", None),
            P("group", "replica", None),
            P("group", None),
            P("group", None),
            P("group", None, None),
            P("group"),
            P("group", None),
            P("group", None),
            P("group"),
            P("group", None),
            P("group", None),
        ),
        out_specs=(
            P("group", "replica", None),
            P("group", "replica", None),
            P("group"),
            P("group", None),
            P("group", None),
            P("group"),
            P("group", None),
            P("group", None),
        ),
        check_vma=False,
    )
```
